32 devices in a mesh: rows: 8 (over y, x, core), mlp: 4 (over z).
Axes of the slice: x: 2, y: 2, z: 4, core: 2. Of those that a mesh axis runs over, the one named last changes fastest.
Arguments:
- images: bfloat16 [64, 197, 768], P(('rows', 'mlp')), may hold values from -6 to 6
- patch_rank: int32 [64, 197], P(('rows', 'mlp')), may hold values from 0 to 196, each once within a row
- kept_count: int32 [64], P(('rows', 'mlp')), may hold values from 98 to 197
- ln1_gain: float32 [768], replicated, may hold values from 0.1 to 1.9
- router_weight: bfloat16 [768], replicated, may hold values from -0.21875 to 0.21875
- w_qkv: bfloat16 [768, 2304], replicated, may hold values from -0.21875 to 0.21875
- w_out: bfloat16 [768, 768], replicated, may hold values from -2.5 to 2.5
- ln2_gain: float32 [768], replicated, may hold values from 0.1 to 1.9
- w_fc1: bfloat16 [768, 3072], P(None, 'mlp'), may hold values from -0.21875 to 0.21875
- w_fc2: bfloat16 [3072, 768], P('mlp'), may hold values from -0.109375 to 0.109375
- cotangent: bfloat16 [64, 197, 768], P(('rows', 'mlp')), may hold values from -6 to 6
Outputs:
- block_out: bfloat16 [64, 197, 768], P(('rows', 'mlp'))
- grad_images: bfloat16 [64, 197, 768], P(('rows', 'mlp'))
- grad_ln1_gain: float32 [768], replicated
- grad_router: float32 [768], replicated
- grad_qkv: float32 [768, 2304], replicated
- grad_out: float32 [768, 768], replicated
- grad_ln2_gain: float32 [768], replicated
- grad_fc1: float32 [768, 3072], P(None, 'mlp')
- grad_fc2: float32 [3072, 768], P('mlp')
The draws below stay inside these ranges and needn't reach their ends.
All inputs are finite; a program needn't handle non-finite values.
Results may differ from the reference program's by a relative error of at most 0.012.
The reference program's roundings to bfloat16 on the way count: a program that leaves them out, or rounds other values in their place, can miss the bound.
Values may be sent and summed in bfloat16 or wider, within the bound.
A program may use at most 128 MiB of HBM per device.

```python
import jax
import jax.numpy as jnp
from jax import lax

D = 768
FF = 3072
HEADS = 12
HEAD = 64
PATCH = 197
IMG_DEV = 2
IMAGES = 64
N_MLP = 4


def touch_ends(array, rng, least, high):
    shape = array.shape
    spot = [jax.random.randint(jax.random.fold_in(rng, axis), (), 0, shape[axis]) for axis in range(len(shape))]
    array = array.at[tuple(spot)].set(least)
    longest = shape.index(max(shape))
    spot[longest] = (spot[longest] + 1) % shape[longest]
    return array.at[tuple(spot)].set(high)


def shard_levels(own_key, dims, split, smallest, high):
    factor_of = 1.0
    for position, blocks in split:
        steps = jax.random.uniform(jax.random.fold_in(jax.random.fold_in(own_key, 6), position), (blocks,), jnp.float32, smallest / len(split), high / len(split))
        factor_of = factor_of * jnp.repeat(jnp.exp(steps), dims[position] // blocks).reshape((-1,) + (1,) * (len(dims) - 1 - position))
    return factor_of


def bell_draw(key, dims, scale, limit, cuts=(), dtype=jnp.bfloat16):
    entries = scale * jax.random.normal(key, dims, jnp.float32)
    if cuts:
        entries = entries * shard_levels(key, dims, cuts, -0.22, 0.18)
    return jnp.clip(entries, -limit, limit).astype(dtype)


def setup_inputs(seed: int = 0) -> dict:
    splits = jax.random.split(jax.random.key(seed), 12)
    images = bell_draw(splits[0], (IMAGES, PATCH, D), 1.0, 6.0, ((0, 32),))
    patch_rank = jax.vmap(lambda own: jax.random.permutation(own, PATCH))(jax.random.split(splits[1], IMAGES)).reshape((IMAGES, PATCH)).astype(jnp.int32)
    kept_count = touch_ends(jax.random.randint(splits[2], (IMAGES,), PATCH // 2, PATCH + 1), jax.random.fold_in(splits[2], 1), PATCH // 2, PATCH).astype(jnp.int32)
    ln1_gain = jnp.clip(1.0 + 0.18 * jax.random.normal(splits[3], (D,), jnp.float32), 0.1, 1.9)
    router_weight = bell_draw(splits[4], (D,), D ** -0.5, 0.21875)
    w_qkv = bell_draw(splits[5], (D, 3 * D), D ** -0.5, 0.21875)
    w_out = bell_draw(splits[6], (D, D), (max(D // 128, 1)) ** -0.5, 2.5)
    ln2_gain = jnp.clip(1.0 + 0.18 * jax.random.normal(splits[7], (D,), jnp.float32), 0.1, 1.9)
    w_fc1 = bell_draw(splits[8], (D, FF), D ** -0.5, 0.21875, ((1, 4),))
    w_fc2 = bell_draw(splits[9], (FF, D), FF ** -0.5, 0.109375, ((0, 4),))
    cotangent = bell_draw(splits[10], (IMAGES, PATCH, D), 1.0, 6.0, ((0, 32),))
    return dict(images=images, patch_rank=patch_rank, kept_count=kept_count, ln1_gain=ln1_gain, router_weight=router_weight, w_qkv=w_qkv, w_out=w_out, ln2_gain=ln2_gain, w_fc1=w_fc1, w_fc2=w_fc2, cotangent=cotangent)


epsilon = 1e-06
masked_fill = -1e+30
highest = lax.Precision.HIGHEST

@jax.custom_vjp
def low(v):
    return lax.optimization_barrier(v.astype(jnp.bfloat16)).astype(jnp.float32)

@jax.custom_vjp
def low_back(v):
    return v

def low_keep(v):
    return (low(v), None)

def low_pass(kept, grad):
    return (grad,)

def back_keep(v):
    return (v, None)

def back_low(kept, grad):
    return (low(grad),)
low.defvjp(low_keep, low_pass)
low_back.defvjp(back_keep, back_low)

def layer_norm(value, gain):
    center = value - lax.optimization_barrier(jnp.mean(value, -1, keepdims=True))
    return center * lax.rsqrt(lax.optimization_barrier(jnp.mean(center * center, -1, keepdims=True)) + epsilon) * gain

def attend(block):
    mixed, key_keep = block
    count = mixed.shape[0]
    queries = mixed[..., :D].reshape(count, PATCH, HEADS, HEAD)
    keys = mixed[..., D:2 * D].reshape(count, PATCH, HEADS, HEAD)
    values = mixed[..., 2 * D:].reshape(count, PATCH, HEADS, HEAD)
    scores = low_back(jnp.einsum('iqhd,ikhd->ihqk', queries, keys, precision=highest) * 0.125)
    scores = jnp.where(key_keep[:, None, None, :] > 0.5, scores, masked_fill)
    probs = low(jax.nn.softmax(scores, axis=-1))
    context = jnp.einsum('ihqk,ikhd->iqhd', probs, values, precision=highest)
    return low(low_back(context.reshape(count, PATCH, D)))

def forward(inputs, gain_one, router, weight_qkv, weight_out, gain_two, weight_up, weight_down, keep):
    normed = low(layer_norm(inputs, gain_one))
    gate = jax.nn.sigmoid(jnp.einsum('ipd,d->ip', normed, router, precision=highest))
    mixed = low(low_back(jnp.einsum('ipd,de->ipe', normed, weight_qkv, precision=highest)))
    block_images = IMG_DEV * N_MLP
    blocks = IMAGES // block_images
    context = lax.map(jax.checkpoint(attend), (mixed.reshape(blocks, block_images, PATCH, 3 * D), keep.reshape(blocks, block_images, PATCH)))
    context = context.reshape(IMAGES, PATCH, D)
    attended = low_back(jnp.einsum('ipd,de->ipe', context, weight_out, precision=highest))
    middle = inputs + (keep * gate)[..., None] * attended
    normed_two = low(layer_norm(middle, gain_two))
    pre = low_back(jnp.einsum('ipd,df->ipf', normed_two, weight_up, precision=highest))
    hidden = low(jax.nn.gelu(pre, approximate=False))
    return middle + jnp.einsum('ipf,fd->ipd', hidden, weight_down, precision=highest)

def reference(images, patch_rank, kept_count, ln1_gain, router_weight, w_qkv, w_out, ln2_gain, w_fc1, w_fc2, cotangent):
    keep = (patch_rank < kept_count[:, None]).astype(jnp.float32)

    def wrapped(inputs, gain_one, router, weight_qkv, weight_out, gain_two, weight_up, weight_down):
        return forward(inputs, gain_one, router, weight_qkv, weight_out, gain_two, weight_up, weight_down, keep)
    result, pullback = jax.vjp(wrapped, images.astype(jnp.float32), ln1_gain, router_weight.astype(jnp.float32), w_qkv.astype(jnp.float32), w_out.astype(jnp.float32), ln2_gain, w_fc1.astype(jnp.float32), w_fc2.astype(jnp.float32))
    grads = pullback(cotangent.astype(jnp.float32))
    return (result.astype(jnp.bfloat16), grads[0].astype(jnp.bfloat16), grads[1], grads[2], grads[3], grads[4], grads[5], grads[6], grads[7])
```

```python
import functools
import jax
import jax.numpy as jnp
from jax import lax
from jax.experimental import pallas as pl
from jax.experimental.pallas import tpu as pltpu
from jax.sharding import PartitionSpec as P

HEADS = 12
EPS = 1e-6
FILL = -1e30
BF = jnp.bfloat16
F32 = jnp.float32


def dot_nn(a, b):
    return lax.dot_general(a, b, (((1,), (0,)), ((), ())), preferred_element_type=F32)


def dot_nt(a, b):
    return lax.dot_general(a, b, (((1,), (1,)), ((), ())), preferred_element_type=F32)


def dot_tn(a, b):
    return lax.dot_general(a, b, (((0,), (0,)), ((), ())), preferred_element_type=F32)


def unit_rows(v):
    center = v - jnp.mean(v, -1, keepdims=True)
    scale = lax.rsqrt(jnp.mean(center * center, -1, keepdims=True) + EPS)
    return center * scale, scale


def norm_pull(dy, gain, unit, scale):
    du = dy * gain
    return scale * (
        du
        - jnp.mean(du, -1, keepdims=True)
        - unit * jnp.mean(du * unit, -1, keepdims=True)
    )


def half_mask(rows, h):
    lane = lax.broadcasted_iota(jnp.int32, (rows, 128), 1)
    return (lane < 64) if h == 0 else (lane >= 64)


def forward_rows(i, x_ref, rank_ref, kept_ref, g1_ref, rw_ref, xp, keep, gate, h1, h1t, work):
    patches, width = x_ref.shape[1:]
    tall = xp.shape[0] // x_ref.shape[0]
    rows = pl.ds(pl.multiple_of(i * tall, 16), tall)
    work[...] = jnp.zeros_like(work)
    work[0:patches, :] = x_ref[i]
    v = work[...]
    xp[rows, :] = v
    kept = (rank_ref[pl.ds(i, 1), :] < kept_ref[i]).astype(F32)
    keep_row = jnp.concatenate([kept, jnp.zeros((1, 256 - patches), F32)], 1)
    keep_col = jnp.broadcast_to(keep_row, (128, 256)).T
    keep[rows, :] = keep_col[0:tall, :]
    unit, _ = unit_rows(v.astype(F32))
    low = (unit * g1_ref[...]).astype(BF)
    h1[rows, :] = low
    logit = jnp.sum(low.astype(F32) * rw_ref[...].astype(F32), -1, keepdims=True)
    gate[rows, :] = jnp.broadcast_to(jax.nn.sigmoid(logit), (tall, 128))


def forward_qkv(j, h1, wqkv, qkv):
    cols = pl.ds(pl.multiple_of(j * 256, 256), 256)
    qkv[:, cols] = dot_nn(h1[...], wqkv[:, cols]).astype(BF)


def attend(p, i, width, tall, qkv, keep, probs, context, contextt):
    rows = pl.ds(pl.multiple_of(i * tall, 16), tall)
    qc = pl.ds(pl.multiple_of(p * 128, 128), 128)
    kc = pl.ds(pl.multiple_of(width + p * 128, 128), 128)
    vc = pl.ds(pl.multiple_of(2 * width + p * 128, 128), 128)
    q, k, v = qkv[rows, qc], qkv[rows, kc], qkv[rows, vc]
    vt = v.T
    kept = keep[rows, 0:1] > 0.5
    outs = []
    for h in range(2):
        kh = jnp.where(half_mask(tall, h), k, jnp.zeros_like(k))
        s = jnp.where(kept, dot_nt(kh, q) * 0.125, FILL)
        e = jnp.exp(s - jnp.max(s, 0, keepdims=True))
        pr = e * (1.0 / jnp.sum(e, 0, keepdims=True))
        probs[i, p * 2 + h] = pr
        outs.append(dot_nn(vt[h * 64 : h * 64 + 64, :], pr.astype(BF)))
    ct = jnp.concatenate(outs, 0)
    contextt[i, pl.ds(pl.multiple_of(p * 128, 128), 128), :] = ct.astype(BF)
    context[rows, qc] = ct.T.astype(BF)


def forward_out(i, tall, context, wout, xp, keep, gate, g2_ref, attended, middle, h2):
    rows = pl.ds(pl.multiple_of(i * tall, 16), tall)
    att = dot_nn(context[rows, :], wout[...])
    attended[rows, :] = att
    mid = xp[rows, :].astype(F32) + keep[rows, 0:1] * gate[rows, 0:1] * att
    middle[rows, :] = mid
    unit, _ = unit_rows(mid)
    h2[rows, :] = (unit * g2_ref[...]).astype(BF)


def gelu_pair(pre):
    cdf = 0.5 * (1.0 + lax.erf(pre * 0.7071067811865476))
    pdf = jnp.exp(pre * pre * -0.5) * 0.3989422804014327
    return pre * cdf, cdf + pre * pdf


def mlp_rows(h, c, w1, w2):
    pre = dot_nn(h, w1)
    hidden, slope = gelu_pair(pre)
    grad = dot_nt(c, w2) * slope
    return hidden.astype(BF), grad.astype(BF)


def back_rows(i, tall, c_ref, gh2, middle, keep, gate, attended, g2_ref, gmid, gatt, glogit, dg2):
    rows = pl.ds(pl.multiple_of(i * tall, 16), tall)
    dy = gh2[rows, :]
    unit, scale = unit_rows(middle[rows, :])
    gm = c_ref[rows, :].astype(F32) + norm_pull(dy, g2_ref[...], unit, scale)
    gmid[rows, :] = gm
    dg2[...] += jnp.sum(dy * unit, 0, keepdims=True)
    k, g = keep[rows, 0:1], gate[rows, 0:1]
    kept = gm * k
    gatt[rows, :] = (kept * g).astype(BF)
    gl = jnp.sum(kept * attended[rows, :], -1, keepdims=True) * g * (1.0 - g)
    glogit[rows, :] = jnp.broadcast_to(gl, (tall, 128))


def attend_back(p, i, width, tall, qkv, probs, gctx, gqkv):
    rows = pl.ds(pl.multiple_of(i * tall, 16), tall)
    qc = pl.ds(pl.multiple_of(p * 128, 128), 128)
    kc = pl.ds(pl.multiple_of(width + p * 128, 128), 128)
    vc = pl.ds(pl.multiple_of(2 * width + p * 128, 128), 128)
    q, k, v = qkv[rows, qc], qkv[rows, kc], qkv[rows, vc]
    gc = gctx[rows, qc]
    kt = k.T
    gv, gk, gq = 0.0, 0.0, []
    for h in range(2):
        mask = half_mask(tall, h)
        zero = jnp.zeros_like(v)
        pr = probs[i, p * 2 + h]
        gp = dot_nt(jnp.where(mask, v, zero), gc)
        gs = (pr * (gp - jnp.sum(pr * gp, 0, keepdims=True))).astype(BF)
        gv = gv + dot_nn(pr.astype(BF), jnp.where(mask, gc, zero))
        gk = gk + dot_nn(gs, jnp.where(mask, q, zero))
        gq.append(dot_nn(kt[h * 64 : h * 64 + 64, :], gs))
    gqkv[p, rows, 0:128] = (jnp.concatenate(gq, 0).T * 0.125).astype(BF)
    gqkv[p, rows, 128:256] = (gk * 0.125).astype(BF)
    gqkv[p, rows, 256:384] = gv.astype(BF)


def pair_columns(wqkv, p, width):
    return jnp.concatenate(
        [wqkv[:, pl.ds(pl.multiple_of(b * width + p * 128, 128), 128)] for b in range(3)], 1
    )


def back_input(i, tall, gh1, glogit, rw_ref, xp, h1, g1_ref, gmid, gx_ref, dg1, drw):
    rows = pl.ds(pl.multiple_of(i * tall, 16), tall)
    patches = gx_ref.shape[1]
    gl = glogit[rows, 0:1]
    dy = gh1[rows, :] + gl * rw_ref[...].astype(F32)
    unit, scale = unit_rows(xp[rows, :].astype(F32))
    dg1[...] += jnp.sum(dy * unit, 0, keepdims=True)
    drw[...] += jnp.sum(h1[rows, :].astype(F32) * gl, 0, keepdims=True)
    out = gmid[rows, :] + norm_pull(dy, g1_ref[...], unit, scale)
    gx_ref[i] = out.astype(BF)[0:patches, :]


def forward_kernel(x_ref, rank_ref, kept_ref, g1_ref, rw_ref, wqkv, wout, g2_ref,
                   xp, keep, gate, h1, h1t, qkv, probs, contextt, attended, middle, h2, context, work):
    images = x_ref.shape[0]
    width = x_ref.shape[2]
    tall = xp.shape[0] // images

    @pl.loop(0, images)
    def _(i):
        forward_rows(i, x_ref, rank_ref, kept_ref, g1_ref, rw_ref, xp, keep, gate, h1, h1t, work)

    h1t[...] = h1[...].T

    @pl.loop(0, 3 * width // 256)
    def _(j):
        forward_qkv(j, h1, wqkv, qkv)

    @pl.loop(0, HEADS // 2)
    def _(p):
        for i in range(images):
            attend(p, i, width, tall, qkv, keep, probs, context, contextt)

    @pl.loop(0, images)
    def _(i):
        forward_out(i, tall, context, wout, xp, keep, gate, g2_ref, attended, middle, h2)


def mlp_kernel(h2, c_ref, middle, w1, w2, block_ref, cp, gh2, gf1, gf2, out, h2t, hid, gpre, work):
    images, patches, width = c_ref.shape
    tall = h2.shape[0] // images
    for i in range(images):
        work[...] = jnp.zeros_like(work)
        work[0:patches, :] = c_ref[i]
        cp[i * tall : (i + 1) * tall, :] = work[...]
    h2t[...] = h2[...].T
    out[...] = jnp.zeros_like(out)
    gh2[...] = jnp.zeros_like(gh2)

    @pl.loop(0, w1.shape[0])
    def _(k):
        for i in range(images):
            rows = slice(i * tall, (i + 1) * tall)
            hid[rows, :], gpre[rows, :] = mlp_rows(h2[rows, :], cp[rows, :], w1[k], w2[k])
            out[rows, :] += dot_nn(hid[rows, :], w2[k])
            gh2[rows, :] += dot_nt(gpre[rows, :], w1[k])
        gf1[k] = dot_nn(h2t[...], gpre[...]).astype(BF)
        gf2[k] = dot_tn(hid[...], cp[...]).astype(BF)

    for i in range(images):
        rows = slice(i * tall, (i + 1) * tall)
        block_ref[i] = (middle[rows, :] + out[rows, :]).astype(BF)[0:patches, :]


def back_kernel(cp, gh2, middle, keep, gate, attended, g2_ref, contextt, wout, wqkv, qkv, probs, h1, h1t, rw_ref, xp, g1_ref,
                gx_ref, gout, gqkv_w, small, gmid, gatt, glogit, gctx, gqkv, gh1, dg1, dg2, drw):
    images = gx_ref.shape[0]
    width = gx_ref.shape[2]
    tall = gh2.shape[0] // images
    for r in (dg1, dg2, drw):
        r[...] = jnp.zeros_like(r)

    @pl.loop(0, images)
    def _(i):
        back_rows(i, tall, cp, gh2, middle, keep, gate, attended, g2_ref, gmid, gatt, glogit, dg2)

    go = 0.0
    for i in range(images):
        go = go + dot_nn(contextt[i], gatt[i * tall : (i + 1) * tall, :])
    gout[...] = go.astype(BF)
    gctx[...] = dot_nt(gatt[...], wout[...]).astype(BF)
    gh1[...] = jnp.zeros_like(gh1)

    @pl.loop(0, HEADS // 2)
    def _(p):
        for i in range(images):
            attend_back(p, i, width, tall, qkv, probs, gctx, gqkv)
        gqkv_w[p] = dot_nn(h1t[...], gqkv[p]).astype(BF)
        gh1[...] += dot_nt(gqkv[p], pair_columns(wqkv, p, width))

    @pl.loop(0, images)
    def _(i):
        back_input(i, tall, gh1, glogit, rw_ref, xp, h1, g1_ref, gmid, gx_ref, dg1, drw)
    small[...] = jnp.concatenate([dg1[...], drw[...], dg2[...]], 1)


VMEM = pl.BlockSpec(memory_space=pltpu.VMEM)
SMEM = pl.BlockSpec(memory_space=pltpu.SMEM)
PARAMS = pltpu.CompilerParams(vmem_limit_bytes=60 * 1024 * 1024)


def shape(*dims, dtype=F32):
    return jax.ShapeDtypeStruct(dims, dtype)


def local_forward(images, patch_rank, kept_count, g1, rw, w_qkv, w_out, g2):
    count, patches, width = images.shape
    tall = -(-patches // 16) * 16
    t = count * tall
    outs = dict(
        xp=shape(t, width, dtype=BF), keep=shape(t, 128), gate=shape(t, 128), h1=shape(t, width, dtype=BF),
        h1t=shape(width, t, dtype=BF), qkv=shape(t, 3 * width, dtype=BF), probs=shape(count, HEADS, tall, tall),
        contextt=shape(count, width, tall, dtype=BF), attended=shape(t, width), middle=shape(t, width),
        h2=shape(t, width, dtype=BF),
    )
    res = pl.pallas_call(
        forward_kernel, out_shape=list(outs.values()),
        in_specs=[VMEM, VMEM, SMEM] + [VMEM] * 5, out_specs=[VMEM] * len(outs),
        scratch_shapes=[pltpu.VMEM((t, width), BF), pltpu.VMEM((tall, width), BF)],
        compiler_params=PARAMS, name="forward",
    )(images, patch_rank, kept_count, g1, rw, w_qkv, w_out, g2)
    return dict(zip(outs, res))


def local_mlp(h2, cotangent, middle, w1, w2):
    count, patches, width = cotangent.shape
    t = h2.shape[0]
    k, _, f = w1.shape
    outs = dict(block=shape(count, patches, width, dtype=BF), cp=shape(t, width, dtype=BF), gh2=shape(t, width),
                gf1=shape(k, width, f, dtype=BF), gf2=shape(k, f, width, dtype=BF))
    res = pl.pallas_call(
        mlp_kernel, out_shape=list(outs.values()), in_specs=[VMEM] * 5, out_specs=[VMEM] * len(outs),
        scratch_shapes=[pltpu.VMEM((t, width), F32), pltpu.VMEM((width, t), BF), pltpu.VMEM((t, f), BF),
                        pltpu.VMEM((t, f), BF), pltpu.VMEM((t // count, width), BF)],
        compiler_params=PARAMS, name="mlp",
    )(h2, cotangent, middle, w1, w2)
    return dict(zip(outs, res))


def local_back(f, m, g1, g2, rw, w_qkv, w_out, count, patches, width):
    t = m["cp"].shape[0]
    outs = dict(gx=shape(count, patches, width, dtype=BF), gout=shape(width, width, dtype=BF),
                gqkv=shape(HEADS // 2, width, 384, dtype=BF), small=shape(1, 3 * width))
    res = pl.pallas_call(
        back_kernel, out_shape=list(outs.values()), in_specs=[VMEM] * 17, out_specs=[VMEM] * len(outs),
        scratch_shapes=[pltpu.VMEM((t, width), F32), pltpu.VMEM((t, width), BF), pltpu.VMEM((t, 128), F32),
                        pltpu.VMEM((t, width), BF), pltpu.VMEM((HEADS // 2, t, 384), BF), pltpu.VMEM((t, width), F32),
                        pltpu.VMEM((1, width), F32), pltpu.VMEM((1, width), F32), pltpu.VMEM((1, width), F32)],
        compiler_params=PARAMS, name="back",
    )(m["cp"], m["gh2"], f["middle"], f["keep"], f["gate"], f["attended"], g2, f["contextt"], w_out, w_qkv, f["qkv"],
      f["probs"], f["h1"], f["h1t"], rw, f["xp"], g1)
    return dict(zip(outs, res))


def per_device(images, patch_rank, kept_count, ln1_gain, router_weight, w_qkv, w_out, ln2_gain, w_fc1, w_fc2, cotangent):
    count, patches, width = images.shape
    g1, g2, rw = ln1_gain[None], ln2_gain[None], router_weight[None]
    part = w_fc1.shape[1]
    w1 = lax.all_gather(w_fc1, "mlp", axis=0)
    w2 = lax.all_gather(w_fc2, "mlp", axis=0)
    f = local_forward(images, patch_rank, kept_count, g1, rw, w_qkv, w_out, g2)
    m = local_mlp(f["h2"], cotangent, f["middle"], w1, w2)
    gf = jnp.concatenate([m["gf1"], m["gf2"]], 1)
    gf = lax.psum_scatter(gf, "mlp", scatter_dimension=0, tiled=True)
    gf = lax.psum(gf, "rows")[0].astype(F32)
    b = local_back(f, m, g1, g2, rw, w_qkv, w_out, count, patches, width)
    gqkv, gout, small = lax.psum((b["gqkv"], b["gout"], b["small"]), ("rows", "mlp"))
    gqkv = gqkv.reshape(HEADS // 2, width, 3, 128).transpose(1, 2, 0, 3).reshape(width, 3 * width).astype(F32)
    small = small[0]
    return (m["block"], b["gx"], small[:width], small[width : 2 * width], gqkv, gout.astype(F32),
            small[2 * width :], gf[:width], gf[width:])


def solution(mesh):
    return jax.shard_map(
        per_device,
        mesh=mesh,
        in_specs=(
            P(("rows", "mlp"), None, None), P(("rows", "mlp"), None), P(("rows", "mlp")), P(), P(), P(), P(), P(),
            P(None, "mlp"), P("mlp", None), P(("rows", "mlp"), None, None),
        ),
        out_specs=(
            P(("rows", "mlp"), None, None), P(("rows", "mlp"), None, None), P(), P(), P(), P(), P(),
            P(None, "mlp"), P("mlp", None),
        ),
        check_vma=False,
    )
```

```python
import functools
import jax
import jax.numpy as jnp
from jax import lax
from jax.experimental import pallas as pl
from jax.experimental.pallas import tpu as pltpu
from jax.sharding import PartitionSpec as P

HEADS = 12
EPS = 1e-6
FILL = -1e30
BF = jnp.bfloat16
F32 = jnp.float32


def dot_nn(a, b):
    return lax.dot_general(a, b, (((1,), (0,)), ((), ())), preferred_element_type=F32)


def dot_nt(a, b):
    return lax.dot_general(a, b, (((1,), (1,)), ((), ())), preferred_element_type=F32)


def dot_tn(a, b):
    return lax.dot_general(a, b, (((0,), (0,)), ((), ())), preferred_element_type=F32)


def unit_rows(v):
    center = v - jnp.mean(v, -1, keepdims=True)
    scale = lax.rsqrt(jnp.mean(center * center, -1, keepdims=True) + EPS)
    return center * scale, scale


def norm_pull(dy, gain, unit, scale):
    du = dy * gain
    return scale * (
        du
        - jnp.mean(du, -1, keepdims=True)
        - unit * jnp.mean(du * unit, -1, keepdims=True)
    )


def half_mask(rows, h):
    lane = lax.broadcasted_iota(jnp.int32, (rows, 128), 1)
    return (lane < 64) if h == 0 else (lane >= 64)


def forward_rows(i, x_ref, rank_ref, kept_ref, g1_ref, rw_ref, xp, keep, gate, h1, h1t, work):
    patches, width = x_ref.shape[1:]
    tall = xp.shape[0] // x_ref.shape[0]
    rows = pl.ds(pl.multiple_of(i * tall, 16), tall)
    work[...] = jnp.zeros_like(work)
    work[0:patches, :] = x_ref[i]
    v = work[...]
    xp[rows, :] = v
    kept = (rank_ref[pl.ds(i, 1), :] < kept_ref[i]).astype(F32)
    keep_row = jnp.concatenate([kept, jnp.zeros((1, 256 - patches), F32)], 1)
    keep_col = jnp.broadcast_to(keep_row, (128, 256)).T
    keep[rows, :] = keep_col[0:tall, :]
    unit, _ = unit_rows(v.astype(F32))
    low = (unit * g1_ref[...]).astype(BF)
    h1[rows, :] = low
    logit = jnp.sum(low.astype(F32) * rw_ref[...].astype(F32), -1, keepdims=True)
    gate[rows, :] = jnp.broadcast_to(jax.nn.sigmoid(logit), (tall, 128))


def forward_qkv(j, h1, wqkv, qkv):
    cols = pl.ds(pl.multiple_of(j * 256, 256), 256)
    qkv[:, cols] = dot_nn(h1[...], wqkv[:, cols]).astype(BF)


def attend(p, i, width, tall, qkv, keep, probs, context, contextt):
    rows = pl.ds(pl.multiple_of(i * tall, 16), tall)
    qc = pl.ds(pl.multiple_of(p * 128, 128), 128)
    kc = pl.ds(pl.multiple_of(width + p * 128, 128), 128)
    vc = pl.ds(pl.multiple_of(2 * width + p * 128, 128), 128)
    q, k, v = qkv[rows, qc], qkv[rows, kc], qkv[rows, vc]
    vt = v.T
    kept = keep[rows, 0:1] > 0.5
    outs = []
    for h in range(2):
        kh = jnp.where(half_mask(tall, h), k, jnp.zeros_like(k))
        s = jnp.where(kept, dot_nt(kh, q) * 0.125, FILL)
        e = jnp.exp(s - jnp.max(s, 0, keepdims=True))
        pr = e * (1.0 / jnp.sum(e, 0, keepdims=True))
        probs[i, p * 2 + h] = pr
        outs.append(dot_nn(vt[h * 64 : h * 64 + 64, :], pr.astype(BF)))
    ct = jnp.concatenate(outs, 0)
    contextt[i, pl.ds(pl.multiple_of(p * 128, 128), 128), :] = ct.astype(BF)
    context[rows, qc] = ct.T.astype(BF)


def forward_out(i, tall, context, wout, xp, keep, gate, g2_ref, attended, middle, h2):
    rows = pl.ds(pl.multiple_of(i * tall, 16), tall)
    att = dot_nn(context[rows, :], wout[...])
    attended[rows, :] = att
    mid = xp[rows, :].astype(F32) + keep[rows, 0:1] * gate[rows, 0:1] * att
    middle[rows, :] = mid
    unit, _ = unit_rows(mid)
    h2[rows, :] = (unit * g2_ref[...]).astype(BF)


def gelu_pair(pre):
    cdf = 0.5 * (1.0 + lax.erf(pre * 0.7071067811865476))
    pdf = jnp.exp(pre * pre * -0.5) * 0.3989422804014327
    return pre * cdf, cdf + pre * pdf


def mlp_rows(h, c, w1, w2):
    pre = dot_nn(h, w1)
    hidden, slope = gelu_pair(pre)
    grad = dot_nt(c, w2) * slope
    return hidden.astype(BF), grad.astype(BF)


def back_rows(i, tall, c_ref, gh2, middle, keep, gate, attended, g2_ref, gmid, gatt, glogit, dg2):
    rows = pl.ds(pl.multiple_of(i * tall, 16), tall)
    dy = gh2[rows, :]
    unit, scale = unit_rows(middle[rows, :])
    gm = c_ref[rows, :].astype(F32) + norm_pull(dy, g2_ref[...], unit, scale)
    gmid[rows, :] = gm
    dg2[...] += jnp.sum(dy * unit, 0, keepdims=True)
    k, g = keep[rows, 0:1], gate[rows, 0:1]
    kept = gm * k
    gatt[rows, :] = (kept * g).astype(BF)
    gl = jnp.sum(kept * attended[rows, :], -1, keepdims=True) * g * (1.0 - g)
    glogit[rows, :] = jnp.broadcast_to(gl, (tall, 128))


def attend_back(p, i, width, tall, qkv, probs, gctx):
    rows = pl.ds(pl.multiple_of(i * tall, 16), tall)
    qc = pl.ds(pl.multiple_of(p * 128, 128), 128)
    kc = pl.ds(pl.multiple_of(width + p * 128, 128), 128)
    vc = pl.ds(pl.multiple_of(2 * width + p * 128, 128), 128)
    q, k, v = qkv[rows, qc], qkv[rows, kc], qkv[rows, vc]
    gc = gctx[rows, qc]
    kt = k.T
    gv, gk, gq = 0.0, 0.0, []
    for h in range(2):
        mask = half_mask(tall, h)
        zero = jnp.zeros_like(v)
        pr = probs[i, p * 2 + h]
        gp = dot_nt(jnp.where(mask, v, zero), gc)
        gs = (pr * (gp - jnp.sum(pr * gp, 0, keepdims=True))).astype(BF)
        gv = gv + dot_nn(pr.astype(BF), jnp.where(mask, gc, zero))
        gk = gk + dot_nn(gs, jnp.where(mask, q, zero))
        gq.append(dot_nn(kt[h * 64 : h * 64 + 64, :], gs))
    qkv[rows, qc] = (jnp.concatenate(gq, 0).T * 0.125).astype(BF)
    qkv[rows, kc] = (gk * 0.125).astype(BF)
    qkv[rows, vc] = gv.astype(BF)


def pair_columns(wqkv, p, width):
    return jnp.concatenate(
        [wqkv[:, pl.ds(pl.multiple_of(b * width + p * 128, 128), 128)] for b in range(3)], 1
    )


def back_input(i, tall, dy, glogit, rw_ref, xp, h1, g1_ref, gmid, gx_ref, dg1, drw):
    rows = pl.ds(pl.multiple_of(i * tall, 16), tall)
    patches = gx_ref.shape[1]
    gl = glogit[rows, 0:1]
    dy = dy + gl * rw_ref[...].astype(F32)
    unit, scale = unit_rows(xp[rows, :].astype(F32))
    dg1[...] += jnp.sum(dy * unit, 0, keepdims=True)
    drw[...] += jnp.sum(h1[rows, :].astype(F32) * gl, 0, keepdims=True)
    out = gmid[rows, :] + norm_pull(dy, g1_ref[...], unit, scale)
    gx_ref[i] = out.astype(BF)[0:patches, :]

MESH = pl.DeviceIdType.MESH
CHUNKS = HEADS // 2 + 2
LAST = 12 + 8


def mega_kernel(
    ranks, x_ref, rank_ref, kept_ref, g1_ref, rw_ref, wqkv_hbm, wout_hbm, g2_ref, fc1, fc2, c_ref,
    block_ref, gx_ref, gq_out, go_out, f1_out, f2_out, small_out,
    wqkv, wout, w1, w2, xp, keep, gate, glogit, h1, h1t, qkv, probs, contextt, context, attended, middle,
    tok, cot, tokt, out, gh2, out_in, gh2_in, hid, hidt, gpre, work,
    g1w, g2w, r1a, r1b, r2a, r2b, fz1, fz2, rz1, rz2,
    gw, q0, q1, q2, qz, qf, dg1, dg2, drw, sma, smr, smz,
    lsem, gsend, grecv, tsend, trecv, esend, erecv, s1s, s1r, s2s, s2r, s3s, s3r, fs, fr, floc, ssib, rsib,
    q0s, q0r, q1s, q1r, q2s, q2r, q3s, q3r, qloc, q5s, q5r, q6s, q6r, q7s, q7r, sms, smrs, smzs, smzr,
):
    images, patches, width = x_ref.shape
    t_own = xp.shape[0]
    tall = t_own // images
    half = width // 2
    part = w1.shape[2]
    quarter = (width // 4, part // 4)
    r = lax.axis_index("rows")
    z = lax.axis_index("mlp")
    c, x, y = lax.rem(r, 2), lax.rem(lax.div(r, 2), 2), lax.rem(lax.div(r, 4), 2)
    r_sib, r_x, r_y = r + 1 - 2 * c, r + 2 - 4 * x, r + 4 - 8 * y
    r_diag = r_x + r_y - r
    q = 2 * y + x

    def ds(start, size):
        return pl.ds(pl.multiple_of(start, 16), size)

    def lanes(start, size):
        return pl.ds(pl.multiple_of(start, 128), size)

    def remote(src, dst, send, recv, row, column):
        return pltpu.make_async_remote_copy(
            src_ref=src, dst_ref=dst, send_sem=send, recv_sem=recv,
            device_id={"rows": row, "mlp": column}, device_id_type=MESH,
        )

    def gather_copy(k, mat, kind):
        held, size = (w1, w2)[mat], quarter[mat]
        cut = size // 3
        sems = gsend.at[k - 1, mat, kind], grecv.at[k - 1, mat, kind]
        if kind < 2:
            start, count = ((q * size, size), ((3 - q) * size, cut))[kind]
            if mat == 0:
                src = fc1.at[ds(start, count), lanes(c * part, part)]
            else:
                src = fc2.at[ds(c * part + start, count), :]
            return remote(src, held.at[k, ds(start, count), :], *sems, r, lax.rem(z - k + ranks, ranks))
        start, count = (q * size, size) if kind < 4 else (q * size + cut, size - cut)
        place = held.at[k, ds(start, count), :]
        return remote(place, place, *sems, (r_x, r_y, r_diag)[kind - 2], z)

    def gather_forward(k):
        for mat in range(2):
            gather_copy(k, mat, 0).wait_recv()
            for kind in (2, 3, 4):
                gather_copy(k, mat, kind).start()

    def gather_finish(k):
        for mat in range(2):
            for kind in (1, 2, 3, 4):
                gather_copy(k, mat, kind).wait_recv()

    def own_shard(mat):
        if mat == 0:
            return pltpu.make_async_copy(fc1.at[:, lanes(c * part, part)], w1.at[0], lsem.at[0])
        return pltpu.make_async_copy(fc2.at[ds(c * part, part), :], w2.at[0], lsem.at[1])

    load_qkv = pltpu.make_async_copy(wqkv_hbm, wqkv, lsem.at[2])
    load_out = pltpu.make_async_copy(wout_hbm, wout, lsem.at[3])

    def token_copy(i):
        src, dst = tok.at[ds(i * tall, tall), :], tok.at[ds(t_own + i * tall, tall), :]
        return remote(src, dst, tsend.at[i], trecv.at[i], r_sib, z)

    cot_copy = remote(
        cot.at[ds(0, t_own), :], cot.at[ds(t_own, t_own), :], tsend.at[images], trecv.at[images], r_sib, z
    )
    gh2_copy = remote(gh2.at[ds(t_own, t_own), :], gh2_in, esend.at[0], erecv.at[0], r_sib, z)
    out_copy = remote(out.at[ds(t_own, t_own), :], out_in, esend.at[1], erecv.at[1], r_sib, z)

    h1r, q1r_rows = width // 2, width // 4
    h2r, q2r_rows = part // 2, part // 4

    def fc_first(k):
        return (
            remote(g1w.at[k, ds((1 - x) * h1r, h1r), :], r1a.at[k], s1s.at[k, 0], s1r.at[k, 0], r_x, z),
            remote(g2w.at[k, ds((1 - y) * h2r, h2r), :], r1b.at[k], s1s.at[k, 1], s1r.at[k, 1], r_y, z),
        )

    def fc_second(k):
        return (
            remote(
                g1w.at[k, ds(x * h1r + (1 - y) * q1r_rows, q1r_rows), :], r2a.at[k], s2s.at[k, 0], s2r.at[k, 0], r_y, z
            ),
            remote(
                g2w.at[k, ds(y * h2r + (1 - x) * q2r_rows, q2r_rows), :], r2b.at[k], s2s.at[k, 1], s2r.at[k, 1], r_x, z
            ),
        )

    def fc_third(k):
        column = lax.rem(z + k, ranks)
        return (
            remote(fz1.at[k], rz1.at[k - 1], s3s.at[k - 1, 0], s3r.at[k - 1, 0], r, column),
            remote(fz2.at[k], rz2.at[k - 1], s3s.at[k - 1, 1], s3r.at[k - 1, 1], r, column),
        )

    f1_place = f1_out.at[ds(x * h1r + y * q1r_rows, q1r_rows), lanes(c * part, part)]
    f2_place = f2_out.at[ds(c * part + y * h2r + x * q2r_rows, q2r_rows), :]

    def fc_spread(kind):
        row = (r_x, r_y, r_diag)[kind]
        return (
            remote(fz1.at[0], f1_place, fs.at[kind, 0], fr.at[kind, 0], row, z),
            remote(fz2.at[0], f2_place, fs.at[kind, 1], fr.at[kind, 1], row, z),
        )

    fc_keep = (
        pltpu.make_async_copy(fz1.at[0], f1_place, floc.at[0]),
        pltpu.make_async_copy(fz2.at[0], f2_place, floc.at[1]),
    )
    f1_half = f1_out.at[:, lanes(c * part, part)]
    f2_half = f2_out.at[ds(c * part, part), :]
    fc_share = (
        remote(f1_half, f1_half, ssib.at[0], rsib.at[0], r_sib, z),
        remote(f2_half, f2_half, ssib.at[1], rsib.at[1], r_sib, z),
    )

    def fc_fold_second(k):
        for copy in fc_first(k):
            copy.wait_recv()
        rows = ds(x * h1r + (1 - y) * q1r_rows, q1r_rows)
        g1w[k, rows, :] = g1w[k, rows, :] + r1a[k, ds((1 - y) * q1r_rows, q1r_rows), :]
        rows = ds(y * h2r + (1 - x) * q2r_rows, q2r_rows)
        g2w[k, rows, :] = g2w[k, rows, :] + r1b[k, ds((1 - x) * q2r_rows, q2r_rows), :]
        for copy in fc_second(k):
            copy.start()

    def fc_fold_third(k):
        for copy in fc_second(k):
            copy.wait_recv()
        total = g1w[k, ds(x * h1r + y * q1r_rows, q1r_rows), :].astype(F32)
        total = total + r1a[k, ds(y * q1r_rows, q1r_rows), :].astype(F32) + r2a[k].astype(F32)
        fz1[k] = total.astype(BF)
        total = g2w[k, ds(y * h2r + x * q2r_rows, q2r_rows), :].astype(F32)
        total = total + r1b[k, ds(x * q2r_rows, q2r_rows), :].astype(F32) + r2b[k].astype(F32)
        fz2[k] = total.astype(BF)

        @pl.when(k > 0)
        def _():
            for copy in fc_third(k):
                copy.start()

    def fc_finish():
        for k in range(1, ranks):
            for copy in fc_third(k):
                copy.wait_recv()
        for own, arrived in ((fz1, rz1), (fz2, rz2)):
            total = own[0].astype(F32)
            for k in range(ranks - 1):
                total = total + arrived[k].astype(F32)
            own[0] = total.astype(BF)
        for copy in fc_keep:
            copy.start()
        for kind in range(3):
            for copy in fc_spread(kind):
                copy.start()

    def fc_to_sibling():
        for copy in fc_keep:
            copy.wait()
        for kind in range(3):
            for copy in fc_spread(kind):
                copy.wait_recv()
        for copy in fc_share:
            copy.start()

    eighth = width // 8

    def order(j):
        odd = lax.rem(j, 2)
        first, second = r_x + (r_y - r_x) * odd, r_y + (r_x - r_y) * odd
        a1, a2 = x + (y - x) * odd, y + (x - y) * odd
        return first, second, a1, a2

    def chunk_place(j, start, count):
        rows = ds(start, count)
        return (
            (j < 2, go_out.at[pl.ds(3 * lax.min(j, 1), 3), rows, :]),
            (j >= 2, gq_out.at[:, rows, lanes(lax.max(j - 2, 0) * 128, 128)]),
        )

    def core_copy(j):
        return remote(gw.at[j, :, ds((1 - c) * half, half), :], q0.at[j], q0s.at[j], q0r.at[j], r_sib, z)

    def first_copy(j):
        first, _, a1, _ = order(j)
        src = gw.at[j, :, ds(c * half + (1 - a1) * 2 * eighth, 2 * eighth), :]
        return remote(src, q1.at[j], q1s.at[j], q1r.at[j], first, z)

    def second_copy(j):
        _, second, a1, a2 = order(j)
        src = gw.at[j, :, ds(c * half + a1 * 2 * eighth + (1 - a2) * eighth, eighth), :]
        return remote(src, q2.at[j], q2s.at[j], q2r.at[j], second, z)

    def z_copy(j, k):
        return remote(qz.at[j, z], qz.at[j, z], q3s.at[j, k - 1], q3r.at[j, k - 1], r, lax.rem(z + k, ranks))

    def own_start(j):
        _, _, a1, a2 = order(j)
        return c * half + a1 * 2 * eighth + a2 * eighth

    def keep_copy(j, ref):
        return pltpu.make_async_copy(qf.at[j], ref, qloc.at[j])

    def spread_copies(j, ref, level):
        first, second, _, _ = order(j)
        if level == 0:
            return remote(qf.at[j], ref, q5s.at[j], q5r.at[j], second, z)
        if level == 1:
            return remote(ref, ref, q6s.at[j], q6r.at[j], first, z)
        return remote(ref, ref, q7s.at[j], q7r.at[j], r_sib, z)

    def level_place(j, level):
        _, _, a1, _ = order(j)
        if level == 0:
            return chunk_place(j, own_start(j), eighth)
        if level == 1:
            return chunk_place(j, c * half + a1 * 2 * eighth, 2 * eighth)
        return chunk_place(j, c * half, half)

    def each_place(j, level, do):
        for condition, ref in level_place(j, level):

            @pl.when(condition)
            def _(ref=ref):
                do(ref)

    def fold_first(j):
        core_copy(j).wait_recv()
        _, _, a1, _ = order(j)
        rows = ds(c * half + (1 - a1) * 2 * eighth, 2 * eighth)
        gw[j, :, rows, :] = gw[j, :, rows, :] + q0[j, :, ds((1 - a1) * 2 * eighth, 2 * eighth), :]
        first_copy(j).start()

    def fold_second(j):
        first_copy(j).wait_recv()
        _, _, a1, a2 = order(j)
        inner = (1 - a2) * eighth
        rows = ds(c * half + a1 * 2 * eighth + inner, eighth)
        total = gw[j, :, rows, :].astype(F32) + q0[j, :, ds(a1 * 2 * eighth + inner, eighth), :].astype(F32)
        gw[j, :, rows, :] = (total + q1[j, :, ds(inner, eighth), :].astype(F32)).astype(BF)
        second_copy(j).start()

    def fold_z(j):
        second_copy(j).wait_recv()
        _, _, a1, a2 = order(j)
        inner = a2 * eighth
        rows = ds(c * half + a1 * 2 * eighth + inner, eighth)
        total = gw[j, :, rows, :].astype(F32) + q0[j, :, ds(a1 * 2 * eighth + inner, eighth), :].astype(F32)
        total = total + q1[j, :, ds(inner, eighth), :].astype(F32) + q2[j].astype(F32)
        qz[j, z] = total.astype(BF)
        for k in range(1, ranks):
            z_copy(j, k).start()

    def fold_all(j):
        for k in range(1, ranks):
            z_copy(j, k).wait_recv()
        total = qz[j, 0].astype(F32)
        for k in range(1, ranks):
            total = total + qz[j, k].astype(F32)
        qf[j] = total.astype(BF)

        def go(ref):
            keep_copy(j, ref).start()
            spread_copies(j, ref, 0).start()

        each_place(j, 0, go)

    def spread_first(j):
        def done(ref):
            keep_copy(j, ref).wait()
            spread_copies(j, ref, 0).wait_recv()

        each_place(j, 0, done)
        each_place(j, 1, lambda ref: spread_copies(j, ref, 1).start())

    def spread_sibling(j):
        each_place(j, 1, lambda ref: spread_copies(j, ref, 1).wait_recv())
        each_place(j, 2, lambda ref: spread_copies(j, ref, 2).start())

    def chunk_done(j):
        each_place(j, 2, lambda ref: spread_copies(j, ref, 2).wait())
        each_place(j, 1, lambda ref: spread_copies(j, ref, 1).wait_send())
        each_place(j, 0, lambda ref: spread_copies(j, ref, 0).wait_send())
        core_copy(j).wait_send()
        first_copy(j).wait_send()
        second_copy(j).wait_send()
        for k in range(1, ranks):
            z_copy(j, k).wait_send()

    def small_copy(level):
        row = (r_sib, r_x, r_y)[level]
        return remote(sma.at[level], smr.at[level], sms.at[level], smrs.at[level], row, z)

    def small_z(k):
        return remote(smz.at[z], smz.at[z], smzs.at[k - 1], smzr.at[k - 1], r, lax.rem(z + k, ranks))

    barrier = pltpu.get_barrier_semaphore()
    partners = [(r_sib, z), (r_x, z), (r_y, z), (r_diag, z)] + [(r, lax.rem(z + k, ranks)) for k in range(1, ranks)]
    for row, column in partners:
        pl.semaphore_signal(barrier, inc=1, device_id={"rows": row, "mlp": column}, device_id_type=MESH)
    load_qkv.start()
    load_out.start()
    own_shard(0).start()
    own_shard(1).start()
    pl.semaphore_wait(barrier, len(partners))
    for k in range(1, ranks):
        for kind in range(2):
            for mat in range(2):
                gather_copy(k, mat, kind).start()
    for i in range(images):
        work[...] = jnp.zeros_like(work)
        work[0:patches, :] = c_ref[i]
        cot[i * tall : (i + 1) * tall, :] = work[...]
    cot_copy.start()

    @pl.loop(0, images)
    def _(i):
        forward_rows(i, x_ref, rank_ref, kept_ref, g1_ref, rw_ref, xp, keep, gate, h1, h1t, work)

    h1t[...] = h1[...].T
    load_qkv.wait()

    @pl.loop(0, 3 * width // 256)
    def _(j):
        forward_qkv(j, h1, wqkv, qkv)

    @pl.loop(0, HEADS // 2)
    def _(p):
        for i in range(images):
            attend(p, i, width, tall, qkv, keep, probs, context, contextt)

        @pl.when(p == 2)
        def _():
            gather_forward(1)

        @pl.when(p == 5)
        def _():
            gather_forward(2)

    load_out.wait()

    @pl.loop(0, images)
    def _(i):
        forward_out(i, tall, context, wout, xp, keep, gate, g2_ref, attended, middle, tok)
        token_copy(i).start()

    own_shard(0).wait()
    own_shard(1).wait()
    for ref in (out, gh2, dg1, dg2, drw):
        ref[...] = jnp.zeros_like(ref)

    def mlp_step(k):
        @pl.loop(0, 2 * images)
        def _(block):
            @pl.when(jnp.logical_and(k == 0, block == images))
            def _():
                for i in range(images):
                    token_copy(i).wait()
                cot_copy.wait()

            rows = ds(lax.rem(block + images * lax.div(k, ranks - 1), 2 * images) * tall, tall)
            hid[rows, :], gpre[rows, :] = mlp_rows(tok[rows, :], cot[rows, :], w1[k], w2[k])
            out[rows, :] += dot_nn(hid[rows, :], w2[k])
            gh2[rows, :] += dot_nt(gpre[rows, :], w1[k])

            @pl.when(jnp.logical_and(k == ranks - 1, block == images - 1))
            def _():
                gh2_copy.start()
                out_copy.start()

        @pl.when(k == 0)
        def _():
            tokt[...] = tok[...].T

        hidt[...] = hid[...].T
        for m in range(3):
            rows = slice(m * width // 3, (m + 1) * width // 3)
            g1w[k, rows, :] = dot_nn(tokt[rows, :], gpre[...]).astype(BF)
            g2w[k, :, rows] = dot_nn(hidt[...], cot[:, rows]).astype(BF)

    @pl.loop(0, LAST)
    def _(t):
        for k in range(1, ranks):

            @pl.when(t == k)
            def _(k=k):
                gather_finish(k)

        @pl.when(t < ranks)
        def _():
            mlp_step(t)
            for copy in fc_first(t):
                copy.start()

        @pl.when(t == 1)
        def _():
            gather_forward(3)

        @pl.when(t == 4)
        def _():
            gh2_copy.wait()
            out_copy.wait()

            @pl.loop(0, images)
            def _(i):
                rows = ds(i * tall, tall)
                gh2[rows, :] += gh2_in[rows, :]
                back_rows(
                    i, tall, cot, gh2, middle, keep, gate, attended, g2_ref, gh2, tok, glogit, dg2
                )

            context[...] = dot_nt(tok[ds(0, t_own), :], wout[...]).astype(BF)

        @pl.when(jnp.logical_and(t >= 4, t < 6))
        def _():
            cols = lanes((t - 4) * half, half)
            total = 0.0
            for i in range(images):
                total = total + dot_nn(contextt[i], tok[i * tall : (i + 1) * tall, cols])
            for b in range(3):
                gw[t - 4, b] = total[:, b * 128 : (b + 1) * 128].astype(BF)

        @pl.when(jnp.logical_and(t >= 6, t < 12))
        def _():
            p = t - 6
            for i in range(images):
                attend_back(p, i, width, tall, qkv, probs, context)
            total = dot_nn(h1t[...], pair_columns(qkv, p, width))
            for b in range(3):
                gw[t - 4, b] = total[:, b * 128 : (b + 1) * 128].astype(BF)

        @pl.when(jnp.logical_and(t >= 4, t < 12))
        def _():
            core_copy(t - 4).start()

        @pl.when(t == 5)
        def _():
            @pl.loop(0, images)
            def _(i):
                rows = ds(i * tall, tall)
                block_ref[i] = (middle[rows, :] + out[rows, :] + out_in[rows, :]).astype(BF)[0:patches, :]

        @pl.when(t == 12)
        def _():
            @pl.loop(0, images)
            def _(i):
                rows = ds(i * tall, tall)
                dy = dot_nt(qkv[rows, :], wqkv[...])
                back_input(i, tall, dy, glogit, rw_ref, xp, h1, g1_ref, gh2, gx_ref, dg1, drw)

            sma[0] = jnp.concatenate([dg1[...], drw[...], dg2[...], jnp.zeros((5, width), F32)], 0)
            small_copy(0).start()

        for level in range(2):

            @pl.when(t == 13 + level)
            def _(level=level):
                small_copy(level).wait()
                sma[level + 1] = sma[level] + smr[level]
                small_copy(level + 1).start()

        @pl.when(t == 15)
        def _():
            small_copy(2).wait()
            smz[z] = sma[2] + smr[2]
            for k in range(1, ranks):
                small_z(k).start()

        def lagged(lag, do):
            @pl.when(jnp.logical_and(t >= 4 + lag, t < 4 + lag + CHUNKS))
            def _():
                do(t - 4 - lag)

        @pl.when(jnp.logical_and(t >= 2, t < 2 + ranks))
        def _():
            fc_fold_third(t - 2)

        @pl.when(jnp.logical_and(t >= 1, t < 1 + ranks))
        def _():
            fc_fold_second(t - 1)

        @pl.when(t == 7)
        def _():
            fc_finish()

        @pl.when(t == 9)
        def _():
            fc_to_sibling()

        lagged(6, spread_sibling)
        lagged(5, spread_first)
        lagged(4, fold_all)
        lagged(3, fold_z)
        lagged(2, fold_second)
        lagged(1, fold_first)

    for k in range(1, ranks):
        small_z(k).wait()
    total = smz[0]
    for k in range(1, ranks):
        total = total + smz[k]
    small_out[...] = total

    @pl.loop(0, CHUNKS)
    def _(j):
        chunk_done(j)

    for copy in fc_share:
        copy.wait()
    for kind in range(3):
        for copy in fc_spread(kind):
            copy.wait_send()
    for k in range(1, ranks):
        for copy in fc_third(k):
            copy.wait_send()
        for mat in range(2):
            for kind in range(5):
                gather_copy(k, mat, kind).wait_send()

    @pl.loop(0, ranks)
    def _(k):
        for copy in fc_first(k) + fc_second(k):
            copy.wait_send()


VMEM = pl.BlockSpec(memory_space=pltpu.VMEM)
SMEM = pl.BlockSpec(memory_space=pltpu.SMEM)
ANY = pl.BlockSpec(memory_space=pl.ANY)


def per_device(ranks, others, images, patch_rank, kept_count, ln1_gain, router_weight, w_qkv, w_out, ln2_gain, w_fc1, w_fc2, cotangent):
    count, patches, width = images.shape
    tall = -(-patches // 16) * 16
    t = count * tall
    part = w_fc1.shape[1] // 2
    half, eighth = width // 2, width // 8

    def bf(*dims):
        return pltpu.VMEM(dims, BF)

    def f32(*dims):
        return pltpu.VMEM(dims, F32)

    def sem(*dims):
        return pltpu.SemaphoreType.DMA(dims)

    scratch = [
        bf(width, 3 * width), bf(width, width), bf(ranks, width, part), bf(ranks, part, width),
        bf(t, width), f32(t, 128), f32(t, 128), f32(t, 128), bf(t, width), bf(width, t), bf(t, 3 * width),
        f32(count, HEADS, tall, tall), bf(count, width, tall), bf(t, width), f32(t, width), f32(t, width),
        bf(2 * t, width), bf(2 * t, width), bf(width, 2 * t), f32(2 * t, width), f32(2 * t, width),
        f32(t, width), f32(t, width), bf(2 * t, part), bf(part, 2 * t), bf(2 * t, part), bf(tall, width),
        bf(ranks, width, part), bf(ranks, part, width),
        bf(ranks, width // 2, part), bf(ranks, part // 2, width), bf(ranks, width // 4, part), bf(ranks, part // 4, width),
        bf(ranks, width // 4, part), bf(ranks, part // 4, width), bf(ranks - 1, width // 4, part), bf(ranks - 1, part // 4, width),
        bf(CHUNKS, 3, width, 128), bf(CHUNKS, 3, half, 128), bf(CHUNKS, 3, 2 * eighth, 128), bf(CHUNKS, 3, eighth, 128),
        bf(CHUNKS, ranks, 3, eighth, 128), bf(CHUNKS, 3, eighth, 128),
        f32(1, width), f32(1, width), f32(1, width), f32(3, 8, width), f32(3, 8, width), f32(ranks, 8, width),
        sem(4), sem(ranks - 1, 2, 5), sem(ranks - 1, 2, 5), sem(count + 1), sem(count + 1), sem(2), sem(2),
        sem(ranks, 2), sem(ranks, 2), sem(ranks, 2), sem(ranks, 2), sem(ranks - 1, 2), sem(ranks - 1, 2),
        sem(3, 2), sem(3, 2), sem(2), sem(2), sem(2),
        sem(CHUNKS), sem(CHUNKS), sem(CHUNKS), sem(CHUNKS), sem(CHUNKS), sem(CHUNKS),
        sem(CHUNKS, ranks - 1), sem(CHUNKS, ranks - 1), sem(CHUNKS),
        sem(CHUNKS), sem(CHUNKS), sem(CHUNKS), sem(CHUNKS), sem(CHUNKS), sem(CHUNKS),
        sem(3), sem(3), sem(ranks - 1), sem(ranks - 1),
    ]

    def struct(*dims, dtype=BF):
        return jax.ShapeDtypeStruct(dims, dtype)

    block, gx, gq, go, f1, f2, small = pl.pallas_call(
        functools.partial(mega_kernel, ranks),
        out_shape=[
            struct(count, patches, width), struct(count, patches, width), struct(3, width, width), struct(6, width, 128),
            struct(width, 2 * part), struct(2 * part, width), struct(8, width, dtype=F32),
        ],
        in_specs=[VMEM, VMEM, SMEM, VMEM, VMEM, ANY, ANY, VMEM, ANY, ANY, VMEM],
        out_specs=[VMEM, VMEM, ANY, ANY, ANY, ANY, VMEM],
        scratch_shapes=scratch,
        compiler_params=pltpu.CompilerParams(
            collective_id=0, has_side_effects=True, vmem_limit_bytes=63 * 1024 * 1024
        ),
        name="block",
    )(images, patch_rank, kept_count, ln1_gain[None], router_weight[None], w_qkv, w_out, ln2_gain[None], w_fc1, w_fc2, cotangent)
    gq = gq.transpose(1, 0, 2).reshape(width, 3 * width).astype(F32)
    go = go.transpose(1, 0, 2).reshape(width, width).astype(F32)
    f1, f2 = f1.astype(F32), f2.astype(F32)
    if others:
        gq, go, f1, f2, small = lax.psum((gq, go, f1, f2, small), "rows", axis_index_groups=others)
    return block, gx, small[0], small[1], gq, go, small[2], f1, f2


def solution(mesh):
    rows, ranks = mesh.shape["rows"], mesh.shape["mlp"]
    others = [[8 * g + i for g in range(rows // 8)] for i in range(8)] if rows > 8 else None
    return jax.shard_map(
        functools.partial(per_device, ranks, others),
        mesh=mesh,
        in_specs=(
            P(("rows", "mlp"), None, None), P(("rows", "mlp"), None), P(("rows", "mlp")), P(), P(), P(), P(), P(),
            P(None, "mlp"), P("mlp", None), P(("rows", "mlp"), None, None),
        ),
        out_specs=(
            P(("rows", "mlp"), None, None), P(("rows", "mlp"), None, None), P(), P(), P(), P(), P(),
            P(None, "mlp"), P("mlp", None),
        ),
        check_vma=False,
    )
```

```python
import functools
import jax
import jax.numpy as jnp
from jax import lax
from jax.experimental import pallas as pl
from jax.experimental.pallas import tpu as pltpu
from jax.sharding import PartitionSpec as P

HEADS = 12
EPS = 1e-6
FILL = -1e30
BF = jnp.bfloat16
F32 = jnp.float32


def dot_nn(a, b):
    return lax.dot_general(a, b, (((1,), (0,)), ((), ())), preferred_element_type=F32)


def dot_nt(a, b):
    return lax.dot_general(a, b, (((1,), (1,)), ((), ())), preferred_element_type=F32)


def dot_tn(a, b):
    return lax.dot_general(a, b, (((0,), (0,)), ((), ())), preferred_element_type=F32)


def unit_rows(v):
    center = v - jnp.mean(v, -1, keepdims=True)
    scale = lax.rsqrt(jnp.mean(center * center, -1, keepdims=True) + EPS)
    return center * scale, scale


def norm_pull(dy, gain, unit, scale):
    du = dy * gain
    return scale * (
        du
        - jnp.mean(du, -1, keepdims=True)
        - unit * jnp.mean(du * unit, -1, keepdims=True)
    )


def half_mask(rows, h):
    lane = lax.broadcasted_iota(jnp.int32, (rows, 128), 1)
    return (lane < 64) if h == 0 else (lane >= 64)


def forward_rows(i, x_ref, rank_ref, kept_ref, g1_ref, rw_ref, xp, keep, gate, h1, h1t, work):
    patches, width = x_ref.shape[1:]
    tall = xp.shape[0] // x_ref.shape[0]
    rows = pl.ds(pl.multiple_of(i * tall, 16), tall)
    work[...] = jnp.zeros_like(work)
    work[0:patches, :] = x_ref[i]
    v = work[...]
    xp[rows, :] = v
    kept = (rank_ref[pl.ds(i, 1), :] < kept_ref[i]).astype(F32)
    keep_row = jnp.concatenate([kept, jnp.zeros((1, 256 - patches), F32)], 1)
    keep_col = jnp.broadcast_to(keep_row, (128, 256)).T
    keep[rows, :] = keep_col[0:tall, :]
    unit, _ = unit_rows(v.astype(F32))
    low = (unit * g1_ref[...][None]).astype(BF)
    h1[rows, :] = low
    logit = jnp.sum(low.astype(F32) * rw_ref[...][None].astype(F32), -1, keepdims=True)
    gate[rows, :] = jnp.broadcast_to(jax.nn.sigmoid(logit), (tall, 128))


def forward_qkv(j, h1, wqkv, qkv):
    cols = pl.ds(pl.multiple_of(j * 256, 256), 256)
    qkv[:, cols] = dot_nn(h1[...], wqkv[:, cols]).astype(BF)


def attend(p, i, width, tall, qkv, keep, probs, context, contextt):
    rows = pl.ds(pl.multiple_of(i * tall, 16), tall)
    qc = pl.ds(pl.multiple_of(p * 128, 128), 128)
    kc = pl.ds(pl.multiple_of(width + p * 128, 128), 128)
    vc = pl.ds(pl.multiple_of(2 * width + p * 128, 128), 128)
    q, k, v = qkv[rows, qc], qkv[rows, kc], qkv[rows, vc]
    vt = v.T
    kept = keep[rows, 0:1] > 0.5
    outs = []
    for h in range(2):
        kh = jnp.where(half_mask(tall, h), k, jnp.zeros_like(k))
        s = jnp.where(kept, dot_nt(kh, q) * 0.125, FILL)
        e = jnp.exp(s - jnp.max(s, 0, keepdims=True))
        pr = e * (1.0 / jnp.sum(e, 0, keepdims=True))
        probs[i, p * 2 + h] = pr
        outs.append(dot_nn(vt[h * 64 : h * 64 + 64, :], pr.astype(BF)))
    ct = jnp.concatenate(outs, 0)
    contextt[i, pl.ds(pl.multiple_of(p * 128, 128), 128), :] = ct.astype(BF)
    context[rows, qc] = ct.T.astype(BF)


def forward_out(i, tall, context, wout, xp, keep, gate, g2_ref, attended, middle, h2):
    rows = pl.ds(pl.multiple_of(i * tall, 16), tall)
    att = dot_nn(context[rows, :], wout[...])
    attended[rows, :] = att
    mid = xp[rows, :].astype(F32) + keep[rows, 0:1] * gate[rows, 0:1] * att
    middle[rows, :] = mid
    unit, _ = unit_rows(mid)
    h2[rows, :] = (unit * g2_ref[...][None]).astype(BF)


def gelu_pair(pre):
    cdf = 0.5 * (1.0 + lax.erf(pre * 0.7071067811865476))
    pdf = jnp.exp(pre * pre * -0.5) * 0.3989422804014327
    return pre * cdf, cdf + pre * pdf


def mlp_rows(h, c, w1, w2):
    pre = dot_nn(h, w1)
    hidden, slope = gelu_pair(pre)
    grad = dot_nt(c, w2) * slope
    return hidden.astype(BF), grad.astype(BF)


def back_rows(i, tall, c_ref, gh2, middle, keep, gate, attended, g2_ref, gmid, gatt, glogit, dg2):
    rows = pl.ds(pl.multiple_of(i * tall, 16), tall)
    dy = gh2[rows, :]
    unit, scale = unit_rows(middle[rows, :])
    gm = c_ref[rows, :].astype(F32) + norm_pull(dy, g2_ref[...][None], unit, scale)
    gmid[rows, :] = gm
    dg2[...] += jnp.sum(dy * unit, 0, keepdims=True)
    k, g = keep[rows, 0:1], gate[rows, 0:1]
    kept = gm * k
    gatt[rows, :] = (kept * g).astype(BF)
    gl = jnp.sum(kept * attended[rows, :], -1, keepdims=True) * g * (1.0 - g)
    glogit[rows, :] = jnp.broadcast_to(gl, (tall, 128))


def attend_back(p, i, width, tall, qkv, probs, gctx):
    rows = pl.ds(pl.multiple_of(i * tall, 16), tall)
    qc = pl.ds(pl.multiple_of(p * 128, 128), 128)
    kc = pl.ds(pl.multiple_of(width + p * 128, 128), 128)
    vc = pl.ds(pl.multiple_of(2 * width + p * 128, 128), 128)
    q, k, v = qkv[rows, qc], qkv[rows, kc], qkv[rows, vc]
    gc = gctx[rows, qc]
    kt = k.T
    gv, gk, gq = 0.0, 0.0, []
    for h in range(2):
        mask = half_mask(tall, h)
        zero = jnp.zeros_like(v)
        pr = probs[i, p * 2 + h]
        gp = dot_nt(jnp.where(mask, v, zero), gc)
        gs = (pr * (gp - jnp.sum(pr * gp, 0, keepdims=True))).astype(BF)
        gv = gv + dot_nn(pr.astype(BF), jnp.where(mask, gc, zero))
        gk = gk + dot_nn(gs, jnp.where(mask, q, zero))
        gq.append(dot_nn(kt[h * 64 : h * 64 + 64, :], gs))
    qkv[rows, qc] = (jnp.concatenate(gq, 0).T * 0.125).astype(BF)
    qkv[rows, kc] = (gk * 0.125).astype(BF)
    qkv[rows, vc] = gv.astype(BF)


def pair_columns(wqkv, p, width):
    return jnp.concatenate(
        [wqkv[:, pl.ds(pl.multiple_of(b * width + p * 128, 128), 128)] for b in range(3)], 1
    )


def back_input(i, tall, dy, glogit, rw_ref, xp, h1, g1_ref, gmid, gx_ref, dg1, drw):
    rows = pl.ds(pl.multiple_of(i * tall, 16), tall)
    patches = gx_ref.shape[1]
    gl = glogit[rows, 0:1]
    dy = dy + gl * rw_ref[...][None].astype(F32)
    unit, scale = unit_rows(xp[rows, :].astype(F32))
    dg1[...] += jnp.sum(dy * unit, 0, keepdims=True)
    drw[...] += jnp.sum(h1[rows, :].astype(F32) * gl, 0, keepdims=True)
    out = gmid[rows, :] + norm_pull(dy, g1_ref[...][None], unit, scale)
    gx_ref[i] = out.astype(BF)[0:patches, :]

MESH = pl.DeviceIdType.MESH
CHUNKS = HEADS // 2 + 2
LAST = 12 + 8


def mega_kernel(
    ranks, x_ref, rank_ref, kept_ref, g1_ref, rw_ref, wqkv_hbm, wout_hbm, g2_ref, fc1, fc2, c_ref,
    block_ref, gx_ref, gq_out, go_out, f1_out, f2_out, small_out,
    wqkv, wout, w1, w2, xp, keep, gate, glogit, h1, h1t, qkv, probs, contextt, context, attended, middle,
    tok, cot, tokt, out, gh2, out_in, gh2_in, hid, hidt, gpre, work,
    g1w, g2w, r1a, r1b, r2a, r2b, fz1, fz2, rz1, rz2,
    gw, q0, q1, q2, qz, qf, dg1, dg2, drw, sma, smr, smz,
    lsem, gsend, grecv, tsend, trecv, esend, erecv, s1s, s1r, s2s, s2r, s3s, s3r, fs, fr, floc, ssib, rsib,
    q0s, q0r, q1s, q1r, q2s, q2r, q3s, q3r, qloc, q5s, q5r, q6s, q6r, q7s, q7r, sms, smrs, smzs, smzr,
):
    images, patches, width = x_ref.shape
    t_own = xp.shape[0]
    tall = t_own // images
    half = width // 2
    part = w1.shape[2]
    quarter = (width // 4, part // 4)
    r = lax.axis_index("rows")
    z = lax.axis_index("mlp")
    c, x, y = lax.rem(r, 2), lax.rem(lax.div(r, 2), 2), lax.rem(lax.div(r, 4), 2)
    r_sib, r_x, r_y = r + 1 - 2 * c, r + 2 - 4 * x, r + 4 - 8 * y
    r_diag = r_x + r_y - r
    q = 2 * y + x

    def ds(start, size):
        return pl.ds(pl.multiple_of(start, 16), size)

    def lanes(start, size):
        return pl.ds(pl.multiple_of(start, 128), size)

    def remote(src, dst, send, recv, row, column):
        return pltpu.make_async_remote_copy(
            src_ref=src, dst_ref=dst, send_sem=send, recv_sem=recv,
            device_id={"rows": row, "mlp": column}, device_id_type=MESH,
        )

    def gather_copy(k, mat, kind):
        held, size = (w1, w2)[mat], quarter[mat]
        cut = size // 3
        sems = gsend.at[k - 1, mat, kind], grecv.at[k - 1, mat, kind]
        if kind < 2:
            start, count = ((q * size, size), ((3 - q) * size, cut))[kind]
            if mat == 0:
                src = fc1.at[ds(start, count), lanes(c * part, part)]
            else:
                src = fc2.at[ds(c * part + start, count), :]
            return remote(src, held.at[k, ds(start, count), :], *sems, r, lax.rem(z - k + ranks, ranks))
        start, count = (q * size, size) if kind < 4 else (q * size + cut, size - cut)
        place = held.at[k, ds(start, count), :]
        return remote(place, place, *sems, (r_x, r_y, r_diag)[kind - 2], z)

    def gather_forward(k):
        for mat in range(2):
            gather_copy(k, mat, 0).wait_recv()
            for kind in (2, 3, 4):
                gather_copy(k, mat, kind).start()

    def gather_finish(k):
        for mat in range(2):
            for kind in (1, 2, 3, 4):
                gather_copy(k, mat, kind).wait_recv()

    def own_shard(mat):
        if mat == 0:
            return pltpu.make_async_copy(fc1.at[:, lanes(c * part, part)], w1.at[0], lsem.at[0])
        return pltpu.make_async_copy(fc2.at[ds(c * part, part), :], w2.at[0], lsem.at[1])

    load_qkv = pltpu.make_async_copy(wqkv_hbm, wqkv, lsem.at[2])
    load_out = pltpu.make_async_copy(wout_hbm, wout, lsem.at[3])

    def token_copy(i):
        src, dst = tok.at[ds(i * tall, tall), :], tok.at[ds(t_own + i * tall, tall), :]
        return remote(src, dst, tsend.at[i], trecv.at[i], r_sib, z)

    cot_copy = remote(
        cot.at[ds(0, t_own), :], cot.at[ds(t_own, t_own), :], tsend.at[images], trecv.at[images], r_sib, z
    )
    gh2_copy = remote(gh2.at[ds(t_own, t_own), :], gh2_in, esend.at[0], erecv.at[0], r_sib, z)
    out_copy = remote(out.at[ds(t_own, t_own), :], out_in, esend.at[1], erecv.at[1], r_sib, z)

    h1r, q1r_rows = width // 2, width // 4
    h2r, q2r_rows = part // 2, part // 4

    def fc_first(k):
        return (
            remote(g1w.at[k, ds((1 - x) * h1r, h1r), :], r1a.at[k], s1s.at[k, 0], s1r.at[k, 0], r_x, z),
            remote(g2w.at[k, ds((1 - y) * h2r, h2r), :], r1b.at[k], s1s.at[k, 1], s1r.at[k, 1], r_y, z),
        )

    def fc_second(k):
        return (
            remote(
                g1w.at[k, ds(x * h1r + (1 - y) * q1r_rows, q1r_rows), :], r2a.at[k], s2s.at[k, 0], s2r.at[k, 0], r_y, z
            ),
            remote(
                g2w.at[k, ds(y * h2r + (1 - x) * q2r_rows, q2r_rows), :], r2b.at[k], s2s.at[k, 1], s2r.at[k, 1], r_x, z
            ),
        )

    def fc_third(k):
        column = lax.rem(z + k, ranks)
        return (
            remote(fz1.at[k], rz1.at[k - 1], s3s.at[k - 1, 0], s3r.at[k - 1, 0], r, column),
            remote(fz2.at[k], rz2.at[k - 1], s3s.at[k - 1, 1], s3r.at[k - 1, 1], r, column),
        )

    f1_place = f1_out.at[ds(x * h1r + y * q1r_rows, q1r_rows), lanes(c * part, part)]
    f2_place = f2_out.at[ds(c * part + y * h2r + x * q2r_rows, q2r_rows), :]

    def fc_spread(kind):
        row = (r_x, r_y, r_diag)[kind]
        return (
            remote(fz1.at[0], f1_place, fs.at[kind, 0], fr.at[kind, 0], row, z),
            remote(fz2.at[0], f2_place, fs.at[kind, 1], fr.at[kind, 1], row, z),
        )

    fc_keep = (
        pltpu.make_async_copy(fz1.at[0], f1_place, floc.at[0]),
        pltpu.make_async_copy(fz2.at[0], f2_place, floc.at[1]),
    )
    f1_half = f1_out.at[:, lanes(c * part, part)]
    f2_half = f2_out.at[ds(c * part, part), :]
    fc_share = (
        remote(f1_half, f1_half, ssib.at[0], rsib.at[0], r_sib, z),
        remote(f2_half, f2_half, ssib.at[1], rsib.at[1], r_sib, z),
    )

    def fc_fold_second(k):
        for copy in fc_first(k):
            copy.wait_recv()
        rows = ds(x * h1r + (1 - y) * q1r_rows, q1r_rows)
        g1w[k, rows, :] = g1w[k, rows, :] + r1a[k, ds((1 - y) * q1r_rows, q1r_rows), :]
        rows = ds(y * h2r + (1 - x) * q2r_rows, q2r_rows)
        g2w[k, rows, :] = g2w[k, rows, :] + r1b[k, ds((1 - x) * q2r_rows, q2r_rows), :]
        for copy in fc_second(k):
            copy.start()

    def fc_fold_third(k):
        for copy in fc_second(k):
            copy.wait_recv()
        total = g1w[k, ds(x * h1r + y * q1r_rows, q1r_rows), :].astype(F32)
        total = total + r1a[k, ds(y * q1r_rows, q1r_rows), :].astype(F32) + r2a[k].astype(F32)
        fz1[k] = total.astype(BF)
        total = g2w[k, ds(y * h2r + x * q2r_rows, q2r_rows), :].astype(F32)
        total = total + r1b[k, ds(x * q2r_rows, q2r_rows), :].astype(F32) + r2b[k].astype(F32)
        fz2[k] = total.astype(BF)

        @pl.when(k > 0)
        def _():
            for copy in fc_third(k):
                copy.start()

    def fc_finish():
        for k in range(1, ranks):
            for copy in fc_third(k):
                copy.wait_recv()
        for own, arrived in ((fz1, rz1), (fz2, rz2)):
            total = own[0].astype(F32)
            for k in range(ranks - 1):
                total = total + arrived[k].astype(F32)
            own[0] = total.astype(BF)
        for copy in fc_keep:
            copy.start()
        for kind in range(3):
            for copy in fc_spread(kind):
                copy.start()

    def fc_to_sibling():
        for copy in fc_keep:
            copy.wait()
        for kind in range(3):
            for copy in fc_spread(kind):
                copy.wait_recv()
        for copy in fc_share:
            copy.start()

    eighth = width // 8

    def order(j):
        odd = lax.rem(j, 2)
        first, second = r_x + (r_y - r_x) * odd, r_y + (r_x - r_y) * odd
        a1, a2 = x + (y - x) * odd, y + (x - y) * odd
        return first, second, a1, a2

    def chunk_place(j, start, count):
        rows = ds(start, count)
        return (
            (j < 2, go_out.at[pl.ds(3 * lax.min(j, 1), 3), rows, :]),
            (j >= 2, gq_out.at[:, rows, lanes(lax.max(j - 2, 0) * 128, 128)]),
        )

    def core_copy(j):
        return remote(gw.at[j, :, ds((1 - c) * half, half), :], q0.at[j], q0s.at[j], q0r.at[j], r_sib, z)

    def first_copy(j):
        first, _, a1, _ = order(j)
        src = gw.at[j, :, ds(c * half + (1 - a1) * 2 * eighth, 2 * eighth), :]
        return remote(src, q1.at[j], q1s.at[j], q1r.at[j], first, z)

    def second_copy(j):
        _, second, a1, a2 = order(j)
        src = gw.at[j, :, ds(c * half + a1 * 2 * eighth + (1 - a2) * eighth, eighth), :]
        return remote(src, q2.at[j], q2s.at[j], q2r.at[j], second, z)

    def z_copy(j, k):
        return remote(qz.at[j, z], qz.at[j, z], q3s.at[j, k - 1], q3r.at[j, k - 1], r, lax.rem(z + k, ranks))

    def own_start(j):
        _, _, a1, a2 = order(j)
        return c * half + a1 * 2 * eighth + a2 * eighth

    def keep_copy(j, ref):
        return pltpu.make_async_copy(qf.at[j], ref, qloc.at[j])

    def spread_copies(j, ref, level):
        first, second, _, _ = order(j)
        if level == 0:
            return remote(qf.at[j], ref, q5s.at[j], q5r.at[j], second, z)
        if level == 1:
            return remote(ref, ref, q6s.at[j], q6r.at[j], first, z)
        return remote(ref, ref, q7s.at[j], q7r.at[j], r_sib, z)

    def level_place(j, level):
        _, _, a1, _ = order(j)
        if level == 0:
            return chunk_place(j, own_start(j), eighth)
        if level == 1:
            return chunk_place(j, c * half + a1 * 2 * eighth, 2 * eighth)
        return chunk_place(j, c * half, half)

    def each_place(j, level, do):
        for condition, ref in level_place(j, level):

            @pl.when(condition)
            def _(ref=ref):
                do(ref)

    def fold_first(j):
        core_copy(j).wait_recv()
        _, _, a1, _ = order(j)
        rows = ds(c * half + (1 - a1) * 2 * eighth, 2 * eighth)
        gw[j, :, rows, :] = gw[j, :, rows, :] + q0[j, :, ds((1 - a1) * 2 * eighth, 2 * eighth), :]
        first_copy(j).start()

    def fold_second(j):
        first_copy(j).wait_recv()
        _, _, a1, a2 = order(j)
        inner = (1 - a2) * eighth
        rows = ds(c * half + a1 * 2 * eighth + inner, eighth)
        total = gw[j, :, rows, :].astype(F32) + q0[j, :, ds(a1 * 2 * eighth + inner, eighth), :].astype(F32)
        gw[j, :, rows, :] = (total + q1[j, :, ds(inner, eighth), :].astype(F32)).astype(BF)
        second_copy(j).start()

    def fold_z(j):
        second_copy(j).wait_recv()
        _, _, a1, a2 = order(j)
        inner = a2 * eighth
        rows = ds(c * half + a1 * 2 * eighth + inner, eighth)
        total = gw[j, :, rows, :].astype(F32) + q0[j, :, ds(a1 * 2 * eighth + inner, eighth), :].astype(F32)
        total = total + q1[j, :, ds(inner, eighth), :].astype(F32) + q2[j].astype(F32)
        qz[j, z] = total.astype(BF)
        for k in range(1, ranks):
            z_copy(j, k).start()

    def fold_all(j):
        for k in range(1, ranks):
            z_copy(j, k).wait_recv()
        total = qz[j, 0].astype(F32)
        for k in range(1, ranks):
            total = total + qz[j, k].astype(F32)
        qf[j] = total.astype(BF)

        def go(ref):
            keep_copy(j, ref).start()
            spread_copies(j, ref, 0).start()

        each_place(j, 0, go)

    def spread_first(j):
        def done(ref):
            keep_copy(j, ref).wait()
            spread_copies(j, ref, 0).wait_recv()

        each_place(j, 0, done)
        each_place(j, 1, lambda ref: spread_copies(j, ref, 1).start())

    def spread_sibling(j):
        each_place(j, 1, lambda ref: spread_copies(j, ref, 1).wait_recv())
        each_place(j, 2, lambda ref: spread_copies(j, ref, 2).start())

    def chunk_done(j):
        each_place(j, 2, lambda ref: spread_copies(j, ref, 2).wait())
        each_place(j, 1, lambda ref: spread_copies(j, ref, 1).wait_send())
        each_place(j, 0, lambda ref: spread_copies(j, ref, 0).wait_send())
        core_copy(j).wait_send()
        first_copy(j).wait_send()
        second_copy(j).wait_send()
        for k in range(1, ranks):
            z_copy(j, k).wait_send()

    def small_copy(level):
        row = (r_sib, r_x, r_y)[level]
        return remote(sma.at[level], smr.at[level], sms.at[level], smrs.at[level], row, z)

    def small_z(k):
        return remote(smz.at[z], smz.at[z], smzs.at[k - 1], smzr.at[k - 1], r, lax.rem(z + k, ranks))

    barrier = pltpu.get_barrier_semaphore()
    partners = [(r_sib, z), (r_x, z), (r_y, z), (r_diag, z)] + [(r, lax.rem(z + k, ranks)) for k in range(1, ranks)]
    for row, column in partners:
        pl.semaphore_signal(barrier, inc=1, device_id={"rows": row, "mlp": column}, device_id_type=MESH)
    load_qkv.start()
    load_out.start()
    own_shard(0).start()
    own_shard(1).start()
    pl.semaphore_wait(barrier, len(partners))
    for k in range(1, ranks):
        for kind in range(2):
            for mat in range(2):
                gather_copy(k, mat, kind).start()
    for i in range(images):
        work[...] = jnp.zeros_like(work)
        work[0:patches, :] = c_ref[i]
        cot[i * tall : (i + 1) * tall, :] = work[...]
    cot_copy.start()

    @pl.loop(0, images)
    def _(i):
        forward_rows(i, x_ref, rank_ref, kept_ref, g1_ref, rw_ref, xp, keep, gate, h1, h1t, work)

    h1t[...] = h1[...].T
    load_qkv.wait()

    @pl.loop(0, 3 * width // 256)
    def _(j):
        forward_qkv(j, h1, wqkv, qkv)

    @pl.loop(0, HEADS // 2)
    def _(p):
        for i in range(images):
            attend(p, i, width, tall, qkv, keep, probs, context, contextt)

        @pl.when(p == 2)
        def _():
            gather_forward(1)

        @pl.when(p == 5)
        def _():
            gather_forward(2)

    load_out.wait()

    @pl.loop(0, images)
    def _(i):
        forward_out(i, tall, context, wout, xp, keep, gate, g2_ref, attended, middle, tok)
        token_copy(i).start()

    own_shard(0).wait()
    own_shard(1).wait()
    for ref in (out, gh2, dg1, dg2, drw):
        ref[...] = jnp.zeros_like(ref)

    def mlp_step(k):
        @pl.loop(0, 2 * images)
        def _(block):
            @pl.when(jnp.logical_and(k == 0, block == images))
            def _():
                for i in range(images):
                    token_copy(i).wait()
                cot_copy.wait()

            rows = ds(lax.rem(block + images * lax.div(k, ranks - 1), 2 * images) * tall, tall)
            hid[rows, :], gpre[rows, :] = mlp_rows(tok[rows, :], cot[rows, :], w1[k], w2[k])
            out[rows, :] += dot_nn(hid[rows, :], w2[k])
            gh2[rows, :] += dot_nt(gpre[rows, :], w1[k])

            @pl.when(jnp.logical_and(k == ranks - 1, block == images - 1))
            def _():
                gh2_copy.start()
                out_copy.start()

        @pl.when(k == 0)
        def _():
            tokt[...] = tok[...].T

        hidt[...] = hid[...].T
        for m in range(3):
            rows = slice(m * width // 3, (m + 1) * width // 3)
            g1w[k, rows, :] = dot_nn(tokt[rows, :], gpre[...]).astype(BF)
            g2w[k, :, rows] = dot_nn(hidt[...], cot[:, rows]).astype(BF)

    @pl.loop(0, LAST)
    def _(t):
        for k in range(1, ranks):

            @pl.when(t == k)
            def _(k=k):
                gather_finish(k)

        @pl.when(t < ranks)
        def _():
            mlp_step(t)
            for copy in fc_first(t):
                copy.start()

        @pl.when(t == 1)
        def _():
            gather_forward(3)

        @pl.when(t == 4)
        def _():
            gh2_copy.wait()
            out_copy.wait()

            @pl.loop(0, images)
            def _(i):
                rows = ds(i * tall, tall)
                gh2[rows, :] += gh2_in[rows, :]
                back_rows(
                    i, tall, cot, gh2, middle, keep, gate, attended, g2_ref, gh2, tok, glogit, dg2
                )

            context[...] = dot_nt(tok[ds(0, t_own), :], wout[...]).astype(BF)

        @pl.when(jnp.logical_and(t >= 4, t < 6))
        def _():
            cols = lanes((t - 4) * half, half)
            total = 0.0
            for i in range(images):
                total = total + dot_nn(contextt[i], tok[i * tall : (i + 1) * tall, cols])
            for b in range(3):
                gw[t - 4, b] = total[:, b * 128 : (b + 1) * 128].astype(BF)

        @pl.when(jnp.logical_and(t >= 6, t < 12))
        def _():
            p = t - 6
            for i in range(images):
                attend_back(p, i, width, tall, qkv, probs, context)
            total = dot_nn(h1t[...], pair_columns(qkv, p, width))
            for b in range(3):
                gw[t - 4, b] = total[:, b * 128 : (b + 1) * 128].astype(BF)

        @pl.when(jnp.logical_and(t >= 4, t < 12))
        def _():
            core_copy(t - 4).start()

        @pl.when(t == 5)
        def _():
            @pl.loop(0, images)
            def _(i):
                rows = ds(i * tall, tall)
                block_ref[i] = (middle[rows, :] + out[rows, :] + out_in[rows, :]).astype(BF)[0:patches, :]

        @pl.when(t == 12)
        def _():
            @pl.loop(0, images)
            def _(i):
                rows = ds(i * tall, tall)
                dy = dot_nt(qkv[rows, :], wqkv[...])
                back_input(i, tall, dy, glogit, rw_ref, xp, h1, g1_ref, gh2, gx_ref, dg1, drw)

            sma[0] = jnp.concatenate([dg1[...], drw[...], dg2[...], jnp.zeros((5, width), F32)], 0)
            small_copy(0).start()

        for level in range(2):

            @pl.when(t == 13 + level)
            def _(level=level):
                small_copy(level).wait()
                sma[level + 1] = sma[level] + smr[level]
                small_copy(level + 1).start()

        @pl.when(t == 15)
        def _():
            small_copy(2).wait()
            smz[z] = sma[2] + smr[2]
            for k in range(1, ranks):
                small_z(k).start()

        def lagged(lag, do):
            @pl.when(jnp.logical_and(t >= 4 + lag, t < 4 + lag + CHUNKS))
            def _():
                do(t - 4 - lag)

        @pl.when(jnp.logical_and(t >= 2, t < 2 + ranks))
        def _():
            fc_fold_third(t - 2)

        @pl.when(jnp.logical_and(t >= 1, t < 1 + ranks))
        def _():
            fc_fold_second(t - 1)

        @pl.when(t == 7)
        def _():
            fc_finish()

        @pl.when(t == 9)
        def _():
            fc_to_sibling()

        lagged(6, spread_sibling)
        lagged(5, spread_first)
        lagged(4, fold_all)
        lagged(3, fold_z)
        lagged(2, fold_second)
        lagged(1, fold_first)

    for k in range(1, ranks):
        small_z(k).wait()
    total = smz[0]
    for k in range(1, ranks):
        total = total + smz[k]
    small_out[...] = total

    @pl.loop(0, CHUNKS)
    def _(j):
        chunk_done(j)

    for copy in fc_share:
        copy.wait()
    for kind in range(3):
        for copy in fc_spread(kind):
            copy.wait_send()
    for k in range(1, ranks):
        for copy in fc_third(k):
            copy.wait_send()
        for mat in range(2):
            for kind in range(5):
                gather_copy(k, mat, kind).wait_send()

    @pl.loop(0, ranks)
    def _(k):
        for copy in fc_first(k) + fc_second(k):
            copy.wait_send()


VMEM = pl.BlockSpec(memory_space=pltpu.VMEM)
SMEM = pl.BlockSpec(memory_space=pltpu.SMEM)
ANY = pl.BlockSpec(memory_space=pl.ANY)


def widen_kernel(gq, go, f1, f2, small, gq_out, go_out, f1_out, f2_out, g1_out, rw_out, g2_out):
    width = f1.shape[1]
    for b in range(3):
        gq_out[:, b * width : (b + 1) * width] = gq[b].astype(F32)
    for b in range(go.shape[0]):
        go_out[:, b * 128 : (b + 1) * 128] = go[b].astype(F32)
    f1_out[...] = f1[...].astype(F32)
    f2_out[...] = f2[...].astype(F32)
    g1_out[...], rw_out[...], g2_out[...] = small[0], small[1], small[2]


def widen(gq, go, f1, f2, small):
    width = f1.shape[0]
    step = 128

    def rows(*tail):
        return pl.BlockSpec((step,) + tail, lambda i: (i, 0))

    def inner(lead, tail):
        return pl.BlockSpec((lead, step, tail), lambda i: (0, i, 0))

    return pl.pallas_call(
        widen_kernel,
        grid=(width // step,),
        out_shape=[jax.ShapeDtypeStruct((width, n), F32) for n in (3 * width, width, width, width)]
        + [jax.ShapeDtypeStruct((width,), F32)] * 3,
        in_specs=[inner(3, width), inner(6, 128), rows(width), rows(width), pl.BlockSpec((8, width), lambda i: (0, 0))],
        out_specs=[rows(3 * width), rows(width), rows(width), rows(width)] + [pl.BlockSpec((width,), lambda i: (0,))] * 3,
        compiler_params=pltpu.CompilerParams(vmem_limit_bytes=48 * 1024 * 1024),
        name="widen",
    )(gq, go, f1, f2, small)


def per_device(ranks, others, images, patch_rank, kept_count, ln1_gain, router_weight, w_qkv, w_out, ln2_gain, w_fc1, w_fc2, cotangent):
    count, patches, width = images.shape
    tall = -(-patches // 16) * 16
    t = count * tall
    part = w_fc1.shape[1] // 2
    half, eighth = width // 2, width // 8

    def bf(*dims):
        return pltpu.VMEM(dims, BF)

    def f32(*dims):
        return pltpu.VMEM(dims, F32)

    def sem(*dims):
        return pltpu.SemaphoreType.DMA(dims)

    scratch = [
        bf(width, 3 * width), bf(width, width), bf(ranks, width, part), bf(ranks, part, width),
        bf(t, width), f32(t, 128), f32(t, 128), f32(t, 128), bf(t, width), bf(width, t), bf(t, 3 * width),
        f32(count, HEADS, tall, tall), bf(count, width, tall), bf(t, width), f32(t, width), f32(t, width),
        bf(2 * t, width), bf(2 * t, width), bf(width, 2 * t), f32(2 * t, width), f32(2 * t, width),
        f32(t, width), f32(t, width), bf(2 * t, part), bf(part, 2 * t), bf(2 * t, part), bf(tall, width),
        bf(ranks, width, part), bf(ranks, part, width),
        bf(ranks, width // 2, part), bf(ranks, part // 2, width), bf(ranks, width // 4, part), bf(ranks, part // 4, width),
        bf(ranks, width // 4, part), bf(ranks, part // 4, width), bf(ranks - 1, width // 4, part), bf(ranks - 1, part // 4, width),
        bf(CHUNKS, 3, width, 128), bf(CHUNKS, 3, half, 128), bf(CHUNKS, 3, 2 * eighth, 128), bf(CHUNKS, 3, eighth, 128),
        bf(CHUNKS, ranks, 3, eighth, 128), bf(CHUNKS, 3, eighth, 128),
        f32(1, width), f32(1, width), f32(1, width), f32(3, 8, width), f32(3, 8, width), f32(ranks, 8, width),
        sem(4), sem(ranks - 1, 2, 5), sem(ranks - 1, 2, 5), sem(count + 1), sem(count + 1), sem(2), sem(2),
        sem(ranks, 2), sem(ranks, 2), sem(ranks, 2), sem(ranks, 2), sem(ranks - 1, 2), sem(ranks - 1, 2),
        sem(3, 2), sem(3, 2), sem(2), sem(2), sem(2),
        sem(CHUNKS), sem(CHUNKS), sem(CHUNKS), sem(CHUNKS), sem(CHUNKS), sem(CHUNKS),
        sem(CHUNKS, ranks - 1), sem(CHUNKS, ranks - 1), sem(CHUNKS),
        sem(CHUNKS), sem(CHUNKS), sem(CHUNKS), sem(CHUNKS), sem(CHUNKS), sem(CHUNKS),
        sem(3), sem(3), sem(ranks - 1), sem(ranks - 1),
    ]

    def struct(*dims, dtype=BF):
        return jax.ShapeDtypeStruct(dims, dtype)

    block, gx, gq, go, f1, f2, small = pl.pallas_call(
        functools.partial(mega_kernel, ranks),
        out_shape=[
            struct(count, patches, width), struct(count, patches, width), struct(3, width, width), struct(6, width, 128),
            struct(width, 2 * part), struct(2 * part, width), struct(8, width, dtype=F32),
        ],
        in_specs=[VMEM, VMEM, SMEM, VMEM, VMEM, ANY, ANY, VMEM, ANY, ANY, VMEM],
        out_specs=[VMEM, VMEM, ANY, ANY, ANY, ANY, VMEM],
        scratch_shapes=scratch,
        compiler_params=pltpu.CompilerParams(
            collective_id=0, has_side_effects=True, vmem_limit_bytes=63 * 1024 * 1024
        ),
        name="block",
    )(images, patch_rank, kept_count, ln1_gain, router_weight, w_qkv, w_out, ln2_gain, w_fc1, w_fc2, cotangent)
    gq, go, f1, f2, g1, rw, g2 = widen(gq, go, f1, f2, small)
    if others:
        gq, go, f1, f2, g1, rw, g2 = lax.psum((gq, go, f1, f2, g1, rw, g2), "rows", axis_index_groups=others)
    return block, gx, g1, rw, gq, go, g2, f1, f2


def solution(mesh):
    rows, ranks = mesh.shape["rows"], mesh.shape["mlp"]
    others = [[8 * g + i for g in range(rows // 8)] for i in range(8)] if rows > 8 else None
    return jax.shard_map(
        functools.partial(per_device, ranks, others),
        mesh=mesh,
        in_specs=(
            P(("rows", "mlp"), None, None), P(("rows", "mlp"), None), P(("rows", "mlp")), P(), P(), P(), P(), P(),
            P(None, "mlp"), P("mlp", None), P(("rows", "mlp"), None, None),
        ),
        out_specs=(
            P(("rows", "mlp"), None, None), P(("rows", "mlp"), None, None), P(), P(), P(), P(), P(),
            P(None, "mlp"), P("mlp", None),
        ),
        check_vma=False,
    )
```

```python
import functools
import jax
import jax.numpy as jnp
from jax import lax
from jax.experimental import pallas as pl
from jax.experimental.pallas import tpu as pltpu
from jax.sharding import PartitionSpec as P

HEADS = 12
EPS = 1e-6
FILL = -1e30
BF = jnp.bfloat16
F32 = jnp.float32


def dot_nn(a, b):
    return lax.dot_general(a, b, (((1,), (0,)), ((), ())), preferred_element_type=F32)


def dot_nt(a, b):
    return lax.dot_general(a, b, (((1,), (1,)), ((), ())), preferred_element_type=F32)


def dot_tn(a, b):
    return lax.dot_general(a, b, (((0,), (0,)), ((), ())), preferred_element_type=F32)


def unit_rows(v):
    center = v - jnp.mean(v, -1, keepdims=True)
    scale = lax.rsqrt(jnp.mean(center * center, -1, keepdims=True) + EPS)
    return center * scale, scale


def norm_pull(dy, gain, unit, scale):
    du = dy * gain
    return scale * (
        du
        - jnp.mean(du, -1, keepdims=True)
        - unit * jnp.mean(du * unit, -1, keepdims=True)
    )


def half_mask(rows, h):
    lane = lax.broadcasted_iota(jnp.int32, (rows, 128), 1)
    return (lane < 64) if h == 0 else (lane >= 64)


def forward_rows(i, x_ref, rank_ref, kept_ref, g1_ref, rw_ref, xp, keep, gate, h1, h1t, work):
    patches, width = x_ref.shape[1:]
    tall = xp.shape[0] // x_ref.shape[0]
    rows = pl.ds(pl.multiple_of(i * tall, 16), tall)
    work[...] = jnp.zeros_like(work)
    work[0:patches, :] = x_ref[i]
    v = work[...]
    xp[rows, :] = v
    kept = (rank_ref[pl.ds(i, 1), :] < kept_ref[i]).astype(F32)
    keep_row = jnp.concatenate([kept, jnp.zeros((1, 256 - patches), F32)], 1)
    keep_col = jnp.broadcast_to(keep_row, (128, 256)).T
    keep[rows, :] = keep_col[0:tall, :]
    unit, _ = unit_rows(v.astype(F32))
    low = (unit * g1_ref[...][None]).astype(BF)
    h1[rows, :] = low
    logit = jnp.sum(low.astype(F32) * rw_ref[...][None].astype(F32), -1, keepdims=True)
    gate[rows, :] = jnp.broadcast_to(jax.nn.sigmoid(logit), (tall, 128))


def forward_qkv(j, h1, wqkv, qkv):
    cols = pl.ds(pl.multiple_of(j * 256, 256), 256)
    qkv[:, cols] = dot_nn(h1[...], wqkv[:, cols]).astype(BF)


def attend(p, i, width, tall, qkv, keep, probs, context, contextt):
    rows = pl.ds(pl.multiple_of(i * tall, 16), tall)
    qc = pl.ds(pl.multiple_of(p * 128, 128), 128)
    kc = pl.ds(pl.multiple_of(width + p * 128, 128), 128)
    vc = pl.ds(pl.multiple_of(2 * width + p * 128, 128), 128)
    q, k, v = qkv[rows, qc], qkv[rows, kc], qkv[rows, vc]
    vt = v.T
    kept = keep[rows, 0:1] > 0.5
    outs = []
    for h in range(2):
        kh = jnp.where(half_mask(tall, h), k, jnp.zeros_like(k))
        s = jnp.where(kept, dot_nt(kh, q) * 0.125, FILL)
        e = jnp.exp(s - jnp.max(s, 0, keepdims=True))
        pr = e * (1.0 / jnp.sum(e, 0, keepdims=True))
        probs[i, p * 2 + h] = pr
        outs.append(dot_nn(vt[h * 64 : h * 64 + 64, :], pr.astype(BF)))
    ct = jnp.concatenate(outs, 0)
    contextt[i, pl.ds(pl.multiple_of(p * 128, 128), 128), :] = ct.astype(BF)
    context[rows, qc] = ct.T.astype(BF)


def forward_out(i, tall, context, wout, xp, keep, gate, g2_ref, attended, middle, h2):
    rows = pl.ds(pl.multiple_of(i * tall, 16), tall)
    att = dot_nn(context[rows, :], wout[...])
    attended[rows, :] = att
    mid = xp[rows, :].astype(F32) + keep[rows, 0:1] * gate[rows, 0:1] * att
    middle[rows, :] = mid
    unit, _ = unit_rows(mid)
    h2[rows, :] = (unit * g2_ref[...][None]).astype(BF)


def gelu_pair(pre):
    cdf = 0.5 * (1.0 + lax.erf(pre * 0.7071067811865476))
    pdf = jnp.exp(pre * pre * -0.5) * 0.3989422804014327
    return pre * cdf, cdf + pre * pdf


def mlp_rows(h, c, w1, w2):
    pre = dot_nn(h, w1)
    hidden, slope = gelu_pair(pre)
    grad = dot_nt(c, w2) * slope
    return hidden.astype(BF), grad.astype(BF)


def back_rows(i, tall, c_ref, gh2, middle, keep, gate, attended, g2_ref, gmid, gatt, glogit, dg2):
    rows = pl.ds(pl.multiple_of(i * tall, 16), tall)
    dy = gh2[rows, :]
    unit, scale = unit_rows(middle[rows, :])
    gm = c_ref[rows, :].astype(F32) + norm_pull(dy, g2_ref[...][None], unit, scale)
    gmid[rows, :] = gm
    dg2[...] += jnp.sum(dy * unit, 0, keepdims=True)
    k, g = keep[rows, 0:1], gate[rows, 0:1]
    kept = gm * k
    gatt[rows, :] = (kept * g).astype(BF)
    gl = jnp.sum(kept * attended[rows, :], -1, keepdims=True) * g * (1.0 - g)
    glogit[rows, :] = jnp.broadcast_to(gl, (tall, 128))


def attend_back(p, i, width, tall, qkv, probs, gctx):
    rows = pl.ds(pl.multiple_of(i * tall, 16), tall)
    qc = pl.ds(pl.multiple_of(p * 128, 128), 128)
    kc = pl.ds(pl.multiple_of(width + p * 128, 128), 128)
    vc = pl.ds(pl.multiple_of(2 * width + p * 128, 128), 128)
    q, k, v = qkv[rows, qc], qkv[rows, kc], qkv[rows, vc]
    gc = gctx[rows, qc]
    kt = k.T
    gv, gk, gq = 0.0, 0.0, []
    for h in range(2):
        mask = half_mask(tall, h)
        zero = jnp.zeros_like(v)
        pr = probs[i, p * 2 + h]
        gp = dot_nt(jnp.where(mask, v, zero), gc)
        gs = (pr * (gp - jnp.sum(pr * gp, 0, keepdims=True))).astype(BF)
        gv = gv + dot_nn(pr.astype(BF), jnp.where(mask, gc, zero))
        gk = gk + dot_nn(gs, jnp.where(mask, q, zero))
        gq.append(dot_nn(kt[h * 64 : h * 64 + 64, :], gs))
    qkv[rows, qc] = (jnp.concatenate(gq, 0).T * 0.125).astype(BF)
    qkv[rows, kc] = (gk * 0.125).astype(BF)
    qkv[rows, vc] = gv.astype(BF)


def pair_columns(wqkv, p, width):
    return jnp.concatenate(
        [wqkv[:, pl.ds(pl.multiple_of(b * width + p * 128, 128), 128)] for b in range(3)], 1
    )


def back_input(i, tall, dy, glogit, rw_ref, xp, h1, g1_ref, gmid, gx_ref, dg1, drw):
    rows = pl.ds(pl.multiple_of(i * tall, 16), tall)
    patches = gx_ref.shape[1]
    gl = glogit[rows, 0:1]
    dy = dy + gl * rw_ref[...][None].astype(F32)
    unit, scale = unit_rows(xp[rows, :].astype(F32))
    dg1[...] += jnp.sum(dy * unit, 0, keepdims=True)
    drw[...] += jnp.sum(h1[rows, :].astype(F32) * gl, 0, keepdims=True)
    out = gmid[rows, :] + norm_pull(dy, g1_ref[...][None], unit, scale)
    gx_ref[i] = out.astype(BF)[0:patches, :]

MESH = pl.DeviceIdType.MESH
CHUNKS = HEADS // 2 + 2
LAST = 4 + CHUNKS + 9


def mega_kernel(
    ranks, x_ref, rank_ref, kept_ref, g1_ref, rw_ref, wqkv_hbm, wout_hbm, g2_ref, fc1, fc2, c_ref,
    block_ref, gx_ref, gq_out, go_out, f1_out, f2_out, small_out,
    wqkv, wout, w1, w2, xp, keep, gate, glogit, h1, h1t, qkv, probs, contextt, context, attended, middle,
    tok, cot, tokt, out, gh2, out_in, gh2_in, hid, hidt, gpre, work,
    g1w, g2w, r1a, r1b, r2a, r2b, fz1, fz2, rz1, rz2,
    gw, q0, q1, q2, qz, qf, dg1, dg2, drw, sma, smr, smz,
    lsem, gsend, grecv, tsend, trecv, esend, erecv, s1s, s1r, s2s, s2r, s3s, s3r, fs, fr, floc, ssib, rsib,
    q0s, q0r, q1s, q1r, q2s, q2r, q3s, q3r, qloc, q5s, q5r, q6s, q6r, q7s, q7r, sms, smrs, smzs, smzr,
):
    images, patches, width = x_ref.shape
    t_own = xp.shape[0]
    tall = t_own // images
    half = width // 2
    part = w1.shape[2]
    quarter = (width // 4, part // 4)
    r = lax.axis_index("rows")
    z = lax.axis_index("mlp")
    c, x, y = lax.rem(r, 2), lax.rem(lax.div(r, 2), 2), lax.rem(lax.div(r, 4), 2)
    r_sib, r_x, r_y = r + 1 - 2 * c, r + 2 - 4 * x, r + 4 - 8 * y
    r_diag = r_x + r_y - r
    q = 2 * y + x

    def ds(start, size):
        return pl.ds(pl.multiple_of(start, 16), size)

    def lanes(start, size):
        return pl.ds(pl.multiple_of(start, 128), size)

    def remote(src, dst, send, recv, row, column):
        return pltpu.make_async_remote_copy(
            src_ref=src, dst_ref=dst, send_sem=send, recv_sem=recv,
            device_id={"rows": row, "mlp": column}, device_id_type=MESH,
        )

    def distance(k):
        return k + lax.div(k, 2) * (1 - 2 * lax.rem(k, 2))

    def gather_copy(k, mat, kind):
        held, size = (w1, w2)[mat], quarter[mat]
        cut = size // 3
        sems = gsend.at[k - 1, mat, kind], grecv.at[k - 1, mat, kind]
        if kind < 2:
            start, count = ((q * size, size), ((3 - q) * size, cut))[kind]
            if mat == 0:
                src = fc1.at[ds(start, count), lanes(c * part, part)]
            else:
                src = fc2.at[ds(c * part + start, count), :]
            return remote(src, held.at[k, ds(start, count), :], *sems, r, lax.rem(z - distance(k) + ranks, ranks))
        start, count = (q * size, size) if kind < 4 else (q * size + cut, size - cut)
        place = held.at[k, ds(start, count), :]
        return remote(place, place, *sems, (r_x, r_y, r_diag)[kind - 2], z)

    def gather_start(k):
        for kind in range(2):
            for mat in range(2):
                gather_copy(k, mat, kind).start()

    def gather_forward(k):
        for mat in range(2):
            gather_copy(k, mat, 0).wait_recv()
        if k + 1 < ranks:
            gather_start(k + 1)
        for mat in range(2):
            for kind in (2, 3, 4):
                gather_copy(k, mat, kind).start()

    def gather_finish(k):
        for mat in range(2):
            for kind in (1, 2, 3, 4):
                gather_copy(k, mat, kind).wait_recv()

    def own_shard(mat):
        if mat == 0:
            return pltpu.make_async_copy(fc1.at[:, lanes(c * part, part)], w1.at[0], lsem.at[0])
        return pltpu.make_async_copy(fc2.at[ds(c * part, part), :], w2.at[0], lsem.at[1])

    load_qkv = pltpu.make_async_copy(wqkv_hbm, wqkv, lsem.at[2])
    load_out = pltpu.make_async_copy(wout_hbm, wout, lsem.at[3])

    def token_copy(i):
        src, dst = tok.at[ds(i * tall, tall), :], tok.at[ds(t_own + i * tall, tall), :]
        return remote(src, dst, tsend.at[i], trecv.at[i], r_sib, z)

    cot_copy = remote(
        cot.at[ds(0, t_own), :], cot.at[ds(t_own, t_own), :], tsend.at[images], trecv.at[images], r_sib, z
    )
    gh2_copy = remote(gh2.at[ds(t_own, t_own), :], gh2_in, esend.at[0], erecv.at[0], r_sib, z)
    out_copy = remote(out.at[ds(t_own, t_own), :], out_in, esend.at[1], erecv.at[1], r_sib, z)

    h1r, q1r_rows = width // 2, width // 4
    h2r, q2r_rows = part // 2, part // 4

    def fc_first(k):
        return (
            remote(g1w.at[k, ds((1 - x) * h1r, h1r), :], r1a.at[k], s1s.at[k, 0], s1r.at[k, 0], r_x, z),
            remote(g2w.at[k, ds((1 - y) * h2r, h2r), :], r1b.at[k], s1s.at[k, 1], s1r.at[k, 1], r_y, z),
        )

    def fc_second(k):
        return (
            remote(
                g1w.at[k, ds(x * h1r + (1 - y) * q1r_rows, q1r_rows), :], r2a.at[k], s2s.at[k, 0], s2r.at[k, 0], r_y, z
            ),
            remote(
                g2w.at[k, ds(y * h2r + (1 - x) * q2r_rows, q2r_rows), :], r2b.at[k], s2s.at[k, 1], s2r.at[k, 1], r_x, z
            ),
        )

    def fc_third(k):
        column = lax.rem(z + distance(k), ranks)
        return (
            remote(fz1.at[k], rz1.at[k - 1], s3s.at[k - 1, 0], s3r.at[k - 1, 0], r, column),
            remote(fz2.at[k], rz2.at[k - 1], s3s.at[k - 1, 1], s3r.at[k - 1, 1], r, column),
        )

    f1_place = f1_out.at[ds(x * h1r + y * q1r_rows, q1r_rows), lanes(c * part, part)]
    f2_place = f2_out.at[ds(c * part + y * h2r + x * q2r_rows, q2r_rows), :]

    def fc_spread(kind):
        row = (r_x, r_y, r_diag)[kind]
        return (
            remote(fz1.at[0], f1_place, fs.at[kind, 0], fr.at[kind, 0], row, z),
            remote(fz2.at[0], f2_place, fs.at[kind, 1], fr.at[kind, 1], row, z),
        )

    fc_keep = (
        pltpu.make_async_copy(fz1.at[0], f1_place, floc.at[0]),
        pltpu.make_async_copy(fz2.at[0], f2_place, floc.at[1]),
    )
    f1_half = f1_out.at[:, lanes(c * part, part)]
    f2_half = f2_out.at[ds(c * part, part), :]
    fc_share = (
        remote(f1_half, f1_half, ssib.at[0], rsib.at[0], r_sib, z),
        remote(f2_half, f2_half, ssib.at[1], rsib.at[1], r_sib, z),
    )

    def fc_fold_second(k):
        for copy in fc_first(k):
            copy.wait_recv()
        rows = ds(x * h1r + (1 - y) * q1r_rows, q1r_rows)
        g1w[k, rows, :] = g1w[k, rows, :] + r1a[k, ds((1 - y) * q1r_rows, q1r_rows), :]
        rows = ds(y * h2r + (1 - x) * q2r_rows, q2r_rows)
        g2w[k, rows, :] = g2w[k, rows, :] + r1b[k, ds((1 - x) * q2r_rows, q2r_rows), :]
        for copy in fc_second(k):
            copy.start()

    def fc_fold_third(k):
        for copy in fc_second(k):
            copy.wait_recv()
        total = g1w[k, ds(x * h1r + y * q1r_rows, q1r_rows), :].astype(F32)
        total = total + r1a[k, ds(y * q1r_rows, q1r_rows), :].astype(F32) + r2a[k].astype(F32)
        fz1[k] = total.astype(BF)
        total = g2w[k, ds(y * h2r + x * q2r_rows, q2r_rows), :].astype(F32)
        total = total + r1b[k, ds(x * q2r_rows, q2r_rows), :].astype(F32) + r2b[k].astype(F32)
        fz2[k] = total.astype(BF)

        @pl.when(k > 0)
        def _():
            for copy in fc_third(k):
                copy.start()

    def fc_finish():
        for k in range(1, ranks):
            for copy in fc_third(k):
                copy.wait_recv()
        for own, arrived in ((fz1, rz1), (fz2, rz2)):
            total = own[0].astype(F32)
            for k in range(ranks - 1):
                total = total + arrived[k].astype(F32)
            own[0] = total.astype(BF)
        for copy in fc_keep:
            copy.start()
        for kind in range(3):
            for copy in fc_spread(kind):
                copy.start()

    def fc_to_sibling():
        for copy in fc_keep:
            copy.wait()
        for kind in range(3):
            for copy in fc_spread(kind):
                copy.wait_recv()
        for copy in fc_share:
            copy.start()

    eighth = width // 8

    def order(j):
        odd = lax.rem(j, 2)
        first, second = r_x + (r_y - r_x) * odd, r_y + (r_x - r_y) * odd
        a1, a2 = x + (y - x) * odd, y + (x - y) * odd
        return first, second, a1, a2

    def chunk_place(j, start, count):
        rows = ds(start, count)
        return (
            (j < 2, go_out.at[pl.ds(3 * lax.min(j, 1), 3), rows, :]),
            (j >= 2, gq_out.at[:, rows, lanes(lax.max(j - 2, 0) * 128, 128)]),
        )

    def core_copy(j):
        return remote(gw.at[j, :, ds((1 - c) * half, half), :], q0.at[j], q0s.at[j], q0r.at[j], r_sib, z)

    def first_copy(j):
        first, _, a1, _ = order(j)
        src = gw.at[j, :, ds(c * half + (1 - a1) * 2 * eighth, 2 * eighth), :]
        return remote(src, q1.at[j], q1s.at[j], q1r.at[j], first, z)

    def second_copy(j):
        _, second, a1, a2 = order(j)
        src = gw.at[j, :, ds(c * half + a1 * 2 * eighth + (1 - a2) * eighth, eighth), :]
        return remote(src, q2.at[j], q2s.at[j], q2r.at[j], second, z)

    def z_copy(j, step):
        column = (z + 1 - 2 * lax.rem(z, 2), z + 2 - 4 * lax.div(z, 2))[step]
        return remote(qz.at[j, 2 * step], qz.at[j, 2 * step + 1], q3s.at[j, step], q3r.at[j, step], r, column)

    def own_start(j):
        _, _, a1, a2 = order(j)
        return c * half + a1 * 2 * eighth + a2 * eighth

    def keep_copy(j, ref):
        return pltpu.make_async_copy(qf.at[j], ref, qloc.at[j])

    def spread_copies(j, ref, level):
        first, second, _, _ = order(j)
        if level == 0:
            return remote(qf.at[j], ref, q5s.at[j], q5r.at[j], second, z)
        if level == 1:
            return remote(ref, ref, q6s.at[j], q6r.at[j], first, z)
        return remote(ref, ref, q7s.at[j], q7r.at[j], r_sib, z)

    def level_place(j, level):
        _, _, a1, _ = order(j)
        if level == 0:
            return chunk_place(j, own_start(j), eighth)
        if level == 1:
            return chunk_place(j, c * half + a1 * 2 * eighth, 2 * eighth)
        return chunk_place(j, c * half, half)

    def each_place(j, level, do):
        for condition, ref in level_place(j, level):

            @pl.when(condition)
            def _(ref=ref):
                do(ref)

    def fold_first(j):
        core_copy(j).wait_recv()
        _, _, a1, _ = order(j)
        rows = ds(c * half + (1 - a1) * 2 * eighth, 2 * eighth)
        gw[j, :, rows, :] = gw[j, :, rows, :] + q0[j, :, ds((1 - a1) * 2 * eighth, 2 * eighth), :]
        first_copy(j).start()

    def fold_second(j):
        first_copy(j).wait_recv()
        _, _, a1, a2 = order(j)
        inner = (1 - a2) * eighth
        rows = ds(c * half + a1 * 2 * eighth + inner, eighth)
        total = gw[j, :, rows, :].astype(F32) + q0[j, :, ds(a1 * 2 * eighth + inner, eighth), :].astype(F32)
        gw[j, :, rows, :] = (total + q1[j, :, ds(inner, eighth), :].astype(F32)).astype(BF)
        second_copy(j).start()

    def fold_z(j):
        second_copy(j).wait_recv()
        _, _, a1, a2 = order(j)
        inner = a2 * eighth
        rows = ds(c * half + a1 * 2 * eighth + inner, eighth)
        total = gw[j, :, rows, :].astype(F32) + q0[j, :, ds(a1 * 2 * eighth + inner, eighth), :].astype(F32)
        total = total + q1[j, :, ds(inner, eighth), :].astype(F32) + q2[j].astype(F32)
        qz[j, 0] = total.astype(BF)
        z_copy(j, 0).start()

    def fold_pair(j):
        z_copy(j, 0).wait_recv()
        qz[j, 2] = qz[j, 0] + qz[j, 1]
        z_copy(j, 1).start()

    def fold_all(j):
        z_copy(j, 1).wait_recv()
        qf[j] = qz[j, 2] + qz[j, 3]

        def go(ref):
            keep_copy(j, ref).start()
            spread_copies(j, ref, 0).start()

        each_place(j, 0, go)

    def spread_first(j):
        def done(ref):
            keep_copy(j, ref).wait()
            spread_copies(j, ref, 0).wait_recv()

        each_place(j, 0, done)
        each_place(j, 1, lambda ref: spread_copies(j, ref, 1).start())

    def spread_sibling(j):
        each_place(j, 1, lambda ref: spread_copies(j, ref, 1).wait_recv())
        each_place(j, 2, lambda ref: spread_copies(j, ref, 2).start())

    def chunk_done(j):
        each_place(j, 2, lambda ref: spread_copies(j, ref, 2).wait())
        each_place(j, 1, lambda ref: spread_copies(j, ref, 1).wait_send())
        each_place(j, 0, lambda ref: spread_copies(j, ref, 0).wait_send())
        core_copy(j).wait_send()
        first_copy(j).wait_send()
        second_copy(j).wait_send()
        for step in range(2):
            z_copy(j, step).wait_send()

    def small_copy(level):
        row = (r_sib, r_x, r_y)[level]
        return remote(sma.at[level], smr.at[level], sms.at[level], smrs.at[level], row, z)

    def small_z(k):
        return remote(smz.at[z], smz.at[z], smzs.at[k - 1], smzr.at[k - 1], r, lax.rem(z + k, ranks))

    barrier = pltpu.get_barrier_semaphore()
    partners = [(r_sib, z), (r_x, z), (r_y, z), (r_diag, z)] + [(r, lax.rem(z + k, ranks)) for k in range(1, ranks)]
    for row, column in partners:
        pl.semaphore_signal(barrier, inc=1, device_id={"rows": row, "mlp": column}, device_id_type=MESH)
    load_qkv.start()
    load_out.start()
    own_shard(0).start()
    own_shard(1).start()
    pl.semaphore_wait(barrier, len(partners))
    gather_start(1)
    for i in range(images):
        work[...] = jnp.zeros_like(work)
        work[0:patches, :] = c_ref[i]
        cot[i * tall : (i + 1) * tall, :] = work[...]
    cot_copy.start()

    @pl.loop(0, images)
    def _(i):
        forward_rows(i, x_ref, rank_ref, kept_ref, g1_ref, rw_ref, xp, keep, gate, h1, h1t, work)

    h1t[...] = h1[...].T
    load_qkv.wait()

    @pl.loop(0, 3 * width // 256)
    def _(j):
        forward_qkv(j, h1, wqkv, qkv)

    @pl.loop(0, HEADS // 2)
    def _(p):
        for i in range(images):
            attend(p, i, width, tall, qkv, keep, probs, context, contextt)

        @pl.when(p == 3)
        def _():
            gather_forward(1)

    load_out.wait()

    @pl.loop(0, images)
    def _(i):
        forward_out(i, tall, context, wout, xp, keep, gate, g2_ref, attended, middle, tok)
        token_copy(i).start()

    gather_forward(2)
    own_shard(0).wait()
    own_shard(1).wait()
    for ref in (out, gh2, dg1, dg2, drw):
        ref[...] = jnp.zeros_like(ref)

    def mlp_step(k):
        @pl.loop(0, 2 * images)
        def _(block):
            @pl.when(jnp.logical_and(k == 0, block == images))
            def _():
                for i in range(images):
                    token_copy(i).wait()
                cot_copy.wait()

            rows = ds(lax.rem(block + images * lax.div(k, ranks - 1), 2 * images) * tall, tall)
            hid[rows, :], gpre[rows, :] = mlp_rows(tok[rows, :], cot[rows, :], w1[k], w2[k])
            out[rows, :] += dot_nn(hid[rows, :], w2[k])
            gh2[rows, :] += dot_nt(gpre[rows, :], w1[k])

            @pl.when(jnp.logical_and(k == ranks - 1, block == images - 1))
            def _():
                gh2_copy.start()
                out_copy.start()

        @pl.when(k == 0)
        def _():
            tokt[...] = tok[...].T

        hidt[...] = hid[...].T
        for m in range(3):
            rows = slice(m * width // 3, (m + 1) * width // 3)
            g1w[k, rows, :] = dot_nn(tokt[rows, :], gpre[...]).astype(BF)
            g2w[k, :, rows] = dot_nn(hidt[...], cot[:, rows]).astype(BF)

    @pl.loop(0, LAST)
    def _(t):
        for k in range(1, ranks):

            @pl.when(t == k)
            def _(k=k):
                gather_finish(k)

        @pl.when(t < ranks)
        def _():
            mlp_step(t)
            for copy in fc_first(t):
                copy.start()

        @pl.when(t == 2)
        def _():
            gather_forward(3)

        @pl.when(t == 4)
        def _():
            gh2_copy.wait()
            out_copy.wait()

            @pl.loop(0, images)
            def _(i):
                rows = ds(i * tall, tall)
                gh2[rows, :] += gh2_in[rows, :]
                back_rows(
                    i, tall, cot, gh2, middle, keep, gate, attended, g2_ref, gh2, tok, glogit, dg2
                )

            context[...] = dot_nt(tok[ds(0, t_own), :], wout[...]).astype(BF)

        @pl.when(jnp.logical_and(t >= 4, t < 6))
        def _():
            cols = lanes((t - 4) * half, half)
            total = 0.0
            for i in range(images):
                total = total + dot_nn(contextt[i], tok[i * tall : (i + 1) * tall, cols])
            for b in range(3):
                gw[t - 4, b] = total[:, b * 128 : (b + 1) * 128].astype(BF)

        @pl.when(jnp.logical_and(t >= 6, t < 12))
        def _():
            p = t - 6
            for i in range(images):
                attend_back(p, i, width, tall, qkv, probs, context)
            total = dot_nn(h1t[...], pair_columns(qkv, p, width))
            for b in range(3):
                gw[t - 4, b] = total[:, b * 128 : (b + 1) * 128].astype(BF)

        @pl.when(jnp.logical_and(t >= 4, t < 12))
        def _():
            core_copy(t - 4).start()

        @pl.when(t == 5)
        def _():
            @pl.loop(0, images)
            def _(i):
                rows = ds(i * tall, tall)
                block_ref[i] = (middle[rows, :] + out[rows, :] + out_in[rows, :]).astype(BF)[0:patches, :]

        @pl.when(t == 12)
        def _():
            @pl.loop(0, images)
            def _(i):
                rows = ds(i * tall, tall)
                dy = dot_nt(qkv[rows, :], wqkv[...])
                back_input(i, tall, dy, glogit, rw_ref, xp, h1, g1_ref, gh2, gx_ref, dg1, drw)

            sma[0] = jnp.concatenate([dg1[...], drw[...], dg2[...], jnp.zeros((5, width), F32)], 0)
            small_copy(0).start()

        for level in range(2):

            @pl.when(t == 13 + level)
            def _(level=level):
                small_copy(level).wait()
                sma[level + 1] = sma[level] + smr[level]
                small_copy(level + 1).start()

        @pl.when(t == 15)
        def _():
            small_copy(2).wait()
            smz[z] = sma[2] + smr[2]
            for k in range(1, ranks):
                small_z(k).start()

        def lagged(lag, do):
            @pl.when(jnp.logical_and(t >= 4 + lag, t < 4 + lag + CHUNKS))
            def _():
                do(t - 4 - lag)

        @pl.when(jnp.logical_and(t >= 2, t < 2 + ranks))
        def _():
            fc_fold_third(t - 2)

        @pl.when(jnp.logical_and(t >= 1, t < 1 + ranks))
        def _():
            fc_fold_second(t - 1)

        @pl.when(t == 7)
        def _():
            fc_finish()

        @pl.when(t == 9)
        def _():
            fc_to_sibling()

        lagged(8, spread_sibling)
        lagged(7, spread_first)
        lagged(6, fold_all)
        lagged(4, fold_pair)
        lagged(3, fold_z)
        lagged(2, fold_second)
        lagged(1, fold_first)

    for k in range(1, ranks):
        small_z(k).wait()
    total = smz[0]
    for k in range(1, ranks):
        total = total + smz[k]
    small_out[...] = total

    @pl.loop(0, CHUNKS)
    def _(j):
        chunk_done(j)

    for copy in fc_share:
        copy.wait()
    for kind in range(3):
        for copy in fc_spread(kind):
            copy.wait_send()
    for k in range(1, ranks):
        for copy in fc_third(k):
            copy.wait_send()
        for mat in range(2):
            for kind in range(5):
                gather_copy(k, mat, kind).wait_send()

    @pl.loop(0, ranks)
    def _(k):
        for copy in fc_first(k) + fc_second(k):
            copy.wait_send()


VMEM = pl.BlockSpec(memory_space=pltpu.VMEM)
SMEM = pl.BlockSpec(memory_space=pltpu.SMEM)
ANY = pl.BlockSpec(memory_space=pl.ANY)


def widen_kernel(gq, go, f1, f2, small, gq_out, go_out, f1_out, f2_out, g1_out, rw_out, g2_out):
    width = f1.shape[1]
    for b in range(3):
        gq_out[:, b * width : (b + 1) * width] = gq[b].astype(F32)
    for b in range(go.shape[0]):
        go_out[:, b * 128 : (b + 1) * 128] = go[b].astype(F32)
    f1_out[...] = f1[...].astype(F32)
    f2_out[...] = f2[...].astype(F32)
    g1_out[...], rw_out[...], g2_out[...] = small[0], small[1], small[2]


def widen(gq, go, f1, f2, small):
    width = f1.shape[0]
    step = 128

    def rows(*tail):
        return pl.BlockSpec((step,) + tail, lambda i: (i, 0))

    def inner(lead, tail):
        return pl.BlockSpec((lead, step, tail), lambda i: (0, i, 0))

    return pl.pallas_call(
        widen_kernel,
        grid=(width // step,),
        out_shape=[jax.ShapeDtypeStruct((width, n), F32) for n in (3 * width, width, width, width)]
        + [jax.ShapeDtypeStruct((width,), F32)] * 3,
        in_specs=[inner(3, width), inner(6, 128), rows(width), rows(width), pl.BlockSpec((8, width), lambda i: (0, 0))],
        out_specs=[rows(3 * width), rows(width), rows(width), rows(width)] + [pl.BlockSpec((width,), lambda i: (0,))] * 3,
        compiler_params=pltpu.CompilerParams(vmem_limit_bytes=48 * 1024 * 1024),
        name="widen",
    )(gq, go, f1, f2, small)


def per_device(ranks, others, images, patch_rank, kept_count, ln1_gain, router_weight, w_qkv, w_out, ln2_gain, w_fc1, w_fc2, cotangent):
    count, patches, width = images.shape
    tall = -(-patches // 16) * 16
    t = count * tall
    part = w_fc1.shape[1] // 2
    half, eighth = width // 2, width // 8

    def bf(*dims):
        return pltpu.VMEM(dims, BF)

    def f32(*dims):
        return pltpu.VMEM(dims, F32)

    def sem(*dims):
        return pltpu.SemaphoreType.DMA(dims)

    scratch = [
        bf(width, 3 * width), bf(width, width), bf(ranks, width, part), bf(ranks, part, width),
        bf(t, width), f32(t, 128), f32(t, 128), f32(t, 128), bf(t, width), bf(width, t), bf(t, 3 * width),
        f32(count, HEADS, tall, tall), bf(count, width, tall), bf(t, width), f32(t, width), f32(t, width),
        bf(2 * t, width), bf(2 * t, width), bf(width, 2 * t), f32(2 * t, width), f32(2 * t, width),
        f32(t, width), f32(t, width), bf(2 * t, part), bf(part, 2 * t), bf(2 * t, part), bf(tall, width),
        bf(ranks, width, part), bf(ranks, part, width),
        bf(ranks, width // 2, part), bf(ranks, part // 2, width), bf(ranks, width // 4, part), bf(ranks, part // 4, width),
        bf(ranks, width // 4, part), bf(ranks, part // 4, width), bf(ranks - 1, width // 4, part), bf(ranks - 1, part // 4, width),
        bf(CHUNKS, 3, width, 128), bf(CHUNKS, 3, half, 128), bf(CHUNKS, 3, 2 * eighth, 128), bf(CHUNKS, 3, eighth, 128),
        bf(CHUNKS, ranks, 3, eighth, 128), bf(CHUNKS, 3, eighth, 128),
        f32(1, width), f32(1, width), f32(1, width), f32(3, 8, width), f32(3, 8, width), f32(ranks, 8, width),
        sem(4), sem(ranks - 1, 2, 5), sem(ranks - 1, 2, 5), sem(count + 1), sem(count + 1), sem(2), sem(2),
        sem(ranks, 2), sem(ranks, 2), sem(ranks, 2), sem(ranks, 2), sem(ranks - 1, 2), sem(ranks - 1, 2),
        sem(3, 2), sem(3, 2), sem(2), sem(2), sem(2),
        sem(CHUNKS), sem(CHUNKS), sem(CHUNKS), sem(CHUNKS), sem(CHUNKS), sem(CHUNKS),
        sem(CHUNKS, 2), sem(CHUNKS, 2), sem(CHUNKS),
        sem(CHUNKS), sem(CHUNKS), sem(CHUNKS), sem(CHUNKS), sem(CHUNKS), sem(CHUNKS),
        sem(3), sem(3), sem(ranks - 1), sem(ranks - 1),
    ]

    def struct(*dims, dtype=BF):
        return jax.ShapeDtypeStruct(dims, dtype)

    block, gx, gq, go, f1, f2, small = pl.pallas_call(
        functools.partial(mega_kernel, ranks),
        out_shape=[
            struct(count, patches, width), struct(count, patches, width), struct(3, width, width), struct(6, width, 128),
            struct(width, 2 * part), struct(2 * part, width), struct(8, width, dtype=F32),
        ],
        in_specs=[VMEM, VMEM, SMEM, VMEM, VMEM, ANY, ANY, VMEM, ANY, ANY, VMEM],
        out_specs=[VMEM, VMEM, ANY, ANY, ANY, ANY, VMEM],
        scratch_shapes=scratch,
        compiler_params=pltpu.CompilerParams(
            collective_id=0, has_side_effects=True, vmem_limit_bytes=63 * 1024 * 1024
        ),
        name="block",
    )(images, patch_rank, kept_count, ln1_gain, router_weight, w_qkv, w_out, ln2_gain, w_fc1, w_fc2, cotangent)
    gq, go, f1, f2, g1, rw, g2 = widen(gq, go, f1, f2, small)
    if others:
        gq, go, f1, f2, g1, rw, g2 = lax.psum((gq, go, f1, f2, g1, rw, g2), "rows", axis_index_groups=others)
    return block, gx, g1, rw, gq, go, g2, f1, f2


def solution(mesh):
    rows, ranks = mesh.shape["rows"], mesh.shape["mlp"]
    others = [[8 * g + i for g in range(rows // 8)] for i in range(8)] if rows > 8 else None
    return jax.shard_map(
        functools.partial(per_device, ranks, others),
        mesh=mesh,
        in_specs=(
            P(("rows", "mlp"), None, None), P(("rows", "mlp"), None), P(("rows", "mlp")), P(), P(), P(), P(), P(),
            P(None, "mlp"), P("mlp", None), P(("rows", "mlp"), None, None),
        ),
        out_specs=(
            P(("rows", "mlp"), None, None), P(("rows", "mlp"), None, None), P(), P(), P(), P(), P(),
            P(None, "mlp"), P("mlp", None),
        ),
        check_vma=False,
    )
```

```python
import functools
import jax
import jax.numpy as jnp
from jax import lax
from jax.experimental import pallas as pl
from jax.experimental.pallas import tpu as pltpu
from jax.sharding import PartitionSpec as P

HEADS = 12
EPS = 1e-6
FILL = -1e30
BF = jnp.bfloat16
F32 = jnp.float32


def dot_nn(a, b):
    return lax.dot_general(a, b, (((1,), (0,)), ((), ())), preferred_element_type=F32)


def dot_nt(a, b):
    return lax.dot_general(a, b, (((1,), (1,)), ((), ())), preferred_element_type=F32)


def dot_tn(a, b):
    return lax.dot_general(a, b, (((0,), (0,)), ((), ())), preferred_element_type=F32)


def unit_rows(v):
    center = v - jnp.mean(v, -1, keepdims=True)
    scale = lax.rsqrt(jnp.mean(center * center, -1, keepdims=True) + EPS)
    return center * scale, scale


def norm_pull(dy, gain, unit, scale):
    du = dy * gain
    return scale * (
        du
        - jnp.mean(du, -1, keepdims=True)
        - unit * jnp.mean(du * unit, -1, keepdims=True)
    )


def half_mask(rows, h):
    lane = lax.broadcasted_iota(jnp.int32, (rows, 128), 1)
    return (lane < 64) if h == 0 else (lane >= 64)


def forward_rows(i, x_ref, rank_ref, kept_ref, g1_ref, rw_ref, xp, keep, gate, h1, h1t, work):
    patches, width = x_ref.shape[1:]
    tall = xp.shape[0] // x_ref.shape[0]
    rows = pl.ds(pl.multiple_of(i * tall, 16), tall)
    work[...] = jnp.zeros_like(work)
    work[0:patches, :] = x_ref[i]
    v = work[...]
    xp[rows, :] = v
    kept = (rank_ref[pl.ds(i, 1), :] < kept_ref[i]).astype(F32)
    keep_row = jnp.concatenate([kept, jnp.zeros((1, 256 - patches), F32)], 1)
    keep_col = jnp.broadcast_to(keep_row, (128, 256)).T
    keep[rows, :] = keep_col[0:tall, :]
    unit, _ = unit_rows(v.astype(F32))
    low = (unit * g1_ref[...][None]).astype(BF)
    h1[rows, :] = low
    logit = jnp.sum(low.astype(F32) * rw_ref[...][None].astype(F32), -1, keepdims=True)
    gate[rows, :] = jnp.broadcast_to(jax.nn.sigmoid(logit), (tall, 128))


def forward_qkv(j, h1, wqkv, qkv):
    cols = pl.ds(pl.multiple_of(j * 256, 256), 256)
    qkv[:, cols] = dot_nn(h1[...], wqkv[:, cols]).astype(BF)


def attend(p, i, width, tall, qkv, keep, probs, context, contextt):
    rows = pl.ds(pl.multiple_of(i * tall, 16), tall)
    qc = pl.ds(pl.multiple_of(p * 128, 128), 128)
    kc = pl.ds(pl.multiple_of(width + p * 128, 128), 128)
    vc = pl.ds(pl.multiple_of(2 * width + p * 128, 128), 128)
    q, k, v = qkv[rows, qc], qkv[rows, kc], qkv[rows, vc]
    vt = v.T
    kept = keep[rows, 0:1] > 0.5
    outs = []
    for h in range(2):
        kh = jnp.where(half_mask(tall, h), k, jnp.zeros_like(k))
        s = jnp.where(kept, dot_nt(kh, q) * 0.125, FILL)
        e = jnp.exp(s - jnp.max(s, 0, keepdims=True))
        pr = e * (1.0 / jnp.sum(e, 0, keepdims=True))
        probs[i, p * 2 + h] = pr
        outs.append(dot_nn(vt[h * 64 : h * 64 + 64, :], pr.astype(BF)))
    ct = jnp.concatenate(outs, 0)
    contextt[i, pl.ds(pl.multiple_of(p * 128, 128), 128), :] = ct.astype(BF)
    context[rows, qc] = ct.T.astype(BF)


def forward_out(i, tall, context, wout, xp, keep, gate, g2_ref, attended, middle, h2):
    rows = pl.ds(pl.multiple_of(i * tall, 16), tall)
    att = dot_nn(context[rows, :], wout[...])
    attended[rows, :] = att
    mid = xp[rows, :].astype(F32) + keep[rows, 0:1] * gate[rows, 0:1] * att
    middle[rows, :] = mid
    unit, _ = unit_rows(mid)
    h2[rows, :] = (unit * g2_ref[...][None]).astype(BF)


def gelu_pair(pre):
    cdf = 0.5 * (1.0 + lax.erf(pre * 0.7071067811865476))
    pdf = jnp.exp(pre * pre * -0.5) * 0.3989422804014327
    return pre * cdf, cdf + pre * pdf


def mlp_rows(h, c, w1, w2):
    pre = dot_nn(h, w1)
    hidden, slope = gelu_pair(pre)
    grad = dot_nt(c, w2) * slope
    return hidden.astype(BF), grad.astype(BF)


def back_rows(i, tall, c_ref, gh2, middle, keep, gate, attended, g2_ref, gmid, gatt, glogit, dg2):
    rows = pl.ds(pl.multiple_of(i * tall, 16), tall)
    dy = gh2[rows, :]
    unit, scale = unit_rows(middle[rows, :])
    gm = c_ref[rows, :].astype(F32) + norm_pull(dy, g2_ref[...][None], unit, scale)
    gmid[rows, :] = gm
    dg2[...] += jnp.sum(dy * unit, 0, keepdims=True)
    k, g = keep[rows, 0:1], gate[rows, 0:1]
    kept = gm * k
    gatt[rows, :] = (kept * g).astype(BF)
    gl = jnp.sum(kept * attended[rows, :], -1, keepdims=True) * g * (1.0 - g)
    glogit[rows, :] = jnp.broadcast_to(gl, (tall, 128))


def attend_back(p, i, width, tall, qkv, probs, gctx):
    rows = pl.ds(pl.multiple_of(i * tall, 16), tall)
    qc = pl.ds(pl.multiple_of(p * 128, 128), 128)
    kc = pl.ds(pl.multiple_of(width + p * 128, 128), 128)
    vc = pl.ds(pl.multiple_of(2 * width + p * 128, 128), 128)
    q, k, v = qkv[rows, qc], qkv[rows, kc], qkv[rows, vc]
    gc = gctx[rows, qc]
    kt = k.T
    gv, gk, gq = 0.0, 0.0, []
    for h in range(2):
        mask = half_mask(tall, h)
        zero = jnp.zeros_like(v)
        pr = probs[i, p * 2 + h]
        gp = dot_nt(jnp.where(mask, v, zero), gc)
        gs = (pr * (gp - jnp.sum(pr * gp, 0, keepdims=True))).astype(BF)
        gv = gv + dot_nn(pr.astype(BF), jnp.where(mask, gc, zero))
        gk = gk + dot_nn(gs, jnp.where(mask, q, zero))
        gq.append(dot_nn(kt[h * 64 : h * 64 + 64, :], gs))
    qkv[rows, qc] = (jnp.concatenate(gq, 0).T * 0.125).astype(BF)
    qkv[rows, kc] = (gk * 0.125).astype(BF)
    qkv[rows, vc] = gv.astype(BF)


def pair_columns(wqkv, p, width):
    return jnp.concatenate(
        [wqkv[:, pl.ds(pl.multiple_of(b * width + p * 128, 128), 128)] for b in range(3)], 1
    )


def back_input(i, tall, dy, glogit, rw_ref, xp, h1, g1_ref, gmid, gx_ref, dg1, drw):
    rows = pl.ds(pl.multiple_of(i * tall, 16), tall)
    patches = gx_ref.shape[1]
    gl = glogit[rows, 0:1]
    dy = dy + gl * rw_ref[...][None].astype(F32)
    unit, scale = unit_rows(xp[rows, :].astype(F32))
    dg1[...] += jnp.sum(dy * unit, 0, keepdims=True)
    drw[...] += jnp.sum(h1[rows, :].astype(F32) * gl, 0, keepdims=True)
    out = gmid[rows, :] + norm_pull(dy, g1_ref[...][None], unit, scale)
    gx_ref[i] = out.astype(BF)[0:patches, :]

MESH = pl.DeviceIdType.MESH
CHUNKS = HEADS // 2 + 2
LAST = 4 + CHUNKS + 9


def mega_kernel(
    ranks, x_ref, rank_ref, kept_ref, g1_ref, rw_ref, wqkv_hbm, wout_hbm, g2_ref, fc1, fc2, c_ref,
    block_ref, gx_ref, gq_out, go_out, f1_out, f2_out, small_out,
    wqkv, wout, w1, w2, xp, keep, gate, glogit, h1, h1t, qkv, probs, contextt, context, attended, middle,
    tok, cot, tokt, out, gh2, out_low, gh2_low, out_in, gh2_in, hid, hidt, gpre, work,
    g1w, g2w, r1a, r1b, r2a, r2b, fz1, fz2, rz1, rz2,
    gw, q0, q1, q2, qz, qf, dg1, dg2, drw, sma, smr, smz,
    lsem, gsend, grecv, tsend, trecv, esend, erecv, s1s, s1r, s2s, s2r, s3s, s3r, fs, fr, floc, ssib, rsib,
    q0s, q0r, q1s, q1r, q2s, q2r, q3s, q3r, qloc, q5s, q5r, q6s, q6r, q7s, q7r, sms, smrs, smzs, smzr,
):
    images, patches, width = x_ref.shape
    t_own = xp.shape[0]
    tall = t_own // images
    half = width // 2
    part = w1.shape[2]
    quarter = (width // 4, part // 4)
    r = lax.axis_index("rows")
    z = lax.axis_index("mlp")
    c, x, y = lax.rem(r, 2), lax.rem(lax.div(r, 2), 2), lax.rem(lax.div(r, 4), 2)
    r_sib, r_x, r_y = r + 1 - 2 * c, r + 2 - 4 * x, r + 4 - 8 * y
    r_diag = r_x + r_y - r
    q = 2 * y + x

    def ds(start, size):
        return pl.ds(pl.multiple_of(start, 16), size)

    def lanes(start, size):
        return pl.ds(pl.multiple_of(start, 128), size)

    def remote(src, dst, send, recv, row, column):
        return pltpu.make_async_remote_copy(
            src_ref=src, dst_ref=dst, send_sem=send, recv_sem=recv,
            device_id={"rows": row, "mlp": column}, device_id_type=MESH,
        )

    def distance(k):
        return k + lax.div(k, 2) * (1 - 2 * lax.rem(k, 2))

    def gather_copy(k, mat, kind):
        held, size = (w1, w2)[mat], quarter[mat]
        cut = size // 3
        sems = gsend.at[k - 1, mat, kind], grecv.at[k - 1, mat, kind]
        if kind < 2:
            start, count = ((q * size, size), ((3 - q) * size, cut))[kind]
            if mat == 0:
                src = fc1.at[ds(start, count), lanes(c * part, part)]
            else:
                src = fc2.at[ds(c * part + start, count), :]
            return remote(src, held.at[k, ds(start, count), :], *sems, r, lax.rem(z - distance(k) + ranks, ranks))
        start, count = (q * size, size) if kind < 4 else (q * size + cut, size - cut)
        place = held.at[k, ds(start, count), :]
        return remote(place, place, *sems, (r_x, r_y, r_diag)[kind - 2], z)

    def gather_start(k):
        for kind in range(2):
            for mat in range(2):
                gather_copy(k, mat, kind).start()

    def gather_forward(k):
        for mat in range(2):
            gather_copy(k, mat, 0).wait_recv()
        if k + 1 < ranks:
            gather_start(k + 1)
        for mat in range(2):
            for kind in (2, 3, 4):
                gather_copy(k, mat, kind).start()

    def gather_finish(k):
        for mat in range(2):
            for kind in (1, 2, 3, 4):
                gather_copy(k, mat, kind).wait_recv()

    def own_shard(mat):
        if mat == 0:
            return pltpu.make_async_copy(fc1.at[:, lanes(c * part, part)], w1.at[0], lsem.at[0])
        return pltpu.make_async_copy(fc2.at[ds(c * part, part), :], w2.at[0], lsem.at[1])

    load_qkv = pltpu.make_async_copy(wqkv_hbm, wqkv, lsem.at[2])
    load_out = pltpu.make_async_copy(wout_hbm, wout, lsem.at[3])

    def token_copy(i):
        src, dst = tok.at[ds(i * tall, tall), :], tok.at[ds(t_own + i * tall, tall), :]
        return remote(src, dst, tsend.at[i], trecv.at[i], r_sib, z)

    cot_copy = remote(
        cot.at[ds(0, t_own), :], cot.at[ds(t_own, t_own), :], tsend.at[images], trecv.at[images], r_sib, z
    )
    gh2_copy = remote(gh2_low, gh2_in, esend.at[0], erecv.at[0], r_sib, z)
    out_copy = remote(out_low, out_in, esend.at[1], erecv.at[1], r_sib, z)

    h1r, q1r_rows = width // 2, width // 4
    h2r, q2r_rows = part // 2, part // 4

    def fc_first(k):
        return (
            remote(g1w.at[k, ds((1 - x) * h1r, h1r), :], r1a.at[k], s1s.at[k, 0], s1r.at[k, 0], r_x, z),
            remote(g2w.at[k, ds((1 - y) * h2r, h2r), :], r1b.at[k], s1s.at[k, 1], s1r.at[k, 1], r_y, z),
        )

    def fc_second(k):
        return (
            remote(
                g1w.at[k, ds(x * h1r + (1 - y) * q1r_rows, q1r_rows), :], r2a.at[k], s2s.at[k, 0], s2r.at[k, 0], r_y, z
            ),
            remote(
                g2w.at[k, ds(y * h2r + (1 - x) * q2r_rows, q2r_rows), :], r2b.at[k], s2s.at[k, 1], s2r.at[k, 1], r_x, z
            ),
        )

    def fc_third(k):
        column = lax.rem(z + distance(k), ranks)
        return (
            remote(fz1.at[k], rz1.at[k - 1], s3s.at[k - 1, 0], s3r.at[k - 1, 0], r, column),
            remote(fz2.at[k], rz2.at[k - 1], s3s.at[k - 1, 1], s3r.at[k - 1, 1], r, column),
        )

    f1_place = f1_out.at[ds(x * h1r + y * q1r_rows, q1r_rows), lanes(c * part, part)]
    f2_place = f2_out.at[ds(c * part + y * h2r + x * q2r_rows, q2r_rows), :]

    def fc_spread(kind):
        row = (r_x, r_y, r_diag)[kind]
        return (
            remote(fz1.at[0], f1_place, fs.at[kind, 0], fr.at[kind, 0], row, z),
            remote(fz2.at[0], f2_place, fs.at[kind, 1], fr.at[kind, 1], row, z),
        )

    fc_keep = (
        pltpu.make_async_copy(fz1.at[0], f1_place, floc.at[0]),
        pltpu.make_async_copy(fz2.at[0], f2_place, floc.at[1]),
    )
    f1_half = f1_out.at[:, lanes(c * part, part)]
    f2_half = f2_out.at[ds(c * part, part), :]
    fc_share = (
        remote(f1_half, f1_half, ssib.at[0], rsib.at[0], r_sib, z),
        remote(f2_half, f2_half, ssib.at[1], rsib.at[1], r_sib, z),
    )

    def fc_fold_second(k):
        for copy in fc_first(k):
            copy.wait_recv()
        rows = ds(x * h1r + (1 - y) * q1r_rows, q1r_rows)
        g1w[k, rows, :] = g1w[k, rows, :] + r1a[k, ds((1 - y) * q1r_rows, q1r_rows), :]
        rows = ds(y * h2r + (1 - x) * q2r_rows, q2r_rows)
        g2w[k, rows, :] = g2w[k, rows, :] + r1b[k, ds((1 - x) * q2r_rows, q2r_rows), :]
        for copy in fc_second(k):
            copy.start()

    def fc_fold_third(k):
        for copy in fc_second(k):
            copy.wait_recv()
        total = g1w[k, ds(x * h1r + y * q1r_rows, q1r_rows), :].astype(F32)
        total = total + r1a[k, ds(y * q1r_rows, q1r_rows), :].astype(F32) + r2a[k].astype(F32)
        fz1[k] = total.astype(BF)
        total = g2w[k, ds(y * h2r + x * q2r_rows, q2r_rows), :].astype(F32)
        total = total + r1b[k, ds(x * q2r_rows, q2r_rows), :].astype(F32) + r2b[k].astype(F32)
        fz2[k] = total.astype(BF)

        @pl.when(k > 0)
        def _():
            for copy in fc_third(k):
                copy.start()

    def fc_finish():
        for k in range(1, ranks):
            for copy in fc_third(k):
                copy.wait_recv()
        for own, arrived in ((fz1, rz1), (fz2, rz2)):
            total = own[0].astype(F32)
            for k in range(ranks - 1):
                total = total + arrived[k].astype(F32)
            own[0] = total.astype(BF)
        for copy in fc_keep:
            copy.start()
        for kind in range(3):
            for copy in fc_spread(kind):
                copy.start()

    def fc_to_sibling():
        for copy in fc_keep:
            copy.wait()
        for kind in range(3):
            for copy in fc_spread(kind):
                copy.wait_recv()
        for copy in fc_share:
            copy.start()

    eighth = width // 8

    def order(j):
        odd = lax.rem(j, 2)
        first, second = r_x + (r_y - r_x) * odd, r_y + (r_x - r_y) * odd
        a1, a2 = x + (y - x) * odd, y + (x - y) * odd
        return first, second, a1, a2

    def chunk_place(j, start, count):
        rows = ds(start, count)
        return (
            (j < 2, go_out.at[pl.ds(3 * lax.min(j, 1), 3), rows, :]),
            (j >= 2, gq_out.at[:, rows, lanes(lax.max(j - 2, 0) * 128, 128)]),
        )

    def core_copy(j):
        return remote(gw.at[j, :, ds((1 - c) * half, half), :], q0.at[j], q0s.at[j], q0r.at[j], r_sib, z)

    def first_copy(j):
        first, _, a1, _ = order(j)
        src = gw.at[j, :, ds(c * half + (1 - a1) * 2 * eighth, 2 * eighth), :]
        return remote(src, q1.at[j], q1s.at[j], q1r.at[j], first, z)

    def second_copy(j):
        _, second, a1, a2 = order(j)
        src = gw.at[j, :, ds(c * half + a1 * 2 * eighth + (1 - a2) * eighth, eighth), :]
        return remote(src, q2.at[j], q2s.at[j], q2r.at[j], second, z)

    def z_copy(j, step):
        column = (z + 1 - 2 * lax.rem(z, 2), z + 2 - 4 * lax.div(z, 2))[step]
        return remote(qz.at[j, 2 * step], qz.at[j, 2 * step + 1], q3s.at[j, step], q3r.at[j, step], r, column)

    def own_start(j):
        _, _, a1, a2 = order(j)
        return c * half + a1 * 2 * eighth + a2 * eighth

    def keep_copy(j, ref):
        return pltpu.make_async_copy(qf.at[j], ref, qloc.at[j])

    def spread_copies(j, ref, level):
        first, second, _, _ = order(j)
        if level == 0:
            return remote(qf.at[j], ref, q5s.at[j], q5r.at[j], second, z)
        if level == 1:
            return remote(ref, ref, q6s.at[j], q6r.at[j], first, z)
        return remote(ref, ref, q7s.at[j], q7r.at[j], r_sib, z)

    def level_place(j, level):
        _, _, a1, _ = order(j)
        if level == 0:
            return chunk_place(j, own_start(j), eighth)
        if level == 1:
            return chunk_place(j, c * half + a1 * 2 * eighth, 2 * eighth)
        return chunk_place(j, c * half, half)

    def each_place(j, level, do):
        for condition, ref in level_place(j, level):

            @pl.when(condition)
            def _(ref=ref):
                do(ref)

    def fold_first(j):
        core_copy(j).wait_recv()
        _, _, a1, _ = order(j)
        rows = ds(c * half + (1 - a1) * 2 * eighth, 2 * eighth)
        gw[j, :, rows, :] = gw[j, :, rows, :] + q0[j, :, ds((1 - a1) * 2 * eighth, 2 * eighth), :]
        first_copy(j).start()

    def fold_second(j):
        first_copy(j).wait_recv()
        _, _, a1, a2 = order(j)
        inner = (1 - a2) * eighth
        rows = ds(c * half + a1 * 2 * eighth + inner, eighth)
        total = gw[j, :, rows, :].astype(F32) + q0[j, :, ds(a1 * 2 * eighth + inner, eighth), :].astype(F32)
        gw[j, :, rows, :] = (total + q1[j, :, ds(inner, eighth), :].astype(F32)).astype(BF)
        second_copy(j).start()

    def fold_z(j):
        second_copy(j).wait_recv()
        _, _, a1, a2 = order(j)
        inner = a2 * eighth
        rows = ds(c * half + a1 * 2 * eighth + inner, eighth)
        total = gw[j, :, rows, :].astype(F32) + q0[j, :, ds(a1 * 2 * eighth + inner, eighth), :].astype(F32)
        total = total + q1[j, :, ds(inner, eighth), :].astype(F32) + q2[j].astype(F32)
        qz[j, 0] = total.astype(BF)
        z_copy(j, 0).start()

    def fold_pair(j):
        z_copy(j, 0).wait_recv()
        qz[j, 2] = qz[j, 0] + qz[j, 1]
        z_copy(j, 1).start()

    def fold_all(j):
        z_copy(j, 1).wait_recv()
        qf[j] = qz[j, 2] + qz[j, 3]

        def go(ref):
            keep_copy(j, ref).start()
            spread_copies(j, ref, 0).start()

        each_place(j, 0, go)

    def spread_first(j):
        def done(ref):
            keep_copy(j, ref).wait()
            spread_copies(j, ref, 0).wait_recv()

        each_place(j, 0, done)
        each_place(j, 1, lambda ref: spread_copies(j, ref, 1).start())

    def spread_sibling(j):
        each_place(j, 1, lambda ref: spread_copies(j, ref, 1).wait_recv())
        each_place(j, 2, lambda ref: spread_copies(j, ref, 2).start())

    def chunk_done(j):
        each_place(j, 2, lambda ref: spread_copies(j, ref, 2).wait())
        each_place(j, 1, lambda ref: spread_copies(j, ref, 1).wait_send())
        each_place(j, 0, lambda ref: spread_copies(j, ref, 0).wait_send())
        core_copy(j).wait_send()
        first_copy(j).wait_send()
        second_copy(j).wait_send()
        for step in range(2):
            z_copy(j, step).wait_send()

    def small_copy(level):
        row = (r_sib, r_x, r_y)[level]
        return remote(sma.at[level], smr.at[level], sms.at[level], smrs.at[level], row, z)

    def small_z(k):
        return remote(smz.at[z], smz.at[z], smzs.at[k - 1], smzr.at[k - 1], r, lax.rem(z + k, ranks))

    barrier = pltpu.get_barrier_semaphore()
    partners = [(r_sib, z), (r_x, z), (r_y, z), (r_diag, z)] + [(r, lax.rem(z + k, ranks)) for k in range(1, ranks)]
    for row, column in partners:
        pl.semaphore_signal(barrier, inc=1, device_id={"rows": row, "mlp": column}, device_id_type=MESH)
    load_qkv.start()
    load_out.start()
    own_shard(0).start()
    own_shard(1).start()
    pl.semaphore_wait(barrier, len(partners))
    gather_start(1)
    for i in range(images):
        work[...] = jnp.zeros_like(work)
        work[0:patches, :] = c_ref[i]
        cot[i * tall : (i + 1) * tall, :] = work[...]
    cot_copy.start()

    @pl.loop(0, images)
    def _(i):
        forward_rows(i, x_ref, rank_ref, kept_ref, g1_ref, rw_ref, xp, keep, gate, h1, h1t, work)

    h1t[...] = h1[...].T
    load_qkv.wait()

    @pl.loop(0, 3 * width // 256)
    def _(j):
        forward_qkv(j, h1, wqkv, qkv)

    @pl.loop(0, HEADS // 2)
    def _(p):
        for i in range(images):
            attend(p, i, width, tall, qkv, keep, probs, context, contextt)

        @pl.when(p == 3)
        def _():
            gather_forward(1)

    load_out.wait()

    @pl.loop(0, images)
    def _(i):
        forward_out(i, tall, context, wout, xp, keep, gate, g2_ref, attended, middle, tok)
        token_copy(i).start()

    gather_forward(2)
    own_shard(0).wait()
    own_shard(1).wait()
    for ref in (out, gh2, dg1, dg2, drw):
        ref[...] = jnp.zeros_like(ref)

    def mlp_step(k):
        @pl.loop(0, 2 * images)
        def _(block):
            @pl.when(jnp.logical_and(k == 0, block == images))
            def _():
                for i in range(images):
                    token_copy(i).wait()
                cot_copy.wait()

            rows = ds(lax.rem(block + images * lax.div(k, ranks - 1), 2 * images) * tall, tall)
            hid[rows, :], gpre[rows, :] = mlp_rows(tok[rows, :], cot[rows, :], w1[k], w2[k])
            out[rows, :] += dot_nn(hid[rows, :], w2[k])
            gh2[rows, :] += dot_nt(gpre[rows, :], w1[k])

            @pl.when(jnp.logical_and(k == ranks - 1, block == images - 1))
            def _():
                gh2_low[...] = gh2[ds(t_own, t_own), :].astype(BF)
                gh2_copy.start()
                out_low[...] = out[ds(t_own, t_own), :].astype(BF)
                out_copy.start()

        @pl.when(k == 0)
        def _():
            tokt[...] = tok[...].T

        hidt[...] = hid[...].T
        for m in range(3):
            rows = slice(m * width // 3, (m + 1) * width // 3)
            g1w[k, rows, :] = dot_nn(tokt[rows, :], gpre[...]).astype(BF)
            g2w[k, :, rows] = dot_nn(hidt[...], cot[:, rows]).astype(BF)

    @pl.loop(0, LAST)
    def _(t):
        for k in range(1, ranks):

            @pl.when(t == k)
            def _(k=k):
                gather_finish(k)

        @pl.when(t < ranks)
        def _():
            mlp_step(t)
            for copy in fc_first(t):
                copy.start()

        @pl.when(t == 2)
        def _():
            gather_forward(3)

        @pl.when(t == 4)
        def _():
            gh2_copy.wait()

            @pl.loop(0, images)
            def _(i):
                rows = ds(i * tall, tall)
                gh2[rows, :] += gh2_in[rows, :].astype(F32)
                back_rows(
                    i, tall, cot, gh2, middle, keep, gate, attended, g2_ref, gh2, tok, glogit, dg2
                )

            context[...] = dot_nt(tok[ds(0, t_own), :], wout[...]).astype(BF)

        @pl.when(jnp.logical_and(t >= 4, t < 6))
        def _():
            cols = lanes((t - 4) * half, half)
            total = 0.0
            for i in range(images):
                total = total + dot_nn(contextt[i], tok[i * tall : (i + 1) * tall, cols])
            for b in range(3):
                gw[t - 4, b] = total[:, b * 128 : (b + 1) * 128].astype(BF)

        @pl.when(jnp.logical_and(t >= 6, t < 12))
        def _():
            p = t - 6
            for i in range(images):
                attend_back(p, i, width, tall, qkv, probs, context)
            total = dot_nn(h1t[...], pair_columns(qkv, p, width))
            for b in range(3):
                gw[t - 4, b] = total[:, b * 128 : (b + 1) * 128].astype(BF)

        @pl.when(jnp.logical_and(t >= 4, t < 12))
        def _():
            core_copy(t - 4).start()

        @pl.when(t == 5)
        def _():
            out_copy.wait()

            @pl.loop(0, images)
            def _(i):
                rows = ds(i * tall, tall)
                block_ref[i] = (middle[rows, :] + out[rows, :] + out_in[rows, :].astype(F32)).astype(BF)[0:patches, :]

        @pl.when(t == 12)
        def _():
            @pl.loop(0, images)
            def _(i):
                rows = ds(i * tall, tall)
                dy = dot_nt(qkv[rows, :], wqkv[...])
                back_input(i, tall, dy, glogit, rw_ref, xp, h1, g1_ref, gh2, gx_ref, dg1, drw)

            sma[0] = jnp.concatenate([dg1[...], drw[...], dg2[...], jnp.zeros((5, width), F32)], 0)
            small_copy(0).start()

        for level in range(2):

            @pl.when(t == 13 + level)
            def _(level=level):
                small_copy(level).wait()
                sma[level + 1] = sma[level] + smr[level]
                small_copy(level + 1).start()

        @pl.when(t == 15)
        def _():
            small_copy(2).wait()
            smz[z] = sma[2] + smr[2]
            for k in range(1, ranks):
                small_z(k).start()

        def lagged(lag, do):
            @pl.when(jnp.logical_and(t >= 4 + lag, t < 4 + lag + CHUNKS))
            def _():
                do(t - 4 - lag)

        @pl.when(jnp.logical_and(t >= 2, t < 2 + ranks))
        def _():
            fc_fold_third(t - 2)

        @pl.when(jnp.logical_and(t >= 1, t < 1 + ranks))
        def _():
            fc_fold_second(t - 1)

        @pl.when(t == 7)
        def _():
            fc_finish()

        @pl.when(t == 9)
        def _():
            fc_to_sibling()

        lagged(8, spread_sibling)
        lagged(7, spread_first)
        lagged(6, fold_all)
        lagged(4, fold_pair)
        lagged(3, fold_z)
        lagged(2, fold_second)
        lagged(1, fold_first)

    for k in range(1, ranks):
        small_z(k).wait()
    total = smz[0]
    for k in range(1, ranks):
        total = total + smz[k]
    small_out[...] = total

    @pl.loop(0, CHUNKS)
    def _(j):
        chunk_done(j)

    for copy in fc_share:
        copy.wait()
    for kind in range(3):
        for copy in fc_spread(kind):
            copy.wait_send()
    for k in range(1, ranks):
        for copy in fc_third(k):
            copy.wait_send()
        for mat in range(2):
            for kind in range(5):
                gather_copy(k, mat, kind).wait_send()

    @pl.loop(0, ranks)
    def _(k):
        for copy in fc_first(k) + fc_second(k):
            copy.wait_send()


VMEM = pl.BlockSpec(memory_space=pltpu.VMEM)
SMEM = pl.BlockSpec(memory_space=pltpu.SMEM)
ANY = pl.BlockSpec(memory_space=pl.ANY)


def widen_kernel(gq, go, f1, f2, small, gq_out, go_out, f1_out, f2_out, g1_out, rw_out, g2_out):
    width = f1.shape[1]
    for b in range(3):
        gq_out[:, b * width : (b + 1) * width] = gq[b].astype(F32)
    for b in range(go.shape[0]):
        go_out[:, b * 128 : (b + 1) * 128] = go[b].astype(F32)
    f1_out[...] = f1[...].astype(F32)
    f2_out[...] = f2[...].astype(F32)
    g1_out[...], rw_out[...], g2_out[...] = small[0], small[1], small[2]


def widen(gq, go, f1, f2, small):
    width = f1.shape[0]
    step = 128

    def rows(*tail):
        return pl.BlockSpec((step,) + tail, lambda i: (i, 0))

    def inner(lead, tail):
        return pl.BlockSpec((lead, step, tail), lambda i: (0, i, 0))

    return pl.pallas_call(
        widen_kernel,
        grid=(width // step,),
        out_shape=[jax.ShapeDtypeStruct((width, n), F32) for n in (3 * width, width, width, width)]
        + [jax.ShapeDtypeStruct((width,), F32)] * 3,
        in_specs=[inner(3, width), inner(6, 128), rows(width), rows(width), pl.BlockSpec((8, width), lambda i: (0, 0))],
        out_specs=[rows(3 * width), rows(width), rows(width), rows(width)] + [pl.BlockSpec((width,), lambda i: (0,))] * 3,
        compiler_params=pltpu.CompilerParams(vmem_limit_bytes=48 * 1024 * 1024),
        name="widen",
    )(gq, go, f1, f2, small)


def per_device(ranks, others, images, patch_rank, kept_count, ln1_gain, router_weight, w_qkv, w_out, ln2_gain, w_fc1, w_fc2, cotangent):
    count, patches, width = images.shape
    tall = -(-patches // 16) * 16
    t = count * tall
    part = w_fc1.shape[1] // 2
    half, eighth = width // 2, width // 8

    def bf(*dims):
        return pltpu.VMEM(dims, BF)

    def f32(*dims):
        return pltpu.VMEM(dims, F32)

    def sem(*dims):
        return pltpu.SemaphoreType.DMA(dims)

    scratch = [
        bf(width, 3 * width), bf(width, width), bf(ranks, width, part), bf(ranks, part, width),
        bf(t, width), f32(t, 128), f32(t, 128), f32(t, 128), bf(t, width), bf(width, t), bf(t, 3 * width),
        f32(count, HEADS, tall, tall), bf(count, width, tall), bf(t, width), f32(t, width), f32(t, width),
        bf(2 * t, width), bf(2 * t, width), bf(width, 2 * t), f32(2 * t, width), f32(2 * t, width),
        bf(t, width), bf(t, width), bf(t, width), bf(t, width), bf(2 * t, part), bf(part, 2 * t), bf(2 * t, part), bf(tall, width),
        bf(ranks, width, part), bf(ranks, part, width),
        bf(ranks, width // 2, part), bf(ranks, part // 2, width), bf(ranks, width // 4, part), bf(ranks, part // 4, width),
        bf(ranks, width // 4, part), bf(ranks, part // 4, width), bf(ranks - 1, width // 4, part), bf(ranks - 1, part // 4, width),
        bf(CHUNKS, 3, width, 128), bf(CHUNKS, 3, half, 128), bf(CHUNKS, 3, 2 * eighth, 128), bf(CHUNKS, 3, eighth, 128),
        bf(CHUNKS, ranks, 3, eighth, 128), bf(CHUNKS, 3, eighth, 128),
        f32(1, width), f32(1, width), f32(1, width), f32(3, 8, width), f32(3, 8, width), f32(ranks, 8, width),
        sem(4), sem(ranks - 1, 2, 5), sem(ranks - 1, 2, 5), sem(count + 1), sem(count + 1), sem(2), sem(2),
        sem(ranks, 2), sem(ranks, 2), sem(ranks, 2), sem(ranks, 2), sem(ranks - 1, 2), sem(ranks - 1, 2),
        sem(3, 2), sem(3, 2), sem(2), sem(2), sem(2),
        sem(CHUNKS), sem(CHUNKS), sem(CHUNKS), sem(CHUNKS), sem(CHUNKS), sem(CHUNKS),
        sem(CHUNKS, 2), sem(CHUNKS, 2), sem(CHUNKS),
        sem(CHUNKS), sem(CHUNKS), sem(CHUNKS), sem(CHUNKS), sem(CHUNKS), sem(CHUNKS),
        sem(3), sem(3), sem(ranks - 1), sem(ranks - 1),
    ]

    def struct(*dims, dtype=BF):
        return jax.ShapeDtypeStruct(dims, dtype)

    block, gx, gq, go, f1, f2, small = pl.pallas_call(
        functools.partial(mega_kernel, ranks),
        out_shape=[
            struct(count, patches, width), struct(count, patches, width), struct(3, width, width), struct(6, width, 128),
            struct(width, 2 * part), struct(2 * part, width), struct(8, width, dtype=F32),
        ],
        in_specs=[VMEM, VMEM, SMEM, VMEM, VMEM, ANY, ANY, VMEM, ANY, ANY, VMEM],
        out_specs=[VMEM, VMEM, ANY, ANY, ANY, ANY, VMEM],
        scratch_shapes=scratch,
        compiler_params=pltpu.CompilerParams(
            collective_id=0, has_side_effects=True, vmem_limit_bytes=63 * 1024 * 1024
        ),
        name="block",
    )(images, patch_rank, kept_count, ln1_gain, router_weight, w_qkv, w_out, ln2_gain, w_fc1, w_fc2, cotangent)
    gq, go, f1, f2, g1, rw, g2 = widen(gq, go, f1, f2, small)
    if others:
        gq, go, f1, f2, g1, rw, g2 = lax.psum((gq, go, f1, f2, g1, rw, g2), "rows", axis_index_groups=others)
    return block, gx, g1, rw, gq, go, g2, f1, f2


def solution(mesh):
    rows, ranks = mesh.shape["rows"], mesh.shape["mlp"]
    others = [[8 * g + i for g in range(rows // 8)] for i in range(8)] if rows > 8 else None
    return jax.shard_map(
        functools.partial(per_device, ranks, others),
        mesh=mesh,
        in_specs=(
            P(("rows", "mlp"), None, None), P(("rows", "mlp"), None), P(("rows", "mlp")), P(), P(), P(), P(), P(),
            P(None, "mlp"), P("mlp", None), P(("rows", "mlp"), None, None),
        ),
        out_specs=(
            P(("rows", "mlp"), None, None), P(("rows", "mlp"), None, None), P(), P(), P(), P(), P(),
            P(None, "mlp"), P("mlp", None),
        ),
        check_vma=False,
    )
```

```python
import functools
import jax
import jax.numpy as jnp
from jax import lax
from jax.experimental import pallas as pl
from jax.experimental.pallas import tpu as pltpu
from jax.sharding import PartitionSpec as P

HEADS = 12
EPS = 1e-6
FILL = -1e30
BF = jnp.bfloat16
F32 = jnp.float32


def dot_nn(a, b):
    return lax.dot_general(a, b, (((1,), (0,)), ((), ())), preferred_element_type=F32)


def dot_nt(a, b):
    return lax.dot_general(a, b, (((1,), (1,)), ((), ())), preferred_element_type=F32)


def dot_tn(a, b):
    return lax.dot_general(a, b, (((0,), (0,)), ((), ())), preferred_element_type=F32)


def unit_rows(v):
    center = v - jnp.mean(v, -1, keepdims=True)
    scale = lax.rsqrt(jnp.mean(center * center, -1, keepdims=True) + EPS)
    return center * scale, scale


def norm_pull(dy, gain, unit, scale):
    du = dy * gain
    return scale * (
        du
        - jnp.mean(du, -1, keepdims=True)
        - unit * jnp.mean(du * unit, -1, keepdims=True)
    )


def half_mask(rows, h):
    lane = lax.broadcasted_iota(jnp.int32, (rows, 128), 1)
    return (lane < 64) if h == 0 else (lane >= 64)


def forward_rows(i, x_ref, rank_ref, kept_ref, g1_ref, rw_ref, xp, keep, gate, h1, h1t, work):
    patches, width = x_ref.shape[1:]
    tall = xp.shape[0] // x_ref.shape[0]
    rows = pl.ds(pl.multiple_of(i * tall, 16), tall)
    work[...] = jnp.zeros_like(work)
    work[0:patches, :] = x_ref[i]
    v = work[...]
    xp[rows, :] = v
    kept = (rank_ref[pl.ds(i, 1), :] < kept_ref[i]).astype(F32)
    keep_row = jnp.concatenate([kept, jnp.zeros((1, 256 - patches), F32)], 1)
    keep_col = jnp.broadcast_to(keep_row, (128, 256)).T
    keep[rows, :] = keep_col[0:tall, :]
    unit, _ = unit_rows(v.astype(F32))
    low = (unit * g1_ref[...][None]).astype(BF)
    h1[rows, :] = low
    logit = jnp.sum(low.astype(F32) * rw_ref[...][None].astype(F32), -1, keepdims=True)
    gate[rows, :] = jnp.broadcast_to(jax.nn.sigmoid(logit), (tall, 128))


def forward_qkv(j, h1, wqkv, qkv):
    cols = pl.ds(pl.multiple_of(j * 256, 256), 256)
    qkv[:, cols] = dot_nn(h1[...], wqkv[:, cols]).astype(BF)


def attend(p, i, width, tall, qkv, keep, probs, context, contextt):
    rows = pl.ds(pl.multiple_of(i * tall, 16), tall)
    qc = pl.ds(pl.multiple_of(p * 128, 128), 128)
    kc = pl.ds(pl.multiple_of(width + p * 128, 128), 128)
    vc = pl.ds(pl.multiple_of(2 * width + p * 128, 128), 128)
    q, k, v = qkv[rows, qc], qkv[rows, kc], qkv[rows, vc]
    vt = v.T
    kept = keep[rows, 0:1] > 0.5
    outs = []
    for h in range(2):
        kh = jnp.where(half_mask(tall, h), k, jnp.zeros_like(k))
        s = jnp.where(kept, dot_nt(kh, q) * 0.125, FILL)
        e = jnp.exp(s - jnp.max(s, 0, keepdims=True))
        pr = e * (1.0 / jnp.sum(e, 0, keepdims=True))
        probs[i, p * 2 + h] = pr
        outs.append(dot_nn(vt[h * 64 : h * 64 + 64, :], pr.astype(BF)))
    ct = jnp.concatenate(outs, 0)
    contextt[i, pl.ds(pl.multiple_of(p * 128, 128), 128), :] = ct.astype(BF)
    context[rows, qc] = ct.T.astype(BF)


def forward_out(i, tall, context, wout, xp, keep, gate, g2_ref, attended, middle, h2):
    rows = pl.ds(pl.multiple_of(i * tall, 16), tall)
    att = dot_nn(context[rows, :], wout[...])
    attended[rows, :] = att
    mid = xp[rows, :].astype(F32) + keep[rows, 0:1] * gate[rows, 0:1] * att
    middle[rows, :] = mid
    unit, _ = unit_rows(mid)
    h2[rows, :] = (unit * g2_ref[...][None]).astype(BF)


def gelu_pair(pre):
    cdf = 0.5 * (1.0 + lax.erf(pre * 0.7071067811865476))
    pdf = jnp.exp(pre * pre * -0.5) * 0.3989422804014327
    return pre * cdf, cdf + pre * pdf


def mlp_rows(h, c, w1, w2):
    pre = dot_nn(h, w1)
    hidden, slope = gelu_pair(pre)
    grad = dot_nt(c, w2) * slope
    return hidden.astype(BF), grad.astype(BF)


def back_rows(i, tall, c_ref, gh2, middle, keep, gate, attended, g2_ref, gmid, gatt, glogit, dg2):
    rows = pl.ds(pl.multiple_of(i * tall, 16), tall)
    dy = gh2[rows, :]
    unit, scale = unit_rows(middle[rows, :])
    gm = c_ref[rows, :].astype(F32) + norm_pull(dy, g2_ref[...][None], unit, scale)
    gmid[rows, :] = gm
    dg2[...] += jnp.sum(dy * unit, 0, keepdims=True)
    k, g = keep[rows, 0:1], gate[rows, 0:1]
    kept = gm * k
    gatt[rows, :] = (kept * g).astype(BF)
    gl = jnp.sum(kept * attended[rows, :], -1, keepdims=True) * g * (1.0 - g)
    glogit[rows, :] = jnp.broadcast_to(gl, (tall, 128))


def attend_back(p, i, width, tall, qkv, probs, gctx):
    rows = pl.ds(pl.multiple_of(i * tall, 16), tall)
    qc = pl.ds(pl.multiple_of(p * 128, 128), 128)
    kc = pl.ds(pl.multiple_of(width + p * 128, 128), 128)
    vc = pl.ds(pl.multiple_of(2 * width + p * 128, 128), 128)
    q, k, v = qkv[rows, qc], qkv[rows, kc], qkv[rows, vc]
    gc = gctx[rows, qc]
    kt = k.T
    gv, gk, gq = 0.0, 0.0, []
    for h in range(2):
        mask = half_mask(tall, h)
        zero = jnp.zeros_like(v)
        pr = probs[i, p * 2 + h]
        gp = dot_nt(jnp.where(mask, v, zero), gc)
        gs = (pr * (gp - jnp.sum(pr * gp, 0, keepdims=True))).astype(BF)
        gv = gv + dot_nn(pr.astype(BF), jnp.where(mask, gc, zero))
        gk = gk + dot_nn(gs, jnp.where(mask, q, zero))
        gq.append(dot_nn(kt[h * 64 : h * 64 + 64, :], gs))
    qkv[rows, qc] = (jnp.concatenate(gq, 0).T * 0.125).astype(BF)
    qkv[rows, kc] = (gk * 0.125).astype(BF)
    qkv[rows, vc] = gv.astype(BF)


def pair_columns(wqkv, p, width):
    return jnp.concatenate(
        [wqkv[:, pl.ds(pl.multiple_of(b * width + p * 128, 128), 128)] for b in range(3)], 1
    )


def back_input(i, tall, dy, glogit, rw_ref, xp, h1, g1_ref, gmid, gx_ref, dg1, drw):
    rows = pl.ds(pl.multiple_of(i * tall, 16), tall)
    patches = gx_ref.shape[1]
    gl = glogit[rows, 0:1]
    dy = dy + gl * rw_ref[...][None].astype(F32)
    unit, scale = unit_rows(xp[rows, :].astype(F32))
    dg1[...] += jnp.sum(dy * unit, 0, keepdims=True)
    drw[...] += jnp.sum(h1[rows, :].astype(F32) * gl, 0, keepdims=True)
    out = gmid[rows, :] + norm_pull(dy, g1_ref[...][None], unit, scale)
    gx_ref[i] = out.astype(BF)[0:patches, :]

MESH = pl.DeviceIdType.MESH
CHUNKS = HEADS // 2 + 2
LAGS = (0, 1, 3, 4, 7, 11, 12, 15)
LAST = 4 + CHUNKS + LAGS[7]


def mega_kernel(
    ranks, x_ref, rank_ref, kept_ref, g1_ref, rw_ref, wqkv_hbm, wout_hbm, g2_ref, fc1, fc2, c_ref,
    block_ref, gx_ref, gq_out, go_out, f1_out, f2_out, small_out,
    wqkv, wout, w1, w2, xp, keep, gate, glogit, h1, h1t, qkv, probs, contextt, context, attended, middle,
    tok, cot, tokt, out, gh2, out_low, gh2_low, out_in, gh2_in, hid, hidt, gpre, work,
    g1w, g2w, r1a, r1b, r2a, r2b, fz1, fz2, rz1, rz2,
    gw, q0, q1, q2, qz, qf, dg1, dg2, drw, sma, smr, smz,
    lsem, gsend, grecv, tsend, trecv, esend, erecv, s1s, s1r, s2s, s2r, s3s, s3r, fs, fr, floc, ssib, rsib,
    q0s, q0r, q1s, q1r, q2s, q2r, q3s, q3r, qloc, q5s, q5r, q6s, q6r, q7s, q7r, sms, smrs, smzs, smzr,
):
    images, patches, width = x_ref.shape
    t_own = xp.shape[0]
    tall = t_own // images
    half = width // 2
    part = w1.shape[2]
    quarter = (width // 4, part // 4)
    r = lax.axis_index("rows")
    z = lax.axis_index("mlp")
    c, x, y = lax.rem(r, 2), lax.rem(lax.div(r, 2), 2), lax.rem(lax.div(r, 4), 2)
    r_sib, r_x, r_y = r + 1 - 2 * c, r + 2 - 4 * x, r + 4 - 8 * y
    r_diag = r_x + r_y - r
    q = 2 * y + x

    def ds(start, size):
        return pl.ds(pl.multiple_of(start, 16), size)

    def lanes(start, size):
        return pl.ds(pl.multiple_of(start, 128), size)

    def remote(src, dst, send, recv, row, column):
        return pltpu.make_async_remote_copy(
            src_ref=src, dst_ref=dst, send_sem=send, recv_sem=recv,
            device_id={"rows": row, "mlp": column}, device_id_type=MESH,
        )

    def distance(k):
        return k + lax.div(k, 2) * (1 - 2 * lax.rem(k, 2))

    def gather_copy(k, mat, kind):
        held, size = (w1, w2)[mat], quarter[mat]
        cut = size // 3
        sems = gsend.at[k - 1, mat, kind], grecv.at[k - 1, mat, kind]
        if kind < 2:
            start, count = ((q * size, size), ((3 - q) * size, cut))[kind]
            if mat == 0:
                src = fc1.at[ds(start, count), lanes(c * part, part)]
            else:
                src = fc2.at[ds(c * part + start, count), :]
            return remote(src, held.at[k, ds(start, count), :], *sems, r, lax.rem(z - distance(k) + ranks, ranks))
        start, count = (q * size, size) if kind < 4 else (q * size + cut, size - cut)
        place = held.at[k, ds(start, count), :]
        return remote(place, place, *sems, (r_x, r_y, r_diag)[kind - 2], z)

    def gather_start(k):
        for kind in range(2):
            for mat in range(2):
                gather_copy(k, mat, kind).start()

    def gather_forward(k):
        for mat in range(2):
            gather_copy(k, mat, 0).wait_recv()
        if k + 1 < ranks:
            gather_start(k + 1)
        for mat in range(2):
            for kind in (2, 3, 4):
                gather_copy(k, mat, kind).start()

    def gather_finish(k):
        for mat in range(2):
            for kind in (1, 2, 3, 4):
                gather_copy(k, mat, kind).wait_recv()

    def own_shard(mat):
        if mat == 0:
            return pltpu.make_async_copy(fc1.at[:, lanes(c * part, part)], w1.at[0], lsem.at[0])
        return pltpu.make_async_copy(fc2.at[ds(c * part, part), :], w2.at[0], lsem.at[1])

    load_qkv = pltpu.make_async_copy(wqkv_hbm, wqkv, lsem.at[2])
    load_out = pltpu.make_async_copy(wout_hbm, wout, lsem.at[3])

    def token_copy(i):
        src, dst = tok.at[ds(i * tall, tall), :], tok.at[ds(t_own + i * tall, tall), :]
        return remote(src, dst, tsend.at[i], trecv.at[i], r_sib, z)

    cot_copy = remote(
        cot.at[ds(0, t_own), :], cot.at[ds(t_own, t_own), :], tsend.at[images], trecv.at[images], r_sib, z
    )
    gh2_copy = remote(gh2_low, gh2_in, esend.at[0], erecv.at[0], r_sib, z)
    out_copy = remote(out_low, out_in, esend.at[1], erecv.at[1], r_sib, z)

    h1r, q1r_rows = width // 2, width // 4
    h2r, q2r_rows = part // 2, part // 4

    def fc_first(k):
        return (
            remote(g1w.at[k, ds((1 - x) * h1r, h1r), :], r1a.at[k], s1s.at[k, 0], s1r.at[k, 0], r_x, z),
            remote(g2w.at[k, ds((1 - y) * h2r, h2r), :], r1b.at[k], s1s.at[k, 1], s1r.at[k, 1], r_y, z),
        )

    def fc_second(k):
        return (
            remote(
                g1w.at[k, ds(x * h1r + (1 - y) * q1r_rows, q1r_rows), :], r2a.at[k], s2s.at[k, 0], s2r.at[k, 0], r_y, z
            ),
            remote(
                g2w.at[k, ds(y * h2r + (1 - x) * q2r_rows, q2r_rows), :], r2b.at[k], s2s.at[k, 1], s2r.at[k, 1], r_x, z
            ),
        )

    def fc_third(k):
        column = lax.rem(z + distance(k), ranks)
        return (
            remote(fz1.at[k], rz1.at[k - 1], s3s.at[k - 1, 0], s3r.at[k - 1, 0], r, column),
            remote(fz2.at[k], rz2.at[k - 1], s3s.at[k - 1, 1], s3r.at[k - 1, 1], r, column),
        )

    f1_place = f1_out.at[ds(x * h1r + y * q1r_rows, q1r_rows), lanes(c * part, part)]
    f2_place = f2_out.at[ds(c * part + y * h2r + x * q2r_rows, q2r_rows), :]

    f1_level = (f1_place, f1_out.at[ds(x * h1r, h1r), lanes(c * part, part)])
    f2_level = (f2_place, f2_out.at[ds(c * part + y * h2r, h2r), :])

    def fc_spread(level):
        src1, src2 = (fz1.at[0], fz2.at[0]) if level == 0 else (f1_level[1], f2_level[1])
        row1, row2 = (r_y, r_x) if level == 0 else (r_x, r_y)
        return (
            remote(src1, f1_level[level], fs.at[level, 0], fr.at[level, 0], row1, z),
            remote(src2, f2_level[level], fs.at[level, 1], fr.at[level, 1], row2, z),
        )

    fc_keep = (
        pltpu.make_async_copy(fz1.at[0], f1_place, floc.at[0]),
        pltpu.make_async_copy(fz2.at[0], f2_place, floc.at[1]),
    )
    f1_half = f1_out.at[:, lanes(c * part, part)]
    f2_half = f2_out.at[ds(c * part, part), :]
    fc_share = (
        remote(f1_half, f1_half, ssib.at[0], rsib.at[0], r_sib, z),
        remote(f2_half, f2_half, ssib.at[1], rsib.at[1], r_sib, z),
    )

    def fc_fold_second(k):
        for copy in fc_first(k):
            copy.wait_recv()
        rows = ds(x * h1r + (1 - y) * q1r_rows, q1r_rows)
        g1w[k, rows, :] = g1w[k, rows, :] + r1a[k, ds((1 - y) * q1r_rows, q1r_rows), :]
        rows = ds(y * h2r + (1 - x) * q2r_rows, q2r_rows)
        g2w[k, rows, :] = g2w[k, rows, :] + r1b[k, ds((1 - x) * q2r_rows, q2r_rows), :]
        for copy in fc_second(k):
            copy.start()

    def fc_fold_third(k):
        for copy in fc_second(k):
            copy.wait_recv()
        total = g1w[k, ds(x * h1r + y * q1r_rows, q1r_rows), :].astype(F32)
        total = total + r1a[k, ds(y * q1r_rows, q1r_rows), :].astype(F32) + r2a[k].astype(F32)
        fz1[k] = total.astype(BF)
        total = g2w[k, ds(y * h2r + x * q2r_rows, q2r_rows), :].astype(F32)
        total = total + r1b[k, ds(x * q2r_rows, q2r_rows), :].astype(F32) + r2b[k].astype(F32)
        fz2[k] = total.astype(BF)

        @pl.when(k > 0)
        def _():
            for copy in fc_third(k):
                copy.start()

    def fc_finish():
        for k in range(1, ranks):
            for copy in fc_third(k):
                copy.wait_recv()
        for own, arrived in ((fz1, rz1), (fz2, rz2)):
            total = own[0].astype(F32)
            for k in range(ranks - 1):
                total = total + arrived[k].astype(F32)
            own[0] = total.astype(BF)
        for copy in fc_keep:
            copy.start()
        for copy in fc_spread(0):
            copy.start()

    def fc_widen():
        for copy in fc_keep:
            copy.wait()
        for copy in fc_spread(0):
            copy.wait_recv()
        for copy in fc_spread(1):
            copy.start()

    def fc_to_sibling():
        for copy in fc_spread(1):
            copy.wait_recv()
        for copy in fc_share:
            copy.start()

    eighth = width // 8

    def order(j):
        odd = lax.rem(j, 2)
        first, second = r_x + (r_y - r_x) * odd, r_y + (r_x - r_y) * odd
        a1, a2 = x + (y - x) * odd, y + (x - y) * odd
        return first, second, a1, a2

    def chunk_place(j, start, count):
        rows = ds(start, count)
        return (
            (j < 2, go_out.at[pl.ds(3 * lax.min(j, 1), 3), rows, :]),
            (j >= 2, gq_out.at[:, rows, lanes(lax.max(j - 2, 0) * 128, 128)]),
        )

    def core_copy(j):
        return remote(gw.at[j, :, ds((1 - c) * half, half), :], q0.at[j], q0s.at[j], q0r.at[j], r_sib, z)

    def first_copy(j):
        first, _, a1, _ = order(j)
        src = gw.at[j, :, ds(c * half + (1 - a1) * 2 * eighth, 2 * eighth), :]
        return remote(src, q1.at[j], q1s.at[j], q1r.at[j], first, z)

    def second_copy(j):
        _, second, a1, a2 = order(j)
        src = gw.at[j, :, ds(c * half + a1 * 2 * eighth + (1 - a2) * eighth, eighth), :]
        return remote(src, q2.at[j], q2s.at[j], q2r.at[j], second, z)

    def z_copy(j, step):
        column = (z + 1 - 2 * lax.rem(z, 2), z + 2 - 4 * lax.div(z, 2))[step]
        return remote(qz.at[j, 2 * step], qz.at[j, 2 * step + 1], q3s.at[j, step], q3r.at[j, step], r, column)

    def own_start(j):
        _, _, a1, a2 = order(j)
        return c * half + a1 * 2 * eighth + a2 * eighth

    def keep_copy(j, ref):
        return pltpu.make_async_copy(qf.at[j], ref, qloc.at[j])

    def spread_copies(j, ref, level):
        first, second, _, _ = order(j)
        if level == 0:
            return remote(qf.at[j], ref, q5s.at[j], q5r.at[j], second, z)
        if level == 1:
            return remote(ref, ref, q6s.at[j], q6r.at[j], first, z)
        return remote(ref, ref, q7s.at[j], q7r.at[j], r_sib, z)

    def level_place(j, level):
        _, _, a1, _ = order(j)
        if level == 0:
            return chunk_place(j, own_start(j), eighth)
        if level == 1:
            return chunk_place(j, c * half + a1 * 2 * eighth, 2 * eighth)
        return chunk_place(j, c * half, half)

    def each_place(j, level, do):
        for condition, ref in level_place(j, level):

            @pl.when(condition)
            def _(ref=ref):
                do(ref)

    def fold_first(j):
        core_copy(j).wait_recv()
        _, _, a1, _ = order(j)
        rows = ds(c * half + (1 - a1) * 2 * eighth, 2 * eighth)
        gw[j, :, rows, :] = gw[j, :, rows, :] + q0[j, :, ds((1 - a1) * 2 * eighth, 2 * eighth), :]
        first_copy(j).start()

    def fold_second(j):
        first_copy(j).wait_recv()
        _, _, a1, a2 = order(j)
        inner = (1 - a2) * eighth
        rows = ds(c * half + a1 * 2 * eighth + inner, eighth)
        total = gw[j, :, rows, :].astype(F32) + q0[j, :, ds(a1 * 2 * eighth + inner, eighth), :].astype(F32)
        gw[j, :, rows, :] = (total + q1[j, :, ds(inner, eighth), :].astype(F32)).astype(BF)
        second_copy(j).start()

    def fold_z(j):
        second_copy(j).wait_recv()
        _, _, a1, a2 = order(j)
        inner = a2 * eighth
        rows = ds(c * half + a1 * 2 * eighth + inner, eighth)
        total = gw[j, :, rows, :].astype(F32) + q0[j, :, ds(a1 * 2 * eighth + inner, eighth), :].astype(F32)
        total = total + q1[j, :, ds(inner, eighth), :].astype(F32) + q2[j].astype(F32)
        qz[j, 0] = total.astype(BF)
        z_copy(j, 0).start()

    def fold_pair(j):
        z_copy(j, 0).wait_recv()
        qz[j, 2] = qz[j, 0] + qz[j, 1]
        z_copy(j, 1).start()

    def fold_all(j):
        z_copy(j, 1).wait_recv()
        qf[j] = qz[j, 2] + qz[j, 3]

        def go(ref):
            keep_copy(j, ref).start()
            spread_copies(j, ref, 0).start()

        each_place(j, 0, go)

    def spread_first(j):
        def done(ref):
            keep_copy(j, ref).wait()
            spread_copies(j, ref, 0).wait_recv()

        each_place(j, 0, done)
        each_place(j, 1, lambda ref: spread_copies(j, ref, 1).start())

    def spread_sibling(j):
        each_place(j, 1, lambda ref: spread_copies(j, ref, 1).wait_recv())
        each_place(j, 2, lambda ref: spread_copies(j, ref, 2).start())

    def chunk_done(j):
        each_place(j, 2, lambda ref: spread_copies(j, ref, 2).wait())
        each_place(j, 1, lambda ref: spread_copies(j, ref, 1).wait_send())
        each_place(j, 0, lambda ref: spread_copies(j, ref, 0).wait_send())
        core_copy(j).wait_send()
        first_copy(j).wait_send()
        second_copy(j).wait_send()
        for step in range(2):
            z_copy(j, step).wait_send()

    def small_copy(level):
        row = (r_sib, r_x, r_y)[level]
        return remote(sma.at[level], smr.at[level], sms.at[level], smrs.at[level], row, z)

    def small_z(k):
        return remote(smz.at[z], smz.at[z], smzs.at[k - 1], smzr.at[k - 1], r, lax.rem(z + k, ranks))

    barrier = pltpu.get_barrier_semaphore()
    partners = [(r_sib, z), (r_x, z), (r_y, z), (r_diag, z)] + [(r, lax.rem(z + k, ranks)) for k in range(1, ranks)]
    for row, column in partners:
        pl.semaphore_signal(barrier, inc=1, device_id={"rows": row, "mlp": column}, device_id_type=MESH)
    load_qkv.start()
    load_out.start()
    own_shard(0).start()
    own_shard(1).start()
    pl.semaphore_wait(barrier, len(partners))
    gather_start(1)
    for i in range(images):
        work[...] = jnp.zeros_like(work)
        work[0:patches, :] = c_ref[i]
        cot[i * tall : (i + 1) * tall, :] = work[...]
    cot_copy.start()

    @pl.loop(0, images)
    def _(i):
        forward_rows(i, x_ref, rank_ref, kept_ref, g1_ref, rw_ref, xp, keep, gate, h1, h1t, work)

    h1t[...] = h1[...].T
    load_qkv.wait()

    @pl.loop(0, 3 * width // 256)
    def _(j):
        forward_qkv(j, h1, wqkv, qkv)

    @pl.loop(0, HEADS // 2)
    def _(p):
        for i in range(images):
            attend(p, i, width, tall, qkv, keep, probs, context, contextt)

        @pl.when(p == 3)
        def _():
            gather_forward(1)

    load_out.wait()

    @pl.loop(0, images)
    def _(i):
        forward_out(i, tall, context, wout, xp, keep, gate, g2_ref, attended, middle, tok)
        token_copy(i).start()

    gather_forward(2)
    own_shard(0).wait()
    own_shard(1).wait()
    for ref in (out, gh2, dg1, dg2, drw):
        ref[...] = jnp.zeros_like(ref)

    def mlp_step(k):
        @pl.loop(0, 2 * images)
        def _(block):
            @pl.when(jnp.logical_and(k == 0, block == images))
            def _():
                for i in range(images):
                    token_copy(i).wait()
                cot_copy.wait()

            rows = ds(lax.rem(block + images * lax.div(k, ranks - 1), 2 * images) * tall, tall)
            hid[rows, :], gpre[rows, :] = mlp_rows(tok[rows, :], cot[rows, :], w1[k], w2[k])
            out[rows, :] += dot_nn(hid[rows, :], w2[k])
            gh2[rows, :] += dot_nt(gpre[rows, :], w1[k])

            @pl.when(jnp.logical_and(k == ranks - 1, block == images - 1))
            def _():
                gh2_low[...] = gh2[ds(t_own, t_own), :].astype(BF)
                gh2_copy.start()
                out_low[...] = out[ds(t_own, t_own), :].astype(BF)
                out_copy.start()

        @pl.when(k == 0)
        def _():
            tokt[...] = tok[...].T

        hidt[...] = hid[...].T
        for m in range(3):
            rows = slice(m * width // 3, (m + 1) * width // 3)
            g1w[k, rows, :] = dot_nn(tokt[rows, :], gpre[...]).astype(BF)
            g2w[k, :, rows] = dot_nn(hidt[...], cot[:, rows]).astype(BF)

    @pl.loop(0, LAST)
    def _(t):
        for k in range(1, ranks):

            @pl.when(t == k)
            def _(k=k):
                gather_finish(k)

        @pl.when(t < ranks)
        def _():
            mlp_step(t)
            for copy in fc_first(t):
                copy.start()

        @pl.when(t == 1)
        def _():
            gather_forward(3)

        @pl.when(t == 4)
        def _():
            gh2_copy.wait()

            @pl.loop(0, images)
            def _(i):
                rows = ds(i * tall, tall)
                gh2[rows, :] += gh2_in[rows, :].astype(F32)
                back_rows(
                    i, tall, cot, gh2, middle, keep, gate, attended, g2_ref, gh2, tok, glogit, dg2
                )

            context[...] = dot_nt(tok[ds(0, t_own), :], wout[...]).astype(BF)

        @pl.when(jnp.logical_and(t >= 4, t < 6))
        def _():
            cols = lanes((t - 4) * half, half)
            total = 0.0
            for i in range(images):
                total = total + dot_nn(contextt[i], tok[i * tall : (i + 1) * tall, cols])
            for b in range(3):
                gw[t - 4, b] = total[:, b * 128 : (b + 1) * 128].astype(BF)

        @pl.when(jnp.logical_and(t >= 6, t < 12))
        def _():
            p = t - 6
            for i in range(images):
                attend_back(p, i, width, tall, qkv, probs, context)
            total = dot_nn(h1t[...], pair_columns(qkv, p, width))
            for b in range(3):
                gw[t - 4, b] = total[:, b * 128 : (b + 1) * 128].astype(BF)

        @pl.when(jnp.logical_and(t >= 4, t < 12))
        def _():
            core_copy(t - 4).start()

        @pl.when(t == 5)
        def _():
            out_copy.wait()

            @pl.loop(0, images)
            def _(i):
                rows = ds(i * tall, tall)
                block_ref[i] = (middle[rows, :] + out[rows, :] + out_in[rows, :].astype(F32)).astype(BF)[0:patches, :]

        @pl.when(t == 12)
        def _():
            @pl.loop(0, images)
            def _(i):
                rows = ds(i * tall, tall)
                dy = dot_nt(qkv[rows, :], wqkv[...])
                back_input(i, tall, dy, glogit, rw_ref, xp, h1, g1_ref, gh2, gx_ref, dg1, drw)

            sma[0] = jnp.concatenate([dg1[...], drw[...], dg2[...], jnp.zeros((5, width), F32)], 0)
            small_copy(0).start()

        for level in range(2):

            @pl.when(t == 14 + 2 * level)
            def _(level=level):
                small_copy(level).wait()
                sma[level + 1] = sma[level] + smr[level]
                small_copy(level + 1).start()

        @pl.when(t == 18)
        def _():
            small_copy(2).wait()
            smz[z] = sma[2] + smr[2]
            for k in range(1, ranks):
                small_z(k).start()

        def lagged(lag, do):
            @pl.when(jnp.logical_and(t >= 4 + lag, t < 4 + lag + CHUNKS))
            def _():
                do(t - 4 - lag)

        @pl.when(jnp.logical_and(t >= 3, t < 3 + ranks))
        def _():
            fc_fold_third(t - 3)

        @pl.when(jnp.logical_and(t >= 1, t < 1 + ranks))
        def _():
            fc_fold_second(t - 1)

        for tick, do in ((13, fc_finish), (16, fc_widen), (22, fc_to_sibling)):

            @pl.when(t == tick)
            def _(do=do):
                do()

        stages = (fold_first, fold_second, fold_z, fold_pair, fold_all, spread_first, spread_sibling)
        for lag, do in zip(LAGS[1:], stages):
            lagged(lag, do)

    for k in range(1, ranks):
        small_z(k).wait()
    total = smz[0]
    for k in range(1, ranks):
        total = total + smz[k]
    small_out[...] = total

    @pl.loop(0, CHUNKS)
    def _(j):
        chunk_done(j)

    for copy in fc_share:
        copy.wait()
    for level in range(2):
        for copy in fc_spread(level):
            copy.wait_send()
    for k in range(1, ranks):
        for copy in fc_third(k):
            copy.wait_send()
        for mat in range(2):
            for kind in range(5):
                gather_copy(k, mat, kind).wait_send()

    @pl.loop(0, ranks)
    def _(k):
        for copy in fc_first(k) + fc_second(k):
            copy.wait_send()


VMEM = pl.BlockSpec(memory_space=pltpu.VMEM)
SMEM = pl.BlockSpec(memory_space=pltpu.SMEM)
ANY = pl.BlockSpec(memory_space=pl.ANY)


def widen_kernel(gq, go, f1, f2, small, gq_out, go_out, f1_out, f2_out, g1_out, rw_out, g2_out):
    width = f1.shape[1]
    for b in range(3):
        gq_out[:, b * width : (b + 1) * width] = gq[b].astype(F32)
    for b in range(go.shape[0]):
        go_out[:, b * 128 : (b + 1) * 128] = go[b].astype(F32)
    f1_out[...] = f1[...].astype(F32)
    f2_out[...] = f2[...].astype(F32)
    g1_out[...], rw_out[...], g2_out[...] = small[0], small[1], small[2]


def widen(gq, go, f1, f2, small):
    width = f1.shape[0]
    step = 128

    def rows(*tail):
        return pl.BlockSpec((step,) + tail, lambda i: (i, 0))

    def inner(lead, tail):
        return pl.BlockSpec((lead, step, tail), lambda i: (0, i, 0))

    return pl.pallas_call(
        widen_kernel,
        grid=(width // step,),
        out_shape=[jax.ShapeDtypeStruct((width, n), F32) for n in (3 * width, width, width, width)]
        + [jax.ShapeDtypeStruct((width,), F32)] * 3,
        in_specs=[inner(3, width), inner(6, 128), rows(width), rows(width), pl.BlockSpec((8, width), lambda i: (0, 0))],
        out_specs=[rows(3 * width), rows(width), rows(width), rows(width)] + [pl.BlockSpec((width,), lambda i: (0,))] * 3,
        compiler_params=pltpu.CompilerParams(vmem_limit_bytes=48 * 1024 * 1024),
        name="widen",
    )(gq, go, f1, f2, small)


def per_device(ranks, others, images, patch_rank, kept_count, ln1_gain, router_weight, w_qkv, w_out, ln2_gain, w_fc1, w_fc2, cotangent):
    count, patches, width = images.shape
    tall = -(-patches // 16) * 16
    t = count * tall
    part = w_fc1.shape[1] // 2
    half, eighth = width // 2, width // 8

    def bf(*dims):
        return pltpu.VMEM(dims, BF)

    def f32(*dims):
        return pltpu.VMEM(dims, F32)

    def sem(*dims):
        return pltpu.SemaphoreType.DMA(dims)

    scratch = [
        bf(width, 3 * width), bf(width, width), bf(ranks, width, part), bf(ranks, part, width),
        bf(t, width), f32(t, 128), f32(t, 128), f32(t, 128), bf(t, width), bf(width, t), bf(t, 3 * width),
        f32(count, HEADS, tall, tall), bf(count, width, tall), bf(t, width), f32(t, width), f32(t, width),
        bf(2 * t, width), bf(2 * t, width), bf(width, 2 * t), f32(2 * t, width), f32(2 * t, width),
        bf(t, width), bf(t, width), bf(t, width), bf(t, width), bf(2 * t, part), bf(part, 2 * t), bf(2 * t, part), bf(tall, width),
        bf(ranks, width, part), bf(ranks, part, width),
        bf(ranks, width // 2, part), bf(ranks, part // 2, width), bf(ranks, width // 4, part), bf(ranks, part // 4, width),
        bf(ranks, width // 4, part), bf(ranks, part // 4, width), bf(ranks - 1, width // 4, part), bf(ranks - 1, part // 4, width),
        bf(CHUNKS, 3, width, 128), bf(CHUNKS, 3, half, 128), bf(CHUNKS, 3, 2 * eighth, 128), bf(CHUNKS, 3, eighth, 128),
        bf(CHUNKS, ranks, 3, eighth, 128), bf(CHUNKS, 3, eighth, 128),
        f32(1, width), f32(1, width), f32(1, width), f32(3, 8, width), f32(3, 8, width), f32(ranks, 8, width),
        sem(4), sem(ranks - 1, 2, 5), sem(ranks - 1, 2, 5), sem(count + 1), sem(count + 1), sem(2), sem(2),
        sem(ranks, 2), sem(ranks, 2), sem(ranks, 2), sem(ranks, 2), sem(ranks - 1, 2), sem(ranks - 1, 2),
        sem(2, 2), sem(2, 2), sem(2), sem(2), sem(2),
        sem(CHUNKS), sem(CHUNKS), sem(CHUNKS), sem(CHUNKS), sem(CHUNKS), sem(CHUNKS),
        sem(CHUNKS, 2), sem(CHUNKS, 2), sem(CHUNKS),
        sem(CHUNKS), sem(CHUNKS), sem(CHUNKS), sem(CHUNKS), sem(CHUNKS), sem(CHUNKS),
        sem(3), sem(3), sem(ranks - 1), sem(ranks - 1),
    ]

    def struct(*dims, dtype=BF):
        return jax.ShapeDtypeStruct(dims, dtype)

    block, gx, gq, go, f1, f2, small = pl.pallas_call(
        functools.partial(mega_kernel, ranks),
        out_shape=[
            struct(count, patches, width), struct(count, patches, width), struct(3, width, width), struct(6, width, 128),
            struct(width, 2 * part), struct(2 * part, width), struct(8, width, dtype=F32),
        ],
        in_specs=[VMEM, VMEM, SMEM, VMEM, VMEM, ANY, ANY, VMEM, ANY, ANY, VMEM],
        out_specs=[VMEM, VMEM, ANY, ANY, ANY, ANY, VMEM],
        scratch_shapes=scratch,
        compiler_params=pltpu.CompilerParams(
            collective_id=0, has_side_effects=True, vmem_limit_bytes=63 * 1024 * 1024
        ),
        name="block",
    )(images, patch_rank, kept_count, ln1_gain, router_weight, w_qkv, w_out, ln2_gain, w_fc1, w_fc2, cotangent)
    gq, go, f1, f2, g1, rw, g2 = widen(gq, go, f1, f2, small)
    if others:
        gq, go, f1, f2, g1, rw, g2 = lax.psum((gq, go, f1, f2, g1, rw, g2), "rows", axis_index_groups=others)
    return block, gx, g1, rw, gq, go, g2, f1, f2


def solution(mesh):
    rows, ranks = mesh.shape["rows"], mesh.shape["mlp"]
    others = [[8 * g + i for g in range(rows // 8)] for i in range(8)] if rows > 8 else None
    return jax.shard_map(
        functools.partial(per_device, ranks, others),
        mesh=mesh,
        in_specs=(
            P(("rows", "mlp"), None, None), P(("rows", "mlp"), None), P(("rows", "mlp")), P(), P(), P(), P(), P(),
            P(None, "mlp"), P("mlp", None), P(("rows", "mlp"), None, None),
        ),
        out_specs=(
            P(("rows", "mlp"), None, None), P(("rows", "mlp"), None, None), P(), P(), P(), P(), P(),
            P(None, "mlp"), P("mlp", None),
        ),
        check_vma=False,
    )
```

```python
import functools
import jax
import jax.numpy as jnp
from jax import lax
from jax.experimental import pallas as pl
from jax.experimental.pallas import tpu as pltpu
from jax.sharding import PartitionSpec as P

HEADS = 12
EPS = 1e-6
FILL = -1e30
BF = jnp.bfloat16
F32 = jnp.float32


def dot_nn(a, b):
    return lax.dot_general(a, b, (((1,), (0,)), ((), ())), preferred_element_type=F32)


def dot_nt(a, b):
    return lax.dot_general(a, b, (((1,), (1,)), ((), ())), preferred_element_type=F32)


def dot_tn(a, b):
    return lax.dot_general(a, b, (((0,), (0,)), ((), ())), preferred_element_type=F32)


def unit_rows(v):
    center = v - jnp.mean(v, -1, keepdims=True)
    scale = lax.rsqrt(jnp.mean(center * center, -1, keepdims=True) + EPS)
    return center * scale, scale


def norm_pull(dy, gain, unit, scale):
    du = dy * gain
    return scale * (
        du
        - jnp.mean(du, -1, keepdims=True)
        - unit * jnp.mean(du * unit, -1, keepdims=True)
    )


def half_mask(rows, h):
    lane = lax.broadcasted_iota(jnp.int32, (rows, 128), 1)
    return (lane < 64) if h == 0 else (lane >= 64)


def forward_rows(i, x_ref, rank_ref, kept_ref, g1_ref, rw_ref, xp, keep, gate, h1, h1t, work):
    patches = x_ref.shape[0]
    tall = xp.shape[0] // x_ref.shape[1]
    rows = pl.ds(pl.multiple_of(i * tall, 16), tall)
    work[...] = jnp.zeros_like(work)
    work[0:patches, :] = x_ref[:, i, :]
    v = work[...]
    xp[rows, :] = v
    kept = (rank_ref[pl.ds(i, 1), :] < kept_ref[i]).astype(F32)
    keep_row = jnp.concatenate([kept, jnp.zeros((1, 256 - patches), F32)], 1)
    keep_col = jnp.broadcast_to(keep_row, (128, 256)).T
    keep[rows, :] = keep_col[0:tall, :]
    unit, _ = unit_rows(v.astype(F32))
    low = (unit * g1_ref[...][None]).astype(BF)
    h1[rows, :] = low
    logit = jnp.sum(low.astype(F32) * rw_ref[...][None].astype(F32), -1, keepdims=True)
    gate[rows, :] = jnp.broadcast_to(jax.nn.sigmoid(logit), (tall, 128))


def forward_qkv(j, h1, wqkv, qkv):
    cols = pl.ds(pl.multiple_of(j * 256, 256), 256)
    qkv[:, cols] = dot_nn(h1[...], wqkv[:, cols]).astype(BF)


def attend(p, i, width, tall, qkv, keep, probs, context, contextt):
    rows = pl.ds(pl.multiple_of(i * tall, 16), tall)
    qc = pl.ds(pl.multiple_of(p * 128, 128), 128)
    kc = pl.ds(pl.multiple_of(width + p * 128, 128), 128)
    vc = pl.ds(pl.multiple_of(2 * width + p * 128, 128), 128)
    q, k, v = qkv[rows, qc], qkv[rows, kc], qkv[rows, vc]
    vt = v.T
    kept = keep[rows, 0:1] > 0.5
    outs = []
    for h in range(2):
        kh = jnp.where(half_mask(tall, h), k, jnp.zeros_like(k))
        s = jnp.where(kept, dot_nt(kh, q) * 0.125, FILL)
        e = jnp.exp(s - jnp.max(s, 0, keepdims=True))
        pr = e * (1.0 / jnp.sum(e, 0, keepdims=True))
        probs[i, p * 2 + h] = pr
        outs.append(dot_nn(vt[h * 64 : h * 64 + 64, :], pr.astype(BF)))
    ct = jnp.concatenate(outs, 0)
    contextt[i, pl.ds(pl.multiple_of(p * 128, 128), 128), :] = ct.astype(BF)
    context[rows, qc] = ct.T.astype(BF)


def forward_out(i, tall, context, wout, xp, keep, gate, g2_ref, attended, middle, h2):
    rows = pl.ds(pl.multiple_of(i * tall, 16), tall)
    att = dot_nn(context[rows, :], wout[...])
    attended[rows, :] = att
    mid = xp[rows, :].astype(F32) + keep[rows, 0:1] * gate[rows, 0:1] * att
    middle[rows, :] = mid
    unit, _ = unit_rows(mid)
    h2[rows, :] = (unit * g2_ref[...][None]).astype(BF)


def gelu_pair(pre):
    cdf = 0.5 * (1.0 + lax.erf(pre * 0.7071067811865476))
    pdf = jnp.exp(pre * pre * -0.5) * 0.3989422804014327
    return pre * cdf, cdf + pre * pdf


def mlp_rows(h, c, w1, w2):
    pre = dot_nn(h, w1)
    hidden, slope = gelu_pair(pre)
    grad = dot_nt(c, w2) * slope
    return hidden.astype(BF), grad.astype(BF)


def back_rows(i, tall, c_ref, gh2, middle, keep, gate, attended, g2_ref, gmid, gatt, glogit, dg2):
    rows = pl.ds(pl.multiple_of(i * tall, 16), tall)
    dy = gh2[rows, :]
    unit, scale = unit_rows(middle[rows, :])
    gm = c_ref[rows, :].astype(F32) + norm_pull(dy, g2_ref[...][None], unit, scale)
    gmid[rows, :] = gm
    dg2[...] += jnp.sum(dy * unit, 0, keepdims=True)
    k, g = keep[rows, 0:1], gate[rows, 0:1]
    kept = gm * k
    gatt[rows, :] = (kept * g).astype(BF)
    gl = jnp.sum(kept * attended[rows, :], -1, keepdims=True) * g * (1.0 - g)
    glogit[rows, :] = jnp.broadcast_to(gl, (tall, 128))


def attend_back(p, i, width, tall, qkv, probs, gctx):
    rows = pl.ds(pl.multiple_of(i * tall, 16), tall)
    qc = pl.ds(pl.multiple_of(p * 128, 128), 128)
    kc = pl.ds(pl.multiple_of(width + p * 128, 128), 128)
    vc = pl.ds(pl.multiple_of(2 * width + p * 128, 128), 128)
    q, k, v = qkv[rows, qc], qkv[rows, kc], qkv[rows, vc]
    gc = gctx[rows, qc]
    kt = k.T
    gv, gk, gq = 0.0, 0.0, []
    for h in range(2):
        mask = half_mask(tall, h)
        zero = jnp.zeros_like(v)
        pr = probs[i, p * 2 + h]
        gp = dot_nt(jnp.where(mask, v, zero), gc)
        gs = (pr * (gp - jnp.sum(pr * gp, 0, keepdims=True))).astype(BF)
        gv = gv + dot_nn(pr.astype(BF), jnp.where(mask, gc, zero))
        gk = gk + dot_nn(gs, jnp.where(mask, q, zero))
        gq.append(dot_nn(kt[h * 64 : h * 64 + 64, :], gs))
    qkv[rows, qc] = (jnp.concatenate(gq, 0).T * 0.125).astype(BF)
    qkv[rows, kc] = (gk * 0.125).astype(BF)
    qkv[rows, vc] = gv.astype(BF)


def pair_columns(wqkv, p, width):
    return jnp.concatenate(
        [wqkv[:, pl.ds(pl.multiple_of(b * width + p * 128, 128), 128)] for b in range(3)], 1
    )


def back_input(i, tall, dy, glogit, rw_ref, xp, h1, g1_ref, gmid, gx_ref, dg1, drw):
    rows = pl.ds(pl.multiple_of(i * tall, 16), tall)
    patches = gx_ref.shape[1]
    gl = glogit[rows, 0:1]
    dy = dy + gl * rw_ref[...][None].astype(F32)
    unit, scale = unit_rows(xp[rows, :].astype(F32))
    dg1[...] += jnp.sum(dy * unit, 0, keepdims=True)
    drw[...] += jnp.sum(h1[rows, :].astype(F32) * gl, 0, keepdims=True)
    out = gmid[rows, :] + norm_pull(dy, g1_ref[...][None], unit, scale)
    gx_ref[i] = out.astype(BF)[0:patches, :]

MESH = pl.DeviceIdType.MESH
CHUNKS = HEADS // 2 + 2
LAGS = (0, 1, 3, 4, 7, 11, 12, 15)
LAST = 4 + CHUNKS + LAGS[7]


def mega_kernel(
    ranks, x_ref, rank_ref, kept_ref, g1_ref, rw_ref, wqkv_hbm, wout_hbm, g2_ref, fc1, fc2, c_ref,
    block_ref, gx_ref, gq_out, go_out, f1_out, f2_out, small_out,
    wqkv, wout, w1, w2, xp, keep, gate, glogit, h1, h1t, qkv, probs, contextt, context, attended, middle,
    tok, cot, tokt, out, gh2, out_low, gh2_low, out_in, gh2_in, hid, hidt, gpre, work,
    g1w, g2w, r1a, r1b, r2a, r2b, fz1, fz2, rz1, rz2,
    gw, q0, q1, q2, qz, qf, dg1, dg2, drw, sma, smr, smz,
    lsem, gsend, grecv, tsend, trecv, esend, erecv, s1s, s1r, s2s, s2r, s3s, s3r, fs, fr, floc, ssib, rsib,
    q0s, q0r, q1s, q1r, q2s, q2r, q3s, q3r, qloc, q5s, q5r, q6s, q6r, q7s, q7r, sms, smrs, smzs, smzr,
):
    patches, images, width = x_ref.shape
    t_own = xp.shape[0]
    tall = t_own // images
    half = width // 2
    part = w1.shape[2]
    quarter = (width // 4, part // 4)
    r = lax.axis_index("rows")
    z = lax.axis_index("mlp")
    c, x, y = lax.rem(r, 2), lax.rem(lax.div(r, 2), 2), lax.rem(lax.div(r, 4), 2)
    r_sib, r_x, r_y = r + 1 - 2 * c, r + 2 - 4 * x, r + 4 - 8 * y
    r_diag = r_x + r_y - r
    q = 2 * y + x

    def ds(start, size):
        return pl.ds(pl.multiple_of(start, 16), size)

    def lanes(start, size):
        return pl.ds(pl.multiple_of(start, 128), size)

    def remote(src, dst, send, recv, row, column):
        return pltpu.make_async_remote_copy(
            src_ref=src, dst_ref=dst, send_sem=send, recv_sem=recv,
            device_id={"rows": row, "mlp": column}, device_id_type=MESH,
        )

    def distance(k):
        return k + lax.div(k, 2) * (1 - 2 * lax.rem(k, 2))

    def gather_copy(k, mat, kind):
        held, size = (w1, w2)[mat], quarter[mat]
        cut = size // 3
        sems = gsend.at[k - 1, mat, kind], grecv.at[k - 1, mat, kind]
        if kind < 2:
            start, count = ((q * size, size), ((3 - q) * size, cut))[kind]
            if mat == 0:
                src = fc1.at[ds(start, count), lanes(c * part, part)]
            else:
                src = fc2.at[ds(c * part + start, count), :]
            return remote(src, held.at[k, ds(start, count), :], *sems, r, lax.rem(z - distance(k) + ranks, ranks))
        start, count = (q * size, size) if kind < 4 else (q * size + cut, size - cut)
        place = held.at[k, ds(start, count), :]
        return remote(place, place, *sems, (r_x, r_y, r_diag)[kind - 2], z)

    def gather_start(k):
        for kind in range(2):
            for mat in range(2):
                gather_copy(k, mat, kind).start()

    def gather_forward(k):
        for mat in range(2):
            gather_copy(k, mat, 0).wait_recv()
        if k + 1 < ranks:
            gather_start(k + 1)
        for mat in range(2):
            for kind in (2, 3, 4):
                gather_copy(k, mat, kind).start()

    def gather_finish(k):
        for mat in range(2):
            for kind in (1, 2, 3, 4):
                gather_copy(k, mat, kind).wait_recv()

    def own_shard(mat):
        if mat == 0:
            return pltpu.make_async_copy(fc1.at[:, lanes(c * part, part)], w1.at[0], lsem.at[0])
        return pltpu.make_async_copy(fc2.at[ds(c * part, part), :], w2.at[0], lsem.at[1])

    load_qkv = pltpu.make_async_copy(wqkv_hbm, wqkv, lsem.at[2])
    load_out = pltpu.make_async_copy(wout_hbm, wout, lsem.at[3])

    def token_copy(i):
        src, dst = tok.at[ds(i * tall, tall), :], tok.at[ds(t_own + i * tall, tall), :]
        return remote(src, dst, tsend.at[i], trecv.at[i], r_sib, z)

    cot_copy = remote(
        cot.at[ds(0, t_own), :], cot.at[ds(t_own, t_own), :], tsend.at[images], trecv.at[images], r_sib, z
    )
    gh2_copy = remote(gh2_low, gh2_in, esend.at[0], erecv.at[0], r_sib, z)
    out_copy = remote(out_low, out_in, esend.at[1], erecv.at[1], r_sib, z)

    h1r, q1r_rows = width // 2, width // 4
    h2r, q2r_rows = part // 2, part // 4

    def fc_first(k):
        return (
            remote(g1w.at[k, ds((1 - x) * h1r, h1r), :], r1a.at[k], s1s.at[k, 0], s1r.at[k, 0], r_x, z),
            remote(g2w.at[k, ds((1 - y) * h2r, h2r), :], r1b.at[k], s1s.at[k, 1], s1r.at[k, 1], r_y, z),
        )

    def fc_second(k):
        return (
            remote(
                g1w.at[k, ds(x * h1r + (1 - y) * q1r_rows, q1r_rows), :], r2a.at[k], s2s.at[k, 0], s2r.at[k, 0], r_y, z
            ),
            remote(
                g2w.at[k, ds(y * h2r + (1 - x) * q2r_rows, q2r_rows), :], r2b.at[k], s2s.at[k, 1], s2r.at[k, 1], r_x, z
            ),
        )

    def fc_third(k):
        column = lax.rem(z + distance(k), ranks)
        return (
            remote(fz1.at[k], rz1.at[k - 1], s3s.at[k - 1, 0], s3r.at[k - 1, 0], r, column),
            remote(fz2.at[k], rz2.at[k - 1], s3s.at[k - 1, 1], s3r.at[k - 1, 1], r, column),
        )

    f1_place = f1_out.at[ds(x * h1r + y * q1r_rows, q1r_rows), lanes(c * part, part)]
    f2_place = f2_out.at[ds(c * part + y * h2r + x * q2r_rows, q2r_rows), :]

    f1_level = (f1_place, f1_out.at[ds(x * h1r, h1r), lanes(c * part, part)])
    f2_level = (f2_place, f2_out.at[ds(c * part + y * h2r, h2r), :])

    def fc_spread(level):
        src1, src2 = (fz1.at[0], fz2.at[0]) if level == 0 else (f1_level[1], f2_level[1])
        row1, row2 = (r_y, r_x) if level == 0 else (r_x, r_y)
        return (
            remote(src1, f1_level[level], fs.at[level, 0], fr.at[level, 0], row1, z),
            remote(src2, f2_level[level], fs.at[level, 1], fr.at[level, 1], row2, z),
        )

    fc_keep = (
        pltpu.make_async_copy(fz1.at[0], f1_place, floc.at[0]),
        pltpu.make_async_copy(fz2.at[0], f2_place, floc.at[1]),
    )
    f1_half = f1_out.at[:, lanes(c * part, part)]
    f2_half = f2_out.at[ds(c * part, part), :]
    fc_share = (
        remote(f1_half, f1_half, ssib.at[0], rsib.at[0], r_sib, z),
        remote(f2_half, f2_half, ssib.at[1], rsib.at[1], r_sib, z),
    )

    def fc_fold_second(k):
        for copy in fc_first(k):
            copy.wait_recv()
        rows = ds(x * h1r + (1 - y) * q1r_rows, q1r_rows)
        g1w[k, rows, :] = g1w[k, rows, :] + r1a[k, ds((1 - y) * q1r_rows, q1r_rows), :]
        rows = ds(y * h2r + (1 - x) * q2r_rows, q2r_rows)
        g2w[k, rows, :] = g2w[k, rows, :] + r1b[k, ds((1 - x) * q2r_rows, q2r_rows), :]
        for copy in fc_second(k):
            copy.start()

    def fc_fold_third(k):
        for copy in fc_second(k):
            copy.wait_recv()
        total = g1w[k, ds(x * h1r + y * q1r_rows, q1r_rows), :].astype(F32)
        total = total + r1a[k, ds(y * q1r_rows, q1r_rows), :].astype(F32) + r2a[k].astype(F32)
        fz1[k] = total.astype(BF)
        total = g2w[k, ds(y * h2r + x * q2r_rows, q2r_rows), :].astype(F32)
        total = total + r1b[k, ds(x * q2r_rows, q2r_rows), :].astype(F32) + r2b[k].astype(F32)
        fz2[k] = total.astype(BF)

        @pl.when(k > 0)
        def _():
            for copy in fc_third(k):
                copy.start()

    def fc_finish():
        for k in range(1, ranks):
            for copy in fc_third(k):
                copy.wait_recv()
        for own, arrived in ((fz1, rz1), (fz2, rz2)):
            total = own[0].astype(F32)
            for k in range(ranks - 1):
                total = total + arrived[k].astype(F32)
            own[0] = total.astype(BF)
        for copy in fc_keep:
            copy.start()
        for copy in fc_spread(0):
            copy.start()

    def fc_widen():
        for copy in fc_keep:
            copy.wait()
        for copy in fc_spread(0):
            copy.wait_recv()
        for copy in fc_spread(1):
            copy.start()

    def fc_to_sibling():
        for copy in fc_spread(1):
            copy.wait_recv()
        for copy in fc_share:
            copy.start()

    eighth = width // 8

    def order(j):
        odd = lax.rem(j, 2)
        first, second = r_x + (r_y - r_x) * odd, r_y + (r_x - r_y) * odd
        a1, a2 = x + (y - x) * odd, y + (x - y) * odd
        return first, second, a1, a2

    def chunk_place(j, start, count):
        rows = ds(start, count)
        return (
            (j < 2, go_out.at[pl.ds(3 * lax.min(j, 1), 3), rows, :]),
            (j >= 2, gq_out.at[:, rows, lanes(lax.max(j - 2, 0) * 128, 128)]),
        )

    def core_copy(j):
        return remote(gw.at[j, :, ds((1 - c) * half, half), :], q0.at[j], q0s.at[j], q0r.at[j], r_sib, z)

    def first_copy(j):
        first, _, a1, _ = order(j)
        src = gw.at[j, :, ds(c * half + (1 - a1) * 2 * eighth, 2 * eighth), :]
        return remote(src, q1.at[j], q1s.at[j], q1r.at[j], first, z)

    def second_copy(j):
        _, second, a1, a2 = order(j)
        src = gw.at[j, :, ds(c * half + a1 * 2 * eighth + (1 - a2) * eighth, eighth), :]
        return remote(src, q2.at[j], q2s.at[j], q2r.at[j], second, z)

    def z_copy(j, step):
        column = (z + 1 - 2 * lax.rem(z, 2), z + 2 - 4 * lax.div(z, 2))[step]
        return remote(qz.at[j, 2 * step], qz.at[j, 2 * step + 1], q3s.at[j, step], q3r.at[j, step], r, column)

    def own_start(j):
        _, _, a1, a2 = order(j)
        return c * half + a1 * 2 * eighth + a2 * eighth

    def keep_copy(j, ref):
        return pltpu.make_async_copy(qf.at[j], ref, qloc.at[j])

    def spread_copies(j, ref, level):
        first, second, _, _ = order(j)
        if level == 0:
            return remote(qf.at[j], ref, q5s.at[j], q5r.at[j], second, z)
        if level == 1:
            return remote(ref, ref, q6s.at[j], q6r.at[j], first, z)
        return remote(ref, ref, q7s.at[j], q7r.at[j], r_sib, z)

    def level_place(j, level):
        _, _, a1, _ = order(j)
        if level == 0:
            return chunk_place(j, own_start(j), eighth)
        if level == 1:
            return chunk_place(j, c * half + a1 * 2 * eighth, 2 * eighth)
        return chunk_place(j, c * half, half)

    def each_place(j, level, do):
        for condition, ref in level_place(j, level):

            @pl.when(condition)
            def _(ref=ref):
                do(ref)

    def fold_first(j):
        core_copy(j).wait_recv()
        _, _, a1, _ = order(j)
        rows = ds(c * half + (1 - a1) * 2 * eighth, 2 * eighth)
        gw[j, :, rows, :] = gw[j, :, rows, :] + q0[j, :, ds((1 - a1) * 2 * eighth, 2 * eighth), :]
        first_copy(j).start()

    def fold_second(j):
        first_copy(j).wait_recv()
        _, _, a1, a2 = order(j)
        inner = (1 - a2) * eighth
        rows = ds(c * half + a1 * 2 * eighth + inner, eighth)
        total = gw[j, :, rows, :].astype(F32) + q0[j, :, ds(a1 * 2 * eighth + inner, eighth), :].astype(F32)
        gw[j, :, rows, :] = (total + q1[j, :, ds(inner, eighth), :].astype(F32)).astype(BF)
        second_copy(j).start()

    def fold_z(j):
        second_copy(j).wait_recv()
        _, _, a1, a2 = order(j)
        inner = a2 * eighth
        rows = ds(c * half + a1 * 2 * eighth + inner, eighth)
        total = gw[j, :, rows, :].astype(F32) + q0[j, :, ds(a1 * 2 * eighth + inner, eighth), :].astype(F32)
        total = total + q1[j, :, ds(inner, eighth), :].astype(F32) + q2[j].astype(F32)
        qz[j, 0] = total.astype(BF)
        z_copy(j, 0).start()

    def fold_pair(j):
        z_copy(j, 0).wait_recv()
        qz[j, 2] = qz[j, 0] + qz[j, 1]
        z_copy(j, 1).start()

    def fold_all(j):
        z_copy(j, 1).wait_recv()
        qf[j] = qz[j, 2] + qz[j, 3]

        def go(ref):
            keep_copy(j, ref).start()
            spread_copies(j, ref, 0).start()

        each_place(j, 0, go)

    def spread_first(j):
        def done(ref):
            keep_copy(j, ref).wait()
            spread_copies(j, ref, 0).wait_recv()

        each_place(j, 0, done)
        each_place(j, 1, lambda ref: spread_copies(j, ref, 1).start())

    def spread_sibling(j):
        each_place(j, 1, lambda ref: spread_copies(j, ref, 1).wait_recv())
        each_place(j, 2, lambda ref: spread_copies(j, ref, 2).start())

    def chunk_done(j):
        each_place(j, 2, lambda ref: spread_copies(j, ref, 2).wait())
        each_place(j, 1, lambda ref: spread_copies(j, ref, 1).wait_send())
        each_place(j, 0, lambda ref: spread_copies(j, ref, 0).wait_send())
        core_copy(j).wait_send()
        first_copy(j).wait_send()
        second_copy(j).wait_send()
        for step in range(2):
            z_copy(j, step).wait_send()

    def small_copy(level):
        row = (r_sib, r_x, r_y)[level]
        return remote(sma.at[level], smr.at[level], sms.at[level], smrs.at[level], row, z)

    def small_z(k):
        return remote(smz.at[z], smz.at[z], smzs.at[k - 1], smzr.at[k - 1], r, lax.rem(z + k, ranks))

    barrier = pltpu.get_barrier_semaphore()
    partners = [(r_sib, z), (r_x, z), (r_y, z), (r_diag, z)] + [(r, lax.rem(z + k, ranks)) for k in range(1, ranks)]
    for row, column in partners:
        pl.semaphore_signal(barrier, inc=1, device_id={"rows": row, "mlp": column}, device_id_type=MESH)
    load_qkv.start()
    load_out.start()
    own_shard(0).start()
    own_shard(1).start()
    pl.semaphore_wait(barrier, len(partners))
    gather_start(1)
    for i in range(images):
        work[...] = jnp.zeros_like(work)
        work[0:patches, :] = c_ref[:, i, :]
        cot[i * tall : (i + 1) * tall, :] = work[...]
    cot_copy.start()

    for i in range(images):
        forward_rows(i, x_ref, rank_ref, kept_ref, g1_ref, rw_ref, xp, keep, gate, h1, h1t, work)

    h1t[...] = h1[...].T
    load_qkv.wait()

    @pl.loop(0, 3 * width // 256)
    def _(j):
        forward_qkv(j, h1, wqkv, qkv)

    @pl.loop(0, HEADS // 2)
    def _(p):
        for i in range(images):
            attend(p, i, width, tall, qkv, keep, probs, context, contextt)

        @pl.when(p == 3)
        def _():
            gather_forward(1)

    load_out.wait()

    @pl.loop(0, images)
    def _(i):
        forward_out(i, tall, context, wout, xp, keep, gate, g2_ref, attended, middle, tok)
        token_copy(i).start()

    gather_forward(2)
    own_shard(0).wait()
    own_shard(1).wait()
    for ref in (out, gh2, dg1, dg2, drw):
        ref[...] = jnp.zeros_like(ref)

    def mlp_step(k):
        @pl.loop(0, 2 * images)
        def _(block):
            @pl.when(jnp.logical_and(k == 0, block == images))
            def _():
                for i in range(images):
                    token_copy(i).wait()
                cot_copy.wait()

            rows = ds(lax.rem(block + images * lax.div(k, ranks - 1), 2 * images) * tall, tall)
            hid[rows, :], gpre[rows, :] = mlp_rows(tok[rows, :], cot[rows, :], w1[k], w2[k])
            out[rows, :] += dot_nn(hid[rows, :], w2[k])
            gh2[rows, :] += dot_nt(gpre[rows, :], w1[k])

            @pl.when(jnp.logical_and(k == ranks - 1, block == images - 1))
            def _():
                gh2_low[...] = gh2[ds(t_own, t_own), :].astype(BF)
                gh2_copy.start()
                out_low[...] = out[ds(t_own, t_own), :].astype(BF)
                out_copy.start()

        @pl.when(k == 0)
        def _():
            tokt[...] = tok[...].T

        hidt[...] = hid[...].T
        for m in range(3):
            rows = slice(m * width // 3, (m + 1) * width // 3)
            g1w[k, rows, :] = dot_nn(tokt[rows, :], gpre[...]).astype(BF)
            g2w[k, :, rows] = dot_nn(hidt[...], cot[:, rows]).astype(BF)

    @pl.loop(0, LAST)
    def _(t):
        for k in range(1, ranks):

            @pl.when(t == k)
            def _(k=k):
                gather_finish(k)

        @pl.when(t < ranks)
        def _():
            mlp_step(t)
            for copy in fc_first(t):
                copy.start()

        @pl.when(t == 1)
        def _():
            gather_forward(3)

        @pl.when(t == 4)
        def _():
            gh2_copy.wait()

            @pl.loop(0, images)
            def _(i):
                rows = ds(i * tall, tall)
                gh2[rows, :] += gh2_in[rows, :].astype(F32)
                back_rows(
                    i, tall, cot, gh2, middle, keep, gate, attended, g2_ref, gh2, tok, glogit, dg2
                )

            context[...] = dot_nt(tok[ds(0, t_own), :], wout[...]).astype(BF)

        @pl.when(jnp.logical_and(t >= 4, t < 6))
        def _():
            cols = lanes((t - 4) * half, half)
            total = 0.0
            for i in range(images):
                total = total + dot_nn(contextt[i], tok[i * tall : (i + 1) * tall, cols])
            for b in range(3):
                gw[t - 4, b] = total[:, b * 128 : (b + 1) * 128].astype(BF)

        @pl.when(jnp.logical_and(t >= 6, t < 12))
        def _():
            p = t - 6
            for i in range(images):
                attend_back(p, i, width, tall, qkv, probs, context)
            total = dot_nn(h1t[...], pair_columns(qkv, p, width))
            for b in range(3):
                gw[t - 4, b] = total[:, b * 128 : (b + 1) * 128].astype(BF)

        @pl.when(jnp.logical_and(t >= 4, t < 12))
        def _():
            core_copy(t - 4).start()

        @pl.when(t == 5)
        def _():
            out_copy.wait()

            @pl.loop(0, images)
            def _(i):
                rows = ds(i * tall, tall)
                block_ref[i] = (middle[rows, :] + out[rows, :] + out_in[rows, :].astype(F32)).astype(BF)[0:patches, :]

        @pl.when(t == 12)
        def _():
            @pl.loop(0, images)
            def _(i):
                rows = ds(i * tall, tall)
                dy = dot_nt(qkv[rows, :], wqkv[...])
                back_input(i, tall, dy, glogit, rw_ref, xp, h1, g1_ref, gh2, gx_ref, dg1, drw)

            sma[0] = jnp.concatenate([dg1[...], drw[...], dg2[...], jnp.zeros((5, width), F32)], 0)
            small_copy(0).start()

        for level in range(2):

            @pl.when(t == 14 + 2 * level)
            def _(level=level):
                small_copy(level).wait()
                sma[level + 1] = sma[level] + smr[level]
                small_copy(level + 1).start()

        @pl.when(t == 18)
        def _():
            small_copy(2).wait()
            smz[z] = sma[2] + smr[2]
            for k in range(1, ranks):
                small_z(k).start()

        def lagged(lag, do):
            @pl.when(jnp.logical_and(t >= 4 + lag, t < 4 + lag + CHUNKS))
            def _():
                do(t - 4 - lag)

        @pl.when(jnp.logical_and(t >= 3, t < 3 + ranks))
        def _():
            fc_fold_third(t - 3)

        @pl.when(jnp.logical_and(t >= 1, t < 1 + ranks))
        def _():
            fc_fold_second(t - 1)

        for tick, do in ((13, fc_finish), (16, fc_widen), (22, fc_to_sibling)):

            @pl.when(t == tick)
            def _(do=do):
                do()

        stages = (fold_first, fold_second, fold_z, fold_pair, fold_all, spread_first, spread_sibling)
        for lag, do in zip(LAGS[1:], stages):
            lagged(lag, do)

    for k in range(1, ranks):
        small_z(k).wait()
    total = smz[0]
    for k in range(1, ranks):
        total = total + smz[k]
    small_out[...] = total

    @pl.loop(0, CHUNKS)
    def _(j):
        chunk_done(j)

    for copy in fc_share:
        copy.wait()
    for level in range(2):
        for copy in fc_spread(level):
            copy.wait_send()
    for k in range(1, ranks):
        for copy in fc_third(k):
            copy.wait_send()
        for mat in range(2):
            for kind in range(5):
                gather_copy(k, mat, kind).wait_send()

    @pl.loop(0, ranks)
    def _(k):
        for copy in fc_first(k) + fc_second(k):
            copy.wait_send()


VMEM = pl.BlockSpec(memory_space=pltpu.VMEM)
SMEM = pl.BlockSpec(memory_space=pltpu.SMEM)
ANY = pl.BlockSpec(memory_space=pl.ANY)


def widen_kernel(block, gx, gq, go, f1, f2, small, block_out, gx_out, gq_out, go_out, f1_out, f2_out, g1_out, rw_out, g2_out):
    width = f1.shape[1]
    for step, (src, dst) in enumerate(((block, block_out), (gx, gx_out))):

        @pl.when(pl.program_id(0) == step)
        def _(src=src, dst=dst):
            for i in range(src.shape[0]):
                dst[:, i, :] = src[i]

    for b in range(3):
        gq_out[:, b * width : (b + 1) * width] = gq[b].astype(F32)
    for b in range(go.shape[0]):
        go_out[:, b * 128 : (b + 1) * 128] = go[b].astype(F32)
    f1_out[...] = f1[...].astype(F32)
    f2_out[...] = f2[...].astype(F32)
    g1_out[...], rw_out[...], g2_out[...] = small[0], small[1], small[2]


def widen(block, gx, gq, go, f1, f2, small):
    width = f1.shape[0]
    images, patches, _ = block.shape
    step = 128
    tokens = jax.ShapeDtypeStruct((patches, images, width), BF)
    whole_in = pl.BlockSpec((images, patches, width), lambda i: (0, 0, 0))
    whole_out = pl.BlockSpec((patches, images, width), lambda i: (0, 0, 0))

    def rows(*tail):
        return pl.BlockSpec((step,) + tail, lambda i: (i, 0))

    def inner(lead, tail):
        return pl.BlockSpec((lead, step, tail), lambda i: (0, i, 0))

    return pl.pallas_call(
        widen_kernel,
        grid=(width // step,),
        out_shape=[tokens, tokens] + [jax.ShapeDtypeStruct((width, n), F32) for n in (3 * width, width, width, width)]
        + [jax.ShapeDtypeStruct((width,), F32)] * 3,
        in_specs=[whole_in, whole_in, inner(3, width), inner(6, 128), rows(width), rows(width), pl.BlockSpec((8, width), lambda i: (0, 0))],
        out_specs=[whole_out, whole_out, rows(3 * width), rows(width), rows(width), rows(width)] + [pl.BlockSpec((width,), lambda i: (0,))] * 3,
        compiler_params=pltpu.CompilerParams(vmem_limit_bytes=63 * 1024 * 1024),
        name="widen",
    )(block, gx, gq, go, f1, f2, small)


def per_device(ranks, others, images, patch_rank, kept_count, ln1_gain, router_weight, w_qkv, w_out, ln2_gain, w_fc1, w_fc2, cotangent):
    count, patches, width = images.shape
    tall = -(-patches // 16) * 16
    t = count * tall
    part = w_fc1.shape[1] // 2
    half, eighth = width // 2, width // 8

    def bf(*dims):
        return pltpu.VMEM(dims, BF)

    def f32(*dims):
        return pltpu.VMEM(dims, F32)

    def sem(*dims):
        return pltpu.SemaphoreType.DMA(dims)

    scratch = [
        bf(width, 3 * width), bf(width, width), bf(ranks, width, part), bf(ranks, part, width),
        bf(t, width), f32(t, 128), f32(t, 128), f32(t, 128), bf(t, width), bf(width, t), bf(t, 3 * width),
        f32(count, HEADS, tall, tall), bf(count, width, tall), bf(t, width), f32(t, width), f32(t, width),
        bf(2 * t, width), bf(2 * t, width), bf(width, 2 * t), f32(2 * t, width), f32(2 * t, width),
        bf(t, width), bf(t, width), bf(t, width), bf(t, width), bf(2 * t, part), bf(part, 2 * t), bf(2 * t, part), bf(tall, width),
        bf(ranks, width, part), bf(ranks, part, width),
        bf(ranks, width // 2, part), bf(ranks, part // 2, width), bf(ranks, width // 4, part), bf(ranks, part // 4, width),
        bf(ranks, width // 4, part), bf(ranks, part // 4, width), bf(ranks - 1, width // 4, part), bf(ranks - 1, part // 4, width),
        bf(CHUNKS, 3, width, 128), bf(CHUNKS, 3, half, 128), bf(CHUNKS, 3, 2 * eighth, 128), bf(CHUNKS, 3, eighth, 128),
        bf(CHUNKS, ranks, 3, eighth, 128), bf(CHUNKS, 3, eighth, 128),
        f32(1, width), f32(1, width), f32(1, width), f32(3, 8, width), f32(3, 8, width), f32(ranks, 8, width),
        sem(4), sem(ranks - 1, 2, 5), sem(ranks - 1, 2, 5), sem(count + 1), sem(count + 1), sem(2), sem(2),
        sem(ranks, 2), sem(ranks, 2), sem(ranks, 2), sem(ranks, 2), sem(ranks - 1, 2), sem(ranks - 1, 2),
        sem(2, 2), sem(2, 2), sem(2), sem(2), sem(2),
        sem(CHUNKS), sem(CHUNKS), sem(CHUNKS), sem(CHUNKS), sem(CHUNKS), sem(CHUNKS),
        sem(CHUNKS, 2), sem(CHUNKS, 2), sem(CHUNKS),
        sem(CHUNKS), sem(CHUNKS), sem(CHUNKS), sem(CHUNKS), sem(CHUNKS), sem(CHUNKS),
        sem(3), sem(3), sem(ranks - 1), sem(ranks - 1),
    ]

    def struct(*dims, dtype=BF):
        return jax.ShapeDtypeStruct(dims, dtype)

    block, gx, gq, go, f1, f2, small = pl.pallas_call(
        functools.partial(mega_kernel, ranks),
        out_shape=[
            struct(count, patches, width), struct(count, patches, width), struct(3, width, width), struct(6, width, 128),
            struct(width, 2 * part), struct(2 * part, width), struct(8, width, dtype=F32),
        ],
        in_specs=[VMEM, VMEM, SMEM, VMEM, VMEM, ANY, ANY, VMEM, ANY, ANY, VMEM],
        out_specs=[VMEM, VMEM, ANY, ANY, ANY, ANY, VMEM],
        scratch_shapes=scratch,
        compiler_params=pltpu.CompilerParams(
            collective_id=0, has_side_effects=True, vmem_limit_bytes=64 * 1024 * 1024
        ),
        name="block",
    )(images.transpose(1, 0, 2), patch_rank, kept_count, ln1_gain, router_weight, w_qkv, w_out, ln2_gain, w_fc1, w_fc2,
      cotangent.transpose(1, 0, 2))
    block, gx, gq, go, f1, f2, g1, rw, g2 = widen(block, gx, gq, go, f1, f2, small)
    if others:
        gq, go, f1, f2, g1, rw, g2 = lax.psum((gq, go, f1, f2, g1, rw, g2), "rows", axis_index_groups=others)
    return block.transpose(1, 0, 2), gx.transpose(1, 0, 2), g1, rw, gq, go, g2, f1, f2


def solution(mesh):
    rows, ranks = mesh.shape["rows"], mesh.shape["mlp"]
    others = [[8 * g + i for g in range(rows // 8)] for i in range(8)] if rows > 8 else None
    return jax.shard_map(
        functools.partial(per_device, ranks, others),
        mesh=mesh,
        in_specs=(
            P(("rows", "mlp"), None, None), P(("rows", "mlp"), None), P(("rows", "mlp")), P(), P(), P(), P(), P(),
            P(None, "mlp"), P("mlp", None), P(("rows", "mlp"), None, None),
        ),
        out_specs=(
            P(("rows", "mlp"), None, None), P(("rows", "mlp"), None, None), P(), P(), P(), P(), P(),
            P(None, "mlp"), P("mlp", None),
        ),
        check_vma=False,
    )
```

```python
import functools
import jax
import jax.numpy as jnp
from jax import lax
from jax.experimental import pallas as pl
from jax.experimental.pallas import tpu as pltpu
from jax.sharding import PartitionSpec as P

HEADS = 12
EPS = 1e-6
FILL = -1e30
BF = jnp.bfloat16
F32 = jnp.float32


def dot_nn(a, b):
    return lax.dot_general(a, b, (((1,), (0,)), ((), ())), preferred_element_type=F32)


def dot_nt(a, b):
    return lax.dot_general(a, b, (((1,), (1,)), ((), ())), preferred_element_type=F32)


def dot_tn(a, b):
    return lax.dot_general(a, b, (((0,), (0,)), ((), ())), preferred_element_type=F32)


def unit_rows(v):
    center = v - jnp.mean(v, -1, keepdims=True)
    scale = lax.rsqrt(jnp.mean(center * center, -1, keepdims=True) + EPS)
    return center * scale, scale


def norm_pull(dy, gain, unit, scale):
    du = dy * gain
    return scale * (
        du
        - jnp.mean(du, -1, keepdims=True)
        - unit * jnp.mean(du * unit, -1, keepdims=True)
    )


def half_mask(rows, h):
    lane = lax.broadcasted_iota(jnp.int32, (rows, 128), 1)
    return (lane < 64) if h == 0 else (lane >= 64)


def forward_rows(i, x_ref, rank_ref, kept_ref, g1_ref, rw_ref, xp, keep, gate, h1, work):
    patches = x_ref.shape[0]
    tall = xp.shape[0] // x_ref.shape[1]
    rows = pl.ds(pl.multiple_of(i * tall, 16), tall)
    work[...] = jnp.zeros_like(work)
    work[0:patches, :] = x_ref[:, i, :]
    v = work[...]
    xp[rows, :] = v
    kept = (rank_ref[pl.ds(i, 1), :] < kept_ref[i]).astype(F32)
    keep_row = jnp.concatenate([kept, jnp.zeros((1, 256 - patches), F32)], 1)
    keep_col = jnp.broadcast_to(keep_row, (128, 256)).T
    keep[rows, :] = keep_col[0:tall, :]
    unit, _ = unit_rows(v.astype(F32))
    low = (unit * g1_ref[...][None]).astype(BF)
    h1[rows, :] = low
    logit = jnp.sum(low.astype(F32) * rw_ref[...][None].astype(F32), -1, keepdims=True)
    gate[rows, :] = jnp.broadcast_to(jax.nn.sigmoid(logit), (tall, 128))


def forward_qkv(j, h1, wqkv, qkv):
    cols = pl.ds(pl.multiple_of(j * 256, 256), 256)
    qkv[:, cols] = dot_nn(h1[...], wqkv[:, cols]).astype(BF)


def attend(p, i, width, tall, qkv, keep, probs, context, contextt):
    rows = pl.ds(pl.multiple_of(i * tall, 16), tall)
    qc = pl.ds(pl.multiple_of(p * 128, 128), 128)
    kc = pl.ds(pl.multiple_of(width + p * 128, 128), 128)
    vc = pl.ds(pl.multiple_of(2 * width + p * 128, 128), 128)
    q, k, v = qkv[rows, qc], qkv[rows, kc], qkv[rows, vc]
    vt = v.T
    kept = keep[rows, 0:1] > 0.5
    outs = []
    for h in range(2):
        kh = jnp.where(half_mask(tall, h), k, jnp.zeros_like(k))
        s = jnp.where(kept, dot_nt(kh, q) * 0.125, FILL)
        e = jnp.exp(s - jnp.max(s, 0, keepdims=True))
        pr = e * (1.0 / jnp.sum(e, 0, keepdims=True))
        probs[i, p * 2 + h] = pr
        outs.append(dot_nn(vt[h * 64 : h * 64 + 64, :], pr.astype(BF)))
    ct = jnp.concatenate(outs, 0)
    contextt[i, pl.ds(pl.multiple_of(p * 128, 128), 128), :] = ct.astype(BF)
    context[rows, qc] = ct.T.astype(BF)


def forward_out(i, tall, context, wout, xp, keep, gate, g2_ref, attended, middle, h2):
    rows = pl.ds(pl.multiple_of(i * tall, 16), tall)
    att = dot_nn(context[rows, :], wout[...])
    attended[rows, :] = att
    mid = xp[rows, :].astype(F32) + keep[rows, 0:1] * gate[rows, 0:1] * att
    middle[rows, :] = mid
    unit, _ = unit_rows(mid)
    h2[rows, :] = (unit * g2_ref[...][None]).astype(BF)


def gelu_pair(pre):
    cdf = 0.5 * (1.0 + lax.erf(pre * 0.7071067811865476))
    pdf = jnp.exp(pre * pre * -0.5) * 0.3989422804014327
    return pre * cdf, cdf + pre * pdf


def mlp_rows(h, c, w1, w2):
    pre = dot_nn(h, w1)
    hidden, slope = gelu_pair(pre)
    grad = dot_nt(c, w2) * slope
    return hidden.astype(BF), grad.astype(BF)


def back_rows(i, tall, c_ref, gh2, middle, keep, gate, attended, g2_ref, gmid, gatt, glogit, dg2):
    rows = pl.ds(pl.multiple_of(i * tall, 16), tall)
    dy = gh2[rows, :]
    unit, scale = unit_rows(middle[rows, :])
    gm = c_ref[rows, :].astype(F32) + norm_pull(dy, g2_ref[...][None], unit, scale)
    gmid[rows, :] = gm
    dg2[...] += jnp.sum(dy * unit, 0, keepdims=True)
    k, g = keep[rows, 0:1], gate[rows, 0:1]
    kept = gm * k
    gatt[rows, :] = (kept * g).astype(BF)
    gl = jnp.sum(kept * attended[rows, :], -1, keepdims=True) * g * (1.0 - g)
    glogit[rows, :] = jnp.broadcast_to(gl, (tall, 128))


def attend_back(p, i, width, tall, qkv, probs, gctx):
    rows = pl.ds(pl.multiple_of(i * tall, 16), tall)
    qc = pl.ds(pl.multiple_of(p * 128, 128), 128)
    kc = pl.ds(pl.multiple_of(width + p * 128, 128), 128)
    vc = pl.ds(pl.multiple_of(2 * width + p * 128, 128), 128)
    q, k, v = qkv[rows, qc], qkv[rows, kc], qkv[rows, vc]
    gc = gctx[rows, qc]
    kt = k.T
    gv, gk, gq = 0.0, 0.0, []
    for h in range(2):
        mask = half_mask(tall, h)
        zero = jnp.zeros_like(v)
        pr = probs[i, p * 2 + h]
        gp = dot_nt(jnp.where(mask, v, zero), gc)
        gs = (pr * (gp - jnp.sum(pr * gp, 0, keepdims=True))).astype(BF)
        gv = gv + dot_nn(pr.astype(BF), jnp.where(mask, gc, zero))
        gk = gk + dot_nn(gs, jnp.where(mask, q, zero))
        gq.append(dot_nn(kt[h * 64 : h * 64 + 64, :], gs))
    qkv[rows, qc] = (jnp.concatenate(gq, 0).T * 0.125).astype(BF)
    qkv[rows, kc] = (gk * 0.125).astype(BF)
    qkv[rows, vc] = gv.astype(BF)


def pair_columns(wqkv, p, width):
    return jnp.concatenate(
        [wqkv[:, pl.ds(pl.multiple_of(b * width + p * 128, 128), 128)] for b in range(3)], 1
    )


def back_input(i, tall, dy, glogit, rw_ref, xp, h1, g1_ref, gmid, gx_ref, dg1, drw):
    rows = pl.ds(pl.multiple_of(i * tall, 16), tall)
    patches = gx_ref.shape[1]
    gl = glogit[rows, 0:1]
    dy = dy + gl * rw_ref[...][None].astype(F32)
    unit, scale = unit_rows(xp[rows, :].astype(F32))
    dg1[...] += jnp.sum(dy * unit, 0, keepdims=True)
    drw[...] += jnp.sum(h1[rows, :].astype(F32) * gl, 0, keepdims=True)
    out = gmid[rows, :] + norm_pull(dy, g1_ref[...][None], unit, scale)
    gx_ref[i] = out.astype(BF)[0:patches, :]

MESH = pl.DeviceIdType.MESH
CHUNKS = HEADS // 2 + 2
LAGS = (0, 2, 5, 7, 9, 11, 14, 20)
LAST = 4 + CHUNKS + LAGS[7]


def mega_kernel(
    x_ref, rank_ref, kept_ref, g1_ref, rw_ref, wqkv_hbm, wout_hbm, g2_ref, fc1, fc2, c_ref,
    block_ref, gx_ref, gq_out, go_out, f1_out, f2_out, small_out,
    wqkv, wout, w1, w2, xp, keep, gate, glogit, h1, qkv, probs, contextt, context, attended, middle,
    tok, cot, turned, out, gh2, out_part, gh2_part, out_sib, gh2_sib, out_near, gh2_near, out_far, gh2_far, hid, gpre, work,
    g1w, g2w, r1a, r1b, r2a, r2b, fz1, fz2, rz1, rz2,
    gw, q0, q1, q2, qz, qf, dg1, dg2, drw, sma, smr, smz,
    lsem, gsend, grecv, hsend, hrecv, csend, crecv, esend, erecv, s1s, s1r, s2s, s2r, s3s, s3r, fs, fr, floc, ssib, rsib,
    q0s, q0r, q1s, q1r, q2s, q2r, q3s, q3r, qloc, q5s, q5r, q6s, q6r, q7s, q7r, sms, smrs, smzs, smzr,
):
    patches, images, width = x_ref.shape
    t_own = xp.shape[0]
    tall = t_own // images
    half = width // 2
    part = w1.shape[1] // 2
    quarter = (width // 4, part // 4)
    r = lax.axis_index("rows")
    z = lax.axis_index("mlp")
    c, x, y = lax.rem(r, 2), lax.rem(lax.div(r, 2), 2), lax.rem(lax.div(r, 4), 2)
    r_sib, r_x, r_y = r + 1 - 2 * c, r + 2 - 4 * x, r + 4 - 8 * y
    r_diag = r_x + r_y - r
    z_pair, z_far = z + 1 - 2 * lax.rem(z, 2), z + 2 - 4 * lax.div(z, 2)
    q = 2 * y + x

    def ds(start, size):
        return pl.ds(pl.multiple_of(start, 16), size)

    def lanes(start, size):
        return pl.ds(pl.multiple_of(start, 128), size)

    def remote(src, dst, send, recv, row, column):
        return pltpu.make_async_remote_copy(
            src_ref=src, dst_ref=dst, send_sem=send, recv_sem=recv,
            device_id={"rows": row, "mlp": column}, device_id_type=MESH,
        )

    def gather_copy(mat, kind):
        size = quarter[mat]
        sems = gsend.at[mat, kind], grecv.at[mat, kind]
        if mat == 0:
            place = w1.at[ds(q * size, size), pl.ds(part, part)]
            own = fc1.at[ds(q * size, size), lanes(c * part, part)]
        else:
            place = w2.at[ds(part + q * size, size), :]
            own = fc2.at[ds(c * part + q * size, size), :]
        if kind == 0:
            return remote(own, place, *sems, r, z_far)
        return remote(place, place, *sems, (r_x, r_y, r_diag)[kind - 1], z)

    def gather_forward(mat):
        gather_copy(mat, 0).wait_recv()
        for kind in (1, 2, 3):
            gather_copy(mat, kind).start()

    def own_shard(mat):
        if mat == 0:
            return pltpu.make_async_copy(fc1.at[:, lanes(c * part, part)], w1.at[:, pl.ds(0, part)], lsem.at[0])
        return pltpu.make_async_copy(fc2.at[ds(c * part, part), :], w2.at[pl.ds(0, part), :], lsem.at[1])

    load_qkv = pltpu.make_async_copy(wqkv_hbm, wqkv, lsem.at[2])
    load_out = pltpu.make_async_copy(wout_hbm, wout, lsem.at[3])

    def token_copy(i, hop):
        start = (0, 0, 2 * t_own)[hop] + i * tall
        src, dst = tok.at[ds(start, tall), :], tok.at[ds((1, 2, 3)[hop] * t_own + i * tall, tall), :]
        row, column = (r, z_pair) if hop == 1 else (r_sib, z)
        return remote(src, dst, hsend.at[i, hop], hrecv.at[i, hop], row, column)

    def cot_copy(hop):
        src, dst = cot.at[ds((0, 0, 2)[hop] * t_own, t_own), :], cot.at[ds((1, 2, 3)[hop] * t_own, t_own), :]
        row, column = (r, z_pair) if hop == 1 else (r_sib, z)
        return remote(src, dst, csend.at[hop], crecv.at[hop], row, column)

    gh2_to_sib = remote(gh2_part.at[ds(0, t_own), :], gh2_sib, esend.at[0], erecv.at[0], r_sib, z)
    out_to_sib = remote(out_part.at[ds(0, t_own), :], out_sib, esend.at[1], erecv.at[1], r_sib, z)
    out_over = remote(out_part.at[ds(2 * t_own, t_own), :], out_near, esend.at[2], erecv.at[2], r_sib, z)
    out_far_copy = remote(out_part.at[ds(t_own, t_own), :], out_far, esend.at[3], erecv.at[3], r, z_pair)

    def gh2_over(i):
        src = gh2_part.at[ds(2 * t_own + i * tall, tall), :]
        return remote(src, gh2_near.at[ds(i * tall, tall), :], esend.at[4 + i], erecv.at[4 + i], r_sib, z)

    def gh2_far_copy(i):
        src = gh2_part.at[ds(t_own + i * tall, tall), :]
        return remote(src, gh2_far.at[ds(i * tall, tall), :], esend.at[6 + i], erecv.at[6 + i], r, z_pair)

    h1r, q1r_rows = width // 2, width // 4
    h2r, q2r_rows = part // 2, part // 4

    def fc_first(k):
        return (
            remote(g1w.at[k, ds((1 - x) * h1r, h1r), :], r1a.at[k], s1s.at[k, 0], s1r.at[k, 0], r_x, z),
            remote(g2w.at[k, ds((1 - y) * h2r, h2r), :], r1b.at[k], s1s.at[k, 1], s1r.at[k, 1], r_y, z),
        )

    def fc_second(k):
        return (
            remote(
                g1w.at[k, ds(x * h1r + (1 - y) * q1r_rows, q1r_rows), :], r2a.at[k], s2s.at[k, 0], s2r.at[k, 0], r_y, z
            ),
            remote(
                g2w.at[k, ds(y * h2r + (1 - x) * q2r_rows, q2r_rows), :], r2b.at[k], s2s.at[k, 1], s2r.at[k, 1], r_x, z
            ),
        )

    fc_third = (
        remote(fz1.at[1], rz1, s3s.at[0], s3r.at[0], r, z_far),
        remote(fz2.at[1], rz2, s3s.at[1], s3r.at[1], r, z_far),
    )

    f1_place = f1_out.at[ds(x * h1r + y * q1r_rows, q1r_rows), lanes(c * part, part)]
    f2_place = f2_out.at[ds(c * part + y * h2r + x * q2r_rows, q2r_rows), :]

    f1_level = (f1_place, f1_out.at[ds(x * h1r, h1r), lanes(c * part, part)])
    f2_level = (f2_place, f2_out.at[ds(c * part + y * h2r, h2r), :])

    def fc_spread(level):
        src1, src2 = (fz1.at[0], fz2.at[0]) if level == 0 else (f1_level[1], f2_level[1])
        row1, row2 = (r_y, r_x) if level == 0 else (r_x, r_y)
        return (
            remote(src1, f1_level[level], fs.at[level, 0], fr.at[level, 0], row1, z),
            remote(src2, f2_level[level], fs.at[level, 1], fr.at[level, 1], row2, z),
        )

    fc_keep = (
        pltpu.make_async_copy(fz1.at[0], f1_place, floc.at[0]),
        pltpu.make_async_copy(fz2.at[0], f2_place, floc.at[1]),
    )
    f1_half = f1_out.at[:, lanes(c * part, part)]
    f2_half = f2_out.at[ds(c * part, part), :]
    fc_share = (
        remote(f1_half, f1_half, ssib.at[0], rsib.at[0], r_sib, z),
        remote(f2_half, f2_half, ssib.at[1], rsib.at[1], r_sib, z),
    )

    def fc_fold_second(k):
        for copy in fc_first(k):
            copy.wait_recv()
        rows = ds(x * h1r + (1 - y) * q1r_rows, q1r_rows)
        g1w[k, rows, :] = g1w[k, rows, :] + r1a[k, ds((1 - y) * q1r_rows, q1r_rows), :]
        rows = ds(y * h2r + (1 - x) * q2r_rows, q2r_rows)
        g2w[k, rows, :] = g2w[k, rows, :] + r1b[k, ds((1 - x) * q2r_rows, q2r_rows), :]
        for copy in fc_second(k):
            copy.start()

    def fc_fold_third(k):
        for copy in fc_second(k):
            copy.wait_recv()
        total = g1w[k, ds(x * h1r + y * q1r_rows, q1r_rows), :].astype(F32)
        total = total + r1a[k, ds(y * q1r_rows, q1r_rows), :].astype(F32) + r2a[k].astype(F32)
        fz1[k] = total.astype(BF)
        total = g2w[k, ds(y * h2r + x * q2r_rows, q2r_rows), :].astype(F32)
        total = total + r1b[k, ds(x * q2r_rows, q2r_rows), :].astype(F32) + r2b[k].astype(F32)
        fz2[k] = total.astype(BF)

        if k == 1:
            for copy in fc_third:
                copy.start()

    def fc_finish():
        for copy in fc_third:
            copy.wait_recv()
        fz1[0] = fz1[0] + rz1[...]
        fz2[0] = fz2[0] + rz2[...]
        for copy in fc_keep:
            copy.start()
        for copy in fc_spread(0):
            copy.start()

    def fc_widen():
        for copy in fc_keep:
            copy.wait()
        for copy in fc_spread(0):
            copy.wait_recv()
        for copy in fc_spread(1):
            copy.start()

    def fc_to_sibling():
        for copy in fc_spread(1):
            copy.wait_recv()
        for copy in fc_share:
            copy.start()

    eighth = width // 8

    def order(j):
        odd = lax.rem(j, 2)
        first, second = r_x + (r_y - r_x) * odd, r_y + (r_x - r_y) * odd
        a1, a2 = x + (y - x) * odd, y + (x - y) * odd
        return first, second, a1, a2

    def chunk_place(j, start, count):
        rows = ds(start, count)
        return (
            (j < 2, go_out.at[pl.ds(3 * lax.min(j, 1), 3), rows, :]),
            (j >= 2, gq_out.at[:, rows, lanes(lax.max(j - 2, 0) * 128, 128)]),
        )

    def core_copy(j):
        return remote(gw.at[j, :, ds((1 - c) * half, half), :], q0.at[j], q0s.at[j], q0r.at[j], r_sib, z)

    def first_copy(j):
        first, _, a1, _ = order(j)
        src = gw.at[j, :, ds(c * half + (1 - a1) * 2 * eighth, 2 * eighth), :]
        return remote(src, q1.at[j], q1s.at[j], q1r.at[j], first, z)

    def second_copy(j):
        _, second, a1, a2 = order(j)
        src = gw.at[j, :, ds(c * half + a1 * 2 * eighth + (1 - a2) * eighth, eighth), :]
        return remote(src, q2.at[j], q2s.at[j], q2r.at[j], second, z)

    def z_copy(j, step):
        if step == 0:
            src = gw.at[j, :, ds(own_start(j), eighth), :]
            return remote(src, qz.at[j, 0], q3s.at[j, 0], q3r.at[j, 0], r, z_pair)
        return remote(q2.at[j], qz.at[j, 1], q3s.at[j, 1], q3r.at[j, 1], r, z_far)

    def own_start(j):
        _, _, a1, a2 = order(j)
        return c * half + a1 * 2 * eighth + a2 * eighth

    def keep_copy(j, ref):
        return pltpu.make_async_copy(qf.at[j], ref, qloc.at[j])

    def spread_copies(j, ref, level):
        first, second, _, _ = order(j)
        if level == 0:
            return remote(qf.at[j], ref, q5s.at[j], q5r.at[j], second, z)
        if level == 1:
            return remote(ref, ref, q6s.at[j], q6r.at[j], first, z)
        return remote(ref, ref, q7s.at[j], q7r.at[j], r_sib, z)

    def level_place(j, level):
        _, _, a1, _ = order(j)
        if level == 0:
            return chunk_place(j, own_start(j), eighth)
        if level == 1:
            return chunk_place(j, c * half + a1 * 2 * eighth, 2 * eighth)
        return chunk_place(j, c * half, half)

    def each_place(j, level, do):
        for condition, ref in level_place(j, level):

            @pl.when(condition)
            def _(ref=ref):
                do(ref)

    def fold_first(j):
        core_copy(j).wait_recv()
        _, _, a1, _ = order(j)
        rows = ds(c * half + (1 - a1) * 2 * eighth, 2 * eighth)
        gw[j, :, rows, :] = gw[j, :, rows, :] + q0[j, :, ds((1 - a1) * 2 * eighth, 2 * eighth), :]
        first_copy(j).start()

    def fold_second(j):
        first_copy(j).wait_recv()
        _, _, a1, a2 = order(j)
        inner = (1 - a2) * eighth
        rows = ds(c * half + a1 * 2 * eighth + inner, eighth)
        total = gw[j, :, rows, :].astype(F32) + q0[j, :, ds(a1 * 2 * eighth + inner, eighth), :].astype(F32)
        gw[j, :, rows, :] = (total + q1[j, :, ds(inner, eighth), :].astype(F32)).astype(BF)
        second_copy(j).start()

    def fold_z(j):
        second_copy(j).wait_recv()
        _, _, a1, a2 = order(j)
        inner = a2 * eighth
        rows = ds(c * half + a1 * 2 * eighth + inner, eighth)
        total = gw[j, :, rows, :].astype(F32) + q0[j, :, ds(a1 * 2 * eighth + inner, eighth), :].astype(F32)
        total = total + q1[j, :, ds(inner, eighth), :].astype(F32) + q2[j].astype(F32)
        gw[j, :, rows, :] = total.astype(BF)
        z_copy(j, 0).start()

    def fold_pair(j):
        z_copy(j, 0).wait_recv()
        q2[j] = gw[j, :, ds(own_start(j), eighth), :] + qz[j, 0]
        z_copy(j, 1).start()

    def fold_all(j):
        z_copy(j, 1).wait_recv()
        qf[j] = q2[j] + qz[j, 1]

        def go(ref):
            keep_copy(j, ref).start()
            spread_copies(j, ref, 0).start()

        each_place(j, 0, go)

    def spread_first(j):
        def done(ref):
            keep_copy(j, ref).wait()
            spread_copies(j, ref, 0).wait_recv()

        each_place(j, 0, done)
        each_place(j, 1, lambda ref: spread_copies(j, ref, 1).start())

    def spread_sibling(j):
        each_place(j, 1, lambda ref: spread_copies(j, ref, 1).wait_recv())
        each_place(j, 2, lambda ref: spread_copies(j, ref, 2).start())

    def chunk_done(j):
        each_place(j, 2, lambda ref: spread_copies(j, ref, 2).wait())
        each_place(j, 1, lambda ref: spread_copies(j, ref, 1).wait_send())
        each_place(j, 0, lambda ref: spread_copies(j, ref, 0).wait_send())
        core_copy(j).wait_send()
        first_copy(j).wait_send()
        second_copy(j).wait_send()
        for step in range(2):
            z_copy(j, step).wait_send()

    def small_copy(level):
        row = (r_sib, r_x, r_y)[level]
        return remote(sma.at[level], smr.at[level], sms.at[level], smrs.at[level], row, z)

    def small_z(step):
        src, dst = smz.at[2 * step], smz.at[2 * step + 1]
        return remote(src, dst, smzs.at[step], smzr.at[step], r, (z_pair, z_far)[step])

    barrier = pltpu.get_barrier_semaphore()
    partners = ((r_sib, z), (r_x, z), (r_y, z), (r_diag, z), (r, z_pair), (r, z_far))
    for row, column in partners:
        pl.semaphore_signal(barrier, inc=1, device_id={"rows": row, "mlp": column}, device_id_type=MESH)
    load_qkv.start()
    load_out.start()
    own_shard(0).start()
    own_shard(1).start()
    pl.semaphore_wait(barrier, len(partners))
    gather_copy(0, 0).start()
    gather_copy(1, 0).start()
    for i in range(images):
        work[...] = jnp.zeros_like(work)
        work[0:patches, :] = c_ref[:, i, :]
        cot[i * tall : (i + 1) * tall, :] = work[...]
    cot_copy(0).start()
    cot_copy(1).start()
    for i in range(images):
        forward_rows(i, x_ref, rank_ref, kept_ref, g1_ref, rw_ref, xp, keep, gate, h1, work)

    load_qkv.wait()

    @pl.loop(0, 3 * width // 256)
    def _(j):
        forward_qkv(j, h1, wqkv, qkv)

    @pl.loop(0, HEADS // 2)
    def _(p):
        for i in range(images):
            attend(p, i, width, tall, qkv, keep, probs, context, contextt)

        @pl.when(p == 2)
        def _():
            gather_forward(0)

        @pl.when(p == 5)
        def _():
            gather_forward(1)

    load_out.wait()

    @pl.loop(0, images)
    def _(i):
        forward_out(i, tall, context, wout, xp, keep, gate, g2_ref, attended, middle, tok)
        token_copy(i, 0).start()
        token_copy(i, 1).start()

    cot_copy(1).wait_recv()
    cot_copy(2).start()
    own_shard(0).wait()
    own_shard(1).wait()
    for mat in range(2):
        for kind in (1, 2, 3):
            gather_copy(mat, kind).wait_recv()
    for ref in (dg1, dg2, drw):
        ref[...] = jnp.zeros_like(ref)

    def at(block, number, do):
        @pl.when(block == number)
        def _():
            do()

    def before_sibling():
        for i in range(images):
            token_copy(i, 0).wait_recv()
        cot_copy(0).wait_recv()

    def before_near():
        cot_copy(2).wait_recv()
        gh2_to_sib.start()
        out_to_sib.start()

    def forward_token(i):
        token_copy(i, 1).wait_recv()
        token_copy(i, 2).start()

    def send_far(i):
        gh2_over(i).wait_recv()
        rows = ds(t_own + i * tall, tall)
        gh2_part[rows, :] = gh2_part[rows, :] + gh2_near[ds(i * tall, tall), :]
        gh2_far_copy(i).start()

    def before_last():
        send_far(0)
        token_copy(1, 2).wait_recv()

    @pl.loop(0, 8)
    def _(block):
        at(block, 2, before_sibling)
        at(block, 3, lambda: forward_token(0))
        at(block, 4, before_near)
        at(block, 5, lambda: token_copy(0, 2).wait_recv())
        at(block, 6, lambda: forward_token(1))
        at(block, 7, before_last)
        inner = lax.rem(block, 5)
        swap = lax.div(block, 5) * (1 - 2 * inner + 3 * lax.div(inner * (inner - 1), 2))
        spot = block + swap
        rows = ds(spot * tall, tall)
        hid[rows, :], gpre[rows, :] = mlp_rows(tok[rows, :], cot[rows, :], w1[...], w2[...])
        share_out = dot_nn(hid[rows, :], w2[...])
        share_gh2 = dot_nt(gpre[rows, :], w1[...])

        @pl.when(block < images)
        def _():
            out[rows, :] = share_out
            gh2[rows, :] = share_gh2

        @pl.when(block >= images)
        def _():
            there = ds(lax.max(spot - images, 0) * tall, tall)
            out_part[there, :] = share_out.astype(BF)
            gh2_part[there, :] = share_gh2.astype(BF)

        at(block, 5, lambda: gh2_over(0).start())
        at(block, 7, lambda: gh2_over(1).start())

    out_over.start()
    turned[...] = tok[...].T
    for m in range(3):
        rows = slice(m * width // 3, (m + 1) * width // 3)
        total = dot_nn(turned[rows, :], gpre[...]).astype(BF)
        g1w[0, rows, :] = total[:, 0:part]
        g1w[1, rows, :] = total[:, part:]
    send_far(1)
    out_over.wait_recv()
    rows = pl.ds(t_own, t_own)
    out_part[rows, :] = out_part[rows, :] + out_near[...]
    out_far_copy.start()
    turned[...] = hid[...].T
    for m in range(2):
        g2w[m] = dot_nn(turned[m * part : (m + 1) * part, :], cot[...]).astype(BF)
    for k in range(2):
        for copy in fc_first(k):
            copy.start()

    @pl.loop(4, LAST)
    def _(t):
        @pl.when(t == 4)
        def _():
            gh2_to_sib.wait_recv()
            for i in range(images):
                token_copy(i, 0).wait_send()
                token_copy(i, 1).wait_send()

            @pl.loop(0, images)
            def _(i):
                for n in range(images):
                    at(i, n, lambda n=n: gh2_far_copy(n).wait_recv())
                rows = ds(i * tall, tall)
                gh2[rows, :] += gh2_sib[rows, :].astype(F32) + gh2_far[rows, :].astype(F32)
                back_rows(
                    i, tall, cot, gh2, middle, keep, gate, attended, g2_ref, gh2, tok, glogit, dg2
                )

            context[...] = dot_nt(tok[ds(0, t_own), :], wout[...]).astype(BF)
            turned[:, 0:t_own] = h1[...].T

        @pl.when(jnp.logical_and(t >= 4, t < 6))
        def _():
            cols = lanes((t - 4) * half, half)
            total = 0.0
            for i in range(images):
                total = total + dot_nn(contextt[i], tok[i * tall : (i + 1) * tall, cols])
            for b in range(3):
                gw[t - 4, b] = total[:, b * 128 : (b + 1) * 128].astype(BF)

        @pl.when(jnp.logical_and(t >= 6, t < 12))
        def _():
            p = t - 6
            for i in range(images):
                attend_back(p, i, width, tall, qkv, probs, context)
            total = dot_nn(turned[:, 0:t_own], pair_columns(qkv, p, width))
            for b in range(3):
                gw[t - 4, b] = total[:, b * 128 : (b + 1) * 128].astype(BF)

        @pl.when(jnp.logical_and(t >= 4, t < 12))
        def _():
            core_copy(t - 4).start()

        @pl.when(t == 12)
        def _():
            @pl.loop(0, images)
            def _(i):
                rows = ds(i * tall, tall)
                dy = dot_nt(qkv[rows, :], wqkv[...])
                back_input(i, tall, dy, glogit, rw_ref, xp, h1, g1_ref, gh2, gx_ref, dg1, drw)

            out_to_sib.wait_recv()
            out_far_copy.wait_recv()

            @pl.loop(0, images)
            def _(i):
                rows = ds(i * tall, tall)
                total = middle[rows, :] + out[rows, :] + out_sib[rows, :].astype(F32) + out_far[rows, :].astype(F32)
                block_ref[i] = total.astype(BF)[0:patches, :]

            sma[0] = jnp.concatenate([dg1[...], drw[...], dg2[...], jnp.zeros((5, width), F32)], 0)
            small_copy(0).start()

        for level in range(2):

            @pl.when(t == 14 + 2 * level)
            def _(level=level):
                small_copy(level).wait()
                sma[level + 1] = sma[level] + smr[level]
                small_copy(level + 1).start()

        @pl.when(t == 18)
        def _():
            small_copy(2).wait()
            smz[0] = sma[2] + smr[2]
            small_z(0).start()

        @pl.when(t == 20)
        def _():
            small_z(0).wait()
            smz[2] = smz[0] + smz[1]
            small_z(1).start()

        def lagged(lag, do):
            @pl.when(jnp.logical_and(t >= 4 + lag, t < 4 + lag + CHUNKS))
            def _():
                do(t - 4 - lag)

        steps = (
            (7, lambda: fc_fold_second(1)), (8, lambda: fc_fold_second(0)), (9, lambda: fc_fold_third(1)),
            (13, lambda: fc_fold_third(0)), (15, fc_finish), (17, fc_widen), (21, fc_to_sibling),
        )
        for tick, do in steps:
            at(t, tick, do)

        stages = (fold_first, fold_second, fold_z, fold_pair, fold_all, spread_first, spread_sibling)
        for stage in (5, 6, 7, 4, 3, 2, 1):
            lagged(LAGS[stage], stages[stage - 1])

    small_z(1).wait()
    small_out[...] = smz[2] + smz[3]

    @pl.loop(0, CHUNKS)
    def _(j):
        chunk_done(j)

    for copy in fc_share:
        copy.wait()
    for level in range(2):
        for copy in fc_spread(level):
            copy.wait_send()
    for copy in fc_third:
        copy.wait_send()
    for mat in range(2):
        for kind in range(4):
            gather_copy(mat, kind).wait_send()
    for i in range(images):
        token_copy(i, 2).wait_send()
        gh2_over(i).wait_send()
        gh2_far_copy(i).wait_send()
    for hop in range(3):
        cot_copy(hop).wait_send()
    for copy in (gh2_to_sib, out_to_sib, out_over, out_far_copy):
        copy.wait_send()
    for k in range(2):
        for copy in fc_first(k) + fc_second(k):
            copy.wait_send()


VMEM = pl.BlockSpec(memory_space=pltpu.VMEM)
SMEM = pl.BlockSpec(memory_space=pltpu.SMEM)
ANY = pl.BlockSpec(memory_space=pl.ANY)


def widen_kernel(block, gx, gq, go, f1, f2, small, block_out, gx_out, gq_out, go_out, f1_out, f2_out, g1_out, rw_out, g2_out):
    width = f1.shape[1]
    for step, (src, dst) in enumerate(((block, block_out), (gx, gx_out))):

        @pl.when(pl.program_id(0) == step)
        def _(src=src, dst=dst):
            for i in range(src.shape[0]):
                dst[:, i, :] = src[i]

    for b in range(3):
        gq_out[:, b * width : (b + 1) * width] = gq[b].astype(F32)
    for b in range(go.shape[0]):
        go_out[:, b * 128 : (b + 1) * 128] = go[b].astype(F32)
    f1_out[...] = f1[...].astype(F32)
    f2_out[...] = f2[...].astype(F32)
    g1_out[...], rw_out[...], g2_out[...] = small[0], small[1], small[2]


def widen(block, gx, gq, go, f1, f2, small):
    width = f1.shape[0]
    images, patches, _ = block.shape
    step = 128
    tokens = jax.ShapeDtypeStruct((patches, images, width), BF)
    whole_in = pl.BlockSpec((images, patches, width), lambda i: (0, 0, 0))
    whole_out = pl.BlockSpec((patches, images, width), lambda i: (0, 0, 0))

    def rows(*tail):
        return pl.BlockSpec((step,) + tail, lambda i: (i, 0))

    def inner(lead, tail):
        return pl.BlockSpec((lead, step, tail), lambda i: (0, i, 0))

    return pl.pallas_call(
        widen_kernel,
        grid=(width // step,),
        out_shape=[tokens, tokens] + [jax.ShapeDtypeStruct((width, n), F32) for n in (3 * width, width, width, width)]
        + [jax.ShapeDtypeStruct((width,), F32)] * 3,
        in_specs=[whole_in, whole_in, inner(3, width), inner(6, 128), rows(width), rows(width), pl.BlockSpec((8, width), lambda i: (0, 0))],
        out_specs=[whole_out, whole_out, rows(3 * width), rows(width), rows(width), rows(width)] + [pl.BlockSpec((width,), lambda i: (0,))] * 3,
        compiler_params=pltpu.CompilerParams(vmem_limit_bytes=63 * 1024 * 1024),
        name="widen",
    )(block, gx, gq, go, f1, f2, small)


def per_device(others, images, patch_rank, kept_count, ln1_gain, router_weight, w_qkv, w_out, ln2_gain, w_fc1, w_fc2, cotangent):
    count, patches, width = images.shape
    tall = -(-patches // 16) * 16
    t = count * tall
    part = w_fc1.shape[1] // 2
    half, eighth = width // 2, width // 8

    def bf(*dims):
        return pltpu.VMEM(dims, BF)

    def f32(*dims):
        return pltpu.VMEM(dims, F32)

    def sem(*dims):
        return pltpu.SemaphoreType.DMA(dims)

    scratch = [
        bf(width, 3 * width), bf(width, width), bf(width, 2 * part), bf(2 * part, width),
        bf(t, width), f32(t, 128), f32(t, 128), f32(t, 128), bf(t, width), bf(t, 3 * width),
        f32(count, HEADS, tall, tall), bf(count, width, tall), bf(t, width), f32(t, width), f32(t, width),
        bf(4 * t, width), bf(4 * t, width), bf(width, 4 * t), f32(t, width), f32(t, width),
        bf(3 * t, width), bf(3 * t, width), bf(t, width), bf(t, width), bf(t, width), bf(t, width), bf(t, width), bf(t, width),
        bf(4 * t, 2 * part), bf(4 * t, 2 * part), bf(tall, width),
        bf(2, width, part), bf(2, part, width),
        bf(2, width // 2, part), bf(2, part // 2, width), bf(2, width // 4, part), bf(2, part // 4, width),
        bf(2, width // 4, part), bf(2, part // 4, width), bf(width // 4, part), bf(part // 4, width),
        bf(CHUNKS, 3, width, 128), bf(CHUNKS, 3, half, 128), bf(CHUNKS, 3, 2 * eighth, 128), bf(CHUNKS, 3, eighth, 128),
        bf(CHUNKS, 2, 3, eighth, 128), bf(CHUNKS, 3, eighth, 128),
        f32(1, width), f32(1, width), f32(1, width), f32(3, 8, width), f32(3, 8, width), f32(4, 8, width),
        sem(4), sem(2, 4), sem(2, 4), sem(count, 3), sem(count, 3), sem(3), sem(3), sem(8), sem(8),
        sem(2, 2), sem(2, 2), sem(2, 2), sem(2, 2), sem(2), sem(2),
        sem(2, 2), sem(2, 2), sem(2), sem(2), sem(2),
        sem(CHUNKS), sem(CHUNKS), sem(CHUNKS), sem(CHUNKS), sem(CHUNKS), sem(CHUNKS),
        sem(CHUNKS, 2), sem(CHUNKS, 2), sem(CHUNKS),
        sem(CHUNKS), sem(CHUNKS), sem(CHUNKS), sem(CHUNKS), sem(CHUNKS), sem(CHUNKS),
        sem(3), sem(3), sem(2), sem(2),
    ]

    def struct(*dims, dtype=BF):
        return jax.ShapeDtypeStruct(dims, dtype)

    block, gx, gq, go, f1, f2, small = pl.pallas_call(
        mega_kernel,
        out_shape=[
            struct(count, patches, width), struct(count, patches, width), struct(3, width, width), struct(6, width, 128),
            struct(width, 2 * part), struct(2 * part, width), struct(8, width, dtype=F32),
        ],
        in_specs=[VMEM, VMEM, SMEM, VMEM, VMEM, ANY, ANY, VMEM, ANY, ANY, VMEM],
        out_specs=[VMEM, VMEM, ANY, ANY, ANY, ANY, VMEM],
        scratch_shapes=scratch,
        compiler_params=pltpu.CompilerParams(
            collective_id=0, has_side_effects=True, vmem_limit_bytes=64 * 1024 * 1024
        ),
        name="block",
    )(images.transpose(1, 0, 2), patch_rank, kept_count, ln1_gain, router_weight, w_qkv, w_out, ln2_gain, w_fc1, w_fc2,
      cotangent.transpose(1, 0, 2))
    block, gx, gq, go, f1, f2, g1, rw, g2 = widen(block, gx, gq, go, f1, f2, small)
    if others:
        gq, go, f1, f2, g1, rw, g2 = lax.psum((gq, go, f1, f2, g1, rw, g2), "rows", axis_index_groups=others)
    return block.transpose(1, 0, 2), gx.transpose(1, 0, 2), g1, rw, gq, go, g2, f1, f2


def solution(mesh):
    rows = mesh.shape["rows"]
    others = [[8 * g + i for g in range(rows // 8)] for i in range(8)] if rows > 8 else None
    return jax.shard_map(
        functools.partial(per_device, others),
        mesh=mesh,
        in_specs=(
            P(("rows", "mlp"), None, None), P(("rows", "mlp"), None), P(("rows", "mlp")), P(), P(), P(), P(), P(),
            P(None, "mlp"), P("mlp", None), P(("rows", "mlp"), None, None),
        ),
        out_specs=(
            P(("rows", "mlp"), None, None), P(("rows", "mlp"), None, None), P(), P(), P(), P(), P(),
            P(None, "mlp"), P("mlp", None),
        ),
        check_vma=False,
    )
```

```python
import functools
import jax
import jax.numpy as jnp
from jax import lax
from jax.experimental import pallas as pl
from jax.experimental.pallas import tpu as pltpu
from jax.sharding import PartitionSpec as P

HEADS = 12
EPS = 1e-6
FILL = -1e30
BF = jnp.bfloat16
F32 = jnp.float32


def dot_nn(a, b):
    return lax.dot_general(a, b, (((1,), (0,)), ((), ())), preferred_element_type=F32)


def dot_nt(a, b):
    return lax.dot_general(a, b, (((1,), (1,)), ((), ())), preferred_element_type=F32)


def dot_tn(a, b):
    return lax.dot_general(a, b, (((0,), (0,)), ((), ())), preferred_element_type=F32)


def unit_rows(v):
    center = v - jnp.mean(v, -1, keepdims=True)
    scale = lax.rsqrt(jnp.mean(center * center, -1, keepdims=True) + EPS)
    return center * scale, scale


def norm_pull(dy, gain, unit, scale):
    du = dy * gain
    return scale * (
        du
        - jnp.mean(du, -1, keepdims=True)
        - unit * jnp.mean(du * unit, -1, keepdims=True)
    )


def half_mask(rows, h):
    lane = lax.broadcasted_iota(jnp.int32, (rows, 128), 1)
    return (lane < 64) if h == 0 else (lane >= 64)


def forward_rows(i, x_ref, rank_ref, kept_ref, g1_ref, rw_ref, xp, keep, gate, h1, work):
    patches = x_ref.shape[0]
    tall = xp.shape[0] // x_ref.shape[1]
    rows = pl.ds(pl.multiple_of(i * tall, 16), tall)
    work[...] = jnp.zeros_like(work)
    work[0:patches, :] = x_ref[:, i, :]
    v = work[...]
    xp[rows, :] = v
    kept = (rank_ref[pl.ds(i, 1), :] < kept_ref[i]).astype(F32)
    keep_row = jnp.concatenate([kept, jnp.zeros((1, 256 - patches), F32)], 1)
    keep_col = jnp.broadcast_to(keep_row, (128, 256)).T
    keep[rows, :] = keep_col[0:tall, :]
    unit, _ = unit_rows(v.astype(F32))
    low = (unit * g1_ref[...][None]).astype(BF)
    h1[rows, :] = low
    logit = jnp.sum(low.astype(F32) * rw_ref[...][None].astype(F32), -1, keepdims=True)
    gate[rows, :] = jnp.broadcast_to(jax.nn.sigmoid(logit), (tall, 128))


def forward_qkv(j, h1, wqkv, qkv):
    cols = pl.ds(pl.multiple_of(j * 256, 256), 256)
    qkv[:, cols] = dot_nn(h1[...], wqkv[:, cols]).astype(BF)


def attend(p, i, width, tall, qkv, keep, probs, context, contextt):
    rows = pl.ds(pl.multiple_of(i * tall, 16), tall)
    qc = pl.ds(pl.multiple_of(p * 128, 128), 128)
    kc = pl.ds(pl.multiple_of(width + p * 128, 128), 128)
    vc = pl.ds(pl.multiple_of(2 * width + p * 128, 128), 128)
    q, k, v = qkv[rows, qc], qkv[rows, kc], qkv[rows, vc]
    vt = v.T
    kept = keep[rows, 0:1] > 0.5
    outs = []
    for h in range(2):
        kh = jnp.where(half_mask(tall, h), k, jnp.zeros_like(k))
        s = jnp.where(kept, dot_nt(kh, q) * 0.125, FILL)
        e = jnp.exp(s - jnp.max(s, 0, keepdims=True))
        pr = e * (1.0 / jnp.sum(e, 0, keepdims=True))
        probs[i, p * 2 + h] = pr
        outs.append(dot_nn(vt[h * 64 : h * 64 + 64, :], pr.astype(BF)))
    ct = jnp.concatenate(outs, 0)
    contextt[i, pl.ds(pl.multiple_of(p * 128, 128), 128), :] = ct.astype(BF)
    context[rows, qc] = ct.T.astype(BF)


def forward_out(i, tall, context, wout, xp, keep, gate, g2_ref, attended, middle, h2):
    rows = pl.ds(pl.multiple_of(i * tall, 16), tall)
    att = dot_nn(context[rows, :], wout[...])
    attended[rows, :] = att
    mid = xp[rows, :].astype(F32) + keep[rows, 0:1] * gate[rows, 0:1] * att
    middle[rows, :] = mid
    unit, _ = unit_rows(mid)
    h2[rows, :] = (unit * g2_ref[...][None]).astype(BF)


def gelu_pair(pre):
    cdf = 0.5 * (1.0 + lax.erf(pre * 0.7071067811865476))
    pdf = jnp.exp(pre * pre * -0.5) * 0.3989422804014327
    return pre * cdf, cdf + pre * pdf


def mlp_rows(h, c, w1, w2):
    pre = dot_nn(h, w1)
    hidden, slope = gelu_pair(pre)
    grad = dot_nt(c, w2) * slope
    return hidden.astype(BF), grad.astype(BF)


def back_rows(i, tall, c_ref, gh2, middle, keep, gate, attended, g2_ref, gmid, gatt, glogit, dg2):
    rows = pl.ds(pl.multiple_of(i * tall, 16), tall)
    dy = gh2[rows, :]
    unit, scale = unit_rows(middle[rows, :])
    gm = c_ref[rows, :].astype(F32) + norm_pull(dy, g2_ref[...][None], unit, scale)
    gmid[rows, :] = gm
    dg2[...] += jnp.sum(dy * unit, 0, keepdims=True)
    k, g = keep[rows, 0:1], gate[rows, 0:1]
    kept = gm * k
    gatt[rows, :] = (kept * g).astype(BF)
    gl = jnp.sum(kept * attended[rows, :], -1, keepdims=True) * g * (1.0 - g)
    glogit[rows, :] = jnp.broadcast_to(gl, (tall, 128))


def attend_back(p, i, width, tall, qkv, probs, gctx):
    rows = pl.ds(pl.multiple_of(i * tall, 16), tall)
    qc = pl.ds(pl.multiple_of(p * 128, 128), 128)
    kc = pl.ds(pl.multiple_of(width + p * 128, 128), 128)
    vc = pl.ds(pl.multiple_of(2 * width + p * 128, 128), 128)
    q, k, v = qkv[rows, qc], qkv[rows, kc], qkv[rows, vc]
    gc = gctx[rows, qc]
    kt = k.T
    gv, gk, gq = 0.0, 0.0, []
    for h in range(2):
        mask = half_mask(tall, h)
        zero = jnp.zeros_like(v)
        pr = probs[i, p * 2 + h]
        gp = dot_nt(jnp.where(mask, v, zero), gc)
        gs = (pr * (gp - jnp.sum(pr * gp, 0, keepdims=True))).astype(BF)
        gv = gv + dot_nn(pr.astype(BF), jnp.where(mask, gc, zero))
        gk = gk + dot_nn(gs, jnp.where(mask, q, zero))
        gq.append(dot_nn(kt[h * 64 : h * 64 + 64, :], gs))
    qkv[rows, qc] = (jnp.concatenate(gq, 0).T * 0.125).astype(BF)
    qkv[rows, kc] = (gk * 0.125).astype(BF)
    qkv[rows, vc] = gv.astype(BF)


def pair_columns(wqkv, p, width):
    return jnp.concatenate(
        [wqkv[:, pl.ds(pl.multiple_of(b * width + p * 128, 128), 128)] for b in range(3)], 1
    )


def back_input(i, tall, dy, glogit, rw_ref, xp, h1, g1_ref, gmid, gx_ref, dg1, drw):
    rows = pl.ds(pl.multiple_of(i * tall, 16), tall)
    patches = gx_ref.shape[0]
    gl = glogit[rows, 0:1]
    dy = dy + gl * rw_ref[...][None].astype(F32)
    unit, scale = unit_rows(xp[rows, :].astype(F32))
    dg1[...] += jnp.sum(dy * unit, 0, keepdims=True)
    drw[...] += jnp.sum(h1[rows, :].astype(F32) * gl, 0, keepdims=True)
    out = gmid[rows, :] + norm_pull(dy, g1_ref[...][None], unit, scale)
    gx_ref[:, i, :] = out.astype(BF)[0:patches, :]

MESH = pl.DeviceIdType.MESH
CHUNKS = HEADS // 2 + 2
LAGS = (0, 2, 6, 9, 11, 13, 16, 22)
FIRST = 8
LAST = FIRST + CHUNKS + LAGS[7]


def mega_kernel(
    x_hbm, rank_ref, kept_ref, g1_ref, rw_ref, wqkv_hbm, wout_hbm, g2_ref, fc1, fc2, c_hbm,
    block_hbm, gx_hbm, gq_out, go_out, f1_out, f2_out, small_out,
    x_ref, c_ref, wqkv, wout, w1, w2, xp, keep, gate, glogit, h1, qkv, probs, contextt, context, attended, middle,
    tok, cot, turned, out, gh2, out_part, gh2_part, out_sib, gh2_sib, out_near, gh2_near, out_far, gh2_far, hid, gpre, work,
    g1w, g2w, r1a, r1b, r2a, r2b, fz1, fz2, rz1, rz2,
    gw, q0, q1, q2, qz, qf, dg1, dg2, drw, sma, smr, smz,
    lsem, gsend, grecv, hsend, hrecv, csend, crecv, esend, erecv, s1s, s1r, s2s, s2r, s3s, s3r, fs, fr, floc, ssib, rsib,
    q0s, q0r, q1s, q1r, q2s, q2r, q3s, q3r, qloc, q5s, q5r, q6s, q6r, q7s, q7r, sms, smrs, smzs, smzr,
):
    patches, images, width = x_ref.shape
    t_own = xp.shape[0]
    tall = t_own // images
    half = width // 2
    part = w1.shape[1] // 2
    quarter = (width // 4, part // 4)
    r = lax.axis_index("rows")
    z = lax.axis_index("mlp")
    c, x, y = lax.rem(r, 2), lax.rem(lax.div(r, 2), 2), lax.rem(lax.div(r, 4), 2)
    r_sib, r_x, r_y = r + 1 - 2 * c, r + 2 - 4 * x, r + 4 - 8 * y
    r_diag = r_x + r_y - r
    z_pair, z_far = z + 1 - 2 * lax.rem(z, 2), z + 2 - 4 * lax.div(z, 2)
    q = 2 * y + x

    def ds(start, size):
        return pl.ds(pl.multiple_of(start, 16), size)

    def lanes(start, size):
        return pl.ds(pl.multiple_of(start, 128), size)

    def remote(src, dst, send, recv, row, column):
        return pltpu.make_async_remote_copy(
            src_ref=src, dst_ref=dst, send_sem=send, recv_sem=recv,
            device_id={"rows": row, "mlp": column}, device_id_type=MESH,
        )

    def gather_copy(mat, kind):
        size = quarter[mat]
        sems = gsend.at[mat, kind], grecv.at[mat, kind]
        if mat == 0:
            place = w1.at[ds(q * size, size), pl.ds(part, part)]
            own = fc1.at[ds(q * size, size), lanes(c * part, part)]
        else:
            place = w2.at[ds(part + q * size, size), :]
            own = fc2.at[ds(c * part + q * size, size), :]
        if kind == 0:
            return remote(own, place, *sems, r, z_far)
        return remote(place, place, *sems, (r_x, r_y, r_diag)[kind - 1], z)

    def gather_forward(mat):
        gather_copy(mat, 0).wait_recv()
        for kind in (1, 2, 3):
            gather_copy(mat, kind).start()

    def own_shard(mat):
        if mat == 0:
            return pltpu.make_async_copy(fc1.at[:, lanes(c * part, part)], w1.at[:, pl.ds(0, part)], lsem.at[0])
        return pltpu.make_async_copy(fc2.at[ds(c * part, part), :], w2.at[pl.ds(0, part), :], lsem.at[1])

    load_qkv = pltpu.make_async_copy(wqkv_hbm, wqkv, lsem.at[2])
    load_out = pltpu.make_async_copy(wout_hbm, wout, lsem.at[3])
    load_x = pltpu.make_async_copy(x_hbm, x_ref, lsem.at[4])
    load_c = pltpu.make_async_copy(c_hbm, c_ref, lsem.at[5])
    store_block = pltpu.make_async_copy(c_ref, block_hbm, lsem.at[6])
    store_gx = pltpu.make_async_copy(x_ref, gx_hbm, lsem.at[7])

    def token_copy(i, hop):
        start = (0, 0, 2 * t_own)[hop] + i * tall
        src, dst = tok.at[ds(start, tall), :], tok.at[ds((1, 2, 3)[hop] * t_own + i * tall, tall), :]
        row, column = (r, z_pair) if hop == 1 else (r_sib, z)
        return remote(src, dst, hsend.at[i, hop], hrecv.at[i, hop], row, column)

    def cot_copy(hop):
        src, dst = cot.at[ds((0, 0, 2)[hop] * t_own, t_own), :], cot.at[ds((1, 2, 3)[hop] * t_own, t_own), :]
        row, column = (r, z_pair) if hop == 1 else (r_sib, z)
        return remote(src, dst, csend.at[hop], crecv.at[hop], row, column)

    gh2_to_sib = remote(gh2_part.at[ds(0, t_own), :], gh2_sib, esend.at[0], erecv.at[0], r_sib, z)
    out_to_sib = remote(out_part.at[ds(0, t_own), :], out_sib, esend.at[1], erecv.at[1], r_sib, z)
    out_over = remote(out_part.at[ds(2 * t_own, t_own), :], out_near, esend.at[2], erecv.at[2], r_sib, z)
    out_far_copy = remote(out_part.at[ds(t_own, t_own), :], out_far, esend.at[3], erecv.at[3], r, z_pair)

    def gh2_over(i):
        src = gh2_part.at[ds(2 * t_own + i * tall, tall), :]
        return remote(src, gh2_near.at[ds(i * tall, tall), :], esend.at[4 + i], erecv.at[4 + i], r_sib, z)

    def gh2_far_copy(i):
        src = gh2_part.at[ds(t_own + i * tall, tall), :]
        return remote(src, gh2_far.at[ds(i * tall, tall), :], esend.at[6 + i], erecv.at[6 + i], r, z_pair)

    h1r, q1r_rows = width // 2, width // 4
    h2r, q2r_rows = part // 2, part // 4

    def fc_first(k):
        return (
            remote(g1w.at[k, ds((1 - x) * h1r, h1r), :], r1a.at[k], s1s.at[k, 0], s1r.at[k, 0], r_x, z),
            remote(g2w.at[k, ds((1 - y) * h2r, h2r), :], r1b.at[k], s1s.at[k, 1], s1r.at[k, 1], r_y, z),
        )

    def fc_second(k):
        return (
            remote(
                g1w.at[k, ds(x * h1r + (1 - y) * q1r_rows, q1r_rows), :], r2a.at[k], s2s.at[k, 0], s2r.at[k, 0], r_y, z
            ),
            remote(
                g2w.at[k, ds(y * h2r + (1 - x) * q2r_rows, q2r_rows), :], r2b.at[k], s2s.at[k, 1], s2r.at[k, 1], r_x, z
            ),
        )

    fc_third = (
        remote(fz1.at[1], rz1, s3s.at[0], s3r.at[0], r, z_far),
        remote(fz2.at[1], rz2, s3s.at[1], s3r.at[1], r, z_far),
    )

    f1_place = f1_out.at[ds(x * h1r + y * q1r_rows, q1r_rows), lanes(c * part, part)]
    f2_place = f2_out.at[ds(c * part + y * h2r + x * q2r_rows, q2r_rows), :]

    f1_level = (f1_place, f1_out.at[ds(x * h1r, h1r), lanes(c * part, part)])
    f2_level = (f2_place, f2_out.at[ds(c * part + y * h2r, h2r), :])

    def fc_spread(level):
        src1, src2 = (fz1.at[0], fz2.at[0]) if level == 0 else (f1_level[1], f2_level[1])
        row1, row2 = (r_y, r_x) if level == 0 else (r_x, r_y)
        return (
            remote(src1, f1_level[level], fs.at[level, 0], fr.at[level, 0], row1, z),
            remote(src2, f2_level[level], fs.at[level, 1], fr.at[level, 1], row2, z),
        )

    fc_keep = (
        pltpu.make_async_copy(fz1.at[0], f1_place, floc.at[0]),
        pltpu.make_async_copy(fz2.at[0], f2_place, floc.at[1]),
    )
    f1_half = f1_out.at[:, lanes(c * part, part)]
    f2_half = f2_out.at[ds(c * part, part), :]
    fc_share = (
        remote(f1_half, f1_half, ssib.at[0], rsib.at[0], r_sib, z),
        remote(f2_half, f2_half, ssib.at[1], rsib.at[1], r_sib, z),
    )

    def fc_fold_second(k):
        for copy in fc_first(k):
            copy.wait_recv()
        rows = ds(x * h1r + (1 - y) * q1r_rows, q1r_rows)
        g1w[k, rows, :] = g1w[k, rows, :] + r1a[k, ds((1 - y) * q1r_rows, q1r_rows), :]
        rows = ds(y * h2r + (1 - x) * q2r_rows, q2r_rows)
        g2w[k, rows, :] = g2w[k, rows, :] + r1b[k, ds((1 - x) * q2r_rows, q2r_rows), :]
        for copy in fc_second(k):
            copy.start()

    def fc_fold_third(k):
        for copy in fc_second(k):
            copy.wait_recv()
        total = g1w[k, ds(x * h1r + y * q1r_rows, q1r_rows), :].astype(F32)
        total = total + r1a[k, ds(y * q1r_rows, q1r_rows), :].astype(F32) + r2a[k].astype(F32)
        fz1[k] = total.astype(BF)
        total = g2w[k, ds(y * h2r + x * q2r_rows, q2r_rows), :].astype(F32)
        total = total + r1b[k, ds(x * q2r_rows, q2r_rows), :].astype(F32) + r2b[k].astype(F32)
        fz2[k] = total.astype(BF)

        if k == 1:
            for copy in fc_third:
                copy.start()

    def fc_finish():
        for copy in fc_third:
            copy.wait_recv()
        fz1[0] = fz1[0] + rz1[...]
        fz2[0] = fz2[0] + rz2[...]
        for copy in fc_keep:
            copy.start()
        for copy in fc_spread(0):
            copy.start()

    def fc_widen():
        for copy in fc_keep:
            copy.wait()
        for copy in fc_spread(0):
            copy.wait_recv()
        for copy in fc_spread(1):
            copy.start()

    def fc_to_sibling():
        for copy in fc_spread(1):
            copy.wait_recv()
        for copy in fc_share:
            copy.start()

    eighth = width // 8

    def order(j):
        odd = lax.rem(j, 2)
        first, second = r_x + (r_y - r_x) * odd, r_y + (r_x - r_y) * odd
        a1, a2 = x + (y - x) * odd, y + (x - y) * odd
        return first, second, a1, a2

    def chunk_place(j, start, count):
        rows = ds(start, count)
        return (
            (j < 2, go_out.at[pl.ds(3 * lax.min(j, 1), 3), rows, :]),
            (j >= 2, gq_out.at[:, rows, lanes(lax.max(j - 2, 0) * 128, 128)]),
        )

    def core_copy(j):
        return remote(gw.at[j, :, ds((1 - c) * half, half), :], q0.at[j], q0s.at[j], q0r.at[j], r_sib, z)

    def first_copy(j):
        first, _, a1, _ = order(j)
        src = gw.at[j, :, ds(c * half + (1 - a1) * 2 * eighth, 2 * eighth), :]
        return remote(src, q1.at[j], q1s.at[j], q1r.at[j], first, z)

    def second_copy(j):
        _, second, a1, a2 = order(j)
        src = gw.at[j, :, ds(c * half + a1 * 2 * eighth + (1 - a2) * eighth, eighth), :]
        return remote(src, q2.at[j], q2s.at[j], q2r.at[j], second, z)

    def z_copy(j, step):
        if step == 0:
            src = gw.at[j, :, ds(own_start(j), eighth), :]
            return remote(src, qz.at[j, 0], q3s.at[j, 0], q3r.at[j, 0], r, z_pair)
        return remote(q2.at[j], qz.at[j, 1], q3s.at[j, 1], q3r.at[j, 1], r, z_far)

    def own_start(j):
        _, _, a1, a2 = order(j)
        return c * half + a1 * 2 * eighth + a2 * eighth

    def keep_copy(j, ref):
        return pltpu.make_async_copy(qf.at[j], ref, qloc.at[j])

    def spread_copies(j, ref, level):
        first, second, _, _ = order(j)
        if level == 0:
            return remote(qf.at[j], ref, q5s.at[j], q5r.at[j], second, z)
        if level == 1:
            return remote(ref, ref, q6s.at[j], q6r.at[j], first, z)
        return remote(ref, ref, q7s.at[j], q7r.at[j], r_sib, z)

    def level_place(j, level):
        _, _, a1, _ = order(j)
        if level == 0:
            return chunk_place(j, own_start(j), eighth)
        if level == 1:
            return chunk_place(j, c * half + a1 * 2 * eighth, 2 * eighth)
        return chunk_place(j, c * half, half)

    def each_place(j, level, do):
        for condition, ref in level_place(j, level):

            @pl.when(condition)
            def _(ref=ref):
                do(ref)

    def fold_first(j):
        core_copy(j).wait_recv()
        _, _, a1, _ = order(j)
        rows = ds(c * half + (1 - a1) * 2 * eighth, 2 * eighth)
        gw[j, :, rows, :] = gw[j, :, rows, :] + q0[j, :, ds((1 - a1) * 2 * eighth, 2 * eighth), :]
        first_copy(j).start()

    def fold_second(j):
        first_copy(j).wait_recv()
        _, _, a1, a2 = order(j)
        inner = (1 - a2) * eighth
        rows = ds(c * half + a1 * 2 * eighth + inner, eighth)
        total = gw[j, :, rows, :].astype(F32) + q0[j, :, ds(a1 * 2 * eighth + inner, eighth), :].astype(F32)
        gw[j, :, rows, :] = (total + q1[j, :, ds(inner, eighth), :].astype(F32)).astype(BF)
        second_copy(j).start()

    def fold_z(j):
        second_copy(j).wait_recv()
        _, _, a1, a2 = order(j)
        inner = a2 * eighth
        rows = ds(c * half + a1 * 2 * eighth + inner, eighth)
        total = gw[j, :, rows, :].astype(F32) + q0[j, :, ds(a1 * 2 * eighth + inner, eighth), :].astype(F32)
        total = total + q1[j, :, ds(inner, eighth), :].astype(F32) + q2[j].astype(F32)
        gw[j, :, rows, :] = total.astype(BF)
        z_copy(j, 0).start()

    def fold_pair(j):
        z_copy(j, 0).wait_recv()
        q2[j] = gw[j, :, ds(own_start(j), eighth), :] + qz[j, 0]
        z_copy(j, 1).start()

    def fold_all(j):
        z_copy(j, 1).wait_recv()
        qf[j] = q2[j] + qz[j, 1]

        def go(ref):
            keep_copy(j, ref).start()
            spread_copies(j, ref, 0).start()

        each_place(j, 0, go)

    def spread_first(j):
        def done(ref):
            keep_copy(j, ref).wait()
            spread_copies(j, ref, 0).wait_recv()

        each_place(j, 0, done)
        each_place(j, 1, lambda ref: spread_copies(j, ref, 1).start())

    def spread_sibling(j):
        each_place(j, 1, lambda ref: spread_copies(j, ref, 1).wait_recv())
        each_place(j, 2, lambda ref: spread_copies(j, ref, 2).start())

    def chunk_done(j):
        each_place(j, 2, lambda ref: spread_copies(j, ref, 2).wait())
        each_place(j, 1, lambda ref: spread_copies(j, ref, 1).wait_send())
        each_place(j, 0, lambda ref: spread_copies(j, ref, 0).wait_send())
        core_copy(j).wait_send()
        first_copy(j).wait_send()
        second_copy(j).wait_send()
        for step in range(2):
            z_copy(j, step).wait_send()

    def small_copy(level):
        row = (r_sib, r_x, r_y)[level]
        return remote(sma.at[level], smr.at[level], sms.at[level], smrs.at[level], row, z)

    def small_z(step):
        src, dst = smz.at[2 * step], smz.at[2 * step + 1]
        return remote(src, dst, smzs.at[step], smzr.at[step], r, (z_pair, z_far)[step])

    barrier = pltpu.get_barrier_semaphore()
    partners = ((r_sib, z), (r_x, z), (r_y, z), (r_diag, z), (r, z_pair), (r, z_far))
    for row, column in partners:
        pl.semaphore_signal(barrier, inc=1, device_id={"rows": row, "mlp": column}, device_id_type=MESH)
    load_c.start()
    load_x.start()
    load_qkv.start()
    load_out.start()
    own_shard(0).start()
    own_shard(1).start()
    pl.semaphore_wait(barrier, len(partners))
    gather_copy(0, 0).start()
    gather_copy(1, 0).start()
    load_c.wait()
    for i in range(images):
        work[...] = jnp.zeros_like(work)
        work[0:patches, :] = c_ref[:, i, :]
        cot[i * tall : (i + 1) * tall, :] = work[...]
    cot_copy(0).start()
    cot_copy(1).start()
    load_x.wait()
    for i in range(images):
        forward_rows(i, x_ref, rank_ref, kept_ref, g1_ref, rw_ref, xp, keep, gate, h1, work)

    load_qkv.wait()

    @pl.loop(0, 3 * width // 256)
    def _(j):
        forward_qkv(j, h1, wqkv, qkv)

    @pl.loop(0, HEADS // 2)
    def _(p):
        for i in range(images):
            attend(p, i, width, tall, qkv, keep, probs, context, contextt)

        @pl.when(p == 2)
        def _():
            gather_forward(0)

        @pl.when(p == 5)
        def _():
            gather_forward(1)

    load_out.wait()

    @pl.loop(0, images)
    def _(i):
        forward_out(i, tall, context, wout, xp, keep, gate, g2_ref, attended, middle, tok)
        token_copy(i, 0).start()
        token_copy(i, 1).start()

    own_shard(0).wait()
    own_shard(1).wait()

    def at(block, number, do):
        @pl.when(block == number)
        def _():
            do()

    def before_sibling():
        for i in range(images):
            token_copy(i, 0).wait_recv()
        cot_copy(0).wait_recv()

    @pl.loop(0, 2 * images)
    def _(block):
        at(block, images, before_sibling)
        rows = ds(block * tall, tall)
        hid[rows, 0:part], gpre[rows, 0:part] = mlp_rows(tok[rows, :], cot[rows, :], w1[:, 0:part], w2[0:part, :])

    cot_copy(1).wait_recv()
    cot_copy(2).start()
    for mat in range(2):
        for kind in (1, 2, 3):
            gather_copy(mat, kind).wait_recv()
    for ref in (dg1, dg2, drw):
        ref[...] = jnp.zeros_like(ref)

    def before_near():
        cot_copy(2).wait_recv()
        gh2_to_sib.start()
        out_to_sib.start()

    def forward_token(i):
        token_copy(i, 1).wait_recv()
        token_copy(i, 2).start()

    def send_far(i):
        gh2_over(i).wait_recv()
        rows = ds(t_own + i * tall, tall)
        gh2_part[rows, :] = gh2_part[rows, :] + gh2_near[ds(i * tall, tall), :]
        gh2_far_copy(i).start()

    def before_last():
        send_far(0)
        token_copy(1, 2).wait_recv()

    @pl.loop(0, 8)
    def _(block):
        at(block, 3, lambda: forward_token(0))
        at(block, 4, before_near)
        at(block, 5, lambda: token_copy(0, 2).wait_recv())
        at(block, 6, lambda: forward_token(1))
        at(block, 7, before_last)
        inner = lax.rem(block, 5)
        swap = lax.div(block, 5) * (1 - 2 * inner + 3 * lax.div(inner * (inner - 1), 2))
        spot = block + swap
        rows = ds(spot * tall, tall)

        @pl.when(block < 2 * images)
        def _():
            hid[rows, part:], gpre[rows, part:] = mlp_rows(tok[rows, :], cot[rows, :], w1[:, part:], w2[part:, :])

        @pl.when(block >= 2 * images)
        def _():
            hid[rows, :], gpre[rows, :] = mlp_rows(tok[rows, :], cot[rows, :], w1[...], w2[...])

        share_out = dot_nn(hid[rows, :], w2[...])
        share_gh2 = dot_nt(gpre[rows, :], w1[...])

        @pl.when(block < images)
        def _():
            out[rows, :] = share_out
            gh2[rows, :] = share_gh2

        @pl.when(block >= images)
        def _():
            there = ds(lax.max(spot - images, 0) * tall, tall)
            out_part[there, :] = share_out.astype(BF)
            gh2_part[there, :] = share_gh2.astype(BF)

        at(block, 5, lambda: gh2_over(0).start())
        at(block, 7, lambda: gh2_over(1).start())

    out_over.start()
    turned[...] = tok[...].T
    for m in range(3):
        rows = slice(m * width // 3, (m + 1) * width // 3)
        total = dot_nn(turned[rows, :], gpre[...]).astype(BF)
        g1w[0, rows, :] = total[:, 0:part]
        g1w[1, rows, :] = total[:, part:]
    send_far(1)
    turned[...] = hid[...].T
    for m in range(2):
        g2w[m] = dot_nn(turned[m * part : (m + 1) * part, :], cot[...]).astype(BF)
    for k in range(2):
        for copy in fc_first(k):
            copy.start()

    @pl.loop(4, LAST)
    def _(t):
        def back_image(i):
            gh2_far_copy(i).wait_recv()
            rows = pl.ds(i * tall, tall)
            gh2[rows, :] += gh2_sib[rows, :].astype(F32) + gh2_far[rows, :].astype(F32)
            back_rows(i, tall, cot, gh2, middle, keep, gate, attended, g2_ref, gh2, tok, glogit, dg2)
            context[rows, :] = dot_nt(tok[rows, :], wout[...]).astype(BF)

        @pl.when(t == 4)
        def _():
            gh2_to_sib.wait_recv()
            for i in range(images):
                token_copy(i, 0).wait_send()
                token_copy(i, 1).wait_send()
            back_image(0)
            turned[:, 0:t_own] = h1[...].T

        at(t, FIRST, lambda: back_image(1))

        @pl.when(jnp.logical_and(t >= FIRST, t < FIRST + 2))
        def _():
            cols = lanes((t - FIRST) * half, half)
            total = 0.0
            for i in range(images):
                total = total + dot_nn(contextt[i], tok[i * tall : (i + 1) * tall, cols])
            for b in range(3):
                gw[t - FIRST, b] = total[:, b * 128 : (b + 1) * 128].astype(BF)

        late = lax.div(t, FIRST)

        @pl.when(
            jnp.logical_or(
                jnp.logical_and(t >= 5, t < FIRST),
                jnp.logical_and(jnp.logical_and(t >= FIRST + 2, t < FIRST + CHUNKS), lax.rem(t, 2) == 0),
            )
        )
        def _():
            p = 2 * (t - 5) + late * (2 * 5 - FIRST - 2 - t)
            for n in range(2):
                attend_back(p + n, late, width, tall, qkv, probs, context)

        @pl.when(jnp.logical_and(t >= FIRST + 2, t < FIRST + CHUNKS))
        def _():
            total = dot_nn(turned[:, 0:t_own], pair_columns(qkv, t - FIRST - 2, width))
            for b in range(3):
                gw[t - FIRST, b] = total[:, b * 128 : (b + 1) * 128].astype(BF)

        @pl.when(jnp.logical_and(t >= FIRST, t < FIRST + CHUNKS))
        def _():
            core_copy(t - FIRST).start()

        @pl.when(t == 5)
        def _():
            out_over.wait_recv()
            rows = pl.ds(t_own, t_own)
            out_part[rows, :] = out_part[rows, :] + out_near[...]
            out_far_copy.start()

        @pl.when(t == FIRST + CHUNKS)
        def _():
            for i in range(images):
                rows = pl.ds(i * tall, tall)
                dy = dot_nt(qkv[rows, :], wqkv[...])
                back_input(i, tall, dy, glogit, rw_ref, xp, h1, g1_ref, gh2, x_ref, dg1, drw)
            store_gx.start()
            sma[0] = jnp.concatenate([dg1[...], drw[...], dg2[...], jnp.zeros((5, width), F32)], 0)
            small_copy(0).start()

        for level in range(2):

            @pl.when(t == 18 + 2 * level)
            def _(level=level):
                small_copy(level).wait()
                sma[level + 1] = sma[level] + smr[level]
                small_copy(level + 1).start()

        @pl.when(t == 22)
        def _():
            small_copy(2).wait()
            smz[0] = sma[2] + smr[2]
            small_z(0).start()

        @pl.when(t == 24)
        def _():
            small_z(0).wait()
            smz[2] = smz[0] + smz[1]
            small_z(1).start()
            out_to_sib.wait_recv()
            out_far_copy.wait_recv()
            for i in range(images):
                rows = pl.ds(i * tall, tall)
                total = middle[rows, :] + out[rows, :] + out_sib[rows, :].astype(F32) + out_far[rows, :].astype(F32)
                c_ref[:, i, :] = total.astype(BF)[0:patches, :]
            store_block.start()

        def lagged(lag, do):
            @pl.when(jnp.logical_and(t >= FIRST + lag, t < FIRST + lag + CHUNKS))
            def _():
                do(t - FIRST - lag)

        steps = (
            (7, lambda: fc_fold_second(0)), (9, lambda: fc_fold_second(1)), (12, lambda: fc_fold_third(1)),
            (20, lambda: fc_fold_third(0)), (20, fc_finish), (23, fc_widen), (26, fc_to_sibling),
        )
        for tick, do in steps:
            at(t, tick, do)

        stages = (fold_first, fold_second, fold_z, fold_pair, fold_all, spread_first, spread_sibling)
        for stage in (5, 6, 7, 4, 3, 2, 1):
            lagged(LAGS[stage], stages[stage - 1])

    small_z(1).wait()
    small_out[...] = smz[2] + smz[3]

    @pl.loop(0, CHUNKS)
    def _(j):
        chunk_done(j)

    store_gx.wait()
    store_block.wait()
    for copy in fc_share:
        copy.wait()
    for level in range(2):
        for copy in fc_spread(level):
            copy.wait_send()
    for copy in fc_third:
        copy.wait_send()
    for mat in range(2):
        for kind in range(4):
            gather_copy(mat, kind).wait_send()
    for i in range(images):
        token_copy(i, 2).wait_send()
        gh2_over(i).wait_send()
        gh2_far_copy(i).wait_send()
    for hop in range(3):
        cot_copy(hop).wait_send()
    for copy in (gh2_to_sib, out_to_sib, out_over, out_far_copy):
        copy.wait_send()
    for k in range(2):
        for copy in fc_first(k) + fc_second(k):
            copy.wait_send()


VMEM = pl.BlockSpec(memory_space=pltpu.VMEM)
SMEM = pl.BlockSpec(memory_space=pltpu.SMEM)
ANY = pl.BlockSpec(memory_space=pl.ANY)


def widen_kernel(block, gx, gq, go, f1, f2, small, block_out, gx_out, gq_out, go_out, f1_out, f2_out, g1_out, rw_out, g2_out, sem):
    width = f1.shape[1]
    step = pl.program_id(0)
    copies = [pltpu.make_async_copy(block, block_out, sem.at[0]), pltpu.make_async_copy(gx, gx_out, sem.at[1])]

    @pl.when(step == 0)
    def _():
        for copy in copies:
            copy.start()

    @pl.when(step == pl.num_programs(0) - 1)
    def _():
        for copy in copies:
            copy.wait()

    for b in range(3):
        gq_out[:, b * width : (b + 1) * width] = gq[b].astype(F32)
    for b in range(go.shape[0]):
        go_out[:, b * 128 : (b + 1) * 128] = go[b].astype(F32)
    f1_out[...] = f1[...].astype(F32)
    f2_out[...] = f2[...].astype(F32)
    g1_out[...], rw_out[...], g2_out[...] = small[0], small[1], small[2]


def widen(block, gx, gq, go, f1, f2, small):
    width = f1.shape[0]
    step = 128
    tokens = jax.ShapeDtypeStruct(block.shape, BF)

    def rows(*tail):
        return pl.BlockSpec((step,) + tail, lambda i: (i, 0))

    def inner(lead, tail):
        return pl.BlockSpec((lead, step, tail), lambda i: (0, i, 0))

    return pl.pallas_call(
        widen_kernel,
        grid=(width // step,),
        out_shape=[tokens, tokens] + [jax.ShapeDtypeStruct((width, n), F32) for n in (3 * width, width, width, width)]
        + [jax.ShapeDtypeStruct((width,), F32)] * 3,
        in_specs=[ANY, ANY, inner(3, width), inner(6, 128), rows(width), rows(width), pl.BlockSpec((8, width), lambda i: (0, 0))],
        out_specs=[ANY, ANY, rows(3 * width), rows(width), rows(width), rows(width)] + [pl.BlockSpec((width,), lambda i: (0,))] * 3,
        scratch_shapes=[pltpu.SemaphoreType.DMA((2,))],
        compiler_params=pltpu.CompilerParams(vmem_limit_bytes=63 * 1024 * 1024),
        name="widen",
    )(block, gx, gq, go, f1, f2, small)


def per_device(others, images, patch_rank, kept_count, ln1_gain, router_weight, w_qkv, w_out, ln2_gain, w_fc1, w_fc2, cotangent):
    count, patches, width = images.shape
    tall = -(-patches // 16) * 16
    t = count * tall
    part = w_fc1.shape[1] // 2
    half, eighth = width // 2, width // 8

    def bf(*dims):
        return pltpu.VMEM(dims, BF)

    def f32(*dims):
        return pltpu.VMEM(dims, F32)

    def sem(*dims):
        return pltpu.SemaphoreType.DMA(dims)

    scratch = [
        bf(patches, count, width), bf(patches, count, width),
        bf(width, 3 * width), bf(width, width), bf(width, 2 * part), bf(2 * part, width),
        bf(t, width), f32(t, 128), f32(t, 128), f32(t, 128), bf(t, width), bf(t, 3 * width),
        f32(count, HEADS, tall, tall), bf(count, width, tall), bf(t, width), f32(t, width), f32(t, width),
        bf(4 * t, width), bf(4 * t, width), bf(width, 4 * t), f32(t, width), f32(t, width),
        bf(3 * t, width), bf(3 * t, width), bf(t, width), bf(t, width), bf(t, width), bf(t, width), bf(t, width), bf(t, width),
        bf(4 * t, 2 * part), bf(4 * t, 2 * part), bf(tall, width),
        bf(2, width, part), bf(2, part, width),
        bf(2, width // 2, part), bf(2, part // 2, width), bf(2, width // 4, part), bf(2, part // 4, width),
        bf(2, width // 4, part), bf(2, part // 4, width), bf(width // 4, part), bf(part // 4, width),
        bf(CHUNKS, 3, width, 128), bf(CHUNKS, 3, half, 128), bf(CHUNKS, 3, 2 * eighth, 128), bf(CHUNKS, 3, eighth, 128),
        bf(CHUNKS, 2, 3, eighth, 128), bf(CHUNKS, 3, eighth, 128),
        f32(1, width), f32(1, width), f32(1, width), f32(3, 8, width), f32(3, 8, width), f32(4, 8, width),
        sem(8), sem(2, 4), sem(2, 4), sem(count, 3), sem(count, 3), sem(3), sem(3), sem(8), sem(8),
        sem(2, 2), sem(2, 2), sem(2, 2), sem(2, 2), sem(2), sem(2),
        sem(2, 2), sem(2, 2), sem(2), sem(2), sem(2),
        sem(CHUNKS), sem(CHUNKS), sem(CHUNKS), sem(CHUNKS), sem(CHUNKS), sem(CHUNKS),
        sem(CHUNKS, 2), sem(CHUNKS, 2), sem(CHUNKS),
        sem(CHUNKS), sem(CHUNKS), sem(CHUNKS), sem(CHUNKS), sem(CHUNKS), sem(CHUNKS),
        sem(3), sem(3), sem(2), sem(2),
    ]

    def struct(*dims, dtype=BF):
        return jax.ShapeDtypeStruct(dims, dtype)

    block, gx, gq, go, f1, f2, small = pl.pallas_call(
        mega_kernel,
        out_shape=[
            struct(patches, count, width), struct(patches, count, width), struct(3, width, width), struct(6, width, 128),
            struct(width, 2 * part), struct(2 * part, width), struct(8, width, dtype=F32),
        ],
        in_specs=[ANY, VMEM, SMEM, VMEM, VMEM, ANY, ANY, VMEM, ANY, ANY, ANY],
        out_specs=[ANY, ANY, ANY, ANY, ANY, ANY, VMEM],
        scratch_shapes=scratch,
        compiler_params=pltpu.CompilerParams(
            collective_id=0, has_side_effects=True, vmem_limit_bytes=64 * 1024 * 1024
        ),
        name="block",
    )(images.transpose(1, 0, 2), patch_rank, kept_count, ln1_gain, router_weight, w_qkv, w_out, ln2_gain, w_fc1, w_fc2,
      cotangent.transpose(1, 0, 2))
    block, gx, gq, go, f1, f2, g1, rw, g2 = widen(block, gx, gq, go, f1, f2, small)
    if others:
        gq, go, f1, f2, g1, rw, g2 = lax.psum((gq, go, f1, f2, g1, rw, g2), "rows", axis_index_groups=others)
    return block.transpose(1, 0, 2), gx.transpose(1, 0, 2), g1, rw, gq, go, g2, f1, f2


def solution(mesh):
    rows = mesh.shape["rows"]
    others = [[8 * g + i for g in range(rows // 8)] for i in range(8)] if rows > 8 else None
    return jax.shard_map(
        functools.partial(per_device, others),
        mesh=mesh,
        in_specs=(
            P(("rows", "mlp"), None, None), P(("rows", "mlp"), None), P(("rows", "mlp")), P(), P(), P(), P(), P(),
            P(None, "mlp"), P("mlp", None), P(("rows", "mlp"), None, None),
        ),
        out_specs=(
            P(("rows", "mlp"), None, None), P(("rows", "mlp"), None, None), P(), P(), P(), P(), P(),
            P(None, "mlp"), P("mlp", None),
        ),
        check_vma=False,
    )
```

```python
import functools
import jax
import jax.numpy as jnp
from jax import lax
from jax.experimental import pallas as pl
from jax.experimental.pallas import tpu as pltpu
from jax.sharding import PartitionSpec as P

HEADS = 12
EPS = 1e-6
FILL = -1e30
BF = jnp.bfloat16
F32 = jnp.float32


def dot_nn(a, b):
    return lax.dot_general(a, b, (((1,), (0,)), ((), ())), preferred_element_type=F32)


def dot_nt(a, b):
    return lax.dot_general(a, b, (((1,), (1,)), ((), ())), preferred_element_type=F32)


def dot_tn(a, b):
    return lax.dot_general(a, b, (((0,), (0,)), ((), ())), preferred_element_type=F32)


def unit_rows(v):
    center = v - jnp.mean(v, -1, keepdims=True)
    scale = lax.rsqrt(jnp.mean(center * center, -1, keepdims=True) + EPS)
    return center * scale, scale


def norm_pull(dy, gain, unit, scale):
    du = dy * gain
    return scale * (
        du
        - jnp.mean(du, -1, keepdims=True)
        - unit * jnp.mean(du * unit, -1, keepdims=True)
    )


def half_mask(rows, h):
    lane = lax.broadcasted_iota(jnp.int32, (rows, 128), 1)
    return (lane < 64) if h == 0 else (lane >= 64)


def forward_rows(i, x_ref, rank_ref, kept_ref, g1_ref, rw_ref, xp, keep, gate, h1, work):
    patches = x_ref.shape[0]
    tall = xp.shape[0] // x_ref.shape[1]
    rows = pl.ds(pl.multiple_of(i * tall, 16), tall)
    work[...] = jnp.zeros_like(work)
    work[0:patches, :] = x_ref[:, i, :]
    v = work[...]
    xp[rows, :] = v
    kept = (rank_ref[pl.ds(i, 1), :] < kept_ref[i]).astype(F32)
    keep_row = jnp.concatenate([kept, jnp.zeros((1, 256 - patches), F32)], 1)
    keep_col = jnp.broadcast_to(keep_row, (128, 256)).T
    keep[rows, :] = keep_col[0:tall, :]
    unit, _ = unit_rows(v.astype(F32))
    low = (unit * g1_ref[...][None]).astype(BF)
    h1[rows, :] = low
    logit = jnp.sum(low.astype(F32) * rw_ref[...][None].astype(F32), -1, keepdims=True)
    gate[rows, :] = jnp.broadcast_to(jax.nn.sigmoid(logit), (tall, 128))


def forward_qkv(j, h1, wqkv, qkv):
    cols = pl.ds(pl.multiple_of(j * 256, 256), 256)
    qkv[:, cols] = dot_nn(h1[...], wqkv[:, cols]).astype(BF)


def attend(p, i, width, tall, qkv, keep, probs, context, contextt):
    rows = pl.ds(pl.multiple_of(i * tall, 16), tall)
    qc = pl.ds(pl.multiple_of(p * 128, 128), 128)
    kc = pl.ds(pl.multiple_of(width + p * 128, 128), 128)
    vc = pl.ds(pl.multiple_of(2 * width + p * 128, 128), 128)
    q, k, v = qkv[rows, qc], qkv[rows, kc], qkv[rows, vc]
    vt = v.T
    kept = keep[rows, 0:1] > 0.5
    outs = []
    for h in range(2):
        kh = jnp.where(half_mask(tall, h), k, jnp.zeros_like(k))
        s = jnp.where(kept, dot_nt(kh, q) * 0.125, FILL)
        e = jnp.exp(s - jnp.max(s, 0, keepdims=True))
        pr = e * (1.0 / jnp.sum(e, 0, keepdims=True))
        probs[i, p * 2 + h] = pr
        outs.append(dot_nn(vt[h * 64 : h * 64 + 64, :], pr.astype(BF)))
    ct = jnp.concatenate(outs, 0)
    contextt[i, pl.ds(pl.multiple_of(p * 128, 128), 128), :] = ct.astype(BF)
    context[rows, qc] = ct.T.astype(BF)


def forward_out(i, tall, context, wout, xp, keep, gate, g2_ref, attended, middle, h2):
    rows = pl.ds(pl.multiple_of(i * tall, 16), tall)
    att = dot_nn(context[rows, :], wout[...])
    attended[rows, :] = att
    mid = xp[rows, :].astype(F32) + keep[rows, 0:1] * gate[rows, 0:1] * att
    middle[rows, :] = mid
    unit, _ = unit_rows(mid)
    h2[rows, :] = (unit * g2_ref[...][None]).astype(BF)


def gelu_pair(pre):
    cdf = 0.5 * (1.0 + lax.erf(pre * 0.7071067811865476))
    pdf = jnp.exp(pre * pre * -0.5) * 0.3989422804014327
    return pre * cdf, cdf + pre * pdf


def mlp_rows(h, c, w1, w2):
    pre = dot_nn(h, w1)
    hidden, slope = gelu_pair(pre)
    grad = dot_nt(c, w2) * slope
    return hidden.astype(BF), grad.astype(BF)


def back_rows(i, tall, c_ref, gh2, middle, keep, gate, attended, g2_ref, gmid, gatt, glogit, dg2):
    rows = pl.ds(pl.multiple_of(i * tall, 16), tall)
    dy = gh2[rows, :]
    unit, scale = unit_rows(middle[rows, :])
    gm = c_ref[rows, :].astype(F32) + norm_pull(dy, g2_ref[...][None], unit, scale)
    gmid[rows, :] = gm
    dg2[...] += jnp.sum(dy * unit, 0, keepdims=True)
    k, g = keep[rows, 0:1], gate[rows, 0:1]
    kept = gm * k
    gatt[rows, :] = (kept * g).astype(BF)
    gl = jnp.sum(kept * attended[rows, :], -1, keepdims=True) * g * (1.0 - g)
    glogit[rows, :] = jnp.broadcast_to(gl, (tall, 128))


def attend_back(p, i, width, tall, qkv, probs, gctx):
    rows = pl.ds(pl.multiple_of(i * tall, 16), tall)
    qc = pl.ds(pl.multiple_of(p * 128, 128), 128)
    kc = pl.ds(pl.multiple_of(width + p * 128, 128), 128)
    vc = pl.ds(pl.multiple_of(2 * width + p * 128, 128), 128)
    q, k, v = qkv[rows, qc], qkv[rows, kc], qkv[rows, vc]
    gc = gctx[rows, qc]
    kt = k.T
    gv, gk, gq = 0.0, 0.0, []
    for h in range(2):
        mask = half_mask(tall, h)
        zero = jnp.zeros_like(v)
        pr = probs[i, p * 2 + h]
        gp = dot_nt(jnp.where(mask, v, zero), gc)
        gs = (pr * (gp - jnp.sum(pr * gp, 0, keepdims=True))).astype(BF)
        gv = gv + dot_nn(pr.astype(BF), jnp.where(mask, gc, zero))
        gk = gk + dot_nn(gs, jnp.where(mask, q, zero))
        gq.append(dot_nn(kt[h * 64 : h * 64 + 64, :], gs))
    qkv[rows, qc] = (jnp.concatenate(gq, 0).T * 0.125).astype(BF)
    qkv[rows, kc] = (gk * 0.125).astype(BF)
    qkv[rows, vc] = gv.astype(BF)


def pair_columns(wqkv, p, width):
    return jnp.concatenate(
        [wqkv[:, pl.ds(pl.multiple_of(b * width + p * 128, 128), 128)] for b in range(3)], 1
    )


def back_input(i, tall, dy, glogit, rw_ref, xp, h1, g1_ref, gmid, gx_ref, dg1, drw):
    rows = pl.ds(pl.multiple_of(i * tall, 16), tall)
    patches = gx_ref.shape[0]
    gl = glogit[rows, 0:1]
    dy = dy + gl * rw_ref[...][None].astype(F32)
    unit, scale = unit_rows(xp[rows, :].astype(F32))
    dg1[...] += jnp.sum(dy * unit, 0, keepdims=True)
    drw[...] += jnp.sum(h1[rows, :].astype(F32) * gl, 0, keepdims=True)
    out = gmid[rows, :] + norm_pull(dy, g1_ref[...][None], unit, scale)
    gx_ref[:, i, :] = out.astype(BF)[0:patches, :]

MESH = pl.DeviceIdType.MESH
CHUNKS = HEADS // 2 + 2
LAGS = (0, 2, 6, 9, 11, 13, 16, 22, 26)
FIRST = 8
LAST = FIRST + CHUNKS + LAGS[8]


def mega_kernel(
    x_hbm, rank_ref, kept_ref, g1_ref, rw_ref, wqkv_hbm, wout_hbm, g2_ref, fc1, fc2, c_hbm,
    block_hbm, gx_hbm, gq_out, go_out, f1_out, f2_out, small_out,
    x_ref, c_ref, wqkv, wout, w1, w2, xp, keep, gate, glogit, h1, qkv, probs, contextt, context, attended, middle,
    tok, cot, turned, out, gh2, out_part, gh2_part, out_sib, gh2_sib, out_near, gh2_near, out_far, gh2_far, hid, gpre, work,
    g1w, g2w, r1a, r1b, r2a, r2b, fz1, fz2, rz1, rz2,
    gw, q0, q1, q2, qz, dg1, dg2, drw, sma, smr, smz,
    lsem, gsend, grecv, hsend, hrecv, csend, crecv, esend, erecv, s1s, s1r, s2s, s2r, s3s, s3r, fs, fr, floc, ssib, rsib, free, chunk_free,
    q0s, q0r, q1s, q1r, q2s, q2r, q3s, q3r, qloc, q5s, q5r, q6s, q6r, q7s, q7r, sms, smrs, smzs, smzr,
):
    patches, images, width = x_ref.shape
    t_own = xp.shape[0]
    tall = t_own // images
    half = width // 2
    part = w1.shape[1] // 2
    quarter = (width // 4, part // 4)
    r = lax.axis_index("rows")
    z = lax.axis_index("mlp")
    c, x, y = lax.rem(r, 2), lax.rem(lax.div(r, 2), 2), lax.rem(lax.div(r, 4), 2)
    r_sib, r_x, r_y = r + 1 - 2 * c, r + 2 - 4 * x, r + 4 - 8 * y
    r_diag = r_x + r_y - r
    z_pair, z_far = z + 1 - 2 * lax.rem(z, 2), z + 2 - 4 * lax.div(z, 2)
    q = 2 * y + x

    def ds(start, size):
        return pl.ds(pl.multiple_of(start, 16), size)

    def lanes(start, size):
        return pl.ds(pl.multiple_of(start, 128), size)

    def remote(src, dst, send, recv, row, column):
        return pltpu.make_async_remote_copy(
            src_ref=src, dst_ref=dst, send_sem=send, recv_sem=recv,
            device_id={"rows": row, "mlp": column}, device_id_type=MESH,
        )

    def release(semaphore, row):
        pl.semaphore_signal(semaphore, inc=1, device_id={"rows": row, "mlp": z}, device_id_type=MESH)

    def gather_copy(mat, kind):
        size = quarter[mat]
        sems = gsend.at[mat, kind], grecv.at[mat, kind]
        if mat == 0:
            place = w1.at[ds(q * size, size), pl.ds(part, part)]
            own = fc1.at[ds(q * size, size), lanes(c * part, part)]
        else:
            place = w2.at[ds(part + q * size, size), :]
            own = fc2.at[ds(c * part + q * size, size), :]
        if kind == 0:
            return remote(own, place, *sems, r, z_far)
        return remote(place, place, *sems, (r_x, r_y, r_diag)[kind - 1], z)

    def gather_forward(mat):
        gather_copy(mat, 0).wait_recv()
        for kind in (1, 2, 3):
            gather_copy(mat, kind).start()

    def own_shard(mat):
        if mat == 0:
            return pltpu.make_async_copy(fc1.at[:, lanes(c * part, part)], w1.at[:, pl.ds(0, part)], lsem.at[0])
        return pltpu.make_async_copy(fc2.at[ds(c * part, part), :], w2.at[pl.ds(0, part), :], lsem.at[1])

    load_qkv = pltpu.make_async_copy(wqkv_hbm, wqkv, lsem.at[2])
    load_out = pltpu.make_async_copy(wout_hbm, wout, lsem.at[3])
    load_x = pltpu.make_async_copy(x_hbm, x_ref, lsem.at[4])
    load_c = pltpu.make_async_copy(c_hbm, c_ref, lsem.at[5])
    store_block = pltpu.make_async_copy(c_ref, block_hbm, lsem.at[6])
    store_gx = pltpu.make_async_copy(x_ref, gx_hbm, lsem.at[7])

    def token_copy(i, hop):
        start = (0, 0, 2 * t_own)[hop] + i * tall
        src, dst = tok.at[ds(start, tall), :], tok.at[ds((1, 2, 3)[hop] * t_own + i * tall, tall), :]
        row, column = (r, z_pair) if hop == 1 else (r_sib, z)
        return remote(src, dst, hsend.at[i, hop], hrecv.at[i, hop], row, column)

    def cot_copy(hop):
        src, dst = cot.at[ds((0, 0, 2)[hop] * t_own, t_own), :], cot.at[ds((1, 2, 3)[hop] * t_own, t_own), :]
        row, column = (r, z_pair) if hop == 1 else (r_sib, z)
        return remote(src, dst, csend.at[hop], crecv.at[hop], row, column)

    gh2_to_sib = remote(gh2_part.at[ds(0, t_own), :], gh2_sib, esend.at[0], erecv.at[0], r_sib, z)
    out_to_sib = remote(out_part.at[ds(0, t_own), :], out_sib, esend.at[1], erecv.at[1], r_sib, z)
    out_over = remote(out_part.at[ds(2 * t_own, t_own), :], out_near, esend.at[2], erecv.at[2], r_sib, z)
    out_far_copy = remote(out_part.at[ds(t_own, t_own), :], out_far, esend.at[3], erecv.at[3], r, z_pair)

    def gh2_over(i):
        src = gh2_part.at[ds(2 * t_own + i * tall, tall), :]
        return remote(src, gh2_near.at[ds(i * tall, tall), :], esend.at[4 + i], erecv.at[4 + i], r_sib, z)

    def gh2_far_copy(i):
        src = gh2_part.at[ds(t_own + i * tall, tall), :]
        return remote(src, gh2_far.at[ds(i * tall, tall), :], esend.at[6 + i], erecv.at[6 + i], r, z_pair)

    h1r, q1r_rows = width // 2, width // 4
    h2r, q2r_rows = part // 2, part // 4

    def fc_first(k):
        return (
            remote(g1w.at[k, ds((1 - x) * h1r, h1r), :], r1a.at[k], s1s.at[k, 0], s1r.at[k, 0], r_x, z),
            remote(g2w.at[k, ds((1 - y) * h2r, h2r), :], r1b.at[k], s1s.at[k, 1], s1r.at[k, 1], r_y, z),
        )

    def fc_second(k):
        return (
            remote(
                g1w.at[k, ds(x * h1r + (1 - y) * q1r_rows, q1r_rows), :], r2a.at[k], s2s.at[k, 0], s2r.at[k, 0], r_y, z
            ),
            remote(
                g2w.at[k, ds(y * h2r + (1 - x) * q2r_rows, q2r_rows), :], r2b.at[k], s2s.at[k, 1], s2r.at[k, 1], r_x, z
            ),
        )

    fc_third = (
        remote(fz1.at[1], rz1, s3s.at[0], s3r.at[0], r, z_far),
        remote(fz2.at[1], rz2, s3s.at[1], s3r.at[1], r, z_far),
    )

    f1_rows = (ds(x * h1r + y * q1r_rows, q1r_rows), ds(x * h1r, h1r))
    f2_rows = (ds(y * h2r + x * q2r_rows, q2r_rows), ds(y * h2r, h2r))

    def fc_spread(level):
        part1, part2 = g1w.at[0, f1_rows[level], :], g2w.at[0, f2_rows[level], :]
        row1, row2 = ((r_y, r_x), (r_x, r_y))[level]
        return (
            remote(part1, part1, fs.at[level, 0], fr.at[level, 0], row1, z),
            remote(part2, part2, fs.at[level, 1], fr.at[level, 1], row2, z),
        )

    fc_share = (
        remote(g1w.at[0], g1w.at[1], ssib.at[0], rsib.at[0], r_sib, z),
        remote(g2w.at[0], g2w.at[1], ssib.at[1], rsib.at[1], r_sib, z),
    )

    def fc_store(k):
        core = c + k - 2 * c * k
        return (
            pltpu.make_async_copy(g1w.at[k], f1_out.at[:, lanes(core * part, part)], floc.at[k, 0]),
            pltpu.make_async_copy(g2w.at[k], f2_out.at[ds(core * part, part), :], floc.at[k, 1]),
        )

    def fc_fold_second(k):
        for copy in fc_first(k):
            copy.wait_recv()
        rows = ds(x * h1r + (1 - y) * q1r_rows, q1r_rows)
        g1w[k, rows, :] = g1w[k, rows, :] + r1a[k, ds((1 - y) * q1r_rows, q1r_rows), :]
        rows = ds(y * h2r + (1 - x) * q2r_rows, q2r_rows)
        g2w[k, rows, :] = g2w[k, rows, :] + r1b[k, ds((1 - x) * q2r_rows, q2r_rows), :]
        for copy in fc_second(k):
            copy.start()

    def fc_fold_third(k):
        for copy in fc_second(k):
            copy.wait_recv()
        total = g1w[k, ds(x * h1r + y * q1r_rows, q1r_rows), :].astype(F32)
        total = total + r1a[k, ds(y * q1r_rows, q1r_rows), :].astype(F32) + r2a[k].astype(F32)
        fz1[k] = total.astype(BF)
        total = g2w[k, ds(y * h2r + x * q2r_rows, q2r_rows), :].astype(F32)
        total = total + r1b[k, ds(x * q2r_rows, q2r_rows), :].astype(F32) + r2b[k].astype(F32)
        fz2[k] = total.astype(BF)

        if k == 1:
            for copy in fc_third:
                copy.start()
        for copy in fc_first(k) + fc_second(k):
            copy.wait_send()
        if k == 1:
            release(free.at[0], r_sib)
        else:
            release(free.at[1], r_x)
            release(free.at[1], r_y)

    def fc_finish():
        for copy in fc_third:
            copy.wait_recv()
        pl.semaphore_wait(free.at[1], 2)
        g1w[0, f1_rows[0], :] = fz1[0] + rz1[...]
        g2w[0, f2_rows[0], :] = fz2[0] + rz2[...]
        for copy in fc_spread(0):
            copy.start()

    def fc_widen():
        for copy in fc_spread(0):
            copy.wait_recv()
        for copy in fc_spread(1):
            copy.start()

    def fc_to_sibling():
        for copy in fc_spread(1):
            copy.wait_recv()
        pl.semaphore_wait(free.at[0], 1)
        for copy in fc_share + fc_store(0):
            copy.start()

    eighth = width // 8

    def order(j):
        odd = lax.rem(j, 2)
        first, second = r_x + (r_y - r_x) * odd, r_y + (r_x - r_y) * odd
        a1, a2 = x + (y - x) * odd, y + (x - y) * odd
        return first, second, a1, a2

    def each_place(j, do):
        @pl.when(j < 2)
        def _():
            do(pltpu.make_async_copy(gw.at[j], go_out.at[pl.ds(3 * lax.min(j, 1), 3), :, :], qloc.at[j]))

        @pl.when(j >= 2)
        def _():
            do(pltpu.make_async_copy(gw.at[j], gq_out.at[:, :, lanes(lax.max(j - 2, 0) * 128, 128)], qloc.at[j]))

    def core_copy(j):
        return remote(gw.at[j, :, ds((1 - c) * half, half), :], q0.at[j], q0s.at[j], q0r.at[j], r_sib, z)

    def first_copy(j):
        first, _, a1, _ = order(j)
        src = gw.at[j, :, ds(c * half + (1 - a1) * 2 * eighth, 2 * eighth), :]
        return remote(src, q1.at[j], q1s.at[j], q1r.at[j], first, z)

    def second_copy(j):
        _, second, a1, a2 = order(j)
        src = gw.at[j, :, ds(c * half + a1 * 2 * eighth + (1 - a2) * eighth, eighth), :]
        return remote(src, q2.at[j], q2s.at[j], q2r.at[j], second, z)

    def z_copy(j, step):
        if step == 0:
            src = gw.at[j, :, ds(own_start(j), eighth), :]
            return remote(src, qz.at[j, 0], q3s.at[j, 0], q3r.at[j, 0], r, z_pair)
        return remote(q2.at[j], qz.at[j, 1], q3s.at[j, 1], q3r.at[j, 1], r, z_far)

    def own_start(j):
        _, _, a1, a2 = order(j)
        return c * half + a1 * 2 * eighth + a2 * eighth

    def spread_copy(j, level):
        first, second, a1, _ = order(j)
        if level == 0:
            part = gw.at[j, :, ds(own_start(j), eighth), :]
            return remote(part, part, q5s.at[j], q5r.at[j], second, z)
        if level == 1:
            part = gw.at[j, :, ds(c * half + a1 * 2 * eighth, 2 * eighth), :]
            return remote(part, part, q6s.at[j], q6r.at[j], first, z)
        part = gw.at[j, :, ds(c * half, half), :]
        return remote(part, part, q7s.at[j], q7r.at[j], r_sib, z)

    def fold_first(j):
        core_copy(j).wait()
        release(chunk_free.at[j, 2], r_sib)
        _, _, a1, _ = order(j)
        rows = ds(c * half + (1 - a1) * 2 * eighth, 2 * eighth)
        gw[j, :, rows, :] = gw[j, :, rows, :] + q0[j, :, ds((1 - a1) * 2 * eighth, 2 * eighth), :]
        first_copy(j).start()

    def fold_second(j):
        first_copy(j).wait()
        first, _, a1, a2 = order(j)
        release(chunk_free.at[j, 1], first)
        inner = (1 - a2) * eighth
        rows = ds(c * half + a1 * 2 * eighth + inner, eighth)
        total = gw[j, :, rows, :].astype(F32) + q0[j, :, ds(a1 * 2 * eighth + inner, eighth), :].astype(F32)
        gw[j, :, rows, :] = (total + q1[j, :, ds(inner, eighth), :].astype(F32)).astype(BF)
        second_copy(j).start()

    def fold_z(j):
        second_copy(j).wait()
        _, second, a1, a2 = order(j)
        release(chunk_free.at[j, 0], second)
        inner = a2 * eighth
        rows = ds(c * half + a1 * 2 * eighth + inner, eighth)
        total = gw[j, :, rows, :].astype(F32) + q0[j, :, ds(a1 * 2 * eighth + inner, eighth), :].astype(F32)
        total = total + q1[j, :, ds(inner, eighth), :].astype(F32) + q2[j].astype(F32)
        gw[j, :, rows, :] = total.astype(BF)
        z_copy(j, 0).start()

    def fold_pair(j):
        z_copy(j, 0).wait()
        q2[j] = gw[j, :, ds(own_start(j), eighth), :] + qz[j, 0]
        z_copy(j, 1).start()

    def fold_all(j):
        z_copy(j, 1).wait()
        gw[j, :, ds(own_start(j), eighth), :] = q2[j] + qz[j, 1]
        pl.semaphore_wait(chunk_free.at[j, 0], 1)
        spread_copy(j, 0).start()

    def spread_first(j):
        spread_copy(j, 0).wait()
        pl.semaphore_wait(chunk_free.at[j, 1], 1)
        spread_copy(j, 1).start()

    def spread_sibling(j):
        spread_copy(j, 1).wait()
        pl.semaphore_wait(chunk_free.at[j, 2], 1)
        spread_copy(j, 2).start()

    def chunk_store(j):
        spread_copy(j, 2).wait()
        each_place(j, lambda copy: copy.start())

    def chunk_done(j):
        each_place(j, lambda copy: copy.wait())

    def small_copy(level):
        row = (r_sib, r_x, r_y)[level]
        return remote(sma.at[level], smr.at[level], sms.at[level], smrs.at[level], row, z)

    def small_z(step):
        src, dst = smz.at[2 * step], smz.at[2 * step + 1]
        return remote(src, dst, smzs.at[step], smzr.at[step], r, (z_pair, z_far)[step])

    barrier = pltpu.get_barrier_semaphore()
    partners = ((r_sib, z), (r_x, z), (r_y, z), (r_diag, z), (r, z_pair), (r, z_far))
    for row, column in partners:
        pl.semaphore_signal(barrier, inc=1, device_id={"rows": row, "mlp": column}, device_id_type=MESH)
    load_c.start()
    load_x.start()
    load_qkv.start()
    load_out.start()
    own_shard(0).start()
    own_shard(1).start()
    pl.semaphore_wait(barrier, len(partners))
    gather_copy(0, 0).start()
    gather_copy(1, 0).start()
    load_c.wait()
    for i in range(images):
        work[...] = jnp.zeros_like(work)
        work[0:patches, :] = c_ref[:, i, :]
        cot[i * tall : (i + 1) * tall, :] = work[...]
    cot_copy(0).start()
    cot_copy(1).start()
    load_x.wait()
    for i in range(images):
        forward_rows(i, x_ref, rank_ref, kept_ref, g1_ref, rw_ref, xp, keep, gate, h1, work)

    load_qkv.wait()

    @pl.loop(0, 3 * width // 256)
    def _(j):
        forward_qkv(j, h1, wqkv, qkv)

    @pl.loop(0, HEADS // 2)
    def _(p):
        for i in range(images):
            attend(p, i, width, tall, qkv, keep, probs, context, contextt)

        @pl.when(p == 2)
        def _():
            gather_forward(0)

        @pl.when(p == 5)
        def _():
            gather_forward(1)

    load_out.wait()

    @pl.loop(0, images)
    def _(i):
        forward_out(i, tall, context, wout, xp, keep, gate, g2_ref, attended, middle, tok)
        token_copy(i, 0).start()
        token_copy(i, 1).start()

    own_shard(0).wait()
    own_shard(1).wait()

    def at(block, number, do):
        @pl.when(block == number)
        def _():
            do()

    def before_sibling():
        for i in range(images):
            token_copy(i, 0).wait_recv()
        cot_copy(0).wait_recv()

    @pl.loop(0, 2 * images)
    def _(block):
        at(block, images, before_sibling)
        rows = ds(block * tall, tall)
        hid[rows, 0:part], gpre[rows, 0:part] = mlp_rows(tok[rows, :], cot[rows, :], w1[:, 0:part], w2[0:part, :])

    cot_copy(1).wait_recv()
    cot_copy(2).start()
    for mat in range(2):
        for kind in (1, 2, 3):
            gather_copy(mat, kind).wait_recv()
    for ref in (dg1, dg2, drw):
        ref[...] = jnp.zeros_like(ref)

    def before_near():
        cot_copy(2).wait_recv()
        gh2_to_sib.start()
        out_to_sib.start()

    def forward_token(i):
        token_copy(i, 1).wait_recv()
        token_copy(i, 2).start()

    def send_far(i):
        gh2_over(i).wait_recv()
        rows = ds(t_own + i * tall, tall)
        gh2_part[rows, :] = gh2_part[rows, :] + gh2_near[ds(i * tall, tall), :]
        gh2_far_copy(i).start()

    def before_last():
        send_far(0)
        token_copy(1, 2).wait_recv()

    @pl.loop(0, 8)
    def _(block):
        at(block, 3, lambda: forward_token(0))
        at(block, 4, before_near)
        at(block, 5, lambda: token_copy(0, 2).wait_recv())
        at(block, 6, lambda: forward_token(1))
        at(block, 7, before_last)
        inner = lax.rem(block, 5)
        swap = lax.div(block, 5) * (1 - 2 * inner + 3 * lax.div(inner * (inner - 1), 2))
        spot = block + swap
        rows = ds(spot * tall, tall)

        @pl.when(block < 2 * images)
        def _():
            hid[rows, part:], gpre[rows, part:] = mlp_rows(tok[rows, :], cot[rows, :], w1[:, part:], w2[part:, :])

        @pl.when(block >= 2 * images)
        def _():
            hid[rows, :], gpre[rows, :] = mlp_rows(tok[rows, :], cot[rows, :], w1[...], w2[...])

        share_out = dot_nn(hid[rows, :], w2[...])
        share_gh2 = dot_nt(gpre[rows, :], w1[...])

        @pl.when(block < images)
        def _():
            out[rows, :] = share_out
            gh2[rows, :] = share_gh2

        @pl.when(block >= images)
        def _():
            there = ds(lax.max(spot - images, 0) * tall, tall)
            out_part[there, :] = share_out.astype(BF)
            gh2_part[there, :] = share_gh2.astype(BF)

        at(block, 5, lambda: gh2_over(0).start())
        at(block, 7, lambda: gh2_over(1).start())

    out_over.start()
    turned[...] = tok[...].T
    for m in range(3):
        rows = slice(m * width // 3, (m + 1) * width // 3)
        total = dot_nn(turned[rows, :], gpre[...]).astype(BF)
        g1w[0, rows, :] = total[:, 0:part]
        g1w[1, rows, :] = total[:, part:]
    send_far(1)
    turned[...] = hid[...].T
    for m in range(2):
        g2w[m] = dot_nn(turned[m * part : (m + 1) * part, :], cot[...]).astype(BF)
    for k in range(2):
        for copy in fc_first(k):
            copy.start()

    @pl.loop(4, LAST)
    def _(t):
        def back_image(i):
            gh2_far_copy(i).wait_recv()
            rows = pl.ds(i * tall, tall)
            gh2[rows, :] += gh2_sib[rows, :].astype(F32) + gh2_far[rows, :].astype(F32)
            back_rows(i, tall, cot, gh2, middle, keep, gate, attended, g2_ref, gh2, tok, glogit, dg2)
            context[rows, :] = dot_nt(tok[rows, :], wout[...]).astype(BF)

        @pl.when(t == 4)
        def _():
            gh2_to_sib.wait_recv()
            for i in range(images):
                token_copy(i, 0).wait_send()
                token_copy(i, 1).wait_send()
            back_image(0)
            turned[:, 0:t_own] = h1[...].T

        at(t, FIRST, lambda: back_image(1))

        @pl.when(jnp.logical_and(t >= FIRST, t < FIRST + 2))
        def _():
            cols = lanes((t - FIRST) * half, half)
            total = 0.0
            for i in range(images):
                total = total + dot_nn(contextt[i], tok[i * tall : (i + 1) * tall, cols])
            for b in range(3):
                gw[t - FIRST, b] = total[:, b * 128 : (b + 1) * 128].astype(BF)

        late = lax.div(t, FIRST)

        @pl.when(
            jnp.logical_or(
                jnp.logical_and(t >= 5, t < FIRST),
                jnp.logical_and(jnp.logical_and(t >= FIRST + 2, t < FIRST + CHUNKS), lax.rem(t, 2) == 0),
            )
        )
        def _():
            p = 2 * (t - 5) + late * (2 * 5 - FIRST - 2 - t)
            for n in range(2):
                attend_back(p + n, late, width, tall, qkv, probs, context)

        @pl.when(jnp.logical_and(t >= FIRST + 2, t < FIRST + CHUNKS))
        def _():
            total = dot_nn(turned[:, 0:t_own], pair_columns(qkv, t - FIRST - 2, width))
            for b in range(3):
                gw[t - FIRST, b] = total[:, b * 128 : (b + 1) * 128].astype(BF)

        @pl.when(jnp.logical_and(t >= FIRST, t < FIRST + CHUNKS))
        def _():
            core_copy(t - FIRST).start()

        @pl.when(t == 5)
        def _():
            out_over.wait_recv()
            rows = pl.ds(t_own, t_own)
            out_part[rows, :] = out_part[rows, :] + out_near[...]
            out_far_copy.start()

        @pl.when(t == FIRST + CHUNKS)
        def _():
            for i in range(images):
                rows = pl.ds(i * tall, tall)
                dy = dot_nt(qkv[rows, :], wqkv[...])
                back_input(i, tall, dy, glogit, rw_ref, xp, h1, g1_ref, gh2, x_ref, dg1, drw)
            store_gx.start()
            sma[0] = jnp.concatenate([dg1[...], drw[...], dg2[...], jnp.zeros((5, width), F32)], 0)
            small_copy(0).start()

        for level in range(2):

            @pl.when(t == 18 + 2 * level)
            def _(level=level):
                small_copy(level).wait()
                sma[level + 1] = sma[level] + smr[level]
                small_copy(level + 1).start()

        @pl.when(t == 22)
        def _():
            small_copy(2).wait()
            smz[0] = sma[2] + smr[2]
            small_z(0).start()

        @pl.when(t == 24)
        def _():
            small_z(0).wait()
            smz[2] = smz[0] + smz[1]
            small_z(1).start()
            out_to_sib.wait_recv()
            out_far_copy.wait_recv()
            for i in range(images):
                rows = pl.ds(i * tall, tall)
                total = middle[rows, :] + out[rows, :] + out_sib[rows, :].astype(F32) + out_far[rows, :].astype(F32)
                c_ref[:, i, :] = total.astype(BF)[0:patches, :]
            store_block.start()

        def lagged(lag, do):
            @pl.when(jnp.logical_and(t >= FIRST + lag, t < FIRST + lag + CHUNKS))
            def _():
                do(t - FIRST - lag)

        steps = (
            (7, lambda: fc_fold_second(0)), (9, lambda: fc_fold_second(1)), (12, lambda: fc_fold_third(1)),
            (20, lambda: fc_fold_third(0)), (20, fc_finish), (23, fc_widen), (26, fc_to_sibling),
        )
        for tick, do in steps:
            at(t, tick, do)

        stages = (fold_first, fold_second, fold_z, fold_pair, fold_all, spread_first, spread_sibling, chunk_store)
        for stage in (5, 6, 7, 8, 4, 3, 2, 1):
            lagged(LAGS[stage], stages[stage - 1])

    small_z(1).wait()
    small_out[...] = smz[2] + smz[3]

    @pl.loop(0, CHUNKS)
    def _(j):
        chunk_done(j)

    store_gx.wait()
    store_block.wait()
    for copy in fc_share:
        copy.wait()
    for copy in fc_store(1):
        copy.start()
    for copy in fc_store(0) + fc_store(1):
        copy.wait()
    for level in range(2):
        for copy in fc_spread(level):
            copy.wait_send()
    for copy in fc_third:
        copy.wait_send()
    for mat in range(2):
        for kind in range(4):
            gather_copy(mat, kind).wait_send()
    for i in range(images):
        token_copy(i, 2).wait_send()
        gh2_over(i).wait_send()
        gh2_far_copy(i).wait_send()
    for hop in range(3):
        cot_copy(hop).wait_send()
    for copy in (gh2_to_sib, out_to_sib, out_over, out_far_copy):
        copy.wait_send()

VMEM = pl.BlockSpec(memory_space=pltpu.VMEM)
SMEM = pl.BlockSpec(memory_space=pltpu.SMEM)
ANY = pl.BlockSpec(memory_space=pl.ANY)


def widen_kernel(block, gx, gq, go, f1, f2, small, block_out, gx_out, gq_out, go_out, f1_out, f2_out, g1_out, rw_out, g2_out):
    width = f1.shape[1]
    for step, (src, dst) in enumerate(((block, block_out), (gx, gx_out))):

        @pl.when(pl.program_id(0) == step)
        def _(src=src, dst=dst):
            dst[...] = src[...]

    for b in range(3):
        gq_out[:, b * width : (b + 1) * width] = gq[b].astype(F32)
    for b in range(go.shape[0]):
        go_out[:, b * 128 : (b + 1) * 128] = go[b].astype(F32)
    f1_out[...] = f1[...].astype(F32)
    f2_out[...] = f2[...].astype(F32)
    g1_out[...], rw_out[...], g2_out[...] = small[0], small[1], small[2]


def widen(block, gx, gq, go, f1, f2, small):
    width = f1.shape[0]
    step = 128
    tokens = jax.ShapeDtypeStruct(block.shape, BF)
    whole = pl.BlockSpec(block.shape, lambda i: (0, 0, 0))

    def rows(*tail):
        return pl.BlockSpec((step,) + tail, lambda i: (i, 0))

    def inner(lead, tail):
        return pl.BlockSpec((lead, step, tail), lambda i: (0, i, 0))

    return pl.pallas_call(
        widen_kernel,
        grid=(width // step,),
        out_shape=[tokens, tokens] + [jax.ShapeDtypeStruct((width, n), F32) for n in (3 * width, width, width, width)]
        + [jax.ShapeDtypeStruct((width,), F32)] * 3,
        in_specs=[whole, whole, inner(3, width), inner(6, 128), rows(width), rows(width), pl.BlockSpec((8, width), lambda i: (0, 0))],
        out_specs=[whole, whole, rows(3 * width), rows(width), rows(width), rows(width)] + [pl.BlockSpec((width,), lambda i: (0,))] * 3,
        compiler_params=pltpu.CompilerParams(vmem_limit_bytes=63 * 1024 * 1024),
        name="widen",
    )(block, gx, gq, go, f1, f2, small)


def per_device(others, images, patch_rank, kept_count, ln1_gain, router_weight, w_qkv, w_out, ln2_gain, w_fc1, w_fc2, cotangent):
    count, patches, width = images.shape
    tall = -(-patches // 16) * 16
    t = count * tall
    part = w_fc1.shape[1] // 2
    half, eighth = width // 2, width // 8

    def bf(*dims):
        return pltpu.VMEM(dims, BF)

    def f32(*dims):
        return pltpu.VMEM(dims, F32)

    def sem(*dims):
        return pltpu.SemaphoreType.DMA(dims)

    scratch = [
        bf(patches, count, width), bf(patches, count, width),
        bf(width, 3 * width), bf(width, width), bf(width, 2 * part), bf(2 * part, width),
        bf(t, width), f32(t, 128), f32(t, 128), f32(t, 128), bf(t, width), bf(t, 3 * width),
        f32(count, HEADS, tall, tall), bf(count, width, tall), bf(t, width), f32(t, width), f32(t, width),
        bf(4 * t, width), bf(4 * t, width), bf(width, 4 * t), f32(t, width), f32(t, width),
        bf(3 * t, width), bf(3 * t, width), bf(t, width), bf(t, width), bf(t, width), bf(t, width), bf(t, width), bf(t, width),
        bf(4 * t, 2 * part), bf(4 * t, 2 * part), bf(tall, width),
        bf(2, width, part), bf(2, part, width),
        bf(2, width // 2, part), bf(2, part // 2, width), bf(2, width // 4, part), bf(2, part // 4, width),
        bf(2, width // 4, part), bf(2, part // 4, width), bf(width // 4, part), bf(part // 4, width),
        bf(CHUNKS, 3, width, 128), bf(CHUNKS, 3, half, 128), bf(CHUNKS, 3, 2 * eighth, 128), bf(CHUNKS, 3, eighth, 128),
        bf(CHUNKS, 2, 3, eighth, 128),
        f32(1, width), f32(1, width), f32(1, width), f32(3, 8, width), f32(3, 8, width), f32(4, 8, width),
        sem(8), sem(2, 4), sem(2, 4), sem(count, 3), sem(count, 3), sem(3), sem(3), sem(8), sem(8),
        sem(2, 2), sem(2, 2), sem(2, 2), sem(2, 2), sem(2), sem(2),
        sem(2, 2), sem(2, 2), sem(2, 2), sem(2), sem(2), pltpu.SemaphoreType.REGULAR((2,)), pltpu.SemaphoreType.REGULAR((CHUNKS, 3)),
        sem(CHUNKS), sem(CHUNKS), sem(CHUNKS), sem(CHUNKS), sem(CHUNKS), sem(CHUNKS),
        sem(CHUNKS, 2), sem(CHUNKS, 2), sem(CHUNKS),
        sem(CHUNKS), sem(CHUNKS), sem(CHUNKS), sem(CHUNKS), sem(CHUNKS), sem(CHUNKS),
        sem(3), sem(3), sem(2), sem(2),
    ]

    def struct(*dims, dtype=BF):
        return jax.ShapeDtypeStruct(dims, dtype)

    block, gx, gq, go, f1, f2, small = pl.pallas_call(
        mega_kernel,
        out_shape=[
            struct(patches, count, width), struct(patches, count, width), struct(3, width, width), struct(6, width, 128),
            struct(width, 2 * part), struct(2 * part, width), struct(8, width, dtype=F32),
        ],
        in_specs=[ANY, VMEM, SMEM, VMEM, VMEM, ANY, ANY, VMEM, ANY, ANY, ANY],
        out_specs=[ANY, ANY, ANY, ANY, ANY, ANY, VMEM],
        scratch_shapes=scratch,
        compiler_params=pltpu.CompilerParams(
            collective_id=0, has_side_effects=True, vmem_limit_bytes=64 * 1024 * 1024
        ),
        name="block",
    )(images.transpose(1, 0, 2), patch_rank, kept_count, ln1_gain, router_weight, w_qkv, w_out, ln2_gain, w_fc1, w_fc2,
      cotangent.transpose(1, 0, 2))
    block, gx, gq, go, f1, f2, g1, rw, g2 = widen(block, gx, gq, go, f1, f2, small)
    if others:
        gq, go, f1, f2, g1, rw, g2 = lax.psum((gq, go, f1, f2, g1, rw, g2), "rows", axis_index_groups=others)
    return block.transpose(1, 0, 2), gx.transpose(1, 0, 2), g1, rw, gq, go, g2, f1, f2


def solution(mesh):
    rows = mesh.shape["rows"]
    others = [[8 * g + i for g in range(rows // 8)] for i in range(8)] if rows > 8 else None
    return jax.shard_map(
        functools.partial(per_device, others),
        mesh=mesh,
        in_specs=(
            P(("rows", "mlp"), None, None), P(("rows", "mlp"), None), P(("rows", "mlp")), P(), P(), P(), P(), P(),
            P(None, "mlp"), P("mlp", None), P(("rows", "mlp"), None, None),
        ),
        out_specs=(
            P(("rows", "mlp"), None, None), P(("rows", "mlp"), None, None), P(), P(), P(), P(), P(),
            P(None, "mlp"), P("mlp", None),
        ),
        check_vma=False,
    )
```

```python
import functools
import jax
import jax.numpy as jnp
from jax import lax
from jax.experimental import pallas as pl
from jax.experimental.pallas import tpu as pltpu
from jax.sharding import PartitionSpec as P

HEADS = 12
EPS = 1e-6
FILL = -1e30
BF = jnp.bfloat16
F32 = jnp.float32


def dot_nn(a, b):
    return lax.dot_general(a, b, (((1,), (0,)), ((), ())), preferred_element_type=F32)


def dot_nt(a, b):
    return lax.dot_general(a, b, (((1,), (1,)), ((), ())), preferred_element_type=F32)


def dot_tn(a, b):
    return lax.dot_general(a, b, (((0,), (0,)), ((), ())), preferred_element_type=F32)


def unit_rows(v):
    center = v - jnp.mean(v, -1, keepdims=True)
    scale = lax.rsqrt(jnp.mean(center * center, -1, keepdims=True) + EPS)
    return center * scale, scale


def norm_pull(dy, gain, unit, scale):
    du = dy * gain
    return scale * (
        du
        - jnp.mean(du, -1, keepdims=True)
        - unit * jnp.mean(du * unit, -1, keepdims=True)
    )


def half_mask(rows, h):
    lane = lax.broadcasted_iota(jnp.int32, (rows, 128), 1)
    return (lane < 64) if h == 0 else (lane >= 64)


def forward_rows(i, x_ref, rank_ref, kept_ref, g1_ref, rw_ref, xp, keep, gate, h1, work):
    patches = x_ref.shape[0]
    tall = xp.shape[0] // x_ref.shape[1]
    rows = pl.ds(pl.multiple_of(i * tall, 16), tall)
    work[...] = jnp.zeros_like(work)
    work[0:patches, :] = x_ref[:, i, :]
    v = work[...]
    xp[rows, :] = v
    kept = (rank_ref[pl.ds(i, 1), :] < kept_ref[i]).astype(F32)
    keep_row = jnp.concatenate([kept, jnp.zeros((1, 256 - patches), F32)], 1)
    keep_col = jnp.broadcast_to(keep_row, (128, 256)).T
    keep[rows, :] = keep_col[0:tall, :]
    unit, _ = unit_rows(v.astype(F32))
    low = (unit * g1_ref[...][None]).astype(BF)
    h1[rows, :] = low
    logit = jnp.sum(low.astype(F32) * rw_ref[...][None].astype(F32), -1, keepdims=True)
    gate[rows, :] = jnp.broadcast_to(jax.nn.sigmoid(logit), (tall, 128))


def forward_qkv(j, h1, wqkv, qkv):
    cols = pl.ds(pl.multiple_of(j * 256, 256), 256)
    qkv[:, cols] = dot_nn(h1[...], wqkv[:, cols]).astype(BF)


def attend(p, i, width, tall, qkv, keep, probs, context, contextt):
    rows = pl.ds(pl.multiple_of(i * tall, 16), tall)
    qc = pl.ds(pl.multiple_of(p * 128, 128), 128)
    kc = pl.ds(pl.multiple_of(width + p * 128, 128), 128)
    vc = pl.ds(pl.multiple_of(2 * width + p * 128, 128), 128)
    q, k, v = qkv[rows, qc], qkv[rows, kc], qkv[rows, vc]
    vt = v.T
    kept = keep[rows, 0:1] > 0.5
    outs = []
    for h in range(2):
        kh = jnp.where(half_mask(tall, h), k, jnp.zeros_like(k))
        s = jnp.where(kept, dot_nt(kh, q) * 0.125, FILL)
        e = jnp.exp(s - jnp.max(s, 0, keepdims=True))
        pr = e * (1.0 / jnp.sum(e, 0, keepdims=True))
        probs[i, p * 2 + h] = pr
        outs.append(dot_nn(vt[h * 64 : h * 64 + 64, :], pr.astype(BF)))
    ct = jnp.concatenate(outs, 0)
    contextt[i, pl.ds(pl.multiple_of(p * 128, 128), 128), :] = ct.astype(BF)
    context[rows, qc] = ct.T.astype(BF)


def forward_out(i, tall, context, wout, xp, keep, gate, g2_ref, attended, middle, h2):
    rows = pl.ds(pl.multiple_of(i * tall, 16), tall)
    att = dot_nn(context[rows, :], wout[...])
    attended[rows, :] = att
    mid = xp[rows, :].astype(F32) + keep[rows, 0:1] * gate[rows, 0:1] * att
    middle[rows, :] = mid
    unit, _ = unit_rows(mid)
    h2[rows, :] = (unit * g2_ref[...][None]).astype(BF)


def gelu_pair(pre):
    cdf = 0.5 * (1.0 + lax.erf(pre * 0.7071067811865476))
    pdf = jnp.exp(pre * pre * -0.5) * 0.3989422804014327
    return pre * cdf, cdf + pre * pdf


def mlp_rows(h, c, w1, w2):
    pre = dot_nn(h, w1)
    hidden, slope = gelu_pair(pre)
    grad = dot_nt(c, w2) * slope
    return hidden.astype(BF), grad.astype(BF)


def back_rows(i, tall, c_ref, gh2, middle, keep, gate, attended, g2_ref, gmid, gatt, glogit, dg2):
    rows = pl.ds(pl.multiple_of(i * tall, 16), tall)
    dy = gh2[rows, :]
    unit, scale = unit_rows(middle[rows, :])
    gm = c_ref[rows, :].astype(F32) + norm_pull(dy, g2_ref[...][None], unit, scale)
    gmid[rows, :] = gm
    dg2[...] += jnp.sum(dy * unit, 0, keepdims=True)
    k, g = keep[rows, 0:1], gate[rows, 0:1]
    kept = gm * k
    gatt[rows, :] = (kept * g).astype(BF)
    gl = jnp.sum(kept * attended[rows, :], -1, keepdims=True) * g * (1.0 - g)
    glogit[rows, :] = jnp.broadcast_to(gl, (tall, 128))


def attend_back(p, i, width, tall, qkv, probs, gctx):
    rows = pl.ds(pl.multiple_of(i * tall, 16), tall)
    qc = pl.ds(pl.multiple_of(p * 128, 128), 128)
    kc = pl.ds(pl.multiple_of(width + p * 128, 128), 128)
    vc = pl.ds(pl.multiple_of(2 * width + p * 128, 128), 128)
    q, k, v = qkv[rows, qc], qkv[rows, kc], qkv[rows, vc]
    gc = gctx[rows, qc]
    kt = k.T
    gv, gk, gq = 0.0, 0.0, []
    for h in range(2):
        mask = half_mask(tall, h)
        zero = jnp.zeros_like(v)
        pr = probs[i, p * 2 + h]
        gp = dot_nt(jnp.where(mask, v, zero), gc)
        gs = (pr * (gp - jnp.sum(pr * gp, 0, keepdims=True))).astype(BF)
        gv = gv + dot_nn(pr.astype(BF), jnp.where(mask, gc, zero))
        gk = gk + dot_nn(gs, jnp.where(mask, q, zero))
        gq.append(dot_nn(kt[h * 64 : h * 64 + 64, :], gs))
    qkv[rows, qc] = (jnp.concatenate(gq, 0).T * 0.125).astype(BF)
    qkv[rows, kc] = (gk * 0.125).astype(BF)
    qkv[rows, vc] = gv.astype(BF)


def pair_columns(wqkv, p, width):
    return jnp.concatenate(
        [wqkv[:, pl.ds(pl.multiple_of(b * width + p * 128, 128), 128)] for b in range(3)], 1
    )


def back_input(i, tall, dy, glogit, rw_ref, xp, h1, g1_ref, gmid, gx_ref, dg1, drw):
    rows = pl.ds(pl.multiple_of(i * tall, 16), tall)
    patches = gx_ref.shape[0]
    gl = glogit[rows, 0:1]
    dy = dy + gl * rw_ref[...][None].astype(F32)
    unit, scale = unit_rows(xp[rows, :].astype(F32))
    dg1[...] += jnp.sum(dy * unit, 0, keepdims=True)
    drw[...] += jnp.sum(h1[rows, :].astype(F32) * gl, 0, keepdims=True)
    out = gmid[rows, :] + norm_pull(dy, g1_ref[...][None], unit, scale)
    gx_ref[:, i, :] = out.astype(BF)[0:patches, :]

MESH = pl.DeviceIdType.MESH
CHUNKS = HEADS // 2 + 2
PATHS = ("yxz", "zyx", "xzy", "yxz", "zxy", "xyz", "yxz", "xyz")
ORDER = (
    "osend", "back0", "pairs0", "back1", "pairs1", "last0", "fa0", "out1", "pairs2", "fa1", "last1", "out0", "c3.1",
    "c1.1", "c2.1", "pairs3", "fb1", "last2", "c5.1", "c0.1", "finish0", "c3.2", "c2.2", "c1.2", "c4.1", "c7.1",
    "c6.1", "finish1", "c5.2", "c1.3", "c3.3", "c0.2", "c2.3", "c6.2", "c7.2", "c1.4", "g1", "fb0", "c5.3", "c4.2",
    "c0.3", "c2.4", "fc", "c3.4", "c7.3", "c5.4", "c6.3", "c1.5", "c4.3", "c0.4", "g2", "c2.5", "c3.5", "c7.4", "fd",
    "c4.4", "c5.5", "c0.5", "c1.6", "g3", "c2.6", "c3.6", "c6.4", "c7.5", "g4", "c0.6", "c4.5", "c5.6", "c2.7", "fe",
    "c6.5", "c7.6", "c1.7", "c3.7", "c4.6", "o0", "c6.6", "c0.7", "c2.8", "c7.7", "c4.7", "o1", "c1.8", "c6.7", "ff",
    "c3.8", "c5.7", "c0.8", "c7.8", "c4.8", "c6.8", "c5.8", "g5", "c7.9", "c1.9", "c3.9", "c4.9", "c6.9", "c0.9",
    "c2.9", "c5.9",
)


def mega_kernel(
    x_hbm, rank_ref, kept_ref, g1_ref, rw_ref, wqkv_hbm, wout_hbm, g2_ref, fc1, fc2, c_hbm,
    block_hbm, gx_hbm, gq_out, go_out, f1_out, f2_out, small_out,
    x_ref, c_ref, wqkv, wout, w1, w2, xp, keep, gate, glogit, h1, qkv, probs, contextt, context, attended, middle,
    tok, cot, turned, out, gh2, out_part, gh2_part, out_sib, gh2_sib, out_near, gh2_near, out_far, gh2_far, hid, gpre, work,
    g1w, g2w, r1a, r1b, r2a, r2b, fz1, fz2, rz1, rz2,
    gw, q0, q1, q2, q3, far, dg1, dg2, drw, sma, smr, smz,
    lsem, gsend, grecv, hsend, hrecv, csend, crecv, esend, erecv, s1s, s1r, s2s, s2r, s3s, s3r, fs, fr, floc, ssib, rsib, free, chunk_free,
    qs, qr, qloc, sms, smrs, smzs, smzr,
):
    patches, images, width = x_ref.shape
    t_own = xp.shape[0]
    tall = t_own // images
    half = width // 2
    part = w1.shape[1] // 2
    parts = (q0, q1, q2, q3)
    quarter = (width // 4, part // 4)
    r = lax.axis_index("rows")
    z = lax.axis_index("mlp")
    c, x, y = lax.rem(r, 2), lax.rem(lax.div(r, 2), 2), lax.rem(lax.div(r, 4), 2)
    r_sib, r_x, r_y = r + 1 - 2 * c, r + 2 - 4 * x, r + 4 - 8 * y
    r_diag = r_x + r_y - r
    z_pair, z_far = z + 1 - 2 * lax.rem(z, 2), z + 2 - 4 * lax.div(z, 2)
    q = 2 * y + x

    def ds(start, size):
        return pl.ds(pl.multiple_of(start, 16), size)

    def lanes(start, size):
        return pl.ds(pl.multiple_of(start, 128), size)

    def remote(src, dst, send, recv, row, column):
        return pltpu.make_async_remote_copy(
            src_ref=src, dst_ref=dst, send_sem=send, recv_sem=recv,
            device_id={"rows": row, "mlp": column}, device_id_type=MESH,
        )

    def release(semaphore, row):
        pl.semaphore_signal(semaphore, inc=1, device_id={"rows": row, "mlp": z}, device_id_type=MESH)

    def gather_copy(mat, kind):
        size = quarter[mat]
        sems = gsend.at[mat, kind], grecv.at[mat, kind]
        if mat == 0:
            place = w1.at[ds(q * size, size), pl.ds(part, part)]
            own = fc1.at[ds(q * size, size), lanes(c * part, part)]
        else:
            place = w2.at[ds(part + q * size, size), :]
            own = fc2.at[ds(c * part + q * size, size), :]
        if kind == 0:
            return remote(own, place, *sems, r, z_far)
        return remote(place, place, *sems, (r_x, r_y, r_diag)[kind - 1], z)

    def gather_forward(mat):
        gather_copy(mat, 0).wait_recv()
        for kind in (1, 2, 3):
            gather_copy(mat, kind).start()

    def own_shard(mat):
        if mat == 0:
            return pltpu.make_async_copy(fc1.at[:, lanes(c * part, part)], w1.at[:, pl.ds(0, part)], lsem.at[0])
        return pltpu.make_async_copy(fc2.at[ds(c * part, part), :], w2.at[pl.ds(0, part), :], lsem.at[1])

    load_qkv = pltpu.make_async_copy(wqkv_hbm, wqkv, lsem.at[2])
    load_out = pltpu.make_async_copy(wout_hbm, wout, lsem.at[3])
    load_x = pltpu.make_async_copy(x_hbm, x_ref, lsem.at[4])
    load_c = pltpu.make_async_copy(c_hbm, c_ref, lsem.at[5])
    store_block = pltpu.make_async_copy(c_ref, block_hbm, lsem.at[6])
    store_gx = pltpu.make_async_copy(x_ref, gx_hbm, lsem.at[7])

    def token_copy(i, hop):
        start = (0, 0, 2 * t_own)[hop] + i * tall
        src, dst = tok.at[ds(start, tall), :], tok.at[ds((1, 2, 3)[hop] * t_own + i * tall, tall), :]
        row, column = (r, z_pair) if hop == 1 else (r_sib, z)
        return remote(src, dst, hsend.at[i, hop], hrecv.at[i, hop], row, column)

    def cot_copy(hop):
        src, dst = cot.at[ds((0, 0, 2)[hop] * t_own, t_own), :], cot.at[ds((1, 2, 3)[hop] * t_own, t_own), :]
        row, column = (r, z_pair) if hop == 1 else (r_sib, z)
        return remote(src, dst, csend.at[hop], crecv.at[hop], row, column)

    gh2_to_sib = remote(gh2_part.at[ds(0, t_own), :], gh2_sib, esend.at[0], erecv.at[0], r_sib, z)
    out_to_sib = remote(out_part.at[ds(0, t_own), :], out_sib, esend.at[1], erecv.at[1], r_sib, z)
    out_over = remote(out_part.at[ds(2 * t_own, t_own), :], out_near, esend.at[2], erecv.at[2], r_sib, z)
    out_far_copy = remote(out_part.at[ds(t_own, t_own), :], out_far, esend.at[3], erecv.at[3], r, z_pair)

    def gh2_over(i):
        src = gh2_part.at[ds(2 * t_own + i * tall, tall), :]
        return remote(src, gh2_near.at[ds(i * tall, tall), :], esend.at[4 + i], erecv.at[4 + i], r_sib, z)

    def gh2_far_copy(i):
        src = gh2_part.at[ds(t_own + i * tall, tall), :]
        return remote(src, gh2_far.at[ds(i * tall, tall), :], esend.at[6 + i], erecv.at[6 + i], r, z_pair)

    h1r, q1r_rows = width // 2, width // 4
    h2r, q2r_rows = part // 2, part // 4

    def fc_first(k):
        return (
            remote(g1w.at[k, ds((1 - x) * h1r, h1r), :], r1a.at[k], s1s.at[k, 0], s1r.at[k, 0], r_x, z),
            remote(g2w.at[k, ds((1 - y) * h2r, h2r), :], r1b.at[k], s1s.at[k, 1], s1r.at[k, 1], r_y, z),
        )

    def fc_second(k):
        return (
            remote(
                g1w.at[k, ds(x * h1r + (1 - y) * q1r_rows, q1r_rows), :], r2a.at[k], s2s.at[k, 0], s2r.at[k, 0], r_y, z
            ),
            remote(
                g2w.at[k, ds(y * h2r + (1 - x) * q2r_rows, q2r_rows), :], r2b.at[k], s2s.at[k, 1], s2r.at[k, 1], r_x, z
            ),
        )

    fc_third = (
        remote(fz1.at[1], rz1, s3s.at[0], s3r.at[0], r, z_far),
        remote(fz2.at[1], rz2, s3s.at[1], s3r.at[1], r, z_far),
    )

    f1_rows = (ds(x * h1r + y * q1r_rows, q1r_rows), ds(x * h1r, h1r))
    f2_rows = (ds(y * h2r + x * q2r_rows, q2r_rows), ds(y * h2r, h2r))

    def fc_spread(level):
        part1, part2 = g1w.at[0, f1_rows[level], :], g2w.at[0, f2_rows[level], :]
        row1, row2 = ((r_y, r_x), (r_x, r_y))[level]
        return (
            remote(part1, part1, fs.at[level, 0], fr.at[level, 0], row1, z),
            remote(part2, part2, fs.at[level, 1], fr.at[level, 1], row2, z),
        )

    fc_share = (
        remote(g1w.at[0], g1w.at[1], ssib.at[0], rsib.at[0], r_sib, z),
        remote(g2w.at[0], g2w.at[1], ssib.at[1], rsib.at[1], r_sib, z),
    )

    def fc_store(k):
        core = c + k - 2 * c * k
        return (
            pltpu.make_async_copy(g1w.at[k], f1_out.at[:, lanes(core * part, part)], floc.at[k, 0]),
            pltpu.make_async_copy(g2w.at[k], f2_out.at[ds(core * part, part), :], floc.at[k, 1]),
        )

    def fc_fold_second(k):
        for copy in fc_first(k):
            copy.wait_recv()
        rows = ds(x * h1r + (1 - y) * q1r_rows, q1r_rows)
        g1w[k, rows, :] = g1w[k, rows, :] + r1a[k, ds((1 - y) * q1r_rows, q1r_rows), :]
        rows = ds(y * h2r + (1 - x) * q2r_rows, q2r_rows)
        g2w[k, rows, :] = g2w[k, rows, :] + r1b[k, ds((1 - x) * q2r_rows, q2r_rows), :]
        for copy in fc_second(k):
            copy.start()

    def fc_fold_third(k):
        for copy in fc_second(k):
            copy.wait_recv()
        total = g1w[k, ds(x * h1r + y * q1r_rows, q1r_rows), :].astype(F32)
        total = total + r1a[k, ds(y * q1r_rows, q1r_rows), :].astype(F32) + r2a[k].astype(F32)
        fz1[k] = total.astype(BF)
        total = g2w[k, ds(y * h2r + x * q2r_rows, q2r_rows), :].astype(F32)
        total = total + r1b[k, ds(x * q2r_rows, q2r_rows), :].astype(F32) + r2b[k].astype(F32)
        fz2[k] = total.astype(BF)

        if k == 1:
            for copy in fc_third:
                copy.start()
        for copy in fc_first(k) + fc_second(k):
            copy.wait_send()
        if k == 1:
            release(free.at[0], r_sib)
        else:
            release(free.at[1], r_x)
            release(free.at[1], r_y)

    def fc_finish():
        for copy in fc_third:
            copy.wait_recv()
        pl.semaphore_wait(free.at[1], 2)
        g1w[0, f1_rows[0], :] = fz1[0] + rz1[...]
        g2w[0, f2_rows[0], :] = fz2[0] + rz2[...]
        for copy in fc_spread(0):
            copy.start()

    def fc_widen():
        for copy in fc_spread(0):
            copy.wait_recv()
        for copy in fc_spread(1):
            copy.start()

    def fc_to_sibling():
        for copy in fc_spread(1):
            copy.wait_recv()
        pl.semaphore_wait(free.at[0], 1)
        for copy in fc_share + fc_store(0):
            copy.start()

    sizes = tuple(width >> level for level in range(1, 5))

    def hops(j):
        ways = {"x": (r_x, z, x), "y": (r_y, z, y), "z": (r, z_pair, lax.rem(z, 2))}
        return [(r_sib, z, c)] + [ways[axis] for axis in PATHS[j]]

    def base(path, level):
        start = 0
        for (_, _, bit), size in zip(path[:level], sizes):
            start = start + bit * size
        return start

    def core_copy(j):
        src = gw.at[j, :, ds((1 - c) * half, half), :]
        return remote(src, parts[0].at[j], qs.at[j, 0], qr.at[j, 0], r_sib, z)

    def chunk_copy(j, step):
        path = hops(j)
        if step == 0:
            return core_copy(j)
        if step < 4:
            row, column, bit = path[step]
            start = base(path, step) + (1 - bit) * sizes[step]
            return remote(gw.at[j, :, ds(start, sizes[step]), :], parts[step].at[j], qs.at[j, step], qr.at[j, step], row, column)
        if step == 4:
            own = gw.at[j, :, ds(base(path, 4), sizes[3]), :]
            return remote(own, far.at[j], qs.at[j, 4], qr.at[j, 4], r, z_far)
        level = 8 - step
        row, column, _ = path[level]
        held = gw.at[j, :, ds(base(path, level + 1), sizes[level]), :]
        return remote(held, held, qs.at[j, step], qr.at[j, step], row, column)

    def chunk_store(j):
        if j < 2:
            place = go_out.at[pl.ds(3 * j, 3), :, :]
        else:
            place = gq_out.at[:, :, pl.ds((j - 2) * 128, 128)]
        return pltpu.make_async_copy(gw.at[j], place, qloc.at[j])

    def chunk_step(j, step):
        path = hops(j)
        chunk_copy(j, step - 1).wait()
        if step <= 4:
            row, column, _ = path[step - 1]
            pl.semaphore_signal(
                chunk_free.at[j, step - 1], inc=1, device_id={"rows": row, "mlp": column}, device_id_type=MESH
            )
            start = base(path, min(step, 4))
            if step < 4:
                start = base(path, step) + (1 - path[step][2]) * sizes[step]
            size = sizes[min(step, 3)]
            total = gw[j, :, ds(start, size), :].astype(F32)
            for level in range(step):
                total = total + parts[level][j, :, ds(start - base(path, level + 1), size), :].astype(F32)
            gw[j, :, ds(start, size), :] = total.astype(BF)
        if step == 5:
            own = ds(base(path, 4), sizes[3])
            gw[j, :, own, :] = gw[j, :, own, :] + far[j]
        if 5 <= step <= 8:
            pl.semaphore_wait(chunk_free.at[j, 8 - step], 1)
        if step <= 8:
            chunk_copy(j, step).start()
        else:
            chunk_store(j).start()

    def small_copy(level):
        row = (r_sib, r_x, r_y)[level]
        return remote(sma.at[level], smr.at[level], sms.at[level], smrs.at[level], row, z)

    def small_z(step):
        src, dst = smz.at[2 * step], smz.at[2 * step + 1]
        return remote(src, dst, smzs.at[step], smzr.at[step], r, (z_pair, z_far)[step])

    barrier = pltpu.get_barrier_semaphore()
    partners = ((r_sib, z), (r_x, z), (r_y, z), (r_diag, z), (r, z_pair), (r, z_far))
    for row, column in partners:
        pl.semaphore_signal(barrier, inc=1, device_id={"rows": row, "mlp": column}, device_id_type=MESH)
    load_c.start()
    load_x.start()
    load_qkv.start()
    load_out.start()
    own_shard(0).start()
    own_shard(1).start()
    pl.semaphore_wait(barrier, len(partners))
    gather_copy(0, 0).start()
    gather_copy(1, 0).start()
    load_c.wait()
    for i in range(images):
        work[...] = jnp.zeros_like(work)
        work[0:patches, :] = c_ref[:, i, :]
        cot[i * tall : (i + 1) * tall, :] = work[...]
    cot_copy(0).start()
    cot_copy(1).start()
    load_x.wait()
    for i in range(images):
        forward_rows(i, x_ref, rank_ref, kept_ref, g1_ref, rw_ref, xp, keep, gate, h1, work)

    load_qkv.wait()

    @pl.loop(0, 3 * width // 256)
    def _(j):
        forward_qkv(j, h1, wqkv, qkv)

    @pl.loop(0, HEADS // 2)
    def _(p):
        for i in range(images):
            attend(p, i, width, tall, qkv, keep, probs, context, contextt)

        @pl.when(p == 2)
        def _():
            gather_forward(0)

        @pl.when(p == 5)
        def _():
            gather_forward(1)

    load_out.wait()

    @pl.loop(0, images)
    def _(i):
        forward_out(i, tall, context, wout, xp, keep, gate, g2_ref, attended, middle, tok)
        token_copy(i, 0).start()
        token_copy(i, 1).start()

    own_shard(0).wait()
    own_shard(1).wait()

    def at(block, number, do):
        @pl.when(block == number)
        def _():
            do()

    def before_sibling():
        for i in range(images):
            token_copy(i, 0).wait_recv()
        cot_copy(0).wait_recv()

    @pl.loop(0, 2 * images)
    def _(block):
        at(block, images, before_sibling)
        rows = ds(block * tall, tall)
        hid[rows, 0:part], gpre[rows, 0:part] = mlp_rows(tok[rows, :], cot[rows, :], w1[:, 0:part], w2[0:part, :])

    cot_copy(1).wait_recv()
    cot_copy(2).start()
    for mat in range(2):
        for kind in (1, 2, 3):
            gather_copy(mat, kind).wait_recv()
    for ref in (dg1, dg2, drw):
        ref[...] = jnp.zeros_like(ref)

    def before_near():
        cot_copy(2).wait_recv()
        gh2_to_sib.start()
        out_to_sib.start()

    def forward_token(i):
        token_copy(i, 1).wait_recv()
        token_copy(i, 2).start()

    def send_far(i):
        gh2_over(i).wait_recv()
        rows = ds(t_own + i * tall, tall)
        gh2_part[rows, :] = gh2_part[rows, :] + gh2_near[ds(i * tall, tall), :]
        gh2_far_copy(i).start()

    def before_last():
        send_far(0)
        token_copy(1, 2).wait_recv()

    @pl.loop(0, 8)
    def _(block):
        at(block, 3, lambda: forward_token(0))
        at(block, 4, before_near)
        at(block, 5, lambda: token_copy(0, 2).wait_recv())
        at(block, 6, lambda: forward_token(1))
        at(block, 7, before_last)
        inner = lax.rem(block, 5)
        swap = lax.div(block, 5) * (1 - 2 * inner + 3 * lax.div(inner * (inner - 1), 2))
        spot = block + swap
        rows = ds(spot * tall, tall)

        @pl.when(block < 2 * images)
        def _():
            hid[rows, part:], gpre[rows, part:] = mlp_rows(tok[rows, :], cot[rows, :], w1[:, part:], w2[part:, :])

        @pl.when(block >= 2 * images)
        def _():
            hid[rows, :], gpre[rows, :] = mlp_rows(tok[rows, :], cot[rows, :], w1[...], w2[...])

        share_out = dot_nn(hid[rows, :], w2[...])
        share_gh2 = dot_nt(gpre[rows, :], w1[...])

        @pl.when(block < images)
        def _():
            out[rows, :] = share_out
            gh2[rows, :] = share_gh2

        @pl.when(block >= images)
        def _():
            there = ds(lax.max(spot - images, 0) * tall, tall)
            out_part[there, :] = share_out.astype(BF)
            gh2_part[there, :] = share_gh2.astype(BF)

        at(block, 5, lambda: gh2_over(0).start())
        at(block, 7, lambda: gh2_over(1).start())

    out_over.start()
    turned[...] = tok[...].T
    for m in range(3):
        rows = slice(m * width // 3, (m + 1) * width // 3)
        total = dot_nn(turned[rows, :], gpre[...]).astype(BF)
        g1w[0, rows, :] = total[:, 0:part]
        g1w[1, rows, :] = total[:, part:]
    send_far(1)
    turned[...] = hid[...].T
    for m in range(2):
        g2w[m] = dot_nn(turned[m * part : (m + 1) * part, :], cot[...]).astype(BF)
    for k in range(2):
        for copy in fc_first(k):
            copy.start()

    def back_image(i):
        if i == 0:
            gh2_to_sib.wait_recv()
            for n in range(images):
                token_copy(n, 0).wait_send()
                token_copy(n, 1).wait_send()
            turned[:, 0:t_own] = h1[...].T
        gh2_far_copy(i).wait_recv()
        rows = pl.ds(i * tall, tall)
        gh2[rows, :] += gh2_sib[rows, :].astype(F32) + gh2_far[rows, :].astype(F32)
        back_rows(i, tall, cot, gh2, middle, keep, gate, attended, g2_ref, gh2, tok, glogit, dg2)
        context[rows, :] = dot_nt(tok[rows, :], wout[...]).astype(BF)

    def fill(j, total):
        for b in range(3):
            gw[j, b] = total[:, b * 128 : (b + 1) * 128].astype(BF)
        core_copy(j).start()

    def grad_out_half(n):
        total = 0.0
        for i in range(images):
            total = total + dot_nn(contextt[i], tok[i * tall : (i + 1) * tall, n * half : (n + 1) * half])
        fill(n, total)

    def pair_chunk(p):
        fill(p + 2, dot_nn(turned[:, 0:t_own], pair_columns(qkv, p, width)))

    def finish(i):
        rows = pl.ds(i * tall, tall)
        dy = dot_nt(qkv[rows, :], wqkv[...])
        back_input(i, tall, dy, glogit, rw_ref, xp, h1, g1_ref, gh2, x_ref, dg1, drw)
        if i == images - 1:
            store_gx.start()
            sma[0] = jnp.concatenate([dg1[...], drw[...], dg2[...], jnp.zeros((5, width), F32)], 0)
            small_copy(0).start()

    def small_step(step):
        if step < 3:
            small_copy(step - 1).wait()
            sma[step] = sma[step - 1] + smr[step - 1]
            small_copy(step).start()
        elif step == 3:
            small_copy(2).wait()
            smz[0] = sma[2] + smr[2]
            small_z(0).start()
        else:
            small_z(step - 4).wait()
            if step == 4:
                smz[2] = smz[0] + smz[1]
                small_z(1).start()
            else:
                small_out[...] = smz[2] + smz[3]

    def out_send():
        out_over.wait_recv()
        rows = pl.ds(t_own, t_own)
        out_part[rows, :] = out_part[rows, :] + out_near[...]
        out_far_copy.start()

    def out_finish(i):
        if i == 0:
            out_to_sib.wait_recv()
            out_far_copy.wait_recv()
        rows = pl.ds(i * tall, tall)
        total = middle[rows, :] + out[rows, :] + out_sib[rows, :].astype(F32) + out_far[rows, :].astype(F32)
        c_ref[:, i, :] = total.astype(BF)[0:patches, :]
        if i == images - 1:
            store_block.start()

    def fc_share_end():
        for copy in fc_share:
            copy.wait()
        for copy in fc_store(1):
            copy.start()

    single = {"fc": fc_finish, "fd": fc_widen, "fe": fc_to_sibling, "ff": fc_share_end, "osend": out_send}
    numbered = (("finish", finish), ("back", back_image), ("out", grad_out_half), ("fa", fc_fold_second),
                ("fb", fc_fold_third), ("g", small_step), ("o", out_finish))

    def perform(names):
        for name in names:
            if name in single:
                single[name]()
            elif name[0] == "c":
                chunk_step(int(name[1]), int(name[3]))
            else:
                do = next(f for head, f in numbered if name[:-1] == head)
                do(int(name[-1]))

    first, start, stop = ORDER.index("pairs0"), ORDER.index("pairs1"), ORDER.index("last2")
    perform(ORDER[:first])

    @pl.loop(0, HEADS // 4)
    def _(n):
        for p in (2 * n, 2 * n + 1):
            attend_back(p, 0, width, tall, qkv, probs, context)

    perform(ORDER[first + 1 : start])
    marks = [ORDER.index(name) for k in range(3) for name in ("pairs%d" % (k + 1), "last%d" % k)]

    @pl.loop(0, HEADS // 4)
    def _(n):
        for p in (2 * n, 2 * n + 1):
            attend_back(p, 1, width, tall, qkv, probs, context)
        pair_chunk(2 * n)
        for k in range(3):
            at(n, k, lambda k=k: perform(ORDER[marks[2 * k] + 1 : marks[2 * k + 1]]))
        pair_chunk(2 * n + 1)
        for k in range(2):
            at(n, k, lambda k=k: perform(ORDER[marks[2 * k + 1] + 1 : marks[2 * k + 2]]))

    perform(ORDER[stop + 1 :])
    for j in range(CHUNKS):
        chunk_store(j).wait()
    store_gx.wait()
    store_block.wait()
    for copy in fc_store(0) + fc_store(1):
        copy.wait()
    for level in range(2):
        for copy in fc_spread(level):
            copy.wait_send()
    for copy in fc_third:
        copy.wait_send()
    for mat in range(2):
        for kind in range(4):
            gather_copy(mat, kind).wait_send()
    for i in range(images):
        token_copy(i, 2).wait_send()
        gh2_over(i).wait_send()
        gh2_far_copy(i).wait_send()
    for hop in range(3):
        cot_copy(hop).wait_send()
    for copy in (gh2_to_sib, out_to_sib, out_over, out_far_copy):
        copy.wait_send()


VMEM = pl.BlockSpec(memory_space=pltpu.VMEM)
SMEM = pl.BlockSpec(memory_space=pltpu.SMEM)
ANY = pl.BlockSpec(memory_space=pl.ANY)


def widen_kernel(block, gx, gq, go, f1, f2, small, block_out, gx_out, gq_out, go_out, f1_out, f2_out, g1_out, rw_out, g2_out, kept1, kept2, sem):
    width = f1.shape[1]
    step = pl.program_id(0)
    arrive = [pltpu.make_async_copy(src, held, sem.at[k]) for k, (src, held) in enumerate(((block, kept1), (gx, kept2)))]
    leave = [pltpu.make_async_copy(held, dst, sem.at[2 + k]) for k, (held, dst) in enumerate(((kept1, block_out), (kept2, gx_out)))]

    @pl.when(step == 0)
    def _():
        for copy in arrive:
            copy.start()

    @pl.when(step == 2)
    def _():
        for come, go in zip(arrive, leave):
            come.wait()
            go.start()

    @pl.when(step == pl.num_programs(0) - 1)
    def _():
        for copy in leave:
            copy.wait()

    for b in range(3):
        gq_out[:, b * width : (b + 1) * width] = gq[b].astype(F32)
    for b in range(go.shape[0]):
        go_out[:, b * 128 : (b + 1) * 128] = go[b].astype(F32)
    f1_out[...] = f1[...].astype(F32)
    f2_out[...] = f2[...].astype(F32)
    g1_out[...], rw_out[...], g2_out[...] = small[0], small[1], small[2]


def widen(block, gx, gq, go, f1, f2, small):
    width = f1.shape[0]
    step = 128
    tokens = jax.ShapeDtypeStruct(block.shape, BF)

    def rows(*tail):
        return pl.BlockSpec((step,) + tail, lambda i: (i, 0))

    def inner(lead, tail):
        return pl.BlockSpec((lead, step, tail), lambda i: (0, i, 0))

    return pl.pallas_call(
        widen_kernel,
        grid=(width // step,),
        out_shape=[tokens, tokens] + [jax.ShapeDtypeStruct((width, n), F32) for n in (3 * width, width, width, width)]
        + [jax.ShapeDtypeStruct((width,), F32)] * 3,
        in_specs=[ANY, ANY, inner(3, width), inner(6, 128), rows(width), rows(width), pl.BlockSpec((8, width), lambda i: (0, 0))],
        out_specs=[ANY, ANY, rows(3 * width), rows(width), rows(width), rows(width)] + [pl.BlockSpec((width,), lambda i: (0,))] * 3,
        scratch_shapes=[pltpu.VMEM(block.shape, BF), pltpu.VMEM(block.shape, BF), pltpu.SemaphoreType.DMA((4,))],
        compiler_params=pltpu.CompilerParams(vmem_limit_bytes=63 * 1024 * 1024),
        name="widen",
    )(block, gx, gq, go, f1, f2, small)


def per_device(others, images, patch_rank, kept_count, ln1_gain, router_weight, w_qkv, w_out, ln2_gain, w_fc1, w_fc2, cotangent):
    count, patches, width = images.shape
    tall = -(-patches // 16) * 16
    t = count * tall
    part = w_fc1.shape[1] // 2
    half, eighth = width // 2, width // 8

    def bf(*dims):
        return pltpu.VMEM(dims, BF)

    def f32(*dims):
        return pltpu.VMEM(dims, F32)

    def sem(*dims):
        return pltpu.SemaphoreType.DMA(dims)

    scratch = [
        bf(patches, count, width), bf(patches, count, width),
        bf(width, 3 * width), bf(width, width), bf(width, 2 * part), bf(2 * part, width),
        bf(t, width), f32(t, 128), f32(t, 128), f32(t, 128), bf(t, width), bf(t, 3 * width),
        f32(count, HEADS, tall, tall), bf(count, width, tall), bf(t, width), f32(t, width), f32(t, width),
        bf(4 * t, width), bf(4 * t, width), bf(width, 4 * t), f32(t, width), f32(t, width),
        bf(3 * t, width), bf(3 * t, width), bf(t, width), bf(t, width), bf(t, width), bf(t, width), bf(t, width), bf(t, width),
        bf(4 * t, 2 * part), bf(4 * t, 2 * part), bf(tall, width),
        bf(2, width, part), bf(2, part, width),
        bf(2, width // 2, part), bf(2, part // 2, width), bf(2, width // 4, part), bf(2, part // 4, width),
        bf(2, width // 4, part), bf(2, part // 4, width), bf(width // 4, part), bf(part // 4, width),
        bf(CHUNKS, 3, width, 128), bf(CHUNKS, 3, half, 128), bf(CHUNKS, 3, 2 * eighth, 128), bf(CHUNKS, 3, eighth, 128),
        bf(CHUNKS, 3, eighth // 2, 128), bf(CHUNKS, 3, eighth // 2, 128),
        f32(1, width), f32(1, width), f32(1, width), f32(3, 8, width), f32(3, 8, width), f32(4, 8, width),
        sem(8), sem(2, 4), sem(2, 4), sem(count, 3), sem(count, 3), sem(3), sem(3), sem(8), sem(8),
        sem(2, 2), sem(2, 2), sem(2, 2), sem(2, 2), sem(2), sem(2),
        sem(2, 2), sem(2, 2), sem(2, 2), sem(2), sem(2), pltpu.SemaphoreType.REGULAR((2,)), pltpu.SemaphoreType.REGULAR((CHUNKS, 4)),
        sem(CHUNKS, 9), sem(CHUNKS, 9), sem(CHUNKS),
        sem(3), sem(3), sem(2), sem(2),
    ]

    def struct(*dims, dtype=BF):
        return jax.ShapeDtypeStruct(dims, dtype)

    block, gx, gq, go, f1, f2, small = pl.pallas_call(
        mega_kernel,
        out_shape=[
            struct(patches, count, width), struct(patches, count, width), struct(3, width, width), struct(6, width, 128),
            struct(width, 2 * part), struct(2 * part, width), struct(8, width, dtype=F32),
        ],
        in_specs=[ANY, VMEM, SMEM, VMEM, VMEM, ANY, ANY, VMEM, ANY, ANY, ANY],
        out_specs=[ANY, ANY, ANY, ANY, ANY, ANY, VMEM],
        scratch_shapes=scratch,
        compiler_params=pltpu.CompilerParams(
            collective_id=0, has_side_effects=True, vmem_limit_bytes=64 * 1024 * 1024
        ),
        name="block",
    )(images.transpose(1, 0, 2), patch_rank, kept_count, ln1_gain, router_weight, w_qkv, w_out, ln2_gain, w_fc1, w_fc2,
      cotangent.transpose(1, 0, 2))
    block, gx, gq, go, f1, f2, g1, rw, g2 = widen(block, gx, gq, go, f1, f2, small)
    if others:
        gq, go, f1, f2, g1, rw, g2 = lax.psum((gq, go, f1, f2, g1, rw, g2), "rows", axis_index_groups=others)
    return block.transpose(1, 0, 2), gx.transpose(1, 0, 2), g1, rw, gq, go, g2, f1, f2


def solution(mesh):
    rows = mesh.shape["rows"]
    others = [[8 * g + i for g in range(rows // 8)] for i in range(8)] if rows > 8 else None
    return jax.shard_map(
        functools.partial(per_device, others),
        mesh=mesh,
        in_specs=(
            P(("rows", "mlp"), None, None), P(("rows", "mlp"), None), P(("rows", "mlp")), P(), P(), P(), P(), P(),
            P(None, "mlp"), P("mlp", None), P(("rows", "mlp"), None, None),
        ),
        out_specs=(
            P(("rows", "mlp"), None, None), P(("rows", "mlp"), None, None), P(), P(), P(), P(), P(),
            P(None, "mlp"), P("mlp", None),
        ),
        check_vma=False,
    )
```

```python
import functools
import jax
import jax.numpy as jnp
from jax import lax
from jax.experimental import pallas as pl
from jax.experimental.pallas import tpu as pltpu
from jax.sharding import PartitionSpec as P

HEADS = 12
EPS = 1e-6
FILL = -1e30
BF = jnp.bfloat16
F32 = jnp.float32


def dot_nn(a, b):
    return lax.dot_general(a, b, (((1,), (0,)), ((), ())), preferred_element_type=F32)


def dot_nt(a, b):
    return lax.dot_general(a, b, (((1,), (1,)), ((), ())), preferred_element_type=F32)


def dot_tn(a, b):
    return lax.dot_general(a, b, (((0,), (0,)), ((), ())), preferred_element_type=F32)


def unit_rows(v):
    center = v - jnp.mean(v, -1, keepdims=True)
    scale = lax.rsqrt(jnp.mean(center * center, -1, keepdims=True) + EPS)
    return center * scale, scale


def norm_pull(dy, gain, unit, scale):
    du = dy * gain
    return scale * (
        du
        - jnp.mean(du, -1, keepdims=True)
        - unit * jnp.mean(du * unit, -1, keepdims=True)
    )


def half_mask(rows, h):
    lane = lax.broadcasted_iota(jnp.int32, (rows, 128), 1)
    return (lane < 64) if h == 0 else (lane >= 64)


def forward_rows(i, x_ref, rank_ref, kept_ref, g1_ref, rw_ref, xp, keep, gate, h1, work):
    patches = x_ref.shape[0]
    tall = xp.shape[0] // x_ref.shape[1]
    rows = pl.ds(pl.multiple_of(i * tall, 16), tall)
    work[...] = jnp.zeros_like(work)
    work[0:patches, :] = x_ref[:, i, :]
    v = work[...]
    xp[rows, :] = v
    kept = (rank_ref[pl.ds(i, 1), :] < kept_ref[i]).astype(F32)
    keep_row = jnp.concatenate([kept, jnp.zeros((1, 256 - patches), F32)], 1)
    keep_col = jnp.broadcast_to(keep_row, (128, 256)).T
    keep[rows, :] = keep_col[0:tall, :]
    unit, _ = unit_rows(v.astype(F32))
    low = (unit * g1_ref[...][None]).astype(BF)
    h1[rows, :] = low
    logit = jnp.sum(low.astype(F32) * rw_ref[...][None].astype(F32), -1, keepdims=True)
    gate[rows, :] = jnp.broadcast_to(jax.nn.sigmoid(logit), (tall, 128))


def forward_qkv(j, h1, wqkv, qkv):
    cols = pl.ds(pl.multiple_of(j * 256, 256), 256)
    qkv[:, cols] = dot_nn(h1[...], wqkv[:, cols]).astype(BF)


def attend(p, i, width, tall, qkv, keep, probs, context, contextt):
    rows = pl.ds(pl.multiple_of(i * tall, 16), tall)
    qc = pl.ds(pl.multiple_of(p * 128, 128), 128)
    kc = pl.ds(pl.multiple_of(width + p * 128, 128), 128)
    vc = pl.ds(pl.multiple_of(2 * width + p * 128, 128), 128)
    q, k, v = qkv[rows, qc], qkv[rows, kc], qkv[rows, vc]
    vt = v.T
    kept = keep[rows, 0:1] > 0.5
    outs = []
    for h in range(2):
        kh = jnp.where(half_mask(tall, h), k, jnp.zeros_like(k))
        s = jnp.where(kept, dot_nt(kh, q) * 0.125, FILL)
        e = jnp.exp(s - jnp.max(s, 0, keepdims=True))
        pr = e * (1.0 / jnp.sum(e, 0, keepdims=True))
        probs[i, p * 2 + h] = pr
        outs.append(dot_nn(vt[h * 64 : h * 64 + 64, :], pr.astype(BF)))
    ct = jnp.concatenate(outs, 0)
    contextt[i, pl.ds(pl.multiple_of(p * 128, 128), 128), :] = ct.astype(BF)
    context[rows, qc] = ct.T.astype(BF)


def forward_out(i, tall, context, wout, xp, keep, gate, g2_ref, attended, middle, h2):
    rows = pl.ds(pl.multiple_of(i * tall, 16), tall)
    att = dot_nn(context[rows, :], wout[...])
    attended[rows, :] = att
    mid = xp[rows, :].astype(F32) + keep[rows, 0:1] * gate[rows, 0:1] * att
    middle[rows, :] = mid
    unit, _ = unit_rows(mid)
    h2[rows, :] = (unit * g2_ref[...][None]).astype(BF)


def gelu_pair(pre):
    cdf = 0.5 * (1.0 + lax.erf(pre * 0.7071067811865476))
    pdf = jnp.exp(pre * pre * -0.5) * 0.3989422804014327
    return pre * cdf, cdf + pre * pdf


def mlp_rows(h, c, w1, w2):
    pre = dot_nn(h, w1)
    hidden, slope = gelu_pair(pre)
    grad = dot_nt(c, w2) * slope
    return hidden.astype(BF), grad.astype(BF)


def back_rows(i, tall, c_ref, gh2, middle, keep, gate, attended, g2_ref, gmid, gatt, glogit, dg2):
    rows = pl.ds(pl.multiple_of(i * tall, 16), tall)
    dy = gh2[rows, :]
    unit, scale = unit_rows(middle[rows, :])
    gm = c_ref[rows, :].astype(F32) + norm_pull(dy, g2_ref[...][None], unit, scale)
    gmid[rows, :] = gm
    dg2[...] += jnp.sum(dy * unit, 0, keepdims=True)
    k, g = keep[rows, 0:1], gate[rows, 0:1]
    kept = gm * k
    gatt[rows, :] = (kept * g).astype(BF)
    gl = jnp.sum(kept * attended[rows, :], -1, keepdims=True) * g * (1.0 - g)
    glogit[rows, :] = jnp.broadcast_to(gl, (tall, 128))


def attend_back(p, i, width, tall, qkv, probs, gctx):
    rows = pl.ds(pl.multiple_of(i * tall, 16), tall)
    qc = pl.ds(pl.multiple_of(p * 128, 128), 128)
    kc = pl.ds(pl.multiple_of(width + p * 128, 128), 128)
    vc = pl.ds(pl.multiple_of(2 * width + p * 128, 128), 128)
    q, k, v = qkv[rows, qc], qkv[rows, kc], qkv[rows, vc]
    gc = gctx[rows, qc]
    kt = k.T
    gv, gk, gq = 0.0, 0.0, []
    for h in range(2):
        mask = half_mask(tall, h)
        zero = jnp.zeros_like(v)
        pr = probs[i, p * 2 + h]
        gp = dot_nt(jnp.where(mask, v, zero), gc)
        gs = (pr * (gp - jnp.sum(pr * gp, 0, keepdims=True))).astype(BF)
        gv = gv + dot_nn(pr.astype(BF), jnp.where(mask, gc, zero))
        gk = gk + dot_nn(gs, jnp.where(mask, q, zero))
        gq.append(dot_nn(kt[h * 64 : h * 64 + 64, :], gs))
    qkv[rows, qc] = (jnp.concatenate(gq, 0).T * 0.125).astype(BF)
    qkv[rows, kc] = (gk * 0.125).astype(BF)
    qkv[rows, vc] = gv.astype(BF)


def pair_columns(wqkv, p, width):
    return jnp.concatenate(
        [wqkv[:, pl.ds(pl.multiple_of(b * width + p * 128, 128), 128)] for b in range(3)], 1
    )


def back_input(i, tall, dy, glogit, rw_ref, xp, h1, g1_ref, gmid, gx_ref, dg1, drw):
    rows = pl.ds(pl.multiple_of(i * tall, 16), tall)
    patches = gx_ref.shape[0]
    gl = glogit[rows, 0:1]
    dy = dy + gl * rw_ref[...][None].astype(F32)
    unit, scale = unit_rows(xp[rows, :].astype(F32))
    dg1[...] += jnp.sum(dy * unit, 0, keepdims=True)
    drw[...] += jnp.sum(h1[rows, :].astype(F32) * gl, 0, keepdims=True)
    out = gmid[rows, :] + norm_pull(dy, g1_ref[...][None], unit, scale)
    gx_ref[:, i, :] = out.astype(BF)[0:patches, :]

MESH = pl.DeviceIdType.MESH
CHUNKS = HEADS // 2 + 2
WIDEN = 8
PATHS = ("xzy", "zxy", "yzx", "xzy", "yxz", "xyz", "yzx", "yzx")
ORDER = (
    "osend", "back0", "pairs0", "back1", "pairs1", "fa10", "fa11", "last0", "pairs2", "last1", "fa01", "c2.1",
    "pairs3", "fb1", "c4.1", "last2", "c5.1", "out1", "c3.1", "c2.2", "fa00", "out0", "finish0", "c6.1", "c1.1",
    "c4.2", "c0.1", "c5.2", "finish1", "c3.2", "c7.1", "c6.2", "c2.3", "c1.2", "fb0", "c5.3", "fc", "c0.2", "c4.3",
    "c5.4", "g1", "c1.3", "c6.3", "c2.4", "c3.3", "c7.2", "c0.3", "c4.4", "fd", "c1.4", "c5.5", "c0.4", "c4.5",
    "c6.4", "c7.3", "c3.4", "c5.6", "g2", "c2.5", "c0.5", "c4.6", "c7.4", "c6.5", "fe", "c1.5", "c2.6", "c5.7",
    "c3.5", "c4.7", "c0.6", "g3", "c6.6", "c7.5", "c3.6", "c2.7", "c1.6", "c0.7", "c7.6", "c5.8", "ff", "c6.7",
    "c4.8", "o0", "c1.7", "g4", "c3.7", "c2.8", "c7.7", "c0.8", "c4.9", "c6.8", "c1.8", "c3.8", "c7.8", "c0.9",
    "c5.9", "c1.9", "g5", "o1", "c6.9", "c2.9", "c3.9", "c7.9",
)


def mega_kernel(
    x_hbm, rank_ref, kept_ref, g1_ref, rw_ref, wqkv_hbm, wout_hbm, g2_ref, fc1, fc2, c_hbm,
    block_hbm, gx_hbm, gq_out, go_out, f1_out, f2_out, small_out,
    x_ref, c_ref, wqkv, wout, w1, w2, xp, keep, gate, glogit, h1, h1t, qkv, probs, contextt, context, attended, middle,
    tok, cot, turned, out, gh2, out_part, gh2_part, out_sib, gh2_sib, out_near, gh2_near, out_far, gh2_far, hid, gpre, work,
    g1w, g2w, r1a, r1b, r2a, r2b, fz1, fz2, rz1, rz2,
    gw, q0, q1, q2, q3, far, dg1, dg2, drw, sma, smr, smz,
    lsem, gsend, grecv, hsend, hrecv, csend, crecv, esend, erecv, s1s, s1r, s2s, s2r, s3s, s3r, fs, fr, floc, ssib, rsib, free, chunk_free,
    qs, qr, qloc, sms, smrs, smzs, smzr,
):
    patches, images, width = x_ref.shape
    t_own = xp.shape[0]
    tall = t_own // images
    half = width // 2
    part = w1.shape[1] // 2
    parts = (q0, q1, q2, q3)
    quarter = (width // 4, part // 4)
    r = lax.axis_index("rows")
    z = lax.axis_index("mlp")
    c, x, y = lax.rem(r, 2), lax.rem(lax.div(r, 2), 2), lax.rem(lax.div(r, 4), 2)
    r_sib, r_x, r_y = r + 1 - 2 * c, r + 2 - 4 * x, r + 4 - 8 * y
    r_diag = r_x + r_y - r
    z_pair, z_far = z + 1 - 2 * lax.rem(z, 2), z + 2 - 4 * lax.div(z, 2)
    q = 2 * y + x

    def ds(start, size):
        return pl.ds(pl.multiple_of(start, 16), size)

    def lanes(start, size):
        return pl.ds(pl.multiple_of(start, 128), size)

    def remote(src, dst, send, recv, row, column):
        return pltpu.make_async_remote_copy(
            src_ref=src, dst_ref=dst, send_sem=send, recv_sem=recv,
            device_id={"rows": row, "mlp": column}, device_id_type=MESH,
        )

    def release(semaphore, row):
        pl.semaphore_signal(semaphore, inc=1, device_id={"rows": row, "mlp": z}, device_id_type=MESH)

    def gather_copy(mat, kind):
        size = quarter[mat]
        sems = gsend.at[mat, kind], grecv.at[mat, kind]
        if mat == 0:
            place = w1.at[ds(q * size, size), pl.ds(part, part)]
            own = fc1.at[ds(q * size, size), lanes(c * part, part)]
        else:
            place = w2.at[ds(part + q * size, size), :]
            own = fc2.at[ds(c * part + q * size, size), :]
        if kind == 0:
            return remote(own, place, *sems, r, z_far)
        return remote(place, place, *sems, (r_x, r_y, r_diag)[kind - 1], z)

    def gather_forward(mat):
        gather_copy(mat, 0).wait_recv()
        for kind in (1, 2, 3):
            gather_copy(mat, kind).start()

    def own_shard(mat):
        if mat == 0:
            return pltpu.make_async_copy(fc1.at[:, lanes(c * part, part)], w1.at[:, pl.ds(0, part)], lsem.at[0])
        return pltpu.make_async_copy(fc2.at[ds(c * part, part), :], w2.at[pl.ds(0, part), :], lsem.at[1])

    load_qkv = pltpu.make_async_copy(wqkv_hbm, wqkv, lsem.at[2])
    load_out = pltpu.make_async_copy(wout_hbm, wout, lsem.at[3])
    load_x = pltpu.make_async_copy(x_hbm, x_ref, lsem.at[4])
    load_c = pltpu.make_async_copy(c_hbm, c_ref, lsem.at[5])
    store_block = pltpu.make_async_copy(c_ref, block_hbm, lsem.at[6])
    store_gx = pltpu.make_async_copy(x_ref, gx_hbm, lsem.at[7])

    def token_copy(i, hop):
        start = (0, 0, 2 * t_own)[hop] + i * tall
        src, dst = tok.at[ds(start, tall), :], tok.at[ds((1, 2, 3)[hop] * t_own + i * tall, tall), :]
        row, column = (r, z_pair) if hop == 1 else (r_sib, z)
        return remote(src, dst, hsend.at[i, hop], hrecv.at[i, hop], row, column)

    def cot_copy(hop):
        src, dst = cot.at[ds((0, 0, 2)[hop] * t_own, t_own), :], cot.at[ds((1, 2, 3)[hop] * t_own, t_own), :]
        row, column = (r, z_pair) if hop == 1 else (r_sib, z)
        return remote(src, dst, csend.at[hop], crecv.at[hop], row, column)

    gh2_to_sib = remote(gh2_part.at[ds(0, t_own), :], gh2_sib, esend.at[0], erecv.at[0], r_sib, z)
    out_to_sib = remote(out_part.at[ds(0, t_own), :], out_sib, esend.at[1], erecv.at[1], r_sib, z)
    out_over = remote(out_part.at[ds(2 * t_own, t_own), :], out_near, esend.at[2], erecv.at[2], r_sib, z)
    out_far_copy = remote(out_part.at[ds(t_own, t_own), :], out_far, esend.at[3], erecv.at[3], r, z_pair)

    def gh2_over(i):
        src = gh2_part.at[ds(2 * t_own + i * tall, tall), :]
        return remote(src, gh2_near.at[ds(i * tall, tall), :], esend.at[4 + i], erecv.at[4 + i], r_sib, z)

    def gh2_far_copy(i):
        src = gh2_part.at[ds(t_own + i * tall, tall), :]
        return remote(src, gh2_far.at[ds(i * tall, tall), :], esend.at[6 + i], erecv.at[6 + i], r, z_pair)

    fc_whole, fc_half, fc_quarter, fc_done, fc_far = (g1w, g2w), (r1a, r1b), (r2a, r2b), (fz1, fz2), (rz1, rz2)
    fc_rows = ((width // 2, width // 4), (part // 2, part // 4))

    def fc_ways(k, m):
        shard = lax.div(z, 2) if k == 0 else 1 - lax.div(z, 2)
        turn = lax.rem(shard + m, 2)
        return r_x + (r_y - r_x) * turn, r_y + (r_x - r_y) * turn, x + (y - x) * turn, y + (x - y) * turn

    def fc_first(k, m):
        n1, _, a1, _ = fc_ways(k, m)
        rows, _ = fc_rows[m]
        src = fc_whole[m].at[k, ds((1 - a1) * rows, rows), :]
        return remote(src, fc_half[m].at[k], s1s.at[k, m], s1r.at[k, m], n1, z)

    def fc_second(k, m):
        _, n2, a1, a2 = fc_ways(k, m)
        rows, less = fc_rows[m]
        src = fc_whole[m].at[k, ds(a1 * rows + (1 - a2) * less, less), :]
        return remote(src, fc_quarter[m].at[k], s2s.at[k, m], s2r.at[k, m], n2, z)

    fc_third = [remote(fc_done[m].at[1], fc_far[m], s3s.at[m], s3r.at[m], r, z_far) for m in range(2)]

    def fc_spread(level, m):
        n1, n2, a1, a2 = fc_ways(0, m)
        rows, less = fc_rows[m]
        place = ds(a1 * rows + a2 * less, less) if level == 0 else ds(a1 * rows, rows)
        held = fc_whole[m].at[0, place, :]
        return remote(held, held, fs.at[level, m], fr.at[level, m], n2 if level == 0 else n1, z)

    fc_share = (
        remote(g1w.at[0], g1w.at[1], ssib.at[0], rsib.at[0], r_sib, z),
        remote(g2w.at[0], g2w.at[1], ssib.at[1], rsib.at[1], r_sib, z),
    )

    def fc_store(k):
        core = c + k - 2 * c * k
        return (
            pltpu.make_async_copy(g1w.at[k], f1_out.at[:, lanes(core * part, part)], floc.at[k, 0]),
            pltpu.make_async_copy(g2w.at[k], f2_out.at[ds(core * part, part), :], floc.at[k, 1]),
        )

    def fc_fold_second(k, m):
        fc_first(k, m).wait_recv()
        _, _, a1, a2 = fc_ways(k, m)
        rows, less = fc_rows[m]
        place, whole = ds(a1 * rows + (1 - a2) * less, less), fc_whole[m]
        whole[k, place, :] = whole[k, place, :] + fc_half[m][k, ds((1 - a2) * less, less), :]
        fc_second(k, m).start()

    def fc_fold_third(k):
        for m in range(2):
            fc_second(k, m).wait_recv()
            _, _, a1, a2 = fc_ways(k, m)
            rows, less = fc_rows[m]
            total = fc_whole[m][k, ds(a1 * rows + a2 * less, less), :].astype(F32)
            total = total + fc_half[m][k, ds(a2 * less, less), :].astype(F32) + fc_quarter[m][k].astype(F32)
            fc_done[m][k] = total.astype(BF)
        if k == 1:
            for copy in fc_third:
                copy.start()
        for m in range(2):
            fc_first(k, m).wait_send()
            fc_second(k, m).wait_send()
        if k == 1:
            release(free.at[0], r_sib)
        else:
            release(free.at[1], r_x)
            release(free.at[1], r_y)

    def fc_finish():
        for copy in fc_third:
            copy.wait_recv()
        pl.semaphore_wait(free.at[1], 2)
        for m in range(2):
            _, _, a1, a2 = fc_ways(0, m)
            rows, less = fc_rows[m]
            fc_whole[m][0, ds(a1 * rows + a2 * less, less), :] = fc_done[m][0] + fc_far[m][...]
            fc_spread(0, m).start()

    def fc_widen():
        for m in range(2):
            fc_spread(0, m).wait_recv()
        for m in range(2):
            fc_spread(1, m).start()

    def fc_to_sibling():
        for m in range(2):
            fc_spread(1, m).wait_recv()
        pl.semaphore_wait(free.at[0], 1)
        for copy in fc_share + fc_store(0):
            copy.start()

    sizes = tuple(width >> level for level in range(1, 5))

    def hops(j):
        ways = {"x": (r_x, z, x), "y": (r_y, z, y), "z": (r, z_pair, lax.rem(z, 2))}
        return [(r_sib, z, c)] + [ways[axis] for axis in PATHS[j]]

    def base(path, level):
        start = 0
        for (_, _, bit), size in zip(path[:level], sizes):
            start = start + bit * size
        return start

    def core_copy(j):
        src = gw.at[j, :, ds((1 - c) * half, half), :]
        return remote(src, parts[0].at[j], qs.at[j, 0], qr.at[j, 0], r_sib, z)

    def chunk_copy(j, step):
        path = hops(j)
        if step == 0:
            return core_copy(j)
        if step < 4:
            row, column, bit = path[step]
            start = base(path, step) + (1 - bit) * sizes[step]
            return remote(gw.at[j, :, ds(start, sizes[step]), :], parts[step].at[j], qs.at[j, step], qr.at[j, step], row, column)
        if step == 4:
            own = gw.at[j, :, ds(base(path, 4), sizes[3]), :]
            return remote(own, far.at[j], qs.at[j, 4], qr.at[j, 4], r, z_far)
        level = 8 - step
        row, column, _ = path[level]
        held = gw.at[j, :, ds(base(path, level + 1), sizes[level]), :]
        return remote(held, held, qs.at[j, step], qr.at[j, step], row, column)

    def chunk_store(j):
        if j < 2:
            place = go_out.at[pl.ds(3 * j, 3), :, :]
        else:
            place = gq_out.at[:, :, pl.ds((j - 2) * 128, 128)]
        return pltpu.make_async_copy(gw.at[j], place, qloc.at[j])

    def chunk_step(j, step):
        path = hops(j)
        chunk_copy(j, step - 1).wait()
        if step <= 4:
            row, column, _ = path[step - 1]
            pl.semaphore_signal(
                chunk_free.at[j, step - 1], inc=1, device_id={"rows": row, "mlp": column}, device_id_type=MESH
            )
            start = base(path, min(step, 4))
            if step < 4:
                start = base(path, step) + (1 - path[step][2]) * sizes[step]
            size = sizes[min(step, 3)]
            total = gw[j, :, ds(start, size), :].astype(F32)
            for level in range(step):
                total = total + parts[level][j, :, ds(start - base(path, level + 1), size), :].astype(F32)
            gw[j, :, ds(start, size), :] = total.astype(BF)
        if step == 5:
            own = ds(base(path, 4), sizes[3])
            gw[j, :, own, :] = gw[j, :, own, :] + far[j]
        if 5 <= step <= 8:
            pl.semaphore_wait(chunk_free.at[j, 8 - step], 1)
        if step <= 8:
            chunk_copy(j, step).start()
        else:
            chunk_store(j).start()

    def small_copy(level):
        row = (r_sib, r_x, r_y)[level]
        return remote(sma.at[level], smr.at[level], sms.at[level], smrs.at[level], row, z)

    def small_z(step):
        src, dst = smz.at[2 * step], smz.at[2 * step + 1]
        return remote(src, dst, smzs.at[step], smzr.at[step], r, (z_pair, z_far)[step])

    barrier = pltpu.get_barrier_semaphore()
    partners = ((r_sib, z), (r_x, z), (r_y, z), (r_diag, z), (r, z_pair), (r, z_far))
    for row, column in partners:
        pl.semaphore_signal(barrier, inc=1, device_id={"rows": row, "mlp": column}, device_id_type=MESH)
    load_c.start()
    load_x.start()
    load_qkv.start()
    load_out.start()
    own_shard(0).start()
    own_shard(1).start()
    pl.semaphore_wait(barrier, len(partners))
    gather_copy(0, 0).start()
    gather_copy(1, 0).start()
    load_c.wait()
    for i in range(images):
        work[...] = jnp.zeros_like(work)
        work[0:patches, :] = c_ref[:, i, :]
        cot[i * tall : (i + 1) * tall, :] = work[...]
    cot_copy(0).start()
    cot_copy(1).start()
    load_x.wait()
    for i in range(images):
        forward_rows(i, x_ref, rank_ref, kept_ref, g1_ref, rw_ref, xp, keep, gate, h1, work)

    load_qkv.wait()

    @pl.loop(0, 3 * width // 256)
    def _(j):
        forward_qkv(j, h1, wqkv, qkv)

    @pl.loop(0, HEADS // 2)
    def _(p):
        for i in range(images):
            attend(p, i, width, tall, qkv, keep, probs, context, contextt)

        @pl.when(p == 2)
        def _():
            gather_forward(0)

        @pl.when(p == 5)
        def _():
            gather_forward(1)

    load_out.wait()

    @pl.loop(0, images)
    def _(i):
        forward_out(i, tall, context, wout, xp, keep, gate, g2_ref, attended, middle, tok)
        token_copy(i, 0).start()
        token_copy(i, 1).start()

    own_shard(0).wait()
    own_shard(1).wait()

    def at(block, number, do):
        @pl.when(block == number)
        def _():
            do()

    def before_sibling():
        for i in range(images):
            token_copy(i, 0).wait_recv()
        cot_copy(0).wait_recv()

    h1t[...] = h1[...].T

    @pl.loop(0, 2 * images)
    def _(block):
        at(block, images, before_sibling)
        rows = ds(block * tall, tall)
        hid[rows, 0:part], gpre[rows, 0:part] = mlp_rows(tok[rows, :], cot[rows, :], w1[:, 0:part], w2[0:part, :])

    cot_copy(1).wait_recv()
    cot_copy(2).start()
    for mat in range(2):
        for kind in (1, 2, 3):
            gather_copy(mat, kind).wait_recv()
    for ref in (dg1, dg2, drw):
        ref[...] = jnp.zeros_like(ref)

    def before_near():
        cot_copy(2).wait_recv()
        gh2_to_sib.start()
        out_to_sib.start()

    def forward_token(i):
        token_copy(i, 1).wait_recv()
        token_copy(i, 2).start()

    def send_far(i):
        gh2_over(i).wait_recv()
        rows = ds(t_own + i * tall, tall)
        gh2_part[rows, :] = gh2_part[rows, :] + gh2_near[ds(i * tall, tall), :]
        gh2_far_copy(i).start()

    def before_last():
        send_far(0)
        token_copy(1, 2).wait_recv()

    @pl.loop(0, 8)
    def _(block):
        at(block, 3, lambda: forward_token(0))
        at(block, 4, before_near)
        at(block, 5, lambda: token_copy(0, 2).wait_recv())
        at(block, 6, lambda: forward_token(1))
        at(block, 7, before_last)
        inner = lax.rem(block, 5)
        swap = lax.div(block, 5) * (1 - 2 * inner + 3 * lax.div(inner * (inner - 1), 2))
        spot = block + swap
        rows = ds(spot * tall, tall)

        @pl.when(block < 2 * images)
        def _():
            hid[rows, part:], gpre[rows, part:] = mlp_rows(tok[rows, :], cot[rows, :], w1[:, part:], w2[part:, :])

        @pl.when(block >= 2 * images)
        def _():
            hid[rows, :], gpre[rows, :] = mlp_rows(tok[rows, :], cot[rows, :], w1[...], w2[...])

        share_out = dot_nn(hid[rows, :], w2[...])
        share_gh2 = dot_nt(gpre[rows, :], w1[...])

        @pl.when(block < images)
        def _():
            out[rows, :] = share_out
            gh2[rows, :] = share_gh2

        @pl.when(block >= images)
        def _():
            there = ds(lax.max(spot - images, 0) * tall, tall)
            out_part[there, :] = share_out.astype(BF)
            gh2_part[there, :] = share_gh2.astype(BF)

        at(block, 5, lambda: gh2_over(0).start())
        at(block, 7, lambda: gh2_over(1).start())

    out_over.start()
    turned[...] = tok[...].T
    for m in range(3):
        rows = slice(m * width // 3, (m + 1) * width // 3)
        total = dot_nn(turned[rows, :], gpre[...]).astype(BF)
        g1w[0, rows, :] = total[:, 0:part]
        g1w[1, rows, :] = total[:, part:]
    for k in range(2):
        fc_first(k, 0).start()
    send_far(1)
    turned[...] = hid[...].T
    for m in range(2):
        g2w[m] = dot_nn(turned[m * part : (m + 1) * part, :], cot[...]).astype(BF)
    for k in range(2):
        fc_first(k, 1).start()

    def back_image(i):
        if i == 0:
            gh2_to_sib.wait_recv()
            for n in range(images):
                token_copy(n, 0).wait_send()
                token_copy(n, 1).wait_send()
        gh2_far_copy(i).wait_recv()
        rows = pl.ds(i * tall, tall)
        gh2[rows, :] += gh2_sib[rows, :].astype(F32) + gh2_far[rows, :].astype(F32)
        back_rows(i, tall, cot, gh2, middle, keep, gate, attended, g2_ref, gh2, tok, glogit, dg2)
        context[rows, :] = dot_nt(tok[rows, :], wout[...]).astype(BF)

    def fill(j, total):
        for b in range(3):
            gw[j, b] = total[:, b * 128 : (b + 1) * 128].astype(BF)
        core_copy(j).start()

    def grad_out_half(n):
        total = 0.0
        for i in range(images):
            total = total + dot_nn(contextt[i], tok[i * tall : (i + 1) * tall, n * half : (n + 1) * half])
        fill(n, total)

    def pair_chunk(p):
        fill(p + 2, dot_nn(h1t[...], pair_columns(qkv, p, width)))

    def finish(i):
        rows = pl.ds(i * tall, tall)
        dy = dot_nt(qkv[rows, :], wqkv[...])
        back_input(i, tall, dy, glogit, rw_ref, xp, h1, g1_ref, gh2, x_ref, dg1, drw)
        if i == images - 1:
            store_gx.start()
            sma[0] = jnp.concatenate([dg1[...], drw[...], dg2[...], jnp.zeros((5, width), F32)], 0)
            small_copy(0).start()

    def small_step(step):
        if step < 3:
            small_copy(step - 1).wait()
            sma[step] = sma[step - 1] + smr[step - 1]
            small_copy(step).start()
        elif step == 3:
            small_copy(2).wait()
            smz[0] = sma[2] + smr[2]
            small_z(0).start()
        else:
            small_z(step - 4).wait()
            if step == 4:
                smz[2] = smz[0] + smz[1]
                small_z(1).start()
            else:
                small_out[...] = smz[2] + smz[3]

    def out_send():
        out_over.wait_recv()
        rows = pl.ds(t_own, t_own)
        out_part[rows, :] = out_part[rows, :] + out_near[...]
        out_far_copy.start()

    def out_finish(i):
        if i == 0:
            out_to_sib.wait_recv()
            out_far_copy.wait_recv()
        rows = pl.ds(i * tall, tall)
        total = middle[rows, :] + out[rows, :] + out_sib[rows, :].astype(F32) + out_far[rows, :].astype(F32)
        c_ref[:, i, :] = total.astype(BF)[0:patches, :]
        if i == images - 1:
            store_block.start()

    def fc_share_end():
        for copy in fc_share:
            copy.wait()
        for copy in fc_store(1):
            copy.start()

    single = {"fc": fc_finish, "fd": fc_widen, "fe": fc_to_sibling, "ff": fc_share_end, "osend": out_send}
    numbered = (("finish", finish), ("back", back_image), ("out", grad_out_half),
                ("fb", fc_fold_third), ("g", small_step), ("o", out_finish))

    def perform(names):
        for name in names:
            if name in single:
                single[name]()
            elif name[:2] == "fa":
                fc_fold_second(int(name[2]), int(name[3]))
            elif name[0] == "c":
                chunk_step(int(name[1]), int(name[3]))
            else:
                do = next(f for head, f in numbered if name[:-1] == head)
                do(int(name[-1]))

    first, start, stop = ORDER.index("pairs0"), ORDER.index("pairs1"), ORDER.index("last2")
    perform(ORDER[:first])

    @pl.loop(0, HEADS // 4)
    def _(n):
        for p in (2 * n, 2 * n + 1):
            attend_back(p, 0, width, tall, qkv, probs, context)

    perform(ORDER[first + 1 : start])
    marks = [ORDER.index(name) for k in range(3) for name in ("pairs%d" % (k + 1), "last%d" % k)]

    @pl.loop(0, HEADS // 4)
    def _(n):
        for p in (2 * n, 2 * n + 1):
            attend_back(p, 1, width, tall, qkv, probs, context)
        pair_chunk(2 * n)
        for k in range(3):
            at(n, k, lambda k=k: perform(ORDER[marks[2 * k] + 1 : marks[2 * k + 1]]))
        pair_chunk(2 * n + 1)
        for k in range(2):
            at(n, k, lambda k=k: perform(ORDER[marks[2 * k + 1] + 1 : marks[2 * k + 2]]))

    perform(ORDER[stop + 1 :])
    for j in range(CHUNKS):
        chunk_store(j).wait()
    store_gx.wait()
    store_block.wait()
    for copy in fc_store(0) + fc_store(1):
        copy.wait()
    for level in range(2):
        for m in range(2):
            fc_spread(level, m).wait_send()
    for copy in fc_third:
        copy.wait_send()
    for mat in range(2):
        for kind in range(4):
            gather_copy(mat, kind).wait_send()
    for i in range(images):
        token_copy(i, 2).wait_send()
        gh2_over(i).wait_send()
        gh2_far_copy(i).wait_send()
    for hop in range(3):
        cot_copy(hop).wait_send()
    for copy in (gh2_to_sib, out_to_sib, out_over, out_far_copy):
        copy.wait_send()


VMEM = pl.BlockSpec(memory_space=pltpu.VMEM)
SMEM = pl.BlockSpec(memory_space=pltpu.SMEM)
ANY = pl.BlockSpec(memory_space=pl.ANY)


def widen_kernel(
    block, gx, gq, go, f1, f2, small, block_out, gx_out, gq_out, go_out, f1_out, f2_out, g1_out, rw_out, g2_out,
    block_held, gx_held, gq_held, go_held, f1_held, f2_held, gq_wide, go_wide, f1_wide, f2_wide, load_sem, store_sem, pass_sem,
):
    width = f1.shape[1]
    step = width // WIDEN

    def rows_of(i):
        return pl.ds(pl.multiple_of(i * step, 16), step)

    def loads(i):
        rows = rows_of(i)
        pairs = (
            (gq.at[:, rows, :], gq_held.at[:, rows, :]), (go.at[:, rows, :], go_held.at[:, rows, :]),
            (f1.at[rows, :], f1_held.at[rows, :]), (f2.at[rows, :], f2_held.at[rows, :]),
        )
        return [pltpu.make_async_copy(src, dst, load_sem.at[i, k]) for k, (src, dst) in enumerate(pairs)]

    def stores(i):
        rows = rows_of(i)
        pairs = ((gq_wide, gq_out), (go_wide, go_out), (f1_wide, f1_out), (f2_wide, f2_out))
        return [
            pltpu.make_async_copy(src.at[rows, :], dst.at[rows, :], store_sem.at[i, k]) for k, (src, dst) in enumerate(pairs)
        ]

    arrive = [pltpu.make_async_copy(src, dst, pass_sem.at[k]) for k, (src, dst) in enumerate(((block, block_held), (gx, gx_held)))]
    leave = [
        pltpu.make_async_copy(src, dst, pass_sem.at[2 + k]) for k, (src, dst) in enumerate(((block_held, block_out), (gx_held, gx_out)))
    ]

    @pl.loop(0, WIDEN)
    def _(i):
        for copy in loads(i):
            copy.start()

    for copy in arrive:
        copy.start()
    g1_out[...], rw_out[...], g2_out[...] = small[0], small[1], small[2]

    @pl.loop(0, WIDEN)
    def _(i):
        rows = rows_of(i)
        for copy in loads(i):
            copy.wait()
        for b in range(3):
            gq_wide[rows, b * width : (b + 1) * width] = gq_held[b, rows, :].astype(F32)
        for b in range(go.shape[0]):
            go_wide[rows, b * 128 : (b + 1) * 128] = go_held[b, rows, :].astype(F32)
        f1_wide[rows, :] = f1_held[rows, :].astype(F32)
        f2_wide[rows, :] = f2_held[rows, :].astype(F32)
        for copy in stores(i):
            copy.start()

    for come, go_on in zip(arrive, leave):
        come.wait()
        go_on.start()

    @pl.loop(0, WIDEN)
    def _(i):
        for copy in stores(i):
            copy.wait()

    for copy in leave:
        copy.wait()


def widen(block, gx, gq, go, f1, f2, small):
    width = f1.shape[0]
    tokens = jax.ShapeDtypeStruct(block.shape, BF)
    wide = [(width, 3 * width), (width, width), (width, width), (width, width)]
    return pl.pallas_call(
        widen_kernel,
        out_shape=[tokens, tokens] + [jax.ShapeDtypeStruct(dims, F32) for dims in wide] + [jax.ShapeDtypeStruct((width,), F32)] * 3,
        in_specs=[ANY] * 6 + [VMEM],
        out_specs=[ANY] * 6 + [VMEM] * 3,
        scratch_shapes=[pltpu.VMEM(a.shape, BF) for a in (block, gx, gq, go, f1, f2)]
        + [pltpu.VMEM(dims, F32) for dims in wide]
        + [pltpu.SemaphoreType.DMA((WIDEN, 4)), pltpu.SemaphoreType.DMA((WIDEN, 4)), pltpu.SemaphoreType.DMA((4,))],
        compiler_params=pltpu.CompilerParams(vmem_limit_bytes=63 * 1024 * 1024),
        name="widen",
    )(block, gx, gq, go, f1, f2, small)


def per_device(others, images, patch_rank, kept_count, ln1_gain, router_weight, w_qkv, w_out, ln2_gain, w_fc1, w_fc2, cotangent):
    count, patches, width = images.shape
    tall = -(-patches // 16) * 16
    t = count * tall
    part = w_fc1.shape[1] // 2
    half, eighth = width // 2, width // 8

    def bf(*dims):
        return pltpu.VMEM(dims, BF)

    def f32(*dims):
        return pltpu.VMEM(dims, F32)

    def sem(*dims):
        return pltpu.SemaphoreType.DMA(dims)

    scratch = [
        bf(patches, count, width), bf(patches, count, width),
        bf(width, 3 * width), bf(width, width), bf(width, 2 * part), bf(2 * part, width),
        bf(t, width), f32(t, 128), f32(t, 128), f32(t, 128), bf(t, width), bf(width, t), bf(t, 3 * width),
        f32(count, HEADS, tall, tall), bf(count, width, tall), bf(t, width), f32(t, width), f32(t, width),
        bf(4 * t, width), bf(4 * t, width), bf(width, 4 * t), f32(t, width), f32(t, width),
        bf(3 * t, width), bf(3 * t, width), bf(t, width), bf(t, width), bf(t, width), bf(t, width), bf(t, width), bf(t, width),
        bf(4 * t, 2 * part), bf(4 * t, 2 * part), bf(tall, width),
        bf(2, width, part), bf(2, part, width),
        bf(2, width // 2, part), bf(2, part // 2, width), bf(2, width // 4, part), bf(2, part // 4, width),
        bf(2, width // 4, part), bf(2, part // 4, width), bf(width // 4, part), bf(part // 4, width),
        bf(CHUNKS, 3, width, 128), bf(CHUNKS, 3, half, 128), bf(CHUNKS, 3, 2 * eighth, 128), bf(CHUNKS, 3, eighth, 128),
        bf(CHUNKS, 3, eighth // 2, 128), bf(CHUNKS, 3, eighth // 2, 128),
        f32(1, width), f32(1, width), f32(1, width), f32(3, 8, width), f32(3, 8, width), f32(4, 8, width),
        sem(8), sem(2, 4), sem(2, 4), sem(count, 3), sem(count, 3), sem(3), sem(3), sem(8), sem(8),
        sem(2, 2), sem(2, 2), sem(2, 2), sem(2, 2), sem(2), sem(2),
        sem(2, 2), sem(2, 2), sem(2, 2), sem(2), sem(2), pltpu.SemaphoreType.REGULAR((2,)), pltpu.SemaphoreType.REGULAR((CHUNKS, 4)),
        sem(CHUNKS, 9), sem(CHUNKS, 9), sem(CHUNKS),
        sem(3), sem(3), sem(2), sem(2),
    ]

    def struct(*dims, dtype=BF):
        return jax.ShapeDtypeStruct(dims, dtype)

    block, gx, gq, go, f1, f2, small = pl.pallas_call(
        mega_kernel,
        out_shape=[
            struct(patches, count, width), struct(patches, count, width), struct(3, width, width), struct(6, width, 128),
            struct(width, 2 * part), struct(2 * part, width), struct(8, width, dtype=F32),
        ],
        in_specs=[ANY, VMEM, SMEM, VMEM, VMEM, ANY, ANY, VMEM, ANY, ANY, ANY],
        out_specs=[ANY, ANY, ANY, ANY, ANY, ANY, VMEM],
        scratch_shapes=scratch,
        compiler_params=pltpu.CompilerParams(
            collective_id=0, has_side_effects=True, vmem_limit_bytes=64 * 1024 * 1024
        ),
        name="block",
    )(images.transpose(1, 0, 2), patch_rank, kept_count, ln1_gain, router_weight, w_qkv, w_out, ln2_gain, w_fc1, w_fc2,
      cotangent.transpose(1, 0, 2))
    block, gx, gq, go, f1, f2, g1, rw, g2 = widen(block, gx, gq, go, f1, f2, small)
    if others:
        gq, go, f1, f2, g1, rw, g2 = lax.psum((gq, go, f1, f2, g1, rw, g2), "rows", axis_index_groups=others)
    return block.transpose(1, 0, 2), gx.transpose(1, 0, 2), g1, rw, gq, go, g2, f1, f2


def solution(mesh):
    rows = mesh.shape["rows"]
    others = [[8 * g + i for g in range(rows // 8)] for i in range(8)] if rows > 8 else None
    return jax.shard_map(
        functools.partial(per_device, others),
        mesh=mesh,
        in_specs=(
            P(("rows", "mlp"), None, None), P(("rows", "mlp"), None), P(("rows", "mlp")), P(), P(), P(), P(), P(),
            P(None, "mlp"), P("mlp", None), P(("rows", "mlp"), None, None),
        ),
        out_specs=(
            P(("rows", "mlp"), None, None), P(("rows", "mlp"), None, None), P(), P(), P(), P(), P(),
            P(None, "mlp"), P("mlp", None),
        ),
        check_vma=False,
    )
```

```python
import functools
import jax
import jax.numpy as jnp
from jax import lax
from jax.experimental import pallas as pl
from jax.experimental.pallas import tpu as pltpu
from jax.sharding import PartitionSpec as P

HEADS = 12
EPS = 1e-6
FILL = -1e30
BF = jnp.bfloat16
F32 = jnp.float32


def dot_nn(a, b):
    return lax.dot_general(a, b, (((1,), (0,)), ((), ())), preferred_element_type=F32)


def dot_nt(a, b):
    return lax.dot_general(a, b, (((1,), (1,)), ((), ())), preferred_element_type=F32)


def dot_tn(a, b):
    return lax.dot_general(a, b, (((0,), (0,)), ((), ())), preferred_element_type=F32)


def unit_rows(v):
    center = v - jnp.mean(v, -1, keepdims=True)
    scale = lax.rsqrt(jnp.mean(center * center, -1, keepdims=True) + EPS)
    return center * scale, scale


def norm_pull(dy, gain, unit, scale):
    du = dy * gain
    return scale * (
        du
        - jnp.mean(du, -1, keepdims=True)
        - unit * jnp.mean(du * unit, -1, keepdims=True)
    )


def half_mask(rows, h):
    lane = lax.broadcasted_iota(jnp.int32, (rows, 128), 1)
    return (lane < 64) if h == 0 else (lane >= 64)


def forward_rows(i, x_ref, rank_ref, kept_ref, g1_ref, rw_ref, xp, keep, gate, h1, work):
    patches = x_ref.shape[0]
    tall = xp.shape[0] // x_ref.shape[1]
    rows = pl.ds(pl.multiple_of(i * tall, 16), tall)
    work[...] = jnp.zeros_like(work)
    work[0:patches, :] = x_ref[:, i, :]
    v = work[...]
    xp[rows, :] = v
    kept = (rank_ref[pl.ds(i, 1), :] < kept_ref[i]).astype(F32)
    keep_row = jnp.concatenate([kept, jnp.zeros((1, 256 - patches), F32)], 1)
    keep_col = jnp.broadcast_to(keep_row, (128, 256)).T
    keep[rows, :] = keep_col[0:tall, :]
    unit, _ = unit_rows(v.astype(F32))
    low = (unit * g1_ref[...][None]).astype(BF)
    h1[rows, :] = low
    logit = jnp.sum(low.astype(F32) * rw_ref[...][None].astype(F32), -1, keepdims=True)
    gate[rows, :] = jnp.broadcast_to(jax.nn.sigmoid(logit), (tall, 128))


def forward_qkv(j, h1, wqkv, qkv):
    cols = pl.ds(pl.multiple_of(j * 256, 256), 256)
    qkv[:, cols] = dot_nn(h1[...], wqkv[:, cols]).astype(BF)


def attend(p, i, width, tall, qkv, keep, probs, context, contextt):
    rows = pl.ds(pl.multiple_of(i * tall, 16), tall)
    qc = pl.ds(pl.multiple_of(p * 128, 128), 128)
    kc = pl.ds(pl.multiple_of(width + p * 128, 128), 128)
    vc = pl.ds(pl.multiple_of(2 * width + p * 128, 128), 128)
    q, k, v = qkv[rows, qc], qkv[rows, kc], qkv[rows, vc]
    vt = v.T
    kept = keep[rows, 0:1] > 0.5
    outs = []
    for h in range(2):
        kh = jnp.where(half_mask(tall, h), k, jnp.zeros_like(k))
        s = jnp.where(kept, dot_nt(kh, q) * 0.125, FILL)
        e = jnp.exp(s - jnp.max(s, 0, keepdims=True))
        pr = e * (1.0 / jnp.sum(e, 0, keepdims=True))
        probs[i, p * 2 + h] = pr
        outs.append(dot_nn(vt[h * 64 : h * 64 + 64, :], pr.astype(BF)))
    ct = jnp.concatenate(outs, 0)
    contextt[i, pl.ds(pl.multiple_of(p * 128, 128), 128), :] = ct.astype(BF)
    context[rows, qc] = ct.T.astype(BF)


def forward_out(i, tall, context, wout, xp, keep, gate, g2_ref, attended, middle, h2):
    rows = pl.ds(pl.multiple_of(i * tall, 16), tall)
    att = dot_nn(context[rows, :], wout[...])
    attended[rows, :] = att
    mid = xp[rows, :].astype(F32) + keep[rows, 0:1] * gate[rows, 0:1] * att
    middle[rows, :] = mid
    unit, _ = unit_rows(mid)
    h2[rows, :] = (unit * g2_ref[...][None]).astype(BF)


def gelu_pair(pre):
    cdf = 0.5 * (1.0 + lax.erf(pre * 0.7071067811865476))
    pdf = jnp.exp(pre * pre * -0.5) * 0.3989422804014327
    return pre * cdf, cdf + pre * pdf


def mlp_rows(h, c, w1, w2):
    pre = dot_nn(h, w1)
    hidden, slope = gelu_pair(pre)
    grad = dot_nt(c, w2) * slope
    return hidden.astype(BF), grad.astype(BF)


def back_rows(i, tall, c_ref, gh2, middle, keep, gate, attended, g2_ref, gmid, gatt, glogit, dg2):
    rows = pl.ds(pl.multiple_of(i * tall, 16), tall)
    dy = gh2[rows, :]
    unit, scale = unit_rows(middle[rows, :])
    gm = c_ref[rows, :].astype(F32) + norm_pull(dy, g2_ref[...][None], unit, scale)
    gmid[rows, :] = gm
    dg2[...] += jnp.sum(dy * unit, 0, keepdims=True)
    k, g = keep[rows, 0:1], gate[rows, 0:1]
    kept = gm * k
    gatt[rows, :] = (kept * g).astype(BF)
    gl = jnp.sum(kept * attended[rows, :], -1, keepdims=True) * g * (1.0 - g)
    glogit[rows, :] = jnp.broadcast_to(gl, (tall, 128))


def attend_back(p, i, width, tall, qkv, probs, gctx):
    rows = pl.ds(pl.multiple_of(i * tall, 16), tall)
    qc = pl.ds(pl.multiple_of(p * 128, 128), 128)
    kc = pl.ds(pl.multiple_of(width + p * 128, 128), 128)
    vc = pl.ds(pl.multiple_of(2 * width + p * 128, 128), 128)
    q, k, v = qkv[rows, qc], qkv[rows, kc], qkv[rows, vc]
    gc = gctx[rows, qc]
    kt = k.T
    gv, gk, gq = 0.0, 0.0, []
    for h in range(2):
        mask = half_mask(tall, h)
        zero = jnp.zeros_like(v)
        pr = probs[i, p * 2 + h]
        gp = dot_nt(jnp.where(mask, v, zero), gc)
        gs = (pr * (gp - jnp.sum(pr * gp, 0, keepdims=True))).astype(BF)
        gv = gv + dot_nn(pr.astype(BF), jnp.where(mask, gc, zero))
        gk = gk + dot_nn(gs, jnp.where(mask, q, zero))
        gq.append(dot_nn(kt[h * 64 : h * 64 + 64, :], gs))
    qkv[rows, qc] = (jnp.concatenate(gq, 0).T * 0.125).astype(BF)
    qkv[rows, kc] = (gk * 0.125).astype(BF)
    qkv[rows, vc] = gv.astype(BF)


def pair_columns(wqkv, p, width):
    return jnp.concatenate(
        [wqkv[:, pl.ds(pl.multiple_of(b * width + p * 128, 128), 128)] for b in range(3)], 1
    )


def back_input(i, tall, dy, glogit, rw_ref, xp, h1, g1_ref, gmid, gx_ref, dg1, drw):
    rows = pl.ds(pl.multiple_of(i * tall, 16), tall)
    patches = gx_ref.shape[0]
    gl = glogit[rows, 0:1]
    dy = dy + gl * rw_ref[...][None].astype(F32)
    unit, scale = unit_rows(xp[rows, :].astype(F32))
    dg1[...] += jnp.sum(dy * unit, 0, keepdims=True)
    drw[...] += jnp.sum(h1[rows, :].astype(F32) * gl, 0, keepdims=True)
    out = gmid[rows, :] + norm_pull(dy, g1_ref[...][None], unit, scale)
    gx_ref[:, i, :] = out.astype(BF)[0:patches, :]

MESH = pl.DeviceIdType.MESH
CHUNKS = HEADS // 2 + 2
WIDEN = 8
PATHS = ("xzy", "zxy", "yzx", "xzy", "yxz", "xyz", "yzx", "yzx")
ORDER = (
    "osend", "back0", "pairs0", "back1", "pairs1", "fa10", "fa11", "last0", "pairs2", "last1", "fa01", "c2.1",
    "pairs3", "fb1", "c4.1", "last2", "c5.1", "out1", "c3.1", "c2.2", "fa00", "out0", "finish0", "c6.1", "c1.1",
    "c4.2", "c0.1", "c5.2", "finish1", "c3.2", "c7.1", "c6.2", "c2.3", "c1.2", "fb0", "c5.3", "fc", "c0.2", "c4.3",
    "c5.4", "g1", "c1.3", "c6.3", "c2.4", "c3.3", "c7.2", "c0.3", "c4.4", "fd", "c1.4", "c5.5", "c0.4", "c4.5",
    "c6.4", "c7.3", "c3.4", "c5.6", "g2", "c2.5", "c0.5", "c4.6", "c7.4", "c6.5", "fe", "c1.5", "c2.6", "c5.7",
    "c3.5", "c4.7", "c0.6", "g3", "c6.6", "c7.5", "c3.6", "c2.7", "c1.6", "c0.7", "c7.6", "c5.8", "ff", "c6.7",
    "c4.8", "o0", "c1.7", "g4", "c3.7", "c2.8", "c7.7", "c0.8", "c4.9", "c6.8", "c1.8", "c3.8", "c7.8", "c0.9",
    "c5.9", "c1.9", "g5", "o1", "c6.9", "c2.9", "c3.9", "c7.9",
)


def mega_kernel(
    x_hbm, rank_hbm, kept_ref, g1_hbm, rw_hbm, wqkv_hbm, wout_hbm, g2_hbm, fc1, fc2, c_hbm,
    block_hbm, gx_hbm, gq_out, go_out, f1_out, f2_out, small_hbm,
    rank_ref, g1_ref, rw_ref, g2_ref, small_out, x_ref, c_ref, wqkv, wout, w1, w2, xp, keep, gate, glogit, h1, h1t, qkv, probs, contextt, context, attended, middle,
    tok, cot, turned, out, gh2, out_part, gh2_part, out_sib, gh2_sib, out_near, gh2_near, out_far, gh2_far, hid, gpre, work,
    g1w, g2w, r1a, r1b, r2a, r2b, fz1, fz2, rz1, rz2,
    gw, q0, q1, q2, q3, far, dg1, dg2, drw, sma, smr, smz,
    lsem, gsend, grecv, hsend, hrecv, csend, crecv, esend, erecv, s1s, s1r, s2s, s2r, s3s, s3r, fs, fr, floc, ssib, rsib, free, chunk_free,
    qs, qr, qloc, small_sem, sms, smrs, smzs, smzr,
):
    patches, images, width = x_ref.shape
    t_own = xp.shape[0]
    tall = t_own // images
    half = width // 2
    part = w1.shape[1] // 2
    parts = (q0, q1, q2, q3)
    quarter = (width // 4, part // 4)
    r = lax.axis_index("rows")
    z = lax.axis_index("mlp")
    c, x, y = lax.rem(r, 2), lax.rem(lax.div(r, 2), 2), lax.rem(lax.div(r, 4), 2)
    r_sib, r_x, r_y = r + 1 - 2 * c, r + 2 - 4 * x, r + 4 - 8 * y
    r_diag = r_x + r_y - r
    z_pair, z_far = z + 1 - 2 * lax.rem(z, 2), z + 2 - 4 * lax.div(z, 2)
    q = 2 * y + x

    def ds(start, size):
        return pl.ds(pl.multiple_of(start, 16), size)

    def lanes(start, size):
        return pl.ds(pl.multiple_of(start, 128), size)

    def remote(src, dst, send, recv, row, column):
        return pltpu.make_async_remote_copy(
            src_ref=src, dst_ref=dst, send_sem=send, recv_sem=recv,
            device_id={"rows": row, "mlp": column}, device_id_type=MESH,
        )

    def release(semaphore, row):
        pl.semaphore_signal(semaphore, inc=1, device_id={"rows": row, "mlp": z}, device_id_type=MESH)

    def gather_copy(mat, kind):
        size = quarter[mat]
        sems = gsend.at[mat, kind], grecv.at[mat, kind]
        if mat == 0:
            place = w1.at[ds(q * size, size), pl.ds(part, part)]
            own = fc1.at[ds(q * size, size), lanes(c * part, part)]
        else:
            place = w2.at[ds(part + q * size, size), :]
            own = fc2.at[ds(c * part + q * size, size), :]
        if kind == 0:
            return remote(own, place, *sems, r, z_far)
        return remote(place, place, *sems, (r_x, r_y, r_diag)[kind - 1], z)

    def gather_forward(mat):
        gather_copy(mat, 0).wait_recv()
        for kind in (1, 2, 3):
            gather_copy(mat, kind).start()

    def own_shard(mat):
        if mat == 0:
            return pltpu.make_async_copy(fc1.at[:, lanes(c * part, part)], w1.at[:, pl.ds(0, part)], lsem.at[0])
        return pltpu.make_async_copy(fc2.at[ds(c * part, part), :], w2.at[pl.ds(0, part), :], lsem.at[1])

    load_qkv = pltpu.make_async_copy(wqkv_hbm, wqkv, lsem.at[2])
    load_out = pltpu.make_async_copy(wout_hbm, wout, lsem.at[3])
    load_x = pltpu.make_async_copy(x_hbm, x_ref, lsem.at[4])
    load_small = [
        pltpu.make_async_copy(src, dst, small_sem.at[k])
        for k, (src, dst) in enumerate(((rank_hbm, rank_ref), (g1_hbm, g1_ref), (rw_hbm, rw_ref), (g2_hbm, g2_ref)))
    ]
    store_small = pltpu.make_async_copy(small_out, small_hbm, small_sem.at[4])
    load_c = pltpu.make_async_copy(c_hbm, c_ref, lsem.at[5])
    store_block = pltpu.make_async_copy(c_ref, block_hbm, lsem.at[6])
    store_gx = pltpu.make_async_copy(x_ref, gx_hbm, lsem.at[7])

    def token_copy(i, hop):
        start = (0, 0, 2 * t_own)[hop] + i * tall
        src, dst = tok.at[ds(start, tall), :], tok.at[ds((1, 2, 3)[hop] * t_own + i * tall, tall), :]
        row, column = (r, z_pair) if hop == 1 else (r_sib, z)
        return remote(src, dst, hsend.at[i, hop], hrecv.at[i, hop], row, column)

    def cot_copy(hop):
        src, dst = cot.at[ds((0, 0, 2)[hop] * t_own, t_own), :], cot.at[ds((1, 2, 3)[hop] * t_own, t_own), :]
        row, column = (r, z_pair) if hop == 1 else (r_sib, z)
        return remote(src, dst, csend.at[hop], crecv.at[hop], row, column)

    gh2_to_sib = remote(gh2_part.at[ds(0, t_own), :], gh2_sib, esend.at[0], erecv.at[0], r_sib, z)
    out_to_sib = remote(out_part.at[ds(0, t_own), :], out_sib, esend.at[1], erecv.at[1], r_sib, z)
    out_over = remote(out_part.at[ds(2 * t_own, t_own), :], out_near, esend.at[2], erecv.at[2], r_sib, z)
    out_far_copy = remote(out_part.at[ds(t_own, t_own), :], out_far, esend.at[3], erecv.at[3], r, z_pair)

    def gh2_over(i):
        src = gh2_part.at[ds(2 * t_own + i * tall, tall), :]
        return remote(src, gh2_near.at[ds(i * tall, tall), :], esend.at[4 + i], erecv.at[4 + i], r_sib, z)

    def gh2_far_copy(i):
        src = gh2_part.at[ds(t_own + i * tall, tall), :]
        return remote(src, gh2_far.at[ds(i * tall, tall), :], esend.at[6 + i], erecv.at[6 + i], r, z_pair)

    fc_whole, fc_half, fc_quarter, fc_done, fc_far = (g1w, g2w), (r1a, r1b), (r2a, r2b), (fz1, fz2), (rz1, rz2)
    fc_rows = ((width // 2, width // 4), (part // 2, part // 4))

    def fc_ways(k, m):
        shard = lax.div(z, 2) if k == 0 else 1 - lax.div(z, 2)
        turn = lax.rem(shard + m, 2)
        return r_x + (r_y - r_x) * turn, r_y + (r_x - r_y) * turn, x + (y - x) * turn, y + (x - y) * turn

    def fc_first(k, m):
        n1, _, a1, _ = fc_ways(k, m)
        rows, _ = fc_rows[m]
        src = fc_whole[m].at[k, ds((1 - a1) * rows, rows), :]
        return remote(src, fc_half[m].at[k], s1s.at[k, m], s1r.at[k, m], n1, z)

    def fc_second(k, m):
        _, n2, a1, a2 = fc_ways(k, m)
        rows, less = fc_rows[m]
        src = fc_whole[m].at[k, ds(a1 * rows + (1 - a2) * less, less), :]
        return remote(src, fc_quarter[m].at[k], s2s.at[k, m], s2r.at[k, m], n2, z)

    fc_third = [remote(fc_done[m].at[1], fc_far[m], s3s.at[m], s3r.at[m], r, z_far) for m in range(2)]

    def fc_spread(level, m):
        n1, n2, a1, a2 = fc_ways(0, m)
        rows, less = fc_rows[m]
        place = ds(a1 * rows + a2 * less, less) if level == 0 else ds(a1 * rows, rows)
        held = fc_whole[m].at[0, place, :]
        return remote(held, held, fs.at[level, m], fr.at[level, m], n2 if level == 0 else n1, z)

    fc_share = (
        remote(g1w.at[0], g1w.at[1], ssib.at[0], rsib.at[0], r_sib, z),
        remote(g2w.at[0], g2w.at[1], ssib.at[1], rsib.at[1], r_sib, z),
    )

    def fc_store(k):
        core = c + k - 2 * c * k
        return (
            pltpu.make_async_copy(g1w.at[k], f1_out.at[:, lanes(core * part, part)], floc.at[k, 0]),
            pltpu.make_async_copy(g2w.at[k], f2_out.at[ds(core * part, part), :], floc.at[k, 1]),
        )

    def fc_fold_second(k, m):
        fc_first(k, m).wait_recv()
        _, _, a1, a2 = fc_ways(k, m)
        rows, less = fc_rows[m]
        place, whole = ds(a1 * rows + (1 - a2) * less, less), fc_whole[m]
        whole[k, place, :] = whole[k, place, :] + fc_half[m][k, ds((1 - a2) * less, less), :]
        fc_second(k, m).start()

    def fc_fold_third(k):
        for m in range(2):
            fc_second(k, m).wait_recv()
            _, _, a1, a2 = fc_ways(k, m)
            rows, less = fc_rows[m]
            total = fc_whole[m][k, ds(a1 * rows + a2 * less, less), :].astype(F32)
            total = total + fc_half[m][k, ds(a2 * less, less), :].astype(F32) + fc_quarter[m][k].astype(F32)
            fc_done[m][k] = total.astype(BF)
        if k == 1:
            for copy in fc_third:
                copy.start()
        for m in range(2):
            fc_first(k, m).wait_send()
            fc_second(k, m).wait_send()
        if k == 1:
            release(free.at[0], r_sib)
        else:
            release(free.at[1], r_x)
            release(free.at[1], r_y)

    def fc_finish():
        for copy in fc_third:
            copy.wait_recv()
        pl.semaphore_wait(free.at[1], 2)
        for m in range(2):
            _, _, a1, a2 = fc_ways(0, m)
            rows, less = fc_rows[m]
            fc_whole[m][0, ds(a1 * rows + a2 * less, less), :] = fc_done[m][0] + fc_far[m][...]
            fc_spread(0, m).start()

    def fc_widen():
        for m in range(2):
            fc_spread(0, m).wait_recv()
        for m in range(2):
            fc_spread(1, m).start()

    def fc_to_sibling():
        for m in range(2):
            fc_spread(1, m).wait_recv()
        pl.semaphore_wait(free.at[0], 1)
        for copy in fc_share + fc_store(0):
            copy.start()

    sizes = tuple(width >> level for level in range(1, 5))

    def hops(j):
        ways = {"x": (r_x, z, x), "y": (r_y, z, y), "z": (r, z_pair, lax.rem(z, 2))}
        return [(r_sib, z, c)] + [ways[axis] for axis in PATHS[j]]

    def base(path, level):
        start = 0
        for (_, _, bit), size in zip(path[:level], sizes):
            start = start + bit * size
        return start

    def core_copy(j):
        src = gw.at[j, :, ds((1 - c) * half, half), :]
        return remote(src, parts[0].at[j], qs.at[j, 0], qr.at[j, 0], r_sib, z)

    def chunk_copy(j, step):
        path = hops(j)
        if step == 0:
            return core_copy(j)
        if step < 4:
            row, column, bit = path[step]
            start = base(path, step) + (1 - bit) * sizes[step]
            return remote(gw.at[j, :, ds(start, sizes[step]), :], parts[step].at[j], qs.at[j, step], qr.at[j, step], row, column)
        if step == 4:
            own = gw.at[j, :, ds(base(path, 4), sizes[3]), :]
            return remote(own, far.at[j], qs.at[j, 4], qr.at[j, 4], r, z_far)
        level = 8 - step
        row, column, _ = path[level]
        held = gw.at[j, :, ds(base(path, level + 1), sizes[level]), :]
        return remote(held, held, qs.at[j, step], qr.at[j, step], row, column)

    def chunk_store(j, k):
        rows = ds((c + k - 2 * c * k) * half, half)
        place = go_out.at[pl.ds(3 * j, 3), rows, :] if j < 2 else gq_out.at[j - 2, :, rows, :]
        return pltpu.make_async_copy(gw.at[j, :, rows, :], place, qloc.at[j, k])

    def chunk_step(j, step):
        path = hops(j)
        chunk_copy(j, step - 1).wait()
        if step <= 4:
            row, column, _ = path[step - 1]
            pl.semaphore_signal(
                chunk_free.at[j, step - 1], inc=1, device_id={"rows": row, "mlp": column}, device_id_type=MESH
            )
            start = base(path, min(step, 4))
            if step < 4:
                start = base(path, step) + (1 - path[step][2]) * sizes[step]
            size = sizes[min(step, 3)]
            total = gw[j, :, ds(start, size), :].astype(F32)
            for level in range(step):
                total = total + parts[level][j, :, ds(start - base(path, level + 1), size), :].astype(F32)
            gw[j, :, ds(start, size), :] = total.astype(BF)
        if step == 5:
            own = ds(base(path, 4), sizes[3])
            gw[j, :, own, :] = gw[j, :, own, :] + far[j]
        if 5 <= step <= 8:
            pl.semaphore_wait(chunk_free.at[j, 8 - step], 1)
        if step <= 8:
            chunk_copy(j, step).start()
        if step >= 8:
            chunk_store(j, step - 8).start()

    def small_copy(level):
        row = (r_sib, r_x, r_y)[level]
        return remote(sma.at[level], smr.at[level], sms.at[level], smrs.at[level], row, z)

    def small_z(step):
        src, dst = smz.at[2 * step], smz.at[2 * step + 1]
        return remote(src, dst, smzs.at[step], smzr.at[step], r, (z_pair, z_far)[step])

    barrier = pltpu.get_barrier_semaphore()
    partners = ((r_sib, z), (r_x, z), (r_y, z), (r_diag, z), (r, z_pair), (r, z_far))
    for row, column in partners:
        pl.semaphore_signal(barrier, inc=1, device_id={"rows": row, "mlp": column}, device_id_type=MESH)
    load_c.start()
    load_x.start()
    for copy in load_small:
        copy.start()
    load_qkv.start()
    load_out.start()
    own_shard(0).start()
    own_shard(1).start()
    pl.semaphore_wait(barrier, len(partners))
    gather_copy(0, 0).start()
    gather_copy(1, 0).start()
    load_c.wait()
    for i in range(images):
        work[...] = jnp.zeros_like(work)
        work[0:patches, :] = c_ref[:, i, :]
        cot[i * tall : (i + 1) * tall, :] = work[...]
    cot_copy(0).start()
    cot_copy(1).start()
    load_x.wait()
    for copy in load_small:
        copy.wait()
    for i in range(images):
        forward_rows(i, x_ref, rank_ref, kept_ref, g1_ref, rw_ref, xp, keep, gate, h1, work)

    load_qkv.wait()

    @pl.loop(0, 3 * width // 256)
    def _(j):
        forward_qkv(j, h1, wqkv, qkv)

    @pl.loop(0, HEADS // 2)
    def _(p):
        for i in range(images):
            attend(p, i, width, tall, qkv, keep, probs, context, contextt)

        @pl.when(p == 2)
        def _():
            gather_forward(0)

        @pl.when(p == 5)
        def _():
            gather_forward(1)

    load_out.wait()

    @pl.loop(0, images)
    def _(i):
        forward_out(i, tall, context, wout, xp, keep, gate, g2_ref, attended, middle, tok)
        token_copy(i, 0).start()
        token_copy(i, 1).start()

    own_shard(0).wait()
    own_shard(1).wait()

    def at(block, number, do):
        @pl.when(block == number)
        def _():
            do()

    def before_sibling():
        for i in range(images):
            token_copy(i, 0).wait_recv()
        cot_copy(0).wait_recv()

    h1t[...] = h1[...].T

    @pl.loop(0, 2 * images)
    def _(block):
        at(block, images, before_sibling)
        rows = ds(block * tall, tall)
        hid[rows, 0:part], gpre[rows, 0:part] = mlp_rows(tok[rows, :], cot[rows, :], w1[:, 0:part], w2[0:part, :])

    cot_copy(1).wait_recv()
    cot_copy(2).start()
    for mat in range(2):
        for kind in (1, 2, 3):
            gather_copy(mat, kind).wait_recv()
    for ref in (dg1, dg2, drw):
        ref[...] = jnp.zeros_like(ref)

    def before_near():
        cot_copy(2).wait_recv()
        gh2_to_sib.start()
        out_to_sib.start()

    def forward_token(i):
        token_copy(i, 1).wait_recv()
        token_copy(i, 2).start()

    def send_far(i):
        gh2_over(i).wait_recv()
        rows = ds(t_own + i * tall, tall)
        gh2_part[rows, :] = gh2_part[rows, :] + gh2_near[ds(i * tall, tall), :]
        gh2_far_copy(i).start()

    def before_last():
        send_far(0)
        token_copy(1, 2).wait_recv()

    @pl.loop(0, 8)
    def _(block):
        at(block, 3, lambda: forward_token(0))
        at(block, 4, before_near)
        at(block, 5, lambda: token_copy(0, 2).wait_recv())
        at(block, 6, lambda: forward_token(1))
        at(block, 7, before_last)
        inner = lax.rem(block, 5)
        swap = lax.div(block, 5) * (1 - 2 * inner + 3 * lax.div(inner * (inner - 1), 2))
        spot = block + swap
        rows = ds(spot * tall, tall)

        @pl.when(block < 2 * images)
        def _():
            hid[rows, part:], gpre[rows, part:] = mlp_rows(tok[rows, :], cot[rows, :], w1[:, part:], w2[part:, :])

        @pl.when(block >= 2 * images)
        def _():
            hid[rows, :], gpre[rows, :] = mlp_rows(tok[rows, :], cot[rows, :], w1[...], w2[...])

        share_out = dot_nn(hid[rows, :], w2[...])
        share_gh2 = dot_nt(gpre[rows, :], w1[...])

        @pl.when(block < images)
        def _():
            out[rows, :] = share_out
            gh2[rows, :] = share_gh2

        @pl.when(block >= images)
        def _():
            there = ds(lax.max(spot - images, 0) * tall, tall)
            out_part[there, :] = share_out.astype(BF)
            gh2_part[there, :] = share_gh2.astype(BF)

        at(block, 5, lambda: gh2_over(0).start())
        at(block, 7, lambda: gh2_over(1).start())

    out_over.start()
    turned[...] = tok[...].T
    for m in range(3):
        rows = slice(m * width // 3, (m + 1) * width // 3)
        total = dot_nn(turned[rows, :], gpre[...]).astype(BF)
        g1w[0, rows, :] = total[:, 0:part]
        g1w[1, rows, :] = total[:, part:]
    for k in range(2):
        fc_first(k, 0).start()
    send_far(1)
    turned[...] = hid[...].T
    for m in range(2):
        g2w[m] = dot_nn(turned[m * part : (m + 1) * part, :], cot[...]).astype(BF)
    for k in range(2):
        fc_first(k, 1).start()

    def back_image(i):
        if i == 0:
            gh2_to_sib.wait_recv()
            for n in range(images):
                token_copy(n, 0).wait_send()
                token_copy(n, 1).wait_send()
        gh2_far_copy(i).wait_recv()
        rows = pl.ds(i * tall, tall)
        gh2[rows, :] += gh2_sib[rows, :].astype(F32) + gh2_far[rows, :].astype(F32)
        back_rows(i, tall, cot, gh2, middle, keep, gate, attended, g2_ref, gh2, tok, glogit, dg2)
        context[rows, :] = dot_nt(tok[rows, :], wout[...]).astype(BF)

    def fill(j, total):
        for b in range(3):
            gw[j, b] = total[:, b * 128 : (b + 1) * 128].astype(BF)
        core_copy(j).start()

    def grad_out_half(n):
        total = 0.0
        for i in range(images):
            total = total + dot_nn(contextt[i], tok[i * tall : (i + 1) * tall, n * half : (n + 1) * half])
        fill(n, total)

    def pair_chunk(p):
        fill(p + 2, dot_nn(h1t[...], pair_columns(qkv, p, width)))

    def finish(i):
        rows = pl.ds(i * tall, tall)
        dy = dot_nt(qkv[rows, :], wqkv[...])
        back_input(i, tall, dy, glogit, rw_ref, xp, h1, g1_ref, gh2, x_ref, dg1, drw)
        if i == images - 1:
            store_gx.start()
            sma[0] = jnp.concatenate([dg1[...], drw[...], dg2[...], jnp.zeros((5, width), F32)], 0)
            small_copy(0).start()

    def small_step(step):
        if step < 3:
            small_copy(step - 1).wait()
            sma[step] = sma[step - 1] + smr[step - 1]
            small_copy(step).start()
        elif step == 3:
            small_copy(2).wait()
            smz[0] = sma[2] + smr[2]
            small_z(0).start()
        else:
            small_z(step - 4).wait()
            if step == 4:
                smz[2] = smz[0] + smz[1]
                small_z(1).start()
            else:
                small_out[...] = smz[2] + smz[3]
                store_small.start()

    def out_send():
        out_over.wait_recv()
        rows = pl.ds(t_own, t_own)
        out_part[rows, :] = out_part[rows, :] + out_near[...]
        out_far_copy.start()

    def out_finish(i):
        if i == 0:
            out_to_sib.wait_recv()
            out_far_copy.wait_recv()
        rows = pl.ds(i * tall, tall)
        total = middle[rows, :] + out[rows, :] + out_sib[rows, :].astype(F32) + out_far[rows, :].astype(F32)
        c_ref[:, i, :] = total.astype(BF)[0:patches, :]
        if i == images - 1:
            store_block.start()

    def fc_share_end():
        for copy in fc_share:
            copy.wait()
        for copy in fc_store(1):
            copy.start()

    single = {"fc": fc_finish, "fd": fc_widen, "fe": fc_to_sibling, "ff": fc_share_end, "osend": out_send}
    numbered = (("finish", finish), ("back", back_image), ("out", grad_out_half),
                ("fb", fc_fold_third), ("g", small_step), ("o", out_finish))

    def perform(names):
        for name in names:
            if name in single:
                single[name]()
            elif name[:2] == "fa":
                fc_fold_second(int(name[2]), int(name[3]))
            elif name[0] == "c":
                chunk_step(int(name[1]), int(name[3]))
            else:
                do = next(f for head, f in numbered if name[:-1] == head)
                do(int(name[-1]))

    first, start, stop = ORDER.index("pairs0"), ORDER.index("pairs1"), ORDER.index("last2")
    perform(ORDER[:first])

    @pl.loop(0, HEADS // 4)
    def _(n):
        for p in (2 * n, 2 * n + 1):
            attend_back(p, 0, width, tall, qkv, probs, context)

    perform(ORDER[first + 1 : start])
    marks = [ORDER.index(name) for k in range(3) for name in ("pairs%d" % (k + 1), "last%d" % k)]

    @pl.loop(0, HEADS // 4)
    def _(n):
        for p in (2 * n, 2 * n + 1):
            attend_back(p, 1, width, tall, qkv, probs, context)
        pair_chunk(2 * n)
        for k in range(3):
            at(n, k, lambda k=k: perform(ORDER[marks[2 * k] + 1 : marks[2 * k + 1]]))
        pair_chunk(2 * n + 1)
        for k in range(2):
            at(n, k, lambda k=k: perform(ORDER[marks[2 * k + 1] + 1 : marks[2 * k + 2]]))

    perform(ORDER[stop + 1 :])
    for j in range(CHUNKS):
        for k in range(2):
            chunk_store(j, k).wait()
    store_gx.wait()
    store_block.wait()
    store_small.wait()
    for copy in fc_store(0) + fc_store(1):
        copy.wait()
    for level in range(2):
        for m in range(2):
            fc_spread(level, m).wait_send()
    for copy in fc_third:
        copy.wait_send()
    for mat in range(2):
        for kind in range(4):
            gather_copy(mat, kind).wait_send()
    for i in range(images):
        token_copy(i, 2).wait_send()
        gh2_over(i).wait_send()
        gh2_far_copy(i).wait_send()
    for hop in range(3):
        cot_copy(hop).wait_send()
    for copy in (gh2_to_sib, out_to_sib, out_over, out_far_copy):
        copy.wait_send()


VMEM = pl.BlockSpec(memory_space=pltpu.VMEM)
SMEM = pl.BlockSpec(memory_space=pltpu.SMEM)
ANY = pl.BlockSpec(memory_space=pl.ANY)


def widen_kernel(
    block, gx, gq, go, f1, f2, small, block_out, gx_out, gq_out, go_out, f1_out, f2_out, g1_out, rw_out, g2_out,
    block_held, gx_held, gq_held, go_held, f1_held, f2_held, gq_wide, go_wide, f1_wide, f2_wide, load_sem, store_sem, pass_sem,
):
    width = f1.shape[1]
    step = width // WIDEN

    def rows_of(i):
        return pl.ds(pl.multiple_of(i * step, 16), step)

    def loads(i):
        rows = rows_of(i)
        pairs = (
            (gq.at[:, :, rows, :], gq_held.at[:, :, rows, :]), (go.at[:, rows, :], go_held.at[:, rows, :]),
            (f1.at[rows, :], f1_held.at[rows, :]), (f2.at[rows, :], f2_held.at[rows, :]),
        )
        return [pltpu.make_async_copy(src, dst, load_sem.at[i, k]) for k, (src, dst) in enumerate(pairs)]

    def stores(i):
        rows = rows_of(i)
        pairs = ((gq_wide, gq_out), (go_wide, go_out), (f1_wide, f1_out), (f2_wide, f2_out))
        return [
            pltpu.make_async_copy(src.at[rows, :], dst.at[rows, :], store_sem.at[i, k]) for k, (src, dst) in enumerate(pairs)
        ]

    arrive = [pltpu.make_async_copy(src, dst, pass_sem.at[k]) for k, (src, dst) in enumerate(((block, block_held), (gx, gx_held)))]
    leave = [
        pltpu.make_async_copy(src, dst, pass_sem.at[2 + k]) for k, (src, dst) in enumerate(((block_held, block_out), (gx_held, gx_out)))
    ]

    @pl.loop(0, WIDEN)
    def _(i):
        for copy in loads(i):
            copy.start()

    for copy in arrive:
        copy.start()
    g1_out[...], rw_out[...], g2_out[...] = small[0], small[1], small[2]

    @pl.loop(0, WIDEN)
    def _(i):
        rows = rows_of(i)
        for copy in loads(i):
            copy.wait()
        for p in range(gq.shape[0]):
            for b in range(3):
                start = b * width + p * 128
                gq_wide[rows, start : start + 128] = gq_held[p, b, rows, :].astype(F32)
        for b in range(go.shape[0]):
            go_wide[rows, b * 128 : (b + 1) * 128] = go_held[b, rows, :].astype(F32)
        f1_wide[rows, :] = f1_held[rows, :].astype(F32)
        f2_wide[rows, :] = f2_held[rows, :].astype(F32)
        for copy in stores(i):
            copy.start()

    for come, go_on in zip(arrive, leave):
        come.wait()
        go_on.start()

    @pl.loop(0, WIDEN)
    def _(i):
        for copy in stores(i):
            copy.wait()

    for copy in leave:
        copy.wait()


def widen(block, gx, gq, go, f1, f2, small):
    width = f1.shape[0]
    tokens = jax.ShapeDtypeStruct(block.shape, BF)
    wide = [(width, 3 * width), (width, width), (width, width), (width, width)]
    return pl.pallas_call(
        widen_kernel,
        out_shape=[tokens, tokens] + [jax.ShapeDtypeStruct(dims, F32) for dims in wide] + [jax.ShapeDtypeStruct((width,), F32)] * 3,
        in_specs=[ANY] * 6 + [VMEM],
        out_specs=[ANY] * 6 + [VMEM] * 3,
        scratch_shapes=[pltpu.VMEM(a.shape, BF) for a in (block, gx, gq, go, f1, f2)]
        + [pltpu.VMEM(dims, F32) for dims in wide]
        + [pltpu.SemaphoreType.DMA((WIDEN, 4)), pltpu.SemaphoreType.DMA((WIDEN, 4)), pltpu.SemaphoreType.DMA((4,))],
        compiler_params=pltpu.CompilerParams(vmem_limit_bytes=63 * 1024 * 1024),
        name="widen",
    )(block, gx, gq, go, f1, f2, small)


def per_device(others, images, patch_rank, kept_count, ln1_gain, router_weight, w_qkv, w_out, ln2_gain, w_fc1, w_fc2, cotangent):
    count, patches, width = images.shape
    tall = -(-patches // 16) * 16
    t = count * tall
    part = w_fc1.shape[1] // 2
    half, eighth = width // 2, width // 8

    def bf(*dims):
        return pltpu.VMEM(dims, BF)

    def f32(*dims):
        return pltpu.VMEM(dims, F32)

    def sem(*dims):
        return pltpu.SemaphoreType.DMA(dims)

    scratch = [
        pltpu.VMEM(patch_rank.shape, jnp.int32), f32(width), bf(width), f32(width), f32(8, width),
        bf(patches, count, width), bf(patches, count, width),
        bf(width, 3 * width), bf(width, width), bf(width, 2 * part), bf(2 * part, width),
        bf(t, width), f32(t, 128), f32(t, 128), f32(t, 128), bf(t, width), bf(width, t), bf(t, 3 * width),
        f32(count, HEADS, tall, tall), bf(count, width, tall), bf(t, width), f32(t, width), f32(t, width),
        bf(4 * t, width), bf(4 * t, width), bf(width, 4 * t), f32(t, width), f32(t, width),
        bf(3 * t, width), bf(3 * t, width), bf(t, width), bf(t, width), bf(t, width), bf(t, width), bf(t, width), bf(t, width),
        bf(4 * t, 2 * part), bf(4 * t, 2 * part), bf(tall, width),
        bf(2, width, part), bf(2, part, width),
        bf(2, width // 2, part), bf(2, part // 2, width), bf(2, width // 4, part), bf(2, part // 4, width),
        bf(2, width // 4, part), bf(2, part // 4, width), bf(width // 4, part), bf(part // 4, width),
        bf(CHUNKS, 3, width, 128), bf(CHUNKS, 3, half, 128), bf(CHUNKS, 3, 2 * eighth, 128), bf(CHUNKS, 3, eighth, 128),
        bf(CHUNKS, 3, eighth // 2, 128), bf(CHUNKS, 3, eighth // 2, 128),
        f32(1, width), f32(1, width), f32(1, width), f32(3, 8, width), f32(3, 8, width), f32(4, 8, width),
        sem(8), sem(2, 4), sem(2, 4), sem(count, 3), sem(count, 3), sem(3), sem(3), sem(8), sem(8),
        sem(2, 2), sem(2, 2), sem(2, 2), sem(2, 2), sem(2), sem(2),
        sem(2, 2), sem(2, 2), sem(2, 2), sem(2), sem(2), pltpu.SemaphoreType.REGULAR((2,)), pltpu.SemaphoreType.REGULAR((CHUNKS, 4)),
        sem(CHUNKS, 9), sem(CHUNKS, 9), sem(CHUNKS, 2), sem(5),
        sem(3), sem(3), sem(2), sem(2),
    ]

    def struct(*dims, dtype=BF):
        return jax.ShapeDtypeStruct(dims, dtype)

    block, gx, gq, go, f1, f2, small = pl.pallas_call(
        mega_kernel,
        out_shape=[
            struct(patches, count, width), struct(patches, count, width), struct(CHUNKS - 2, 3, width, 128), struct(6, width, 128),
            struct(width, 2 * part), struct(2 * part, width), struct(8, width, dtype=F32),
        ],
        in_specs=[ANY, ANY, SMEM] + [ANY] * 8,
        out_specs=[ANY] * 7,
        scratch_shapes=scratch,
        compiler_params=pltpu.CompilerParams(
            collective_id=0, has_side_effects=True, vmem_limit_bytes=64 * 1024 * 1024
        ),
        name="block",
    )(images.transpose(1, 0, 2), patch_rank, kept_count, ln1_gain, router_weight, w_qkv, w_out, ln2_gain, w_fc1, w_fc2,
      cotangent.transpose(1, 0, 2))
    block, gx, gq, go, f1, f2, g1, rw, g2 = widen(block, gx, gq, go, f1, f2, small)
    if others:
        gq, go, f1, f2, g1, rw, g2 = lax.psum((gq, go, f1, f2, g1, rw, g2), "rows", axis_index_groups=others)
    return block.transpose(1, 0, 2), gx.transpose(1, 0, 2), g1, rw, gq, go, g2, f1, f2


def solution(mesh):
    rows = mesh.shape["rows"]
    others = [[8 * g + i for g in range(rows // 8)] for i in range(8)] if rows > 8 else None
    return jax.shard_map(
        functools.partial(per_device, others),
        mesh=mesh,
        in_specs=(
            P(("rows", "mlp"), None, None), P(("rows", "mlp"), None), P(("rows", "mlp")), P(), P(), P(), P(), P(),
            P(None, "mlp"), P("mlp", None), P(("rows", "mlp"), None, None),
        ),
        out_specs=(
            P(("rows", "mlp"), None, None), P(("rows", "mlp"), None, None), P(), P(), P(), P(), P(),
            P(None, "mlp"), P("mlp", None),
        ),
        check_vma=False,
    )
```

```python
import functools
import jax
import jax.numpy as jnp
from jax import lax
from jax.experimental import pallas as pl
from jax.experimental.pallas import tpu as pltpu
from jax.sharding import PartitionSpec as P

HEADS = 12
EPS = 1e-6
FILL = -1e30
BF = jnp.bfloat16
F32 = jnp.float32


def dot_nn(a, b):
    return lax.dot_general(a, b, (((1,), (0,)), ((), ())), preferred_element_type=F32)


def dot_nt(a, b):
    return lax.dot_general(a, b, (((1,), (1,)), ((), ())), preferred_element_type=F32)


def dot_tn(a, b):
    return lax.dot_general(a, b, (((0,), (0,)), ((), ())), preferred_element_type=F32)


def unit_rows(v):
    center = v - jnp.mean(v, -1, keepdims=True)
    scale = lax.rsqrt(jnp.mean(center * center, -1, keepdims=True) + EPS)
    return center * scale, scale


def norm_pull(dy, gain, unit, scale):
    du = dy * gain
    return scale * (
        du
        - jnp.mean(du, -1, keepdims=True)
        - unit * jnp.mean(du * unit, -1, keepdims=True)
    )


def half_mask(rows, h):
    lane = lax.broadcasted_iota(jnp.int32, (rows, 128), 1)
    return (lane < 64) if h == 0 else (lane >= 64)


def forward_rows(i, x_ref, rank_ref, kept_ref, g1_ref, rw_ref, xp, keep, gate, h1, work):
    patches = x_ref.shape[0]
    tall = xp.shape[0] // x_ref.shape[1]
    rows = pl.ds(pl.multiple_of(i * tall, 16), tall)
    work[...] = jnp.zeros_like(work)
    work[0:patches, :] = x_ref[:, i, :]
    v = work[...]
    xp[rows, :] = v
    kept = (rank_ref[pl.ds(i, 1), :] < kept_ref[i]).astype(F32)
    keep_row = jnp.concatenate([kept, jnp.zeros((1, 256 - patches), F32)], 1)
    keep_col = jnp.broadcast_to(keep_row, (128, 256)).T
    keep[rows, :] = keep_col[0:tall, :]
    unit, _ = unit_rows(v.astype(F32))
    low = (unit * g1_ref[...][None]).astype(BF)
    h1[rows, :] = low
    logit = jnp.sum(low.astype(F32) * rw_ref[...][None].astype(F32), -1, keepdims=True)
    gate[rows, :] = jnp.broadcast_to(jax.nn.sigmoid(logit), (tall, 128))


def forward_qkv(j, h1, wqkv, qkv):
    cols = pl.ds(pl.multiple_of(j * 256, 256), 256)
    qkv[:, cols] = dot_nn(h1[...], wqkv[:, cols]).astype(BF)


def attend(p, i, width, tall, qkv, keep, probs, context, contextt):
    rows = pl.ds(pl.multiple_of(i * tall, 16), tall)
    qc = pl.ds(pl.multiple_of(p * 128, 128), 128)
    kc = pl.ds(pl.multiple_of(width + p * 128, 128), 128)
    vc = pl.ds(pl.multiple_of(2 * width + p * 128, 128), 128)
    q, k, v = qkv[rows, qc], qkv[rows, kc], qkv[rows, vc]
    vt = v.T
    kept = keep[rows, 0:1] > 0.5
    outs = []
    for h in range(2):
        kh = jnp.where(half_mask(tall, h), k, jnp.zeros_like(k))
        s = jnp.where(kept, dot_nt(kh, q) * 0.125, FILL)
        e = jnp.exp(s - jnp.max(s, 0, keepdims=True))
        pr = e * (1.0 / jnp.sum(e, 0, keepdims=True))
        probs[i, p * 2 + h] = pr
        outs.append(dot_nn(vt[h * 64 : h * 64 + 64, :], pr.astype(BF)))
    ct = jnp.concatenate(outs, 0)
    contextt[i, pl.ds(pl.multiple_of(p * 128, 128), 128), :] = ct.astype(BF)
    context[rows, qc] = ct.T.astype(BF)


def forward_out(i, tall, context, wout, xp, keep, gate, g2_ref, attended, middle, h2):
    rows = pl.ds(pl.multiple_of(i * tall, 16), tall)
    att = dot_nn(context[rows, :], wout[...])
    attended[rows, :] = att
    mid = xp[rows, :].astype(F32) + keep[rows, 0:1] * gate[rows, 0:1] * att
    middle[rows, :] = mid
    unit, _ = unit_rows(mid)
    h2[rows, :] = (unit * g2_ref[...][None]).astype(BF)


def gelu_pair(pre):
    cdf = 0.5 * (1.0 + lax.erf(pre * 0.7071067811865476))
    pdf = jnp.exp(pre * pre * -0.5) * 0.3989422804014327
    return pre * cdf, cdf + pre * pdf


def mlp_rows(h, c, w1, w2):
    pre = dot_nn(h, w1)
    hidden, slope = gelu_pair(pre)
    grad = dot_nt(c, w2) * slope
    return hidden.astype(BF), grad.astype(BF)


def back_rows(i, tall, c_ref, gh2, middle, keep, gate, attended, g2_ref, gmid, gatt, glogit, dg2):
    rows = pl.ds(pl.multiple_of(i * tall, 16), tall)
    dy = gh2[rows, :]
    unit, scale = unit_rows(middle[rows, :])
    gm = c_ref[rows, :].astype(F32) + norm_pull(dy, g2_ref[...][None], unit, scale)
    gmid[rows, :] = gm
    dg2[...] += jnp.sum(dy * unit, 0, keepdims=True)
    k, g = keep[rows, 0:1], gate[rows, 0:1]
    kept = gm * k
    gatt[rows, :] = (kept * g).astype(BF)
    gl = jnp.sum(kept * attended[rows, :], -1, keepdims=True) * g * (1.0 - g)
    glogit[rows, :] = jnp.broadcast_to(gl, (tall, 128))


def attend_back(p, i, width, tall, qkv, probs, gctx):
    rows = pl.ds(pl.multiple_of(i * tall, 16), tall)
    qc = pl.ds(pl.multiple_of(p * 128, 128), 128)
    kc = pl.ds(pl.multiple_of(width + p * 128, 128), 128)
    vc = pl.ds(pl.multiple_of(2 * width + p * 128, 128), 128)
    q, k, v = qkv[rows, qc], qkv[rows, kc], qkv[rows, vc]
    gc = gctx[rows, qc]
    kt = k.T
    gv, gk, gq = 0.0, 0.0, []
    for h in range(2):
        mask = half_mask(tall, h)
        zero = jnp.zeros_like(v)
        pr = probs[i, p * 2 + h]
        gp = dot_nt(jnp.where(mask, v, zero), gc)
        gs = (pr * (gp - jnp.sum(pr * gp, 0, keepdims=True))).astype(BF)
        gv = gv + dot_nn(pr.astype(BF), jnp.where(mask, gc, zero))
        gk = gk + dot_nn(gs, jnp.where(mask, q, zero))
        gq.append(dot_nn(kt[h * 64 : h * 64 + 64, :], gs))
    qkv[rows, qc] = (jnp.concatenate(gq, 0).T * 0.125).astype(BF)
    qkv[rows, kc] = (gk * 0.125).astype(BF)
    qkv[rows, vc] = gv.astype(BF)


def pair_columns(wqkv, p, width):
    return jnp.concatenate(
        [wqkv[:, pl.ds(pl.multiple_of(b * width + p * 128, 128), 128)] for b in range(3)], 1
    )


def back_input(i, tall, dy, glogit, rw_ref, xp, h1, g1_ref, gmid, gx_ref, dg1, drw):
    rows = pl.ds(pl.multiple_of(i * tall, 16), tall)
    patches = gx_ref.shape[0]
    gl = glogit[rows, 0:1]
    dy = dy + gl * rw_ref[...][None].astype(F32)
    unit, scale = unit_rows(xp[rows, :].astype(F32))
    dg1[...] += jnp.sum(dy * unit, 0, keepdims=True)
    drw[...] += jnp.sum(h1[rows, :].astype(F32) * gl, 0, keepdims=True)
    out = gmid[rows, :] + norm_pull(dy, g1_ref[...][None], unit, scale)
    gx_ref[:, i, :] = out.astype(BF)[0:patches, :]

MESH = pl.DeviceIdType.MESH
CHUNKS = HEADS // 2 + 2
WIDEN = 8
PATHS = ("xzy", "zxy", "yzx", "xzy", "yxz", "xyz", "yzx", "yzx")
ORDER = (
    "osend", "back0", "pairs0", "back1", "pairs1", "fa10", "fa11", "last0", "pairs2", "last1", "fa01", "c2.1",
    "pairs3", "fb1", "c4.1", "last2", "c5.1", "out1", "c3.1", "c2.2", "fa00", "out0", "finish0", "c6.1", "c1.1",
    "c4.2", "c0.1", "c5.2", "finish1", "c3.2", "c7.1", "c6.2", "c2.3", "c1.2", "fb0", "c5.3", "fc", "c0.2", "c4.3",
    "c5.4", "g1", "c1.3", "c6.3", "c2.4", "c3.3", "c7.2", "c0.3", "c4.4", "fd", "c1.4", "c5.5", "c0.4", "c4.5",
    "c6.4", "c7.3", "c3.4", "c5.6", "g2", "c2.5", "c0.5", "c4.6", "c7.4", "c6.5", "fe", "c1.5", "c2.6", "c5.7",
    "c3.5", "c4.7", "c0.6", "g3", "c6.6", "c7.5", "c3.6", "c2.7", "c1.6", "c0.7", "c7.6", "c5.8", "ff", "c6.7",
    "c4.8", "o0", "c1.7", "g4", "c3.7", "c2.8", "c7.7", "c0.8", "c4.9", "c6.8", "c1.8", "c3.8", "c7.8", "c0.9",
    "c5.9", "c1.9", "g5", "o1", "c6.9", "c2.9", "c3.9", "c7.9",
)


def mega_kernel(
    x_hbm, rank_hbm, kept_ref, g1_hbm, rw_hbm, wqkv_hbm, wout_hbm, g2_hbm, fc1, fc2, c_hbm,
    c_ref, x_ref, gw, g1w, g2w, small_out,
    rank_ref, g1_ref, rw_ref, g2_ref, wqkv, wout, w1, w2, xp, keep, gate, glogit, h1, h1t, qkv, probs, contextt, context, attended, middle,
    tok, cot, turned, out, gh2, out_part, gh2_part, out_sib, gh2_sib, out_near, gh2_near, out_far, gh2_far, hid, gpre, work,
    r1a, r1b, r2a, r2b, fz1, fz2, rz1, rz2,
    q0, q1, q2, q3, far, dg1, dg2, drw, sma, smr, smz,
    lsem, gsend, grecv, hsend, hrecv, csend, crecv, esend, erecv, s1s, s1r, s2s, s2r, s3s, s3r, fs, fr, ssib, rsib, free, chunk_free,
    qs, qr, small_sem, sms, smrs, smzs, smzr,
):
    patches, images, width = x_ref.shape
    t_own = xp.shape[0]
    tall = t_own // images
    half = width // 2
    part = w1.shape[1] // 2
    parts = (q0, q1, q2, q3)
    quarter = (width // 4, part // 4)
    r = lax.axis_index("rows")
    z = lax.axis_index("mlp")
    c, x, y = lax.rem(r, 2), lax.rem(lax.div(r, 2), 2), lax.rem(lax.div(r, 4), 2)
    r_sib, r_x, r_y = r + 1 - 2 * c, r + 2 - 4 * x, r + 4 - 8 * y
    r_diag = r_x + r_y - r
    z_pair, z_far = z + 1 - 2 * lax.rem(z, 2), z + 2 - 4 * lax.div(z, 2)
    q = 2 * y + x

    def ds(start, size):
        return pl.ds(pl.multiple_of(start, 16), size)

    def lanes(start, size):
        return pl.ds(pl.multiple_of(start, 128), size)

    def remote(src, dst, send, recv, row, column):
        return pltpu.make_async_remote_copy(
            src_ref=src, dst_ref=dst, send_sem=send, recv_sem=recv,
            device_id={"rows": row, "mlp": column}, device_id_type=MESH,
        )

    def release(semaphore, row):
        pl.semaphore_signal(semaphore, inc=1, device_id={"rows": row, "mlp": z}, device_id_type=MESH)

    def gather_copy(mat, kind):
        size = quarter[mat]
        sems = gsend.at[mat, kind], grecv.at[mat, kind]
        if mat == 0:
            place = w1.at[ds(q * size, size), pl.ds(part, part)]
            own = fc1.at[ds(q * size, size), lanes(c * part, part)]
        else:
            place = w2.at[ds(part + q * size, size), :]
            own = fc2.at[ds(c * part + q * size, size), :]
        if kind == 0:
            return remote(own, place, *sems, r, z_far)
        return remote(place, place, *sems, (r_x, r_y, r_diag)[kind - 1], z)

    def gather_forward(mat):
        gather_copy(mat, 0).wait_recv()
        for kind in (1, 2, 3):
            gather_copy(mat, kind).start()

    def own_shard(mat):
        if mat == 0:
            return pltpu.make_async_copy(fc1.at[:, lanes(c * part, part)], w1.at[:, pl.ds(0, part)], lsem.at[0])
        return pltpu.make_async_copy(fc2.at[ds(c * part, part), :], w2.at[pl.ds(0, part), :], lsem.at[1])

    load_qkv = pltpu.make_async_copy(wqkv_hbm, wqkv, lsem.at[2])
    load_out = pltpu.make_async_copy(wout_hbm, wout, lsem.at[3])
    load_x = pltpu.make_async_copy(x_hbm, x_ref, lsem.at[4])
    load_small = [
        pltpu.make_async_copy(src, dst, small_sem.at[k])
        for k, (src, dst) in enumerate(((rank_hbm, rank_ref), (g1_hbm, g1_ref), (rw_hbm, rw_ref), (g2_hbm, g2_ref)))
    ]
    load_c = pltpu.make_async_copy(c_hbm, c_ref, lsem.at[5])

    def token_copy(i, hop):
        start = (0, 0, 2 * t_own)[hop] + i * tall
        src, dst = tok.at[ds(start, tall), :], tok.at[ds((1, 2, 3)[hop] * t_own + i * tall, tall), :]
        row, column = (r, z_pair) if hop == 1 else (r_sib, z)
        return remote(src, dst, hsend.at[i, hop], hrecv.at[i, hop], row, column)

    def cot_copy(hop):
        src, dst = cot.at[ds((0, 0, 2)[hop] * t_own, t_own), :], cot.at[ds((1, 2, 3)[hop] * t_own, t_own), :]
        row, column = (r, z_pair) if hop == 1 else (r_sib, z)
        return remote(src, dst, csend.at[hop], crecv.at[hop], row, column)

    gh2_to_sib = remote(gh2_part.at[ds(0, t_own), :], gh2_sib, esend.at[0], erecv.at[0], r_sib, z)
    out_to_sib = remote(out_part.at[ds(0, t_own), :], out_sib, esend.at[1], erecv.at[1], r_sib, z)
    out_over = remote(out_part.at[ds(2 * t_own, t_own), :], out_near, esend.at[2], erecv.at[2], r_sib, z)
    out_far_copy = remote(out_part.at[ds(t_own, t_own), :], out_far, esend.at[3], erecv.at[3], r, z_pair)

    def gh2_over(i):
        src = gh2_part.at[ds(2 * t_own + i * tall, tall), :]
        return remote(src, gh2_near.at[ds(i * tall, tall), :], esend.at[4 + i], erecv.at[4 + i], r_sib, z)

    def gh2_far_copy(i):
        src = gh2_part.at[ds(t_own + i * tall, tall), :]
        return remote(src, gh2_far.at[ds(i * tall, tall), :], esend.at[6 + i], erecv.at[6 + i], r, z_pair)

    fc_whole, fc_half, fc_quarter, fc_done, fc_far = (g1w, g2w), (r1a, r1b), (r2a, r2b), (fz1, fz2), (rz1, rz2)
    fc_rows = ((width // 2, width // 4), (part // 2, part // 4))

    def fc_ways(k, m):
        shard = lax.div(z, 2) if k == 0 else 1 - lax.div(z, 2)
        turn = lax.rem(shard + m, 2)
        return r_x + (r_y - r_x) * turn, r_y + (r_x - r_y) * turn, x + (y - x) * turn, y + (x - y) * turn

    def fc_first(k, m):
        n1, _, a1, _ = fc_ways(k, m)
        rows, _ = fc_rows[m]
        src = fc_whole[m].at[k, ds((1 - a1) * rows, rows), :]
        return remote(src, fc_half[m].at[k], s1s.at[k, m], s1r.at[k, m], n1, z)

    def fc_second(k, m):
        _, n2, a1, a2 = fc_ways(k, m)
        rows, less = fc_rows[m]
        src = fc_whole[m].at[k, ds(a1 * rows + (1 - a2) * less, less), :]
        return remote(src, fc_quarter[m].at[k], s2s.at[k, m], s2r.at[k, m], n2, z)

    fc_third = [remote(fc_done[m].at[1], fc_far[m], s3s.at[m], s3r.at[m], r, z_far) for m in range(2)]

    def fc_spread(level, m):
        n1, n2, a1, a2 = fc_ways(0, m)
        rows, less = fc_rows[m]
        place = ds(a1 * rows + a2 * less, less) if level == 0 else ds(a1 * rows, rows)
        held = fc_whole[m].at[0, place, :]
        return remote(held, held, fs.at[level, m], fr.at[level, m], n2 if level == 0 else n1, z)

    fc_share = (
        remote(g1w.at[0], g1w.at[1], ssib.at[0], rsib.at[0], r_sib, z),
        remote(g2w.at[0], g2w.at[1], ssib.at[1], rsib.at[1], r_sib, z),
    )

    def fc_fold_second(k, m):
        fc_first(k, m).wait_recv()
        _, _, a1, a2 = fc_ways(k, m)
        rows, less = fc_rows[m]
        place, whole = ds(a1 * rows + (1 - a2) * less, less), fc_whole[m]
        whole[k, place, :] = whole[k, place, :] + fc_half[m][k, ds((1 - a2) * less, less), :]
        fc_second(k, m).start()

    def fc_fold_third(k):
        for m in range(2):
            fc_second(k, m).wait_recv()
            _, _, a1, a2 = fc_ways(k, m)
            rows, less = fc_rows[m]
            total = fc_whole[m][k, ds(a1 * rows + a2 * less, less), :].astype(F32)
            total = total + fc_half[m][k, ds(a2 * less, less), :].astype(F32) + fc_quarter[m][k].astype(F32)
            fc_done[m][k] = total.astype(BF)
        if k == 1:
            for copy in fc_third:
                copy.start()
        for m in range(2):
            fc_first(k, m).wait_send()
            fc_second(k, m).wait_send()
        if k == 1:
            release(free.at[0], r_sib)
        else:
            release(free.at[1], r_x)
            release(free.at[1], r_y)

    def fc_finish():
        for copy in fc_third:
            copy.wait_recv()
        pl.semaphore_wait(free.at[1], 2)
        for m in range(2):
            _, _, a1, a2 = fc_ways(0, m)
            rows, less = fc_rows[m]
            fc_whole[m][0, ds(a1 * rows + a2 * less, less), :] = fc_done[m][0] + fc_far[m][...]
            fc_spread(0, m).start()

    def fc_widen():
        for m in range(2):
            fc_spread(0, m).wait_recv()
        for m in range(2):
            fc_spread(1, m).start()

    def fc_to_sibling():
        for m in range(2):
            fc_spread(1, m).wait_recv()
        pl.semaphore_wait(free.at[0], 1)
        for copy in fc_share:
            copy.start()

    sizes = tuple(width >> level for level in range(1, 5))

    def hops(j):
        ways = {"x": (r_x, z, x), "y": (r_y, z, y), "z": (r, z_pair, lax.rem(z, 2))}
        return [(r_sib, z, c)] + [ways[axis] for axis in PATHS[j]]

    def base(path, level):
        start = 0
        for (_, _, bit), size in zip(path[:level], sizes):
            start = start + bit * size
        return start

    def core_copy(j):
        src = gw.at[j, :, ds((1 - c) * half, half), :]
        return remote(src, parts[0].at[j], qs.at[j, 0], qr.at[j, 0], r_sib, z)

    def chunk_copy(j, step):
        path = hops(j)
        if step == 0:
            return core_copy(j)
        if step < 4:
            row, column, bit = path[step]
            start = base(path, step) + (1 - bit) * sizes[step]
            return remote(gw.at[j, :, ds(start, sizes[step]), :], parts[step].at[j], qs.at[j, step], qr.at[j, step], row, column)
        if step == 4:
            own = gw.at[j, :, ds(base(path, 4), sizes[3]), :]
            return remote(own, far.at[j], qs.at[j, 4], qr.at[j, 4], r, z_far)
        level = 8 - step
        row, column, _ = path[level]
        held = gw.at[j, :, ds(base(path, level + 1), sizes[level]), :]
        return remote(held, held, qs.at[j, step], qr.at[j, step], row, column)

    def chunk_step(j, step):
        path = hops(j)
        chunk_copy(j, step - 1).wait()
        if step <= 4:
            row, column, _ = path[step - 1]
            pl.semaphore_signal(
                chunk_free.at[j, step - 1], inc=1, device_id={"rows": row, "mlp": column}, device_id_type=MESH
            )
            start = base(path, min(step, 4))
            if step < 4:
                start = base(path, step) + (1 - path[step][2]) * sizes[step]
            size = sizes[min(step, 3)]
            total = gw[j, :, ds(start, size), :].astype(F32)
            for level in range(step):
                total = total + parts[level][j, :, ds(start - base(path, level + 1), size), :].astype(F32)
            gw[j, :, ds(start, size), :] = total.astype(BF)
        if step == 5:
            own = ds(base(path, 4), sizes[3])
            gw[j, :, own, :] = gw[j, :, own, :] + far[j]
        if 5 <= step <= 8:
            pl.semaphore_wait(chunk_free.at[j, 8 - step], 1)
        if step <= 8:
            chunk_copy(j, step).start()

    def small_copy(level):
        row = (r_sib, r_x, r_y)[level]
        return remote(sma.at[level], smr.at[level], sms.at[level], smrs.at[level], row, z)

    def small_z(step):
        src, dst = smz.at[2 * step], smz.at[2 * step + 1]
        return remote(src, dst, smzs.at[step], smzr.at[step], r, (z_pair, z_far)[step])

    barrier = pltpu.get_barrier_semaphore()
    partners = ((r_sib, z), (r_x, z), (r_y, z), (r_diag, z), (r, z_pair), (r, z_far))
    for row, column in partners:
        pl.semaphore_signal(barrier, inc=1, device_id={"rows": row, "mlp": column}, device_id_type=MESH)
    load_c.start()
    load_x.start()
    for copy in load_small:
        copy.start()
    load_qkv.start()
    load_out.start()
    own_shard(0).start()
    own_shard(1).start()
    pl.semaphore_wait(barrier, len(partners))
    gather_copy(0, 0).start()
    gather_copy(1, 0).start()
    load_c.wait()
    for i in range(images):
        work[...] = jnp.zeros_like(work)
        work[0:patches, :] = c_ref[:, i, :]
        cot[i * tall : (i + 1) * tall, :] = work[...]
    cot_copy(0).start()
    cot_copy(1).start()
    load_x.wait()
    for copy in load_small:
        copy.wait()
    for i in range(images):
        forward_rows(i, x_ref, rank_ref, kept_ref, g1_ref, rw_ref, xp, keep, gate, h1, work)

    load_qkv.wait()

    @pl.loop(0, 3 * width // 256)
    def _(j):
        forward_qkv(j, h1, wqkv, qkv)

    @pl.loop(0, HEADS // 2)
    def _(p):
        for i in range(images):
            attend(p, i, width, tall, qkv, keep, probs, context, contextt)

        @pl.when(p == 2)
        def _():
            gather_forward(0)

        @pl.when(p == 5)
        def _():
            gather_forward(1)

    load_out.wait()

    @pl.loop(0, images)
    def _(i):
        forward_out(i, tall, context, wout, xp, keep, gate, g2_ref, attended, middle, tok)
        token_copy(i, 0).start()
        token_copy(i, 1).start()

    own_shard(0).wait()
    own_shard(1).wait()

    def at(block, number, do):
        @pl.when(block == number)
        def _():
            do()

    def before_sibling():
        for i in range(images):
            token_copy(i, 0).wait_recv()
        cot_copy(0).wait_recv()

    h1t[...] = h1[...].T

    @pl.loop(0, 2 * images)
    def _(block):
        at(block, images, before_sibling)
        rows = ds(block * tall, tall)
        hid[rows, 0:part], gpre[rows, 0:part] = mlp_rows(tok[rows, :], cot[rows, :], w1[:, 0:part], w2[0:part, :])

    cot_copy(1).wait_recv()
    cot_copy(2).start()
    for mat in range(2):
        for kind in (1, 2, 3):
            gather_copy(mat, kind).wait_recv()
    for ref in (dg1, dg2, drw):
        ref[...] = jnp.zeros_like(ref)

    def before_near():
        cot_copy(2).wait_recv()
        gh2_to_sib.start()
        out_to_sib.start()

    def forward_token(i):
        token_copy(i, 1).wait_recv()
        token_copy(i, 2).start()

    def send_far(i):
        gh2_over(i).wait_recv()
        rows = ds(t_own + i * tall, tall)
        gh2_part[rows, :] = gh2_part[rows, :] + gh2_near[ds(i * tall, tall), :]
        gh2_far_copy(i).start()

    def before_last():
        send_far(0)
        token_copy(1, 2).wait_recv()

    @pl.loop(0, 8)
    def _(block):
        at(block, 3, lambda: forward_token(0))
        at(block, 4, before_near)
        at(block, 5, lambda: token_copy(0, 2).wait_recv())
        at(block, 6, lambda: forward_token(1))
        at(block, 7, before_last)
        inner = lax.rem(block, 5)
        swap = lax.div(block, 5) * (1 - 2 * inner + 3 * lax.div(inner * (inner - 1), 2))
        spot = block + swap
        rows = ds(spot * tall, tall)

        @pl.when(block < 2 * images)
        def _():
            hid[rows, part:], gpre[rows, part:] = mlp_rows(tok[rows, :], cot[rows, :], w1[:, part:], w2[part:, :])

        @pl.when(block >= 2 * images)
        def _():
            hid[rows, :], gpre[rows, :] = mlp_rows(tok[rows, :], cot[rows, :], w1[...], w2[...])

        share_out = dot_nn(hid[rows, :], w2[...])
        share_gh2 = dot_nt(gpre[rows, :], w1[...])

        @pl.when(block < images)
        def _():
            out[rows, :] = share_out
            gh2[rows, :] = share_gh2

        @pl.when(block >= images)
        def _():
            there = ds(lax.max(spot - images, 0) * tall, tall)
            out_part[there, :] = share_out.astype(BF)
            gh2_part[there, :] = share_gh2.astype(BF)

        at(block, 5, lambda: gh2_over(0).start())
        at(block, 7, lambda: gh2_over(1).start())

    out_over.start()
    turned[...] = tok[...].T
    for m in range(3):
        rows = slice(m * width // 3, (m + 1) * width // 3)
        total = dot_nn(turned[rows, :], gpre[...]).astype(BF)
        g1w[0, rows, :] = total[:, 0:part]
        g1w[1, rows, :] = total[:, part:]
    for k in range(2):
        fc_first(k, 0).start()
    send_far(1)
    turned[...] = hid[...].T
    for m in range(2):
        g2w[m] = dot_nn(turned[m * part : (m + 1) * part, :], cot[...]).astype(BF)
    for k in range(2):
        fc_first(k, 1).start()

    def back_image(i):
        if i == 0:
            gh2_to_sib.wait_recv()
            for n in range(images):
                token_copy(n, 0).wait_send()
                token_copy(n, 1).wait_send()
        gh2_far_copy(i).wait_recv()
        rows = pl.ds(i * tall, tall)
        gh2[rows, :] += gh2_sib[rows, :].astype(F32) + gh2_far[rows, :].astype(F32)
        back_rows(i, tall, cot, gh2, middle, keep, gate, attended, g2_ref, gh2, tok, glogit, dg2)
        context[rows, :] = dot_nt(tok[rows, :], wout[...]).astype(BF)

    def fill(j, total):
        for b in range(3):
            gw[j, b] = total[:, b * 128 : (b + 1) * 128].astype(BF)
        core_copy(j).start()

    def grad_out_half(n):
        total = 0.0
        for i in range(images):
            total = total + dot_nn(contextt[i], tok[i * tall : (i + 1) * tall, n * half : (n + 1) * half])
        fill(n, total)

    def pair_chunk(p):
        fill(p + 2, dot_nn(h1t[...], pair_columns(qkv, p, width)))

    def finish(i):
        rows = pl.ds(i * tall, tall)
        dy = dot_nt(qkv[rows, :], wqkv[...])
        back_input(i, tall, dy, glogit, rw_ref, xp, h1, g1_ref, gh2, x_ref, dg1, drw)
        if i == images - 1:
            sma[0] = jnp.concatenate([dg1[...], drw[...], dg2[...], jnp.zeros((5, width), F32)], 0)
            small_copy(0).start()

    def small_step(step):
        if step < 3:
            small_copy(step - 1).wait()
            sma[step] = sma[step - 1] + smr[step - 1]
            small_copy(step).start()
        elif step == 3:
            small_copy(2).wait()
            smz[0] = sma[2] + smr[2]
            small_z(0).start()
        else:
            small_z(step - 4).wait()
            if step == 4:
                smz[2] = smz[0] + smz[1]
                small_z(1).start()
            else:
                small_out[...] = smz[2] + smz[3]

    def out_send():
        out_over.wait_recv()
        rows = pl.ds(t_own, t_own)
        out_part[rows, :] = out_part[rows, :] + out_near[...]
        out_far_copy.start()

    def out_finish(i):
        if i == 0:
            out_to_sib.wait_recv()
            out_far_copy.wait_recv()
        rows = pl.ds(i * tall, tall)
        total = middle[rows, :] + out[rows, :] + out_sib[rows, :].astype(F32) + out_far[rows, :].astype(F32)
        c_ref[:, i, :] = total.astype(BF)[0:patches, :]

    def fc_share_end():
        for copy in fc_share:
            copy.wait()

    single = {"fc": fc_finish, "fd": fc_widen, "fe": fc_to_sibling, "ff": fc_share_end, "osend": out_send}
    numbered = (("finish", finish), ("back", back_image), ("out", grad_out_half),
                ("fb", fc_fold_third), ("g", small_step), ("o", out_finish))

    def perform(names):
        for name in names:
            if name in single:
                single[name]()
            elif name[:2] == "fa":
                fc_fold_second(int(name[2]), int(name[3]))
            elif name[0] == "c":
                chunk_step(int(name[1]), int(name[3]))
            else:
                do = next(f for head, f in numbered if name[:-1] == head)
                do(int(name[-1]))

    first, start, stop = ORDER.index("pairs0"), ORDER.index("pairs1"), ORDER.index("last2")
    perform(ORDER[:first])

    @pl.loop(0, HEADS // 4)
    def _(n):
        for p in (2 * n, 2 * n + 1):
            attend_back(p, 0, width, tall, qkv, probs, context)

    perform(ORDER[first + 1 : start])
    marks = [ORDER.index(name) for k in range(3) for name in ("pairs%d" % (k + 1), "last%d" % k)]

    @pl.loop(0, HEADS // 4)
    def _(n):
        for p in (2 * n, 2 * n + 1):
            attend_back(p, 1, width, tall, qkv, probs, context)
        pair_chunk(2 * n)
        for k in range(3):
            at(n, k, lambda k=k: perform(ORDER[marks[2 * k] + 1 : marks[2 * k + 1]]))
        pair_chunk(2 * n + 1)
        for k in range(2):
            at(n, k, lambda k=k: perform(ORDER[marks[2 * k + 1] + 1 : marks[2 * k + 2]]))

    perform(ORDER[stop + 1 :])
    for level in range(2):
        for m in range(2):
            fc_spread(level, m).wait_send()
    for copy in fc_third:
        copy.wait_send()
    for mat in range(2):
        for kind in range(4):
            gather_copy(mat, kind).wait_send()
    for i in range(images):
        token_copy(i, 2).wait_send()
        gh2_over(i).wait_send()
        gh2_far_copy(i).wait_send()
    for hop in range(3):
        cot_copy(hop).wait_send()
    for copy in (gh2_to_sib, out_to_sib, out_over, out_far_copy):
        copy.wait_send()


VMEM = pl.BlockSpec(memory_space=pltpu.VMEM)
SMEM = pl.BlockSpec(memory_space=pltpu.SMEM)
ANY = pl.BlockSpec(memory_space=pl.ANY)


def widen_kernel(
    block, gx, gw, gf1, gf2, small, block_out, gx_out, gq_out, go_out, f1_out, f2_out, g1_out, rw_out, g2_out,
    gq_wide, go_wide, f1_wide, f2_wide, store_sem, pass_sem,
):
    _, width, part = gf1.shape
    step = width // WIDEN
    c = lax.rem(lax.axis_index("rows"), 2)
    passed = [pltpu.make_async_copy(src, dst, pass_sem.at[k]) for k, (src, dst) in enumerate(((block, block_out), (gx, gx_out)))]

    def rows_of(i):
        return pl.ds(pl.multiple_of(i * step, 16), step)

    def stores(i):
        rows = rows_of(i)
        pairs = ((gq_wide, gq_out), (go_wide, go_out), (f1_wide, f1_out), (f2_wide, f2_out))
        return [
            pltpu.make_async_copy(src.at[rows, :], dst.at[rows, :], store_sem.at[i, k]) for k, (src, dst) in enumerate(pairs)
        ]

    @pl.loop(0, WIDEN)
    def _(i):
        rows = rows_of(i)
        for p in range(CHUNKS - 2):
            for b in range(3):
                start = b * width + p * 128
                gq_wide[rows, start : start + 128] = gw[2 + p, b, rows, :].astype(F32)
        for b in range(6):
            go_wide[rows, b * 128 : (b + 1) * 128] = gw[b // 3, b % 3, rows, :].astype(F32)
        for k in range(2):
            core = c + k - 2 * c * k
            f1_wide[rows, pl.ds(pl.multiple_of(core * part, 128), part)] = gf1[k, rows, :].astype(F32)
        core = lax.div(i * step, part)
        inner = pl.ds(pl.multiple_of(i * step - core * part, 16), step)
        f2_wide[rows, :] = gf2[core + c - 2 * core * c, inner, :].astype(F32)
        for copy in stores(i):
            copy.start()

    for copy in passed:
        copy.start()
    g1_out[...], rw_out[...], g2_out[...] = small[0], small[1], small[2]

    @pl.loop(0, WIDEN)
    def _(i):
        for copy in stores(i):
            copy.wait()

    for copy in passed:
        copy.wait()


def widen(*held):
    width = held[3].shape[1]
    tokens = jax.ShapeDtypeStruct(held[0].shape, BF)
    wide = [(width, 3 * width), (width, width), (width, width), (width, width)]
    return pl.pallas_call(
        widen_kernel,
        out_shape=[tokens, tokens] + [jax.ShapeDtypeStruct(dims, F32) for dims in wide] + [jax.ShapeDtypeStruct((width,), F32)] * 3,
        in_specs=[VMEM] * 6,
        out_specs=[ANY] * 6 + [VMEM] * 3,
        scratch_shapes=[pltpu.VMEM(dims, F32) for dims in wide]
        + [pltpu.SemaphoreType.DMA((WIDEN, 4)), pltpu.SemaphoreType.DMA((2,))],
        compiler_params=pltpu.CompilerParams(vmem_limit_bytes=32 * 1024 * 1024),
        name="widen",
    )(*(pltpu.with_memory_space_constraint(a, pltpu.VMEM) for a in held))


def per_device(others, images, patch_rank, kept_count, ln1_gain, router_weight, w_qkv, w_out, ln2_gain, w_fc1, w_fc2, cotangent):
    count, patches, width = images.shape
    tall = -(-patches // 16) * 16
    t = count * tall
    part = w_fc1.shape[1] // 2
    half, eighth = width // 2, width // 8

    def bf(*dims):
        return pltpu.VMEM(dims, BF)

    def f32(*dims):
        return pltpu.VMEM(dims, F32)

    def sem(*dims):
        return pltpu.SemaphoreType.DMA(dims)

    scratch = [
        pltpu.VMEM(patch_rank.shape, jnp.int32), f32(width), bf(width), f32(width),
        bf(width, 3 * width), bf(width, width), bf(width, 2 * part), bf(2 * part, width),
        bf(t, width), f32(t, 128), f32(t, 128), f32(t, 128), bf(t, width), bf(width, t), bf(t, 3 * width),
        f32(count, HEADS, tall, tall), bf(count, width, tall), bf(t, width), f32(t, width), f32(t, width),
        bf(4 * t, width), bf(4 * t, width), bf(width, 4 * t), f32(t, width), f32(t, width),
        bf(3 * t, width), bf(3 * t, width), bf(t, width), bf(t, width), bf(t, width), bf(t, width), bf(t, width), bf(t, width),
        bf(4 * t, 2 * part), bf(4 * t, 2 * part), bf(tall, width),
        bf(2, width // 2, part), bf(2, part // 2, width), bf(2, width // 4, part), bf(2, part // 4, width),
        bf(2, width // 4, part), bf(2, part // 4, width), bf(width // 4, part), bf(part // 4, width),
        bf(CHUNKS, 3, half, 128), bf(CHUNKS, 3, 2 * eighth, 128), bf(CHUNKS, 3, eighth, 128),
        bf(CHUNKS, 3, eighth // 2, 128), bf(CHUNKS, 3, eighth // 2, 128),
        f32(1, width), f32(1, width), f32(1, width), f32(3, 8, width), f32(3, 8, width), f32(4, 8, width),
        sem(6), sem(2, 4), sem(2, 4), sem(count, 3), sem(count, 3), sem(3), sem(3), sem(8), sem(8),
        sem(2, 2), sem(2, 2), sem(2, 2), sem(2, 2), sem(2), sem(2),
        sem(2, 2), sem(2, 2), sem(2), sem(2), pltpu.SemaphoreType.REGULAR((2,)), pltpu.SemaphoreType.REGULAR((CHUNKS, 4)),
        sem(CHUNKS, 9), sem(CHUNKS, 9), sem(4),
        sem(3), sem(3), sem(2), sem(2),
    ]

    block, gx, gw, gf1, gf2, small = pl.pallas_call(
        mega_kernel,
        out_shape=[
            bf(patches, count, width), bf(patches, count, width), bf(CHUNKS, 3, width, 128),
            bf(2, width, part), bf(2, part, width), f32(8, width),
        ],
        in_specs=[ANY, ANY, SMEM] + [ANY] * 8,
        out_specs=[VMEM] * 6,
        scratch_shapes=scratch,
        compiler_params=pltpu.CompilerParams(
            collective_id=0, has_side_effects=True, vmem_limit_bytes=int(55.5 * 1024) * 1024
        ),
        name="block",
    )(images.transpose(1, 0, 2), patch_rank, kept_count, ln1_gain, router_weight, w_qkv, w_out, ln2_gain, w_fc1, w_fc2,
      cotangent.transpose(1, 0, 2))
    block, gx, gq, go, f1, f2, g1, rw, g2 = widen(block, gx, gw, gf1, gf2, small)
    if others:
        gq, go, f1, f2, g1, rw, g2 = lax.psum((gq, go, f1, f2, g1, rw, g2), "rows", axis_index_groups=others)
    return block.transpose(1, 0, 2), gx.transpose(1, 0, 2), g1, rw, gq, go, g2, f1, f2


def solution(mesh):
    rows = mesh.shape["rows"]
    others = [[8 * g + i for g in range(rows // 8)] for i in range(8)] if rows > 8 else None
    return jax.shard_map(
        functools.partial(per_device, others),
        mesh=mesh,
        in_specs=(
            P(("rows", "mlp"), None, None), P(("rows", "mlp"), None), P(("rows", "mlp")), P(), P(), P(), P(), P(),
            P(None, "mlp"), P("mlp", None), P(("rows", "mlp"), None, None),
        ),
        out_specs=(
            P(("rows", "mlp"), None, None), P(("rows", "mlp"), None, None), P(), P(), P(), P(), P(),
            P(None, "mlp"), P("mlp", None),
        ),
        check_vma=False,
    )
```

```python
import functools
import jax
import jax.numpy as jnp
from jax import lax
from jax.experimental import pallas as pl
from jax.experimental.pallas import tpu as pltpu
from jax.sharding import PartitionSpec as P

HEADS = 12
EPS = 1e-6
FILL = -1e30
BF = jnp.bfloat16
F32 = jnp.float32


def dot_nn(a, b):
    return lax.dot_general(a, b, (((1,), (0,)), ((), ())), preferred_element_type=F32)


def dot_nt(a, b):
    return lax.dot_general(a, b, (((1,), (1,)), ((), ())), preferred_element_type=F32)


def dot_tn(a, b):
    return lax.dot_general(a, b, (((0,), (0,)), ((), ())), preferred_element_type=F32)


def unit_rows(v):
    center = v - jnp.mean(v, -1, keepdims=True)
    scale = lax.rsqrt(jnp.mean(center * center, -1, keepdims=True) + EPS)
    return center * scale, scale


def norm_pull(dy, gain, unit, scale):
    du = dy * gain
    return scale * (
        du
        - jnp.mean(du, -1, keepdims=True)
        - unit * jnp.mean(du * unit, -1, keepdims=True)
    )


def half_mask(rows, h):
    lane = lax.broadcasted_iota(jnp.int32, (rows, 128), 1)
    return (lane < 64) if h == 0 else (lane >= 64)


def forward_rows(i, x_ref, rank_ref, kept_ref, g1_ref, rw_ref, xp, keep, gate, h1, work):
    patches = x_ref.shape[0]
    tall = xp.shape[0] // x_ref.shape[1]
    rows = pl.ds(pl.multiple_of(i * tall, 16), tall)
    work[...] = jnp.zeros_like(work)
    work[0:patches, :] = x_ref[:, i, :]
    v = work[...]
    xp[rows, :] = v
    kept = (rank_ref[pl.ds(i, 1), :] < kept_ref[i]).astype(F32)
    keep_row = jnp.concatenate([kept, jnp.zeros((1, 256 - patches), F32)], 1)
    keep_col = jnp.broadcast_to(keep_row, (128, 256)).T
    keep[rows, :] = keep_col[0:tall, :]
    unit, _ = unit_rows(v.astype(F32))
    low = (unit * g1_ref[...][None]).astype(BF)
    h1[rows, :] = low
    logit = jnp.sum(low.astype(F32) * rw_ref[...][None].astype(F32), -1, keepdims=True)
    gate[rows, :] = jnp.broadcast_to(jax.nn.sigmoid(logit), (tall, 128))


def forward_qkv(j, h1, wqkv, qkv):
    cols = pl.ds(pl.multiple_of(j * 256, 256), 256)
    qkv[:, cols] = dot_nn(h1[...], wqkv[:, cols]).astype(BF)


def attend(p, i, width, tall, qkv, keep, probs, context, contextt):
    rows = pl.ds(pl.multiple_of(i * tall, 16), tall)
    qc = pl.ds(pl.multiple_of(p * 128, 128), 128)
    kc = pl.ds(pl.multiple_of(width + p * 128, 128), 128)
    vc = pl.ds(pl.multiple_of(2 * width + p * 128, 128), 128)
    q, k, v = qkv[rows, qc], qkv[rows, kc], qkv[rows, vc]
    vt = v.T
    kept = keep[rows, 0:1] > 0.5
    outs = []
    for h in range(2):
        kh = jnp.where(half_mask(tall, h), k, jnp.zeros_like(k))
        s = jnp.where(kept, dot_nt(kh, q) * 0.125, FILL)
        e = jnp.exp(s - jnp.max(s, 0, keepdims=True))
        pr = e * (1.0 / jnp.sum(e, 0, keepdims=True))
        probs[i, p * 2 + h] = pr
        outs.append(dot_nn(vt[h * 64 : h * 64 + 64, :], pr.astype(BF)))
    ct = jnp.concatenate(outs, 0)
    contextt[i, pl.ds(pl.multiple_of(p * 128, 128), 128), :] = ct.astype(BF)
    context[rows, qc] = ct.T.astype(BF)


def forward_out(i, tall, context, wout, xp, keep, gate, g2_ref, attended, middle, h2):
    rows = pl.ds(pl.multiple_of(i * tall, 16), tall)
    att = dot_nn(context[rows, :], wout[...])
    attended[rows, :] = att
    mid = xp[rows, :].astype(F32) + keep[rows, 0:1] * gate[rows, 0:1] * att
    middle[rows, :] = mid
    unit, _ = unit_rows(mid)
    h2[rows, :] = (unit * g2_ref[...][None]).astype(BF)


def gelu_pair(pre):
    cdf = 0.5 * (1.0 + lax.erf(pre * 0.7071067811865476))
    pdf = jnp.exp(pre * pre * -0.5) * 0.3989422804014327
    return pre * cdf, cdf + pre * pdf


def mlp_rows(h, c, w1, w2):
    pre = dot_nn(h, w1)
    hidden, slope = gelu_pair(pre)
    grad = dot_nt(c, w2) * slope
    return hidden.astype(BF), grad.astype(BF)


def back_rows(i, tall, c_ref, gh2, middle, keep, gate, attended, g2_ref, gmid, gatt, glogit, dg2):
    rows = pl.ds(pl.multiple_of(i * tall, 16), tall)
    dy = gh2[rows, :]
    unit, scale = unit_rows(middle[rows, :])
    gm = c_ref[rows, :].astype(F32) + norm_pull(dy, g2_ref[...][None], unit, scale)
    gmid[rows, :] = gm
    dg2[...] += jnp.sum(dy * unit, 0, keepdims=True)
    k, g = keep[rows, 0:1], gate[rows, 0:1]
    kept = gm * k
    gatt[rows, :] = (kept * g).astype(BF)
    gl = jnp.sum(kept * attended[rows, :], -1, keepdims=True) * g * (1.0 - g)
    glogit[rows, :] = jnp.broadcast_to(gl, (tall, 128))


def attend_back(p, i, width, tall, qkv, probs, gctx):
    rows = pl.ds(pl.multiple_of(i * tall, 16), tall)
    qc = pl.ds(pl.multiple_of(p * 128, 128), 128)
    kc = pl.ds(pl.multiple_of(width + p * 128, 128), 128)
    vc = pl.ds(pl.multiple_of(2 * width + p * 128, 128), 128)
    q, k, v = qkv[rows, qc], qkv[rows, kc], qkv[rows, vc]
    gc = gctx[rows, qc]
    kt = k.T
    gv, gk, gq = 0.0, 0.0, []
    for h in range(2):
        mask = half_mask(tall, h)
        zero = jnp.zeros_like(v)
        pr = probs[i, p * 2 + h]
        gp = dot_nt(jnp.where(mask, v, zero), gc)
        gs = (pr * (gp - jnp.sum(pr * gp, 0, keepdims=True))).astype(BF)
        gv = gv + dot_nn(pr.astype(BF), jnp.where(mask, gc, zero))
        gk = gk + dot_nn(gs, jnp.where(mask, q, zero))
        gq.append(dot_nn(kt[h * 64 : h * 64 + 64, :], gs))
    qkv[rows, qc] = (jnp.concatenate(gq, 0).T * 0.125).astype(BF)
    qkv[rows, kc] = (gk * 0.125).astype(BF)
    qkv[rows, vc] = gv.astype(BF)


def pair_columns(wqkv, p, width):
    return jnp.concatenate(
        [wqkv[:, pl.ds(pl.multiple_of(b * width + p * 128, 128), 128)] for b in range(3)], 1
    )


def back_input(i, tall, dy, glogit, rw_ref, xp, h1, g1_ref, gmid, gx_ref, dg1, drw):
    rows = pl.ds(pl.multiple_of(i * tall, 16), tall)
    patches = gx_ref.shape[0]
    gl = glogit[rows, 0:1]
    dy = dy + gl * rw_ref[...][None].astype(F32)
    unit, scale = unit_rows(xp[rows, :].astype(F32))
    dg1[...] += jnp.sum(dy * unit, 0, keepdims=True)
    drw[...] += jnp.sum(h1[rows, :].astype(F32) * gl, 0, keepdims=True)
    out = gmid[rows, :] + norm_pull(dy, g1_ref[...][None], unit, scale)
    gx_ref[:, i, :] = out.astype(BF)[0:patches, :]

MESH = pl.DeviceIdType.MESH
CHUNKS = HEADS // 2 + 2
WIDEN = 8
PATHS = ("xzy", "zxy", "yzx", "xzy", "yxz", "xyz", "yzx", "yzx")
ORDER = (
    "osend", "back0", "pairs0", "back1", "pairs1", "fa10", "fa11", "last0", "pairs2", "last1", "fa01", "c2.1",
    "pairs3", "fb1", "c4.1", "last2", "c5.1", "out1", "c3.1", "c2.2", "fa00", "out0", "finish0", "c6.1", "c1.1",
    "c4.2", "c0.1", "c5.2", "finish1", "c3.2", "c7.1", "c6.2", "c2.3", "c1.2", "fb0", "c5.3", "fc", "c0.2", "c4.3",
    "c5.4", "g1", "c1.3", "c6.3", "c2.4", "c3.3", "c7.2", "c0.3", "c4.4", "fd", "c1.4", "c5.5", "c0.4", "c4.5",
    "c6.4", "c7.3", "c3.4", "c5.6", "g2", "c2.5", "c0.5", "c4.6", "c7.4", "c6.5", "fe", "c1.5", "c2.6", "c5.7",
    "c3.5", "c4.7", "c0.6", "g3", "c6.6", "c7.5", "c3.6", "c2.7", "c1.6", "c0.7", "c7.6", "c5.8", "ff", "c6.7",
    "c4.8", "o0", "c1.7", "g4", "c3.7", "c2.8", "c7.7", "c0.8", "c4.9", "c6.8", "c1.8", "c3.8", "c7.8", "c0.9",
    "c5.9", "c1.9", "g5", "o1", "c6.9", "c2.9", "c3.9", "c7.9",
)


def mega_kernel(
    x_hbm, rank_hbm, kept_hbm, g1_hbm, rw_hbm, wqkv_hbm, wout_hbm, g2_hbm, fc1, fc2, c_hbm,
    c_ref, x_ref, gw, g1w, g2w, small_out,
    rank_ref, kept_ref, g1_ref, rw_ref, g2_ref, wqkv, wout, w1, w2, xp, keep, gate, glogit, h1, h1t, qkv, probs, contextt, context, attended, middle,
    tok, cot, turned, out, gh2, out_part, gh2_part, out_sib, gh2_sib, out_near, gh2_near, out_far, gh2_far, hid, gpre, work,
    r1a, r1b, r2a, r2b, fz1, fz2, rz1, rz2,
    q0, q1, q2, q3, far, dg1, dg2, drw, sma, smr, smz,
    lsem, gsend, grecv, hsend, hrecv, csend, crecv, esend, erecv, s1s, s1r, s2s, s2r, s3s, s3r, fs, fr, ssib, rsib, free, chunk_free,
    qs, qr, small_sem, sms, smrs, smzs, smzr,
):
    patches, images, width = x_ref.shape
    t_own = xp.shape[0]
    tall = t_own // images
    half = width // 2
    part = w1.shape[1] // 2
    parts = (q0, q1, q2, q3)
    quarter = (width // 4, part // 4)
    r = lax.axis_index("rows")
    z = lax.axis_index("mlp")
    c, x, y = lax.rem(r, 2), lax.rem(lax.div(r, 2), 2), lax.rem(lax.div(r, 4), 2)
    r_sib, r_x, r_y = r + 1 - 2 * c, r + 2 - 4 * x, r + 4 - 8 * y
    r_diag = r_x + r_y - r
    z_pair, z_far = z + 1 - 2 * lax.rem(z, 2), z + 2 - 4 * lax.div(z, 2)
    q = 2 * y + x

    def ds(start, size):
        return pl.ds(pl.multiple_of(start, 16), size)

    def lanes(start, size):
        return pl.ds(pl.multiple_of(start, 128), size)

    def remote(src, dst, send, recv, row, column):
        return pltpu.make_async_remote_copy(
            src_ref=src, dst_ref=dst, send_sem=send, recv_sem=recv,
            device_id={"rows": row, "mlp": column}, device_id_type=MESH,
        )

    def release(semaphore, row):
        pl.semaphore_signal(semaphore, inc=1, device_id={"rows": row, "mlp": z}, device_id_type=MESH)

    def gather_copy(mat, kind):
        size = quarter[mat]
        sems = gsend.at[mat, kind], grecv.at[mat, kind]
        if mat == 0:
            place = w1.at[ds(q * size, size), pl.ds(part, part)]
            own = fc1.at[ds(q * size, size), lanes(c * part, part)]
        else:
            place = w2.at[ds(part + q * size, size), :]
            own = fc2.at[ds(c * part + q * size, size), :]
        if kind == 0:
            return remote(own, place, *sems, r, z_far)
        return remote(place, place, *sems, (r_x, r_y, r_diag)[kind - 1], z)

    def gather_forward(mat):
        gather_copy(mat, 0).wait_recv()
        for kind in (1, 2, 3):
            gather_copy(mat, kind).start()

    def own_shard(mat):
        if mat == 0:
            return pltpu.make_async_copy(fc1.at[:, lanes(c * part, part)], w1.at[:, pl.ds(0, part)], lsem.at[0])
        return pltpu.make_async_copy(fc2.at[ds(c * part, part), :], w2.at[pl.ds(0, part), :], lsem.at[1])

    load_qkv = pltpu.make_async_copy(wqkv_hbm, wqkv, lsem.at[2])
    load_out = pltpu.make_async_copy(wout_hbm, wout, lsem.at[3])
    load_x = pltpu.make_async_copy(x_hbm, x_ref, lsem.at[4])
    load_small = [
        pltpu.make_async_copy(src, dst, small_sem.at[k])
        for k, (src, dst) in enumerate(((rank_hbm, rank_ref), (kept_hbm, kept_ref), (g1_hbm, g1_ref), (rw_hbm, rw_ref), (g2_hbm, g2_ref)))
    ]
    load_c = pltpu.make_async_copy(c_hbm, c_ref, lsem.at[5])

    def token_copy(i, hop):
        start = (0, 0, 2 * t_own)[hop] + i * tall
        src, dst = tok.at[ds(start, tall), :], tok.at[ds((1, 2, 3)[hop] * t_own + i * tall, tall), :]
        row, column = (r, z_pair) if hop == 1 else (r_sib, z)
        return remote(src, dst, hsend.at[i, hop], hrecv.at[i, hop], row, column)

    def cot_copy(hop):
        src, dst = cot.at[ds((0, 0, 2)[hop] * t_own, t_own), :], cot.at[ds((1, 2, 3)[hop] * t_own, t_own), :]
        row, column = (r, z_pair) if hop == 1 else (r_sib, z)
        return remote(src, dst, csend.at[hop], crecv.at[hop], row, column)

    gh2_to_sib = remote(gh2_part.at[ds(0, t_own), :], gh2_sib, esend.at[0], erecv.at[0], r_sib, z)
    out_to_sib = remote(out_part.at[ds(0, t_own), :], out_sib, esend.at[1], erecv.at[1], r_sib, z)
    out_over = remote(out_part.at[ds(2 * t_own, t_own), :], out_near, esend.at[2], erecv.at[2], r_sib, z)
    out_far_copy = remote(out_part.at[ds(t_own, t_own), :], out_far, esend.at[3], erecv.at[3], r, z_pair)

    def gh2_over(i):
        src = gh2_part.at[ds(2 * t_own + i * tall, tall), :]
        return remote(src, gh2_near.at[ds(i * tall, tall), :], esend.at[4 + i], erecv.at[4 + i], r_sib, z)

    def gh2_far_copy(i):
        src = gh2_part.at[ds(t_own + i * tall, tall), :]
        return remote(src, gh2_far.at[ds(i * tall, tall), :], esend.at[6 + i], erecv.at[6 + i], r, z_pair)

    fc_whole, fc_half, fc_quarter, fc_done, fc_far = (g1w, g2w), (r1a, r1b), (r2a, r2b), (fz1, fz2), (rz1, rz2)
    fc_rows = ((width // 2, width // 4), (part // 2, part // 4))

    def fc_ways(k, m):
        shard = lax.div(z, 2) if k == 0 else 1 - lax.div(z, 2)
        turn = lax.rem(shard + m, 2)
        return r_x + (r_y - r_x) * turn, r_y + (r_x - r_y) * turn, x + (y - x) * turn, y + (x - y) * turn

    def fc_first(k, m):
        n1, _, a1, _ = fc_ways(k, m)
        rows, _ = fc_rows[m]
        src = fc_whole[m].at[k, ds((1 - a1) * rows, rows), :]
        return remote(src, fc_half[m].at[k], s1s.at[k, m], s1r.at[k, m], n1, z)

    def fc_second(k, m):
        _, n2, a1, a2 = fc_ways(k, m)
        rows, less = fc_rows[m]
        src = fc_whole[m].at[k, ds(a1 * rows + (1 - a2) * less, less), :]
        return remote(src, fc_quarter[m].at[k], s2s.at[k, m], s2r.at[k, m], n2, z)

    fc_third = [remote(fc_done[m].at[1], fc_far[m], s3s.at[m], s3r.at[m], r, z_far) for m in range(2)]

    def fc_spread(level, m):
        n1, n2, a1, a2 = fc_ways(0, m)
        rows, less = fc_rows[m]
        place = ds(a1 * rows + a2 * less, less) if level == 0 else ds(a1 * rows, rows)
        held = fc_whole[m].at[0, place, :]
        return remote(held, held, fs.at[level, m], fr.at[level, m], n2 if level == 0 else n1, z)

    fc_share = (
        remote(g1w.at[0], g1w.at[1], ssib.at[0], rsib.at[0], r_sib, z),
        remote(g2w.at[0], g2w.at[1], ssib.at[1], rsib.at[1], r_sib, z),
    )

    def fc_fold_second(k, m):
        fc_first(k, m).wait_recv()
        _, _, a1, a2 = fc_ways(k, m)
        rows, less = fc_rows[m]
        place, whole = ds(a1 * rows + (1 - a2) * less, less), fc_whole[m]
        whole[k, place, :] = whole[k, place, :] + fc_half[m][k, ds((1 - a2) * less, less), :]
        fc_second(k, m).start()

    def fc_fold_third(k):
        for m in range(2):
            fc_second(k, m).wait_recv()
            _, _, a1, a2 = fc_ways(k, m)
            rows, less = fc_rows[m]
            total = fc_whole[m][k, ds(a1 * rows + a2 * less, less), :].astype(F32)
            total = total + fc_half[m][k, ds(a2 * less, less), :].astype(F32) + fc_quarter[m][k].astype(F32)
            fc_done[m][k] = total.astype(BF)
        if k == 1:
            for copy in fc_third:
                copy.start()
        for m in range(2):
            fc_first(k, m).wait_send()
            fc_second(k, m).wait_send()
        if k == 1:
            release(free.at[0], r_sib)
        else:
            release(free.at[1], r_x)
            release(free.at[1], r_y)

    def fc_finish():
        for copy in fc_third:
            copy.wait_recv()
        pl.semaphore_wait(free.at[1], 2)
        for m in range(2):
            _, _, a1, a2 = fc_ways(0, m)
            rows, less = fc_rows[m]
            fc_whole[m][0, ds(a1 * rows + a2 * less, less), :] = fc_done[m][0] + fc_far[m][...]
            fc_spread(0, m).start()

    def fc_widen():
        for m in range(2):
            fc_spread(0, m).wait_recv()
        for m in range(2):
            fc_spread(1, m).start()

    def fc_to_sibling():
        for m in range(2):
            fc_spread(1, m).wait_recv()
        pl.semaphore_wait(free.at[0], 1)
        for copy in fc_share:
            copy.start()

    sizes = tuple(width >> level for level in range(1, 5))

    def hops(j):
        ways = {"x": (r_x, z, x), "y": (r_y, z, y), "z": (r, z_pair, lax.rem(z, 2))}
        return [(r_sib, z, c)] + [ways[axis] for axis in PATHS[j]]

    def base(path, level):
        start = 0
        for (_, _, bit), size in zip(path[:level], sizes):
            start = start + bit * size
        return start

    def core_copy(j):
        src = gw.at[j, ds((1 - c) * half, half), :]
        return remote(src, parts[0].at[j], qs.at[j, 0], qr.at[j, 0], r_sib, z)

    def chunk_copy(j, step):
        path = hops(j)
        if step == 0:
            return core_copy(j)
        if step < 4:
            row, column, bit = path[step]
            start = base(path, step) + (1 - bit) * sizes[step]
            return remote(gw.at[j, ds(start, sizes[step]), :], parts[step].at[j], qs.at[j, step], qr.at[j, step], row, column)
        if step == 4:
            own = gw.at[j, ds(base(path, 4), sizes[3]), :]
            return remote(own, far.at[j], qs.at[j, 4], qr.at[j, 4], r, z_far)
        level = 8 - step
        row, column, _ = path[level]
        held = gw.at[j, ds(base(path, level + 1), sizes[level]), :]
        return remote(held, held, qs.at[j, step], qr.at[j, step], row, column)

    def chunk_step(j, step):
        path = hops(j)
        chunk_copy(j, step - 1).wait()
        if step <= 4:
            row, column, _ = path[step - 1]
            pl.semaphore_signal(
                chunk_free.at[j, step - 1], inc=1, device_id={"rows": row, "mlp": column}, device_id_type=MESH
            )
            start = base(path, min(step, 4))
            if step < 4:
                start = base(path, step) + (1 - path[step][2]) * sizes[step]
            size = sizes[min(step, 3)]
            total = gw[j, ds(start, size), :].astype(F32)
            for level in range(step):
                total = total + parts[level][j, ds(start - base(path, level + 1), size), :].astype(F32)
            gw[j, ds(start, size), :] = total.astype(BF)
        if step == 5:
            own = ds(base(path, 4), sizes[3])
            gw[j, own, :] = gw[j, own, :] + far[j]
        if 5 <= step <= 8:
            pl.semaphore_wait(chunk_free.at[j, 8 - step], 1)
        if step <= 8:
            chunk_copy(j, step).start()

    def small_copy(level):
        row = (r_sib, r_x, r_y)[level]
        return remote(sma.at[level], smr.at[level], sms.at[level], smrs.at[level], row, z)

    def small_z(step):
        src, dst = smz.at[2 * step], smz.at[2 * step + 1]
        return remote(src, dst, smzs.at[step], smzr.at[step], r, (z_pair, z_far)[step])

    barrier = pltpu.get_barrier_semaphore()
    partners = ((r_sib, z), (r_x, z), (r_y, z), (r_diag, z), (r, z_pair), (r, z_far))
    for row, column in partners:
        pl.semaphore_signal(barrier, inc=1, device_id={"rows": row, "mlp": column}, device_id_type=MESH)
    load_c.start()
    load_x.start()
    for copy in load_small:
        copy.start()
    load_qkv.start()
    load_out.start()
    own_shard(0).start()
    own_shard(1).start()
    pl.semaphore_wait(barrier, len(partners))
    gather_copy(0, 0).start()
    gather_copy(1, 0).start()
    load_c.wait()
    for i in range(images):
        work[...] = jnp.zeros_like(work)
        work[0:patches, :] = c_ref[:, i, :]
        cot[i * tall : (i + 1) * tall, :] = work[...]
    cot_copy(0).start()
    cot_copy(1).start()
    load_x.wait()
    for copy in load_small:
        copy.wait()
    for i in range(images):
        forward_rows(i, x_ref, rank_ref, kept_ref, g1_ref, rw_ref, xp, keep, gate, h1, work)

    load_qkv.wait()

    @pl.loop(0, 3 * width // 256)
    def _(j):
        forward_qkv(j, h1, wqkv, qkv)

    @pl.loop(0, HEADS // 2)
    def _(p):
        for i in range(images):
            attend(p, i, width, tall, qkv, keep, probs, context, contextt)

        @pl.when(p == 2)
        def _():
            gather_forward(0)

        @pl.when(p == 5)
        def _():
            gather_forward(1)

    load_out.wait()

    @pl.loop(0, images)
    def _(i):
        forward_out(i, tall, context, wout, xp, keep, gate, g2_ref, attended, middle, tok)
        token_copy(i, 0).start()
        token_copy(i, 1).start()

    own_shard(0).wait()
    own_shard(1).wait()

    def at(block, number, do):
        @pl.when(block == number)
        def _():
            do()

    def before_sibling():
        for i in range(images):
            token_copy(i, 0).wait_recv()
        cot_copy(0).wait_recv()

    h1t[...] = h1[...].T

    @pl.loop(0, 2 * images)
    def _(block):
        at(block, images, before_sibling)
        rows = ds(block * tall, tall)
        hid[rows, 0:part], gpre[rows, 0:part] = mlp_rows(tok[rows, :], cot[rows, :], w1[:, 0:part], w2[0:part, :])

    cot_copy(1).wait_recv()
    cot_copy(2).start()
    for mat in range(2):
        for kind in (1, 2, 3):
            gather_copy(mat, kind).wait_recv()
    for ref in (dg1, dg2, drw):
        ref[...] = jnp.zeros_like(ref)

    def before_near():
        cot_copy(2).wait_recv()
        gh2_to_sib.start()
        out_to_sib.start()

    def forward_token(i):
        token_copy(i, 1).wait_recv()
        token_copy(i, 2).start()

    def send_far(i):
        gh2_over(i).wait_recv()
        rows = ds(t_own + i * tall, tall)
        gh2_part[rows, :] = gh2_part[rows, :] + gh2_near[ds(i * tall, tall), :]
        gh2_far_copy(i).start()

    def before_last():
        send_far(0)
        token_copy(1, 2).wait_recv()

    @pl.loop(0, 8)
    def _(block):
        at(block, 3, lambda: forward_token(0))
        at(block, 4, before_near)
        at(block, 5, lambda: token_copy(0, 2).wait_recv())
        at(block, 6, lambda: forward_token(1))
        at(block, 7, before_last)
        inner = lax.rem(block, 5)
        swap = lax.div(block, 5) * (1 - 2 * inner + 3 * lax.div(inner * (inner - 1), 2))
        spot = block + swap
        rows = ds(spot * tall, tall)

        @pl.when(block < 2 * images)
        def _():
            hid[rows, part:], gpre[rows, part:] = mlp_rows(tok[rows, :], cot[rows, :], w1[:, part:], w2[part:, :])

        @pl.when(block >= 2 * images)
        def _():
            hid[rows, :], gpre[rows, :] = mlp_rows(tok[rows, :], cot[rows, :], w1[...], w2[...])

        share_out = dot_nn(hid[rows, :], w2[...])
        share_gh2 = dot_nt(gpre[rows, :], w1[...])

        @pl.when(block < images)
        def _():
            out[rows, :] = share_out
            gh2[rows, :] = share_gh2

        @pl.when(block >= images)
        def _():
            there = ds(lax.max(spot - images, 0) * tall, tall)
            out_part[there, :] = share_out.astype(BF)
            gh2_part[there, :] = share_gh2.astype(BF)

        at(block, 5, lambda: gh2_over(0).start())
        at(block, 7, lambda: gh2_over(1).start())

    out_over.start()
    turned[...] = tok[...].T
    for m in range(3):
        rows = slice(m * width // 3, (m + 1) * width // 3)
        total = dot_nn(turned[rows, :], gpre[...]).astype(BF)
        g1w[0, rows, :] = total[:, 0:part]
        g1w[1, rows, :] = total[:, part:]
    for k in range(2):
        fc_first(k, 0).start()
    send_far(1)
    turned[...] = hid[...].T
    for m in range(2):
        g2w[m] = dot_nn(turned[m * part : (m + 1) * part, :], cot[...]).astype(BF)
    for k in range(2):
        fc_first(k, 1).start()

    def back_image(i):
        if i == 0:
            gh2_to_sib.wait_recv()
            for n in range(images):
                token_copy(n, 0).wait_send()
                token_copy(n, 1).wait_send()
        gh2_far_copy(i).wait_recv()
        rows = pl.ds(i * tall, tall)
        gh2[rows, :] += gh2_sib[rows, :].astype(F32) + gh2_far[rows, :].astype(F32)
        back_rows(i, tall, cot, gh2, middle, keep, gate, attended, g2_ref, gh2, tok, glogit, dg2)
        context[rows, :] = dot_nt(tok[rows, :], wout[...]).astype(BF)

    def fill(j, total):
        gw[j] = total.astype(BF)
        core_copy(j).start()

    def grad_out_half(n):
        total = 0.0
        for i in range(images):
            total = total + dot_nn(contextt[i], tok[i * tall : (i + 1) * tall, n * half : (n + 1) * half])
        fill(n, total)

    def pair_chunk(p):
        fill(p + 2, dot_nn(h1t[...], pair_columns(qkv, p, width)))

    def finish(i):
        rows = pl.ds(i * tall, tall)
        dy = dot_nt(qkv[rows, :], wqkv[...])
        back_input(i, tall, dy, glogit, rw_ref, xp, h1, g1_ref, gh2, x_ref, dg1, drw)
        if i == images - 1:
            sma[0] = jnp.concatenate([dg1[...], drw[...], dg2[...], jnp.zeros((5, width), F32)], 0)
            small_copy(0).start()

    def small_step(step):
        if step < 3:
            small_copy(step - 1).wait()
            sma[step] = sma[step - 1] + smr[step - 1]
            small_copy(step).start()
        elif step == 3:
            small_copy(2).wait()
            smz[0] = sma[2] + smr[2]
            small_z(0).start()
        else:
            small_z(step - 4).wait()
            if step == 4:
                smz[2] = smz[0] + smz[1]
                small_z(1).start()
            else:
                small_out[...] = smz[2] + smz[3]

    def out_send():
        out_over.wait_recv()
        rows = pl.ds(t_own, t_own)
        out_part[rows, :] = out_part[rows, :] + out_near[...]
        out_far_copy.start()

    def out_finish(i):
        if i == 0:
            out_to_sib.wait_recv()
            out_far_copy.wait_recv()
        rows = pl.ds(i * tall, tall)
        total = middle[rows, :] + out[rows, :] + out_sib[rows, :].astype(F32) + out_far[rows, :].astype(F32)
        c_ref[:, i, :] = total.astype(BF)[0:patches, :]

    def fc_share_end():
        for copy in fc_share:
            copy.wait()

    single = {"fc": fc_finish, "fd": fc_widen, "fe": fc_to_sibling, "ff": fc_share_end, "osend": out_send}
    numbered = (("finish", finish), ("back", back_image), ("out", grad_out_half),
                ("fb", fc_fold_third), ("g", small_step), ("o", out_finish))

    def perform(names):
        for name in names:
            if name in single:
                single[name]()
            elif name[:2] == "fa":
                fc_fold_second(int(name[2]), int(name[3]))
            elif name[0] == "c":
                chunk_step(int(name[1]), int(name[3]))
            else:
                do = next(f for head, f in numbered if name[:-1] == head)
                do(int(name[-1]))

    first, start, stop = ORDER.index("pairs0"), ORDER.index("pairs1"), ORDER.index("last2")
    perform(ORDER[:first])

    @pl.loop(0, HEADS // 4)
    def _(n):
        for p in (2 * n, 2 * n + 1):
            attend_back(p, 0, width, tall, qkv, probs, context)

    perform(ORDER[first + 1 : start])
    marks = [ORDER.index(name) for k in range(3) for name in ("pairs%d" % (k + 1), "last%d" % k)]

    @pl.loop(0, HEADS // 4)
    def _(n):
        for p in (2 * n, 2 * n + 1):
            attend_back(p, 1, width, tall, qkv, probs, context)
        pair_chunk(2 * n)
        for k in range(3):
            at(n, k, lambda k=k: perform(ORDER[marks[2 * k] + 1 : marks[2 * k + 1]]))
        pair_chunk(2 * n + 1)
        for k in range(2):
            at(n, k, lambda k=k: perform(ORDER[marks[2 * k + 1] + 1 : marks[2 * k + 2]]))

    perform(ORDER[stop + 1 :])
    for level in range(2):
        for m in range(2):
            fc_spread(level, m).wait_send()
    for copy in fc_third:
        copy.wait_send()
    for mat in range(2):
        for kind in range(4):
            gather_copy(mat, kind).wait_send()
    for i in range(images):
        token_copy(i, 2).wait_send()
        gh2_over(i).wait_send()
        gh2_far_copy(i).wait_send()
    for hop in range(3):
        cot_copy(hop).wait_send()
    for copy in (gh2_to_sib, out_to_sib, out_over, out_far_copy):
        copy.wait_send()


VMEM = pl.BlockSpec(memory_space=pltpu.VMEM)
ANY = pl.BlockSpec(memory_space=pl.ANY)


def widen_kernel(
    block, gx, gw, gf1, gf2, small, block_out, gx_out, gq_out, go_out, f1_out, f2_out, g1_out, rw_out, g2_out,
    gq_wide, go_wide, f1_wide, f2_wide, store_sem, pass_sem,
):
    _, width, part = gf1.shape
    step = width // WIDEN
    c = lax.rem(lax.axis_index("rows"), 2)
    passed = [pltpu.make_async_copy(src, dst, pass_sem.at[k]) for k, (src, dst) in enumerate(((block, block_out), (gx, gx_out)))]

    def rows_of(i):
        return pl.ds(pl.multiple_of(i * step, 16), step)

    def stores(i):
        rows = rows_of(i)
        pairs = ((gq_wide, gq_out), (go_wide, go_out), (f1_wide, f1_out), (f2_wide, f2_out))
        return [
            pltpu.make_async_copy(src.at[rows, :], dst.at[rows, :], store_sem.at[i, k]) for k, (src, dst) in enumerate(pairs)
        ]

    @pl.loop(0, WIDEN)
    def _(i):
        rows = rows_of(i)
        for p in range(CHUNKS - 2):
            for b in range(3):
                start = b * width + p * 128
                gq_wide[rows, start : start + 128] = gw[2 + p, rows, b * 128 : (b + 1) * 128].astype(F32)
        for h in range(2):
            go_wide[rows, h * part : (h + 1) * part] = gw[h, rows, :].astype(F32)
        for k in range(2):
            core = c + k - 2 * c * k
            f1_wide[rows, pl.ds(pl.multiple_of(core * part, 128), part)] = gf1[k, rows, :].astype(F32)
        core = lax.div(i * step, part)
        inner = pl.ds(pl.multiple_of(i * step - core * part, 16), step)
        f2_wide[rows, :] = gf2[core + c - 2 * core * c, inner, :].astype(F32)
        for copy in stores(i):
            copy.start()

    for copy in passed:
        copy.start()
    g1_out[...], rw_out[...], g2_out[...] = small[0], small[1], small[2]

    @pl.loop(0, WIDEN)
    def _(i):
        for copy in stores(i):
            copy.wait()

    for copy in passed:
        copy.wait()


def widen(*held):
    width = held[3].shape[1]
    tokens = jax.ShapeDtypeStruct(held[0].shape, BF)
    wide = [(width, 3 * width), (width, width), (width, width), (width, width)]
    return pl.pallas_call(
        widen_kernel,
        out_shape=[tokens, tokens] + [jax.ShapeDtypeStruct(dims, F32) for dims in wide] + [jax.ShapeDtypeStruct((width,), F32)] * 3,
        in_specs=[VMEM] * 6,
        out_specs=[ANY] * 6 + [VMEM] * 3,
        scratch_shapes=[pltpu.VMEM(dims, F32) for dims in wide]
        + [pltpu.SemaphoreType.DMA((WIDEN, 4)), pltpu.SemaphoreType.DMA((2,))],
        compiler_params=pltpu.CompilerParams(vmem_limit_bytes=32 * 1024 * 1024),
        name="widen",
    )(*(pltpu.with_memory_space_constraint(a, pltpu.VMEM) for a in held))


def per_device(others, images, patch_rank, kept_count, ln1_gain, router_weight, w_qkv, w_out, ln2_gain, w_fc1, w_fc2, cotangent):
    count, patches, width = images.shape
    tall = -(-patches // 16) * 16
    t = count * tall
    part = w_fc1.shape[1] // 2
    half, eighth = width // 2, width // 8

    def bf(*dims):
        return pltpu.VMEM(dims, BF)

    def f32(*dims):
        return pltpu.VMEM(dims, F32)

    def sem(*dims):
        return pltpu.SemaphoreType.DMA(dims)

    scratch = [
        pltpu.VMEM(patch_rank.shape, jnp.int32), pltpu.SMEM(kept_count.shape, jnp.int32), f32(width), bf(width), f32(width),
        bf(width, 3 * width), bf(width, width), bf(width, 2 * part), bf(2 * part, width),
        bf(t, width), f32(t, 128), f32(t, 128), f32(t, 128), bf(t, width), bf(width, t), bf(t, 3 * width),
        f32(count, HEADS, tall, tall), bf(count, width, tall), bf(t, width), f32(t, width), f32(t, width),
        bf(4 * t, width), bf(4 * t, width), bf(width, 4 * t), f32(t, width), f32(t, width),
        bf(3 * t, width), bf(3 * t, width), bf(t, width), bf(t, width), bf(t, width), bf(t, width), bf(t, width), bf(t, width),
        bf(4 * t, 2 * part), bf(4 * t, 2 * part), bf(tall, width),
        bf(2, width // 2, part), bf(2, part // 2, width), bf(2, width // 4, part), bf(2, part // 4, width),
        bf(2, width // 4, part), bf(2, part // 4, width), bf(width // 4, part), bf(part // 4, width),
        bf(CHUNKS, half, 384), bf(CHUNKS, 2 * eighth, 384), bf(CHUNKS, eighth, 384),
        bf(CHUNKS, eighth // 2, 384), bf(CHUNKS, eighth // 2, 384),
        f32(1, width), f32(1, width), f32(1, width), f32(3, 8, width), f32(3, 8, width), f32(4, 8, width),
        sem(6), sem(2, 4), sem(2, 4), sem(count, 3), sem(count, 3), sem(3), sem(3), sem(8), sem(8),
        sem(2, 2), sem(2, 2), sem(2, 2), sem(2, 2), sem(2), sem(2),
        sem(2, 2), sem(2, 2), sem(2), sem(2), pltpu.SemaphoreType.REGULAR((2,)), pltpu.SemaphoreType.REGULAR((CHUNKS, 4)),
        sem(CHUNKS, 9), sem(CHUNKS, 9), sem(5),
        sem(3), sem(3), sem(2), sem(2),
    ]

    block, gx, gw, gf1, gf2, small = pl.pallas_call(
        mega_kernel,
        out_shape=[
            bf(patches, count, width), bf(patches, count, width), bf(CHUNKS, width, 384),
            bf(2, width, part), bf(2, part, width), f32(8, width),
        ],
        in_specs=[ANY] * 11,
        out_specs=[VMEM] * 6,
        scratch_shapes=scratch,
        compiler_params=pltpu.CompilerParams(
            collective_id=0, has_side_effects=True, vmem_limit_bytes=int(55.5 * 1024) * 1024
        ),
        name="block",
    )(images.transpose(1, 0, 2), patch_rank, kept_count, ln1_gain, router_weight, w_qkv, w_out, ln2_gain, w_fc1, w_fc2,
      cotangent.transpose(1, 0, 2))
    block, gx, gq, go, f1, f2, g1, rw, g2 = widen(block, gx, gw, gf1, gf2, small)
    if others:
        gq, go, f1, f2, g1, rw, g2 = lax.psum((gq, go, f1, f2, g1, rw, g2), "rows", axis_index_groups=others)
    return block.transpose(1, 0, 2), gx.transpose(1, 0, 2), g1, rw, gq, go, g2, f1, f2


def solution(mesh):
    rows = mesh.shape["rows"]
    others = [[8 * g + i for g in range(rows // 8)] for i in range(8)] if rows > 8 else None
    return jax.shard_map(
        functools.partial(per_device, others),
        mesh=mesh,
        in_specs=(
            P(("rows", "mlp"), None, None), P(("rows", "mlp"), None), P(("rows", "mlp")), P(), P(), P(), P(), P(),
            P(None, "mlp"), P("mlp", None), P(("rows", "mlp"), None, None),
        ),
        out_specs=(
            P(("rows", "mlp"), None, None), P(("rows", "mlp"), None, None), P(), P(), P(), P(), P(),
            P(None, "mlp"), P("mlp", None),
        ),
        check_vma=False,
    )
```

```python
import functools
import jax
import jax.numpy as jnp
from jax import lax
from jax.experimental import pallas as pl
from jax.experimental.pallas import tpu as pltpu
from jax.sharding import PartitionSpec as P

HEADS = 12
EPS = 1e-6
FILL = -1e30
BF = jnp.bfloat16
F32 = jnp.float32


def dot_nn(a, b):
    return lax.dot_general(a, b, (((1,), (0,)), ((), ())), preferred_element_type=F32)


def dot_nt(a, b):
    return lax.dot_general(a, b, (((1,), (1,)), ((), ())), preferred_element_type=F32)


def dot_tn(a, b):
    return lax.dot_general(a, b, (((0,), (0,)), ((), ())), preferred_element_type=F32)


def unit_rows(v):
    center = v - jnp.mean(v, -1, keepdims=True)
    scale = lax.rsqrt(jnp.mean(center * center, -1, keepdims=True) + EPS)
    return center * scale, scale


def norm_pull(dy, gain, unit, scale):
    du = dy * gain
    return scale * (
        du
        - jnp.mean(du, -1, keepdims=True)
        - unit * jnp.mean(du * unit, -1, keepdims=True)
    )


def half_mask(rows, h):
    lane = lax.broadcasted_iota(jnp.int32, (rows, 128), 1)
    return (lane < 64) if h == 0 else (lane >= 64)


def forward_rows(i, x_ref, rank_ref, kept_ref, g1_ref, rw_ref, xp, keep, gate, h1, work):
    patches = x_ref.shape[0]
    tall = xp.shape[0] // x_ref.shape[1]
    rows = pl.ds(pl.multiple_of(i * tall, 16), tall)
    work[...] = jnp.zeros_like(work)
    work[0:patches, :] = x_ref[:, i, :]
    v = work[...]
    xp[rows, :] = v
    kept = (rank_ref[pl.ds(i, 1), :] < kept_ref[i]).astype(F32)
    keep_row = jnp.concatenate([kept, jnp.zeros((1, 256 - patches), F32)], 1)
    keep_col = jnp.broadcast_to(keep_row, (128, 256)).T
    keep[rows, :] = keep_col[0:tall, :]
    unit, _ = unit_rows(v.astype(F32))
    low = (unit * g1_ref[...][None]).astype(BF)
    h1[rows, :] = low
    logit = jnp.sum(low.astype(F32) * rw_ref[...][None].astype(F32), -1, keepdims=True)
    gate[rows, :] = jnp.broadcast_to(jax.nn.sigmoid(logit), (tall, 128))


def forward_qkv(j, h1, wqkv, qkv):
    cols = pl.ds(pl.multiple_of(j * 256, 256), 256)
    qkv[:, cols] = dot_nn(h1[...], wqkv[:, cols]).astype(BF)


def attend(p, i, width, tall, qkv, keep, probs, context, contextt):
    rows = pl.ds(pl.multiple_of(i * tall, 16), tall)
    qc = pl.ds(pl.multiple_of(p * 128, 128), 128)
    kc = pl.ds(pl.multiple_of(width + p * 128, 128), 128)
    vc = pl.ds(pl.multiple_of(2 * width + p * 128, 128), 128)
    q, k, v = qkv[rows, qc], qkv[rows, kc], qkv[rows, vc]
    vt = v.T
    kept = keep[rows, 0:1] > 0.5
    outs = []
    for h in range(2):
        kh = jnp.where(half_mask(tall, h), k, jnp.zeros_like(k))
        s = jnp.where(kept, dot_nt(kh, q) * 0.125, FILL)
        e = jnp.exp(s - jnp.max(s, 0, keepdims=True))
        pr = e * (1.0 / jnp.sum(e, 0, keepdims=True))
        probs[i, p * 2 + h] = pr
        outs.append(dot_nn(vt[h * 64 : h * 64 + 64, :], pr.astype(BF)))
    ct = jnp.concatenate(outs, 0)
    contextt[i, pl.ds(pl.multiple_of(p * 128, 128), 128), :] = ct.astype(BF)
    context[rows, qc] = ct.T.astype(BF)


def forward_out(i, tall, context, wout, xp, keep, gate, g2_ref, attended, middle, h2):
    rows = pl.ds(pl.multiple_of(i * tall, 16), tall)
    att = dot_nn(context[rows, :], wout[...])
    attended[rows, :] = att
    mid = xp[rows, :].astype(F32) + keep[rows, 0:1] * gate[rows, 0:1] * att
    middle[rows, :] = mid
    unit, _ = unit_rows(mid)
    h2[rows, :] = (unit * g2_ref[...][None]).astype(BF)


def gelu_pair(pre):
    cdf = 0.5 * (1.0 + lax.erf(pre * 0.7071067811865476))
    pdf = jnp.exp(pre * pre * -0.5) * 0.3989422804014327
    return pre * cdf, cdf + pre * pdf


def mlp_rows(h, c, w1, w2):
    pre = dot_nn(h, w1)
    hidden, slope = gelu_pair(pre)
    grad = dot_nt(c, w2) * slope
    return hidden.astype(BF), grad.astype(BF)


def back_rows(i, tall, c_ref, gh2, middle, keep, gate, attended, g2_ref, gmid, gatt, glogit, dg2):
    rows = pl.ds(pl.multiple_of(i * tall, 16), tall)
    dy = gh2[rows, :]
    unit, scale = unit_rows(middle[rows, :])
    gm = c_ref[rows, :].astype(F32) + norm_pull(dy, g2_ref[...][None], unit, scale)
    gmid[rows, :] = gm
    dg2[...] += jnp.sum(dy * unit, 0, keepdims=True)
    k, g = keep[rows, 0:1], gate[rows, 0:1]
    kept = gm * k
    gatt[rows, :] = (kept * g).astype(BF)
    gl = jnp.sum(kept * attended[rows, :], -1, keepdims=True) * g * (1.0 - g)
    glogit[rows, :] = jnp.broadcast_to(gl, (tall, 128))


def attend_back(p, i, width, tall, qkv, probs, gctx):
    rows = pl.ds(pl.multiple_of(i * tall, 16), tall)
    qc = pl.ds(pl.multiple_of(p * 128, 128), 128)
    kc = pl.ds(pl.multiple_of(width + p * 128, 128), 128)
    vc = pl.ds(pl.multiple_of(2 * width + p * 128, 128), 128)
    q, k, v = qkv[rows, qc], qkv[rows, kc], qkv[rows, vc]
    gc = gctx[rows, qc]
    kt = k.T
    gv, gk, gq = 0.0, 0.0, []
    for h in range(2):
        mask = half_mask(tall, h)
        zero = jnp.zeros_like(v)
        pr = probs[i, p * 2 + h]
        gp = dot_nt(jnp.where(mask, v, zero), gc)
        gs = (pr * (gp - jnp.sum(pr * gp, 0, keepdims=True))).astype(BF)
        gv = gv + dot_nn(pr.astype(BF), jnp.where(mask, gc, zero))
        gk = gk + dot_nn(gs, jnp.where(mask, q, zero))
        gq.append(dot_nn(kt[h * 64 : h * 64 + 64, :], gs))
    qkv[rows, qc] = (jnp.concatenate(gq, 0).T * 0.125).astype(BF)
    qkv[rows, kc] = (gk * 0.125).astype(BF)
    qkv[rows, vc] = gv.astype(BF)


def pair_columns(wqkv, p, width):
    return jnp.concatenate(
        [wqkv[:, pl.ds(pl.multiple_of(b * width + p * 128, 128), 128)] for b in range(3)], 1
    )


def back_input(i, tall, dy, glogit, rw_ref, xp, h1, g1_ref, gmid, gx_ref, dg1, drw):
    rows = pl.ds(pl.multiple_of(i * tall, 16), tall)
    patches = gx_ref.shape[0]
    gl = glogit[rows, 0:1]
    dy = dy + gl * rw_ref[...][None].astype(F32)
    unit, scale = unit_rows(xp[rows, :].astype(F32))
    dg1[...] += jnp.sum(dy * unit, 0, keepdims=True)
    drw[...] += jnp.sum(h1[rows, :].astype(F32) * gl, 0, keepdims=True)
    out = gmid[rows, :] + norm_pull(dy, g1_ref[...][None], unit, scale)
    gx_ref[:, i, :] = out.astype(BF)[0:patches, :]

MESH = pl.DeviceIdType.MESH
CHUNKS = HEADS // 2 + 2
WIDEN = 8
PATHS = ("zxy", "yzx", "xyz", "yxz", "xyz", "yzx", "xzy", "yxz")
ORDER = (
    "back0", "osend", "pairs0", "back1", "pairs1", "fa11", "fa10", "fa01", "last0", "fa00", "out1", "pairs2", "out0",
    "last1", "c3.1", "fb1", "c2.1", "pairs3", "c1.1", "last2", "c4.1", "finish0", "c5.1", "c0.1", "c2.2", "c3.2",
    "c6.1", "finish1", "c1.2", "fb0", "c4.2", "c3.3", "c5.2", "c7.1", "c0.2", "g1", "c2.3", "c6.2", "c1.3", "fc",
    "c4.3", "c3.4", "c0.3", "o0", "g2", "c2.4", "c7.2", "c6.3", "c5.3", "c1.4", "c4.4", "c3.5", "fd", "c0.4", "c6.4",
    "c7.3", "c2.5", "c1.5", "c5.4", "c4.5", "c3.6", "g3", "c7.4", "c0.5", "o1", "c2.6", "c4.6", "g4", "c6.5", "c5.5",
    "c1.6", "c0.6", "c7.5", "fe", "c3.7", "c2.7", "c5.6", "c6.6", "c1.7", "c0.7", "c7.6", "c4.7", "c5.7", "c3.8",
    "c2.8", "c6.7", "c7.7", "c1.8", "c0.8", "c3.9", "c4.8", "g5", "c5.8", "c1.9", "c6.8", "c7.8", "ff", "c2.9",
    "c6.9", "c5.9", "c4.9", "c0.9", "c7.9",
)


def mega_kernel(
    x_hbm, rank_hbm, kept_hbm, g1_hbm, rw_hbm, wqkv_hbm, wout_hbm, g2_hbm, fc1, fc2, c_hbm,
    c_ref, x_ref, gw, g1w, g2w, small_out,
    rank_ref, kept_ref, g1_ref, rw_ref, g2_ref, wqkv, wout, w1, w2, xp, keep, gate, glogit, h1, h1t, qkv, probs, contextt, context, attended, middle,
    tok, cot, turned, out, gh2, out_part, gh2_part, out_sib, gh2_sib, out_near, gh2_near, out_far, gh2_far, hid, gpre, work,
    r1a, r1b, r2a, r2b, fz1, fz2, rz1, rz2,
    q0, q1, q2, q3, far, dg1, dg2, drw, sma, smr, smz,
    lsem, gsend, grecv, hsend, hrecv, csend, crecv, esend, erecv, s1s, s1r, s2s, s2r, s3s, s3r, fs, fr, ssib, rsib, free, chunk_free,
    qs, qr, small_sem, sms, smrs, smzs, smzr,
):
    patches, images, width = x_ref.shape
    t_own = xp.shape[0]
    tall = t_own // images
    half = width // 2
    part = w1.shape[1] // 2
    parts = (q0, q1, q2, q3)
    quarter = (width // 4, part // 4)
    r = lax.axis_index("rows")
    z = lax.axis_index("mlp")
    c, x, y = lax.rem(r, 2), lax.rem(lax.div(r, 2), 2), lax.rem(lax.div(r, 4), 2)
    r_sib, r_x, r_y = r + 1 - 2 * c, r + 2 - 4 * x, r + 4 - 8 * y
    r_diag = r_x + r_y - r
    z_pair, z_far = z + 1 - 2 * lax.rem(z, 2), z + 2 - 4 * lax.div(z, 2)
    q = 2 * y + x

    def ds(start, size):
        return pl.ds(pl.multiple_of(start, 16), size)

    def lanes(start, size):
        return pl.ds(pl.multiple_of(start, 128), size)

    def remote(src, dst, send, recv, row, column):
        return pltpu.make_async_remote_copy(
            src_ref=src, dst_ref=dst, send_sem=send, recv_sem=recv,
            device_id={"rows": row, "mlp": column}, device_id_type=MESH,
        )

    def release(semaphore, row):
        pl.semaphore_signal(semaphore, inc=1, device_id={"rows": row, "mlp": z}, device_id_type=MESH)

    def gather_copy(mat, kind):
        size = quarter[mat]
        sems = gsend.at[mat, kind], grecv.at[mat, kind]
        if mat == 0:
            place = w1.at[ds(q * size, size), pl.ds(part, part)]
            own = fc1.at[ds(q * size, size), lanes(c * part, part)]
        else:
            place = w2.at[ds(part + q * size, size), :]
            own = fc2.at[ds(c * part + q * size, size), :]
        if kind == 0:
            return remote(own, place, *sems, r, z_far)
        return remote(place, place, *sems, (r_x, r_y, r_diag)[kind - 1], z)

    def gather_forward(mat):
        gather_copy(mat, 0).wait_recv()
        for kind in (1, 2, 3):
            gather_copy(mat, kind).start()

    def own_shard(mat):
        if mat == 0:
            return pltpu.make_async_copy(fc1.at[:, lanes(c * part, part)], w1.at[:, pl.ds(0, part)], lsem.at[0])
        return pltpu.make_async_copy(fc2.at[ds(c * part, part), :], w2.at[pl.ds(0, part), :], lsem.at[1])

    load_qkv = pltpu.make_async_copy(wqkv_hbm, wqkv, lsem.at[2])
    load_out = pltpu.make_async_copy(wout_hbm, wout, lsem.at[3])
    load_x = pltpu.make_async_copy(x_hbm, x_ref, lsem.at[4])
    load_small = [
        pltpu.make_async_copy(src, dst, small_sem.at[k])
        for k, (src, dst) in enumerate(((rank_hbm, rank_ref), (kept_hbm, kept_ref), (g1_hbm, g1_ref), (rw_hbm, rw_ref), (g2_hbm, g2_ref)))
    ]
    load_c = pltpu.make_async_copy(c_hbm, c_ref, lsem.at[5])

    def token_copy(i, hop):
        start = (0, 0, 2 * t_own)[hop] + i * tall
        src, dst = tok.at[ds(start, tall), :], tok.at[ds((1, 2, 3)[hop] * t_own + i * tall, tall), :]
        row, column = (r, z_pair) if hop == 1 else (r_sib, z)
        return remote(src, dst, hsend.at[i, hop], hrecv.at[i, hop], row, column)

    def cot_copy(hop):
        src, dst = cot.at[ds((0, 0, 2)[hop] * t_own, t_own), :], cot.at[ds((1, 2, 3)[hop] * t_own, t_own), :]
        row, column = (r, z_pair) if hop == 1 else (r_sib, z)
        return remote(src, dst, csend.at[hop], crecv.at[hop], row, column)

    gh2_to_sib = remote(gh2_part.at[ds(0, t_own), :], gh2_sib, esend.at[0], erecv.at[0], r_sib, z)
    out_to_sib = remote(out_part.at[ds(0, t_own), :], out_sib, esend.at[1], erecv.at[1], r_sib, z)
    out_over = remote(out_part.at[ds(2 * t_own, t_own), :], out_near, esend.at[2], erecv.at[2], r_sib, z)
    out_far_copy = remote(out_part.at[ds(t_own, t_own), :], out_far, esend.at[3], erecv.at[3], r, z_pair)

    def gh2_over(i):
        src = gh2_part.at[ds(2 * t_own + i * tall, tall), :]
        return remote(src, gh2_near.at[ds(i * tall, tall), :], esend.at[4 + i], erecv.at[4 + i], r_sib, z)

    def gh2_far_copy(i):
        src = gh2_part.at[ds(t_own + i * tall, tall), :]
        return remote(src, gh2_far.at[ds(i * tall, tall), :], esend.at[6 + i], erecv.at[6 + i], r, z_pair)

    fc_whole, fc_half, fc_quarter, fc_done, fc_far = (g1w, g2w), (r1a, r1b), (r2a, r2b), (fz1, fz2), (rz1, rz2)
    fc_rows = ((width // 2, width // 4), (part // 2, part // 4))

    def fc_ways(k, m):
        shard = lax.div(z, 2) if k == 0 else 1 - lax.div(z, 2)
        turn = lax.rem(shard + m, 2)
        return r_x + (r_y - r_x) * turn, r_y + (r_x - r_y) * turn, x + (y - x) * turn, y + (x - y) * turn

    def fc_first(k, m):
        n1, _, a1, _ = fc_ways(k, m)
        rows, _ = fc_rows[m]
        src = fc_whole[m].at[k, ds((1 - a1) * rows, rows), :]
        return remote(src, fc_half[m].at[k], s1s.at[k, m], s1r.at[k, m], n1, z)

    def fc_second(k, m):
        _, n2, a1, a2 = fc_ways(k, m)
        rows, less = fc_rows[m]
        src = fc_whole[m].at[k, ds(a1 * rows + (1 - a2) * less, less), :]
        return remote(src, fc_quarter[m].at[k], s2s.at[k, m], s2r.at[k, m], n2, z)

    fc_third = [remote(fc_done[m].at[1], fc_far[m], s3s.at[m], s3r.at[m], r, z_far) for m in range(2)]

    def fc_spread(level, m):
        n1, n2, a1, a2 = fc_ways(0, m)
        rows, less = fc_rows[m]
        place = ds(a1 * rows + a2 * less, less) if level == 0 else ds(a1 * rows, rows)
        held = fc_whole[m].at[0, place, :]
        return remote(held, held, fs.at[level, m], fr.at[level, m], n2 if level == 0 else n1, z)

    fc_share = (
        remote(g1w.at[0], g1w.at[1], ssib.at[0], rsib.at[0], r_sib, z),
        remote(g2w.at[0], g2w.at[1], ssib.at[1], rsib.at[1], r_sib, z),
    )

    def fc_fold_second(k, m):
        fc_first(k, m).wait_recv()
        _, _, a1, a2 = fc_ways(k, m)
        rows, less = fc_rows[m]
        place, whole = ds(a1 * rows + (1 - a2) * less, less), fc_whole[m]
        whole[k, place, :] = whole[k, place, :] + fc_half[m][k, ds((1 - a2) * less, less), :]
        fc_second(k, m).start()

    def fc_fold_third(k):
        for m in range(2):
            fc_second(k, m).wait_recv()
            _, _, a1, a2 = fc_ways(k, m)
            rows, less = fc_rows[m]
            total = fc_whole[m][k, ds(a1 * rows + a2 * less, less), :].astype(F32)
            total = total + fc_half[m][k, ds(a2 * less, less), :].astype(F32) + fc_quarter[m][k].astype(F32)
            fc_done[m][k] = total.astype(BF)
        if k == 1:
            for copy in fc_third:
                copy.start()
        for m in range(2):
            fc_first(k, m).wait_send()
            fc_second(k, m).wait_send()
        if k == 1:
            release(free.at[0], r_sib)
        else:
            release(free.at[1], r_x)
            release(free.at[1], r_y)

    def fc_finish():
        for copy in fc_third:
            copy.wait_recv()
        pl.semaphore_wait(free.at[1], 2)
        for m in range(2):
            _, _, a1, a2 = fc_ways(0, m)
            rows, less = fc_rows[m]
            fc_whole[m][0, ds(a1 * rows + a2 * less, less), :] = fc_done[m][0] + fc_far[m][...]
            fc_spread(0, m).start()

    def fc_widen():
        for m in range(2):
            fc_spread(0, m).wait_recv()
        for m in range(2):
            fc_spread(1, m).start()

    def fc_to_sibling():
        for m in range(2):
            fc_spread(1, m).wait_recv()
        pl.semaphore_wait(free.at[0], 1)
        for copy in fc_share:
            copy.start()

    sizes = tuple(width >> level for level in range(1, 5))

    def hops(j):
        ways = {"x": (r_x, z, x), "y": (r_y, z, y), "z": (r, z_pair, lax.rem(z, 2))}
        return [(r_sib, z, c)] + [ways[axis] for axis in PATHS[j]]

    def base(path, level):
        start = 0
        for (_, _, bit), size in zip(path[:level], sizes):
            start = start + bit * size
        return start

    def core_copy(j):
        src = gw.at[j, ds((1 - c) * half, half), :]
        return remote(src, parts[0].at[j], qs.at[j, 0], qr.at[j, 0], r_sib, z)

    def chunk_copy(j, step):
        path = hops(j)
        if step == 0:
            return core_copy(j)
        if step < 4:
            row, column, bit = path[step]
            start = base(path, step) + (1 - bit) * sizes[step]
            return remote(gw.at[j, ds(start, sizes[step]), :], parts[step].at[j], qs.at[j, step], qr.at[j, step], row, column)
        if step == 4:
            own = gw.at[j, ds(base(path, 4), sizes[3]), :]
            return remote(own, far.at[j], qs.at[j, 4], qr.at[j, 4], r, z_far)
        level = 8 - step
        row, column, _ = path[level]
        held = gw.at[j, ds(base(path, level + 1), sizes[level]), :]
        return remote(held, held, qs.at[j, step], qr.at[j, step], row, column)

    def chunk_step(j, step):
        path = hops(j)
        chunk_copy(j, step - 1).wait()
        if step <= 4:
            row, column, _ = path[step - 1]
            pl.semaphore_signal(
                chunk_free.at[j, step - 1], inc=1, device_id={"rows": row, "mlp": column}, device_id_type=MESH
            )
            start = base(path, min(step, 4))
            if step < 4:
                start = base(path, step) + (1 - path[step][2]) * sizes[step]
            size = sizes[min(step, 3)]
            total = gw[j, ds(start, size), :].astype(F32)
            for level in range(step):
                total = total + parts[level][j, ds(start - base(path, level + 1), size), :].astype(F32)
            gw[j, ds(start, size), :] = total.astype(BF)
        if step == 5:
            own = ds(base(path, 4), sizes[3])
            gw[j, own, :] = gw[j, own, :] + far[j]
        if 5 <= step <= 8:
            pl.semaphore_wait(chunk_free.at[j, 8 - step], 1)
        if step <= 8:
            chunk_copy(j, step).start()

    def small_copy(level):
        row = (r_sib, r_x, r_y)[level]
        return remote(sma.at[level], smr.at[level], sms.at[level], smrs.at[level], row, z)

    def small_z(step):
        src, dst = smz.at[2 * step], smz.at[2 * step + 1]
        return remote(src, dst, smzs.at[step], smzr.at[step], r, (z_pair, z_far)[step])

    barrier = pltpu.get_barrier_semaphore()
    partners = ((r_sib, z), (r_x, z), (r_y, z), (r_diag, z), (r, z_pair), (r, z_far))
    for row, column in partners:
        pl.semaphore_signal(barrier, inc=1, device_id={"rows": row, "mlp": column}, device_id_type=MESH)
    load_c.start()
    load_x.start()
    for copy in load_small:
        copy.start()
    load_qkv.start()
    load_out.start()
    own_shard(0).start()
    own_shard(1).start()
    pl.semaphore_wait(barrier, len(partners))
    gather_copy(0, 0).start()
    gather_copy(1, 0).start()
    load_c.wait()
    for i in range(images):
        work[...] = jnp.zeros_like(work)
        work[0:patches, :] = c_ref[:, i, :]
        cot[i * tall : (i + 1) * tall, :] = work[...]
    cot_copy(0).start()
    cot_copy(1).start()
    load_x.wait()
    for copy in load_small:
        copy.wait()
    for i in range(images):
        forward_rows(i, x_ref, rank_ref, kept_ref, g1_ref, rw_ref, xp, keep, gate, h1, work)

    load_qkv.wait()

    @pl.loop(0, 3 * width // 256)
    def _(j):
        forward_qkv(j, h1, wqkv, qkv)

    @pl.loop(0, HEADS // 2)
    def _(p):
        for i in range(images):
            attend(p, i, width, tall, qkv, keep, probs, context, contextt)

        @pl.when(p == 2)
        def _():
            gather_forward(0)

        @pl.when(p == 4)
        def _():
            gather_forward(1)

    load_out.wait()

    @pl.loop(0, images)
    def _(i):
        forward_out(i, tall, context, wout, xp, keep, gate, g2_ref, attended, middle, tok)
        token_copy(i, 0).start()
        token_copy(i, 1).start()

    own_shard(0).wait()
    own_shard(1).wait()

    def at(block, number, do):
        @pl.when(block == number)
        def _():
            do()

    def before_sibling():
        for i in range(images):
            token_copy(i, 0).wait_recv()
        cot_copy(0).wait_recv()

    h1t[...] = h1[...].T

    @pl.loop(0, 2 * images)
    def _(block):
        at(block, images, before_sibling)
        rows = ds(block * tall, tall)
        hid[rows, 0:part], gpre[rows, 0:part] = mlp_rows(tok[rows, :], cot[rows, :], w1[:, 0:part], w2[0:part, :])

    cot_copy(1).wait_recv()
    cot_copy(2).start()
    for mat in range(2):
        for kind in (1, 2, 3):
            gather_copy(mat, kind).wait_recv()
    for ref in (dg1, dg2, drw):
        ref[...] = jnp.zeros_like(ref)

    def before_near():
        cot_copy(2).wait_recv()
        gh2_to_sib.start()
        out_to_sib.start()

    def forward_token(i):
        token_copy(i, 1).wait_recv()
        token_copy(i, 2).start()

    def send_far(i):
        gh2_over(i).wait_recv()
        rows = ds(t_own + i * tall, tall)
        gh2_part[rows, :] = gh2_part[rows, :] + gh2_near[ds(i * tall, tall), :]
        gh2_far_copy(i).start()

    def before_last():
        send_far(0)
        token_copy(1, 2).wait_recv()

    @pl.loop(0, 8)
    def _(block):
        at(block, 3, lambda: forward_token(0))
        at(block, 4, before_near)
        at(block, 5, lambda: token_copy(0, 2).wait_recv())
        at(block, 6, lambda: forward_token(1))
        at(block, 7, before_last)
        inner = lax.rem(block, 5)
        swap = lax.div(block, 5) * (1 - 2 * inner + 3 * lax.div(inner * (inner - 1), 2))
        spot = block + swap
        rows = ds(spot * tall, tall)

        @pl.when(block < 2 * images)
        def _():
            hid[rows, part:], gpre[rows, part:] = mlp_rows(tok[rows, :], cot[rows, :], w1[:, part:], w2[part:, :])

        @pl.when(block >= 2 * images)
        def _():
            hid[rows, :], gpre[rows, :] = mlp_rows(tok[rows, :], cot[rows, :], w1[...], w2[...])

        share_out = dot_nn(hid[rows, :], w2[...])
        share_gh2 = dot_nt(gpre[rows, :], w1[...])

        @pl.when(block < images)
        def _():
            out[rows, :] = share_out
            gh2[rows, :] = share_gh2

        @pl.when(block >= images)
        def _():
            there = ds(lax.max(spot - images, 0) * tall, tall)
            out_part[there, :] = share_out.astype(BF)
            gh2_part[there, :] = share_gh2.astype(BF)

        at(block, 5, lambda: gh2_over(0).start())
        at(block, 7, lambda: gh2_over(1).start())

    out_over.start()
    turned[...] = tok[...].T
    for m in range(3):
        rows = slice(m * width // 3, (m + 1) * width // 3)
        total = dot_nn(turned[rows, :], gpre[...]).astype(BF)
        g1w[0, rows, :] = total[:, 0:part]
        g1w[1, rows, :] = total[:, part:]
    for k in range(2):
        fc_first(k, 0).start()
    send_far(1)
    turned[...] = hid[...].T
    for m in range(2):
        g2w[m] = dot_nn(turned[m * part : (m + 1) * part, :], cot[...]).astype(BF)
    for k in range(2):
        fc_first(k, 1).start()

    def back_image(i):
        if i == 0:
            gh2_to_sib.wait_recv()
            for n in range(images):
                token_copy(n, 0).wait_send()
                token_copy(n, 1).wait_send()
        gh2_far_copy(i).wait_recv()
        rows = pl.ds(i * tall, tall)
        gh2[rows, :] += gh2_sib[rows, :].astype(F32) + gh2_far[rows, :].astype(F32)
        back_rows(i, tall, cot, gh2, middle, keep, gate, attended, g2_ref, gh2, tok, glogit, dg2)
        context[rows, :] = dot_nt(tok[rows, :], wout[...]).astype(BF)

    def fill(j, total):
        gw[j] = total.astype(BF)
        core_copy(j).start()

    def grad_out_half(n):
        total = 0.0
        for i in range(images):
            total = total + dot_nn(contextt[i], tok[i * tall : (i + 1) * tall, n * half : (n + 1) * half])
        fill(n, total)

    def pair_chunk(p):
        fill(p + 2, dot_nn(h1t[...], pair_columns(qkv, p, width)))

    def finish(i):
        rows = pl.ds(i * tall, tall)
        dy = dot_nt(qkv[rows, :], wqkv[...])
        back_input(i, tall, dy, glogit, rw_ref, xp, h1, g1_ref, gh2, x_ref, dg1, drw)
        if i == images - 1:
            sma[0] = jnp.concatenate([dg1[...], drw[...], dg2[...], jnp.zeros((5, width), F32)], 0)
            small_copy(0).start()

    def small_step(step):
        if step < 3:
            small_copy(step - 1).wait()
            sma[step] = sma[step - 1] + smr[step - 1]
            small_copy(step).start()
        elif step == 3:
            small_copy(2).wait()
            smz[0] = sma[2] + smr[2]
            small_z(0).start()
        else:
            small_z(step - 4).wait()
            if step == 4:
                smz[2] = smz[0] + smz[1]
                small_z(1).start()
            else:
                small_out[...] = smz[2] + smz[3]

    def out_send():
        out_over.wait_recv()
        rows = pl.ds(t_own, t_own)
        out_part[rows, :] = out_part[rows, :] + out_near[...]
        out_far_copy.start()

    def out_finish(i):
        if i == 0:
            out_to_sib.wait_recv()
            out_far_copy.wait_recv()
        rows = pl.ds(i * tall, tall)
        total = middle[rows, :] + out[rows, :] + out_sib[rows, :].astype(F32) + out_far[rows, :].astype(F32)
        c_ref[:, i, :] = total.astype(BF)[0:patches, :]

    def fc_share_end():
        for copy in fc_share:
            copy.wait()

    single = {"fc": fc_finish, "fd": fc_widen, "fe": fc_to_sibling, "ff": fc_share_end, "osend": out_send}
    numbered = (("finish", finish), ("back", back_image), ("out", grad_out_half),
                ("fb", fc_fold_third), ("g", small_step), ("o", out_finish))

    def perform(names):
        for name in names:
            if name in single:
                single[name]()
            elif name[:2] == "fa":
                fc_fold_second(int(name[2]), int(name[3]))
            elif name[0] == "c":
                chunk_step(int(name[1]), int(name[3]))
            else:
                do = next(f for head, f in numbered if name[:-1] == head)
                do(int(name[-1]))

    first, start, stop = ORDER.index("pairs0"), ORDER.index("pairs1"), ORDER.index("last2")
    perform(ORDER[:first])

    @pl.loop(0, HEADS // 4)
    def _(n):
        for p in (2 * n, 2 * n + 1):
            attend_back(p, 0, width, tall, qkv, probs, context)

    perform(ORDER[first + 1 : start])
    marks = [ORDER.index(name) for k in range(3) for name in ("pairs%d" % (k + 1), "last%d" % k)]

    @pl.loop(0, HEADS // 4)
    def _(n):
        for p in (2 * n, 2 * n + 1):
            attend_back(p, 1, width, tall, qkv, probs, context)
        pair_chunk(2 * n)
        for k in range(3):
            at(n, k, lambda k=k: perform(ORDER[marks[2 * k] + 1 : marks[2 * k + 1]]))
        pair_chunk(2 * n + 1)
        for k in range(2):
            at(n, k, lambda k=k: perform(ORDER[marks[2 * k + 1] + 1 : marks[2 * k + 2]]))

    perform(ORDER[stop + 1 :])
    for level in range(2):
        for m in range(2):
            fc_spread(level, m).wait_send()
    for copy in fc_third:
        copy.wait_send()
    for mat in range(2):
        for kind in range(4):
            gather_copy(mat, kind).wait_send()
    for i in range(images):
        token_copy(i, 2).wait_send()
        gh2_over(i).wait_send()
        gh2_far_copy(i).wait_send()
    for hop in range(3):
        cot_copy(hop).wait_send()
    for copy in (gh2_to_sib, out_to_sib, out_over, out_far_copy):
        copy.wait_send()


VMEM = pl.BlockSpec(memory_space=pltpu.VMEM)
ANY = pl.BlockSpec(memory_space=pl.ANY)


def widen_kernel(
    block, gx, gw, gf1, gf2, small, block_out, gx_out, gq_out, go_out, f1_out, f2_out, g1_out, rw_out, g2_out,
    gq_wide, go_wide, f1_wide, f2_wide, store_sem, pass_sem,
):
    _, width, part = gf1.shape
    step = width // WIDEN
    c = lax.rem(lax.axis_index("rows"), 2)
    passed = [pltpu.make_async_copy(src, dst, pass_sem.at[k]) for k, (src, dst) in enumerate(((block, block_out), (gx, gx_out)))]

    def rows_of(i):
        return pl.ds(pl.multiple_of(i * step, 16), step)

    def stores(i):
        rows = rows_of(i)
        pairs = ((gq_wide, gq_out), (go_wide, go_out), (f1_wide, f1_out), (f2_wide, f2_out))
        return [
            pltpu.make_async_copy(src.at[rows, :], dst.at[rows, :], store_sem.at[i, k]) for k, (src, dst) in enumerate(pairs)
        ]

    for copy in passed:
        copy.start()
    g1_out[...], rw_out[...], g2_out[...] = small[0], small[1], small[2]

    @pl.loop(0, WIDEN)
    def _(i):
        rows = rows_of(i)
        for p in range(CHUNKS - 2):
            for b in range(3):
                start = b * width + p * 128
                gq_wide[rows, start : start + 128] = gw[2 + p, rows, b * 128 : (b + 1) * 128].astype(F32)
        for h in range(2):
            go_wide[rows, h * part : (h + 1) * part] = gw[h, rows, :].astype(F32)
        for k in range(2):
            core = c + k - 2 * c * k
            f1_wide[rows, pl.ds(pl.multiple_of(core * part, 128), part)] = gf1[k, rows, :].astype(F32)
        core = lax.div(i * step, part)
        inner = pl.ds(pl.multiple_of(i * step - core * part, 16), step)
        f2_wide[rows, :] = gf2[core + c - 2 * core * c, inner, :].astype(F32)
        for copy in stores(i):
            copy.start()

    @pl.loop(0, WIDEN)
    def _(i):
        for copy in stores(i):
            copy.wait()

    for copy in passed:
        copy.wait()


def widen(*held):
    width = held[3].shape[1]
    tokens = jax.ShapeDtypeStruct(held[0].shape, BF)
    wide = [(width, 3 * width), (width, width), (width, width), (width, width)]
    return pl.pallas_call(
        widen_kernel,
        out_shape=[tokens, tokens] + [jax.ShapeDtypeStruct(dims, F32) for dims in wide] + [jax.ShapeDtypeStruct((width,), F32)] * 3,
        in_specs=[VMEM] * 6,
        out_specs=[ANY] * 6 + [VMEM] * 3,
        scratch_shapes=[pltpu.VMEM(dims, F32) for dims in wide]
        + [pltpu.SemaphoreType.DMA((WIDEN, 4)), pltpu.SemaphoreType.DMA((2,))],
        compiler_params=pltpu.CompilerParams(vmem_limit_bytes=32 * 1024 * 1024),
        name="widen",
    )(*(pltpu.with_memory_space_constraint(a, pltpu.VMEM) for a in held))


def per_device(others, images, patch_rank, kept_count, ln1_gain, router_weight, w_qkv, w_out, ln2_gain, w_fc1, w_fc2, cotangent):
    count, patches, width = images.shape
    tall = -(-patches // 16) * 16
    t = count * tall
    part = w_fc1.shape[1] // 2
    half, eighth = width // 2, width // 8

    def bf(*dims):
        return pltpu.VMEM(dims, BF)

    def f32(*dims):
        return pltpu.VMEM(dims, F32)

    def sem(*dims):
        return pltpu.SemaphoreType.DMA(dims)

    scratch = [
        pltpu.VMEM(patch_rank.shape, jnp.int32), pltpu.SMEM(kept_count.shape, jnp.int32), f32(width), bf(width), f32(width),
        bf(width, 3 * width), bf(width, width), bf(width, 2 * part), bf(2 * part, width),
        bf(t, width), f32(t, 128), f32(t, 128), f32(t, 128), bf(t, width), bf(width, t), bf(t, 3 * width),
        f32(count, HEADS, tall, tall), bf(count, width, tall), bf(t, width), f32(t, width), f32(t, width),
        bf(4 * t, width), bf(4 * t, width), bf(width, 4 * t), f32(t, width), f32(t, width),
        bf(3 * t, width), bf(3 * t, width), bf(t, width), bf(t, width), bf(t, width), bf(t, width), bf(t, width), bf(t, width),
        bf(4 * t, 2 * part), bf(4 * t, 2 * part), bf(tall, width),
        bf(2, width // 2, part), bf(2, part // 2, width), bf(2, width // 4, part), bf(2, part // 4, width),
        bf(2, width // 4, part), bf(2, part // 4, width), bf(width // 4, part), bf(part // 4, width),
        bf(CHUNKS, half, 384), bf(CHUNKS, 2 * eighth, 384), bf(CHUNKS, eighth, 384),
        bf(CHUNKS, eighth // 2, 384), bf(CHUNKS, eighth // 2, 384),
        f32(1, width), f32(1, width), f32(1, width), f32(3, 8, width), f32(3, 8, width), f32(4, 8, width),
        sem(6), sem(2, 4), sem(2, 4), sem(count, 3), sem(count, 3), sem(3), sem(3), sem(8), sem(8),
        sem(2, 2), sem(2, 2), sem(2, 2), sem(2, 2), sem(2), sem(2),
        sem(2, 2), sem(2, 2), sem(2), sem(2), pltpu.SemaphoreType.REGULAR((2,)), pltpu.SemaphoreType.REGULAR((CHUNKS, 4)),
        sem(CHUNKS, 9), sem(CHUNKS, 9), sem(5),
        sem(3), sem(3), sem(2), sem(2),
    ]

    block, gx, gw, gf1, gf2, small = pl.pallas_call(
        mega_kernel,
        out_shape=[
            bf(patches, count, width), bf(patches, count, width), bf(CHUNKS, width, 384),
            bf(2, width, part), bf(2, part, width), f32(8, width),
        ],
        in_specs=[ANY] * 11,
        out_specs=[VMEM] * 6,
        scratch_shapes=scratch,
        compiler_params=pltpu.CompilerParams(
            collective_id=0, has_side_effects=True, vmem_limit_bytes=int(55.5 * 1024) * 1024
        ),
        name="block",
    )(images.transpose(1, 0, 2), patch_rank, kept_count, ln1_gain, router_weight, w_qkv, w_out, ln2_gain, w_fc1, w_fc2,
      cotangent.transpose(1, 0, 2))
    block, gx, gq, go, f1, f2, g1, rw, g2 = widen(block, gx, gw, gf1, gf2, small)
    if others:
        gq, go, f1, f2, g1, rw, g2 = lax.psum((gq, go, f1, f2, g1, rw, g2), "rows", axis_index_groups=others)
    return block.transpose(1, 0, 2), gx.transpose(1, 0, 2), g1, rw, gq, go, g2, f1, f2


def solution(mesh):
    rows = mesh.shape["rows"]
    others = [[8 * g + i for g in range(rows // 8)] for i in range(8)] if rows > 8 else None
    return jax.shard_map(
        functools.partial(per_device, others),
        mesh=mesh,
        in_specs=(
            P(("rows", "mlp"), None, None), P(("rows", "mlp"), None), P(("rows", "mlp")), P(), P(), P(), P(), P(),
            P(None, "mlp"), P("mlp", None), P(("rows", "mlp"), None, None),
        ),
        out_specs=(
            P(("rows", "mlp"), None, None), P(("rows", "mlp"), None, None), P(), P(), P(), P(), P(),
            P(None, "mlp"), P("mlp", None),
        ),
        check_vma=False,
    )
```

```python
import functools
import jax
import jax.numpy as jnp
from jax import lax
from jax.experimental import pallas as pl
from jax.experimental.pallas import tpu as pltpu
from jax.sharding import PartitionSpec as P

HEADS = 12
EPS = 1e-6
FILL = -1e30
BF = jnp.bfloat16
F32 = jnp.float32


def dot_nn(a, b):
    return lax.dot_general(a, b, (((1,), (0,)), ((), ())), preferred_element_type=F32)


def dot_nt(a, b):
    return lax.dot_general(a, b, (((1,), (1,)), ((), ())), preferred_element_type=F32)


def dot_tn(a, b):
    return lax.dot_general(a, b, (((0,), (0,)), ((), ())), preferred_element_type=F32)


def unit_rows(v):
    center = v - jnp.mean(v, -1, keepdims=True)
    scale = lax.rsqrt(jnp.mean(center * center, -1, keepdims=True) + EPS)
    return center * scale, scale


def norm_pull(dy, gain, unit, scale):
    du = dy * gain
    return scale * (
        du
        - jnp.mean(du, -1, keepdims=True)
        - unit * jnp.mean(du * unit, -1, keepdims=True)
    )


def half_mask(rows, h):
    lane = lax.broadcasted_iota(jnp.int32, (rows, 128), 1)
    return (lane < 64) if h == 0 else (lane >= 64)


def forward_rows(i, x_ref, rank_ref, kept_ref, g1_ref, rw_ref, xp, keep, gate, h1, work):
    patches = x_ref.shape[0]
    tall = xp.shape[0] // x_ref.shape[1]
    rows = pl.ds(pl.multiple_of(i * tall, 16), tall)
    work[...] = jnp.zeros_like(work)
    work[0:patches, :] = x_ref[:, i, :]
    v = work[...]
    xp[rows, :] = v
    kept = (rank_ref[pl.ds(i, 1), :] < kept_ref[i]).astype(F32)
    keep_row = jnp.concatenate([kept, jnp.zeros((1, 256 - patches), F32)], 1)
    keep_col = jnp.broadcast_to(keep_row, (128, 256)).T
    keep[rows, :] = keep_col[0:tall, :]
    unit, _ = unit_rows(v.astype(F32))
    low = (unit * g1_ref[...][None]).astype(BF)
    h1[rows, :] = low
    logit = jnp.sum(low.astype(F32) * rw_ref[...][None].astype(F32), -1, keepdims=True)
    gate[rows, :] = jnp.broadcast_to(jax.nn.sigmoid(logit), (tall, 128))


def forward_qkv(j, h1, wqkv, qkv):
    cols = pl.ds(pl.multiple_of(j * 256, 256), 256)
    qkv[:, cols] = dot_nn(h1[...], wqkv[:, cols]).astype(BF)


def attend(p, i, width, tall, qkv, keep, probs, context, contextt):
    rows = pl.ds(pl.multiple_of(i * tall, 16), tall)
    qc = pl.ds(pl.multiple_of(p * 128, 128), 128)
    kc = pl.ds(pl.multiple_of(width + p * 128, 128), 128)
    vc = pl.ds(pl.multiple_of(2 * width + p * 128, 128), 128)
    q, k, v = qkv[rows, qc], qkv[rows, kc], qkv[rows, vc]
    vt = v.T
    kept = keep[rows, 0:1] > 0.5
    outs = []
    for h in range(2):
        kh = jnp.where(half_mask(tall, h), k, jnp.zeros_like(k))
        s = jnp.where(kept, dot_nt(kh, q) * 0.125, FILL)
        e = jnp.exp(s - jnp.max(s, 0, keepdims=True))
        pr = e * (1.0 / jnp.sum(e, 0, keepdims=True))
        probs[i, p * 2 + h] = pr
        outs.append(dot_nn(vt[h * 64 : h * 64 + 64, :], pr.astype(BF)))
    ct = jnp.concatenate(outs, 0)
    contextt[i, pl.ds(pl.multiple_of(p * 128, 128), 128), :] = ct.astype(BF)
    context[rows, qc] = ct.T.astype(BF)


def forward_out(i, tall, context, wout, xp, keep, gate, g2_ref, attended, middle, h2):
    rows = pl.ds(pl.multiple_of(i * tall, 16), tall)
    att = dot_nn(context[rows, :], wout[...])
    attended[rows, :] = att
    mid = xp[rows, :].astype(F32) + keep[rows, 0:1] * gate[rows, 0:1] * att
    middle[rows, :] = mid
    unit, _ = unit_rows(mid)
    h2[rows, :] = (unit * g2_ref[...][None]).astype(BF)


def gelu_pair(pre):
    cdf = 0.5 * (1.0 + lax.erf(pre * 0.7071067811865476))
    pdf = jnp.exp(pre * pre * -0.5) * 0.3989422804014327
    return pre * cdf, cdf + pre * pdf


def mlp_rows(h, c, w1, w2):
    pre = dot_nn(h, w1)
    hidden, slope = gelu_pair(pre)
    grad = dot_nt(c, w2) * slope
    return hidden.astype(BF), grad.astype(BF)


def back_rows(i, tall, c_ref, gh2, middle, keep, gate, attended, g2_ref, gmid, gatt, glogit, dg2):
    rows = pl.ds(pl.multiple_of(i * tall, 16), tall)
    dy = gh2[rows, :]
    unit, scale = unit_rows(middle[rows, :])
    gm = c_ref[rows, :].astype(F32) + norm_pull(dy, g2_ref[...][None], unit, scale)
    gmid[rows, :] = gm
    dg2[...] += jnp.sum(dy * unit, 0, keepdims=True)
    k, g = keep[rows, 0:1], gate[rows, 0:1]
    kept = gm * k
    gatt[rows, :] = (kept * g).astype(BF)
    gl = jnp.sum(kept * attended[rows, :], -1, keepdims=True) * g * (1.0 - g)
    glogit[rows, :] = jnp.broadcast_to(gl, (tall, 128))


def attend_back(p, i, width, tall, qkv, probs, gctx):
    rows = pl.ds(pl.multiple_of(i * tall, 16), tall)
    qc = pl.ds(pl.multiple_of(p * 128, 128), 128)
    kc = pl.ds(pl.multiple_of(width + p * 128, 128), 128)
    vc = pl.ds(pl.multiple_of(2 * width + p * 128, 128), 128)
    q, k, v = qkv[rows, qc], qkv[rows, kc], qkv[rows, vc]
    gc = gctx[rows, qc]
    kt = k.T
    gv, gk, gq = 0.0, 0.0, []
    for h in range(2):
        mask = half_mask(tall, h)
        zero = jnp.zeros_like(v)
        pr = probs[i, p * 2 + h]
        gp = dot_nt(jnp.where(mask, v, zero), gc)
        gs = (pr * (gp - jnp.sum(pr * gp, 0, keepdims=True))).astype(BF)
        gv = gv + dot_nn(pr.astype(BF), jnp.where(mask, gc, zero))
        gk = gk + dot_nn(gs, jnp.where(mask, q, zero))
        gq.append(dot_nn(kt[h * 64 : h * 64 + 64, :], gs))
    qkv[rows, qc] = (jnp.concatenate(gq, 0).T * 0.125).astype(BF)
    qkv[rows, kc] = (gk * 0.125).astype(BF)
    qkv[rows, vc] = gv.astype(BF)


def pair_columns(wqkv, p, width):
    return jnp.concatenate(
        [wqkv[:, pl.ds(pl.multiple_of(b * width + p * 128, 128), 128)] for b in range(3)], 1
    )


def back_input(i, tall, dy, glogit, rw_ref, xp, h1, g1_ref, gmid, gx_ref, dg1, drw):
    rows = pl.ds(pl.multiple_of(i * tall, 16), tall)
    patches = gx_ref.shape[0]
    gl = glogit[rows, 0:1]
    dy = dy + gl * rw_ref[...][None].astype(F32)
    unit, scale = unit_rows(xp[rows, :].astype(F32))
    dg1[...] += jnp.sum(dy * unit, 0, keepdims=True)
    drw[...] += jnp.sum(h1[rows, :].astype(F32) * gl, 0, keepdims=True)
    out = gmid[rows, :] + norm_pull(dy, g1_ref[...][None], unit, scale)
    gx_ref[:, i, :] = out.astype(BF)[0:patches, :]

MESH = pl.DeviceIdType.MESH
CHUNKS = HEADS // 2 + 2
WIDEN = 8
PATHS = ("zxy", "zxy", "xyz", "yzx", "xyz", "yxz", "yzx", "xyz")
ORDER = (
    "osend", "back0", "pairs0", "back1", "out1", "pairs1", "fa11", "last0", "fa10", "pairs2", "fa00", "last1",
    "c2.1", "c1.1", "pairs3", "c3.1", "fa01", "fb1", "c5.1", "last2", "out0", "c4.1", "finish0", "c2.2", "c3.2",
    "c1.2", "c6.1", "c0.1", "c7.1", "fb0", "finish1", "c2.3", "c1.3", "c3.3", "c5.2", "c4.2", "c6.2", "c7.2", "g1",
    "c0.2", "c1.4", "c3.4", "fc", "c4.3", "c2.4", "c5.3", "c6.3", "o0", "c0.3", "c1.5", "g2", "c4.4", "c7.3", "c3.5",
    "c5.4", "fd", "c2.5", "c0.4", "c6.4", "c1.6", "c4.5", "c7.4", "c5.5", "c3.6", "c0.5", "c4.6", "c2.6", "c6.5",
    "c5.6", "c7.5", "c3.7", "g3", "c0.6", "fe", "c4.7", "c6.6", "c7.6", "c1.7", "c2.7", "c5.7", "c3.8", "c6.7",
    "c0.7", "c4.8", "g4", "c7.7", "c1.8", "c5.8", "c2.8", "o1", "c3.9", "c0.8", "ff", "c6.8", "c1.9", "c7.8", "c5.9",
    "c4.9", "c0.9", "c2.9", "c6.9", "g5", "c7.9",
)


def mega_kernel(
    x_hbm, rank_hbm, kept_hbm, g1_hbm, rw_hbm, wqkv_hbm, wout_hbm, g2_hbm, fc1, fc2, c_hbm,
    c_ref, x_ref, gw, g1w, g2w, small_out,
    rank_ref, kept_ref, g1_ref, rw_ref, g2_ref, wqkv, wout, w1, w2, xp, keep, gate, glogit, h1, h1t, qkv, probs, contextt, context, attended, middle,
    tok, cot, turned, out, gh2, out_part, gh2_part, out_sib, gh2_sib, out_near, gh2_near, out_far, gh2_far, hid, gpre, work,
    r1a, r1b, r2a, r2b, fz1, fz2, rz1, rz2,
    q0, q1, q2, q3, far, dg1, dg2, drw, sma, smr, smz,
    lsem, gsend, grecv, hsend, hrecv, csend, crecv, esend, erecv, s1s, s1r, s2s, s2r, s3s, s3r, fs, fr, ssib, rsib, free, chunk_free,
    qs, qr, small_sem, sms, smrs, smzs, smzr,
):
    patches, images, width = x_ref.shape
    t_own = xp.shape[0]
    tall = t_own // images
    half = width // 2
    part = w1.shape[1] // 2
    parts = (q0, q1, q2, q3)
    quarter = (width // 4, part // 4)
    r = lax.axis_index("rows")
    z = lax.axis_index("mlp")
    c, x, y = lax.rem(r, 2), lax.rem(lax.div(r, 2), 2), lax.rem(lax.div(r, 4), 2)
    r_sib, r_x, r_y = r + 1 - 2 * c, r + 2 - 4 * x, r + 4 - 8 * y
    r_diag = r_x + r_y - r
    z_pair, z_far = z + 1 - 2 * lax.rem(z, 2), z + 2 - 4 * lax.div(z, 2)
    q = 2 * y + x

    def ds(start, size):
        return pl.ds(pl.multiple_of(start, 16), size)

    def lanes(start, size):
        return pl.ds(pl.multiple_of(start, 128), size)

    def remote(src, dst, send, recv, row, column):
        return pltpu.make_async_remote_copy(
            src_ref=src, dst_ref=dst, send_sem=send, recv_sem=recv,
            device_id={"rows": row, "mlp": column}, device_id_type=MESH,
        )

    def release(semaphore, row):
        pl.semaphore_signal(semaphore, inc=1, device_id={"rows": row, "mlp": z}, device_id_type=MESH)

    def gather_copy(mat, kind):
        size = quarter[mat]
        sems = gsend.at[mat, kind], grecv.at[mat, kind]
        if mat == 0:
            place = w1.at[ds(q * size, size), pl.ds(part, part)]
            own = fc1.at[ds(q * size, size), lanes(c * part, part)]
        else:
            place = w2.at[ds(part + q * size, size), :]
            own = fc2.at[ds(c * part + q * size, size), :]
        if kind == 0:
            return remote(own, place, *sems, r, z_far)
        return remote(place, place, *sems, (r_x, r_y, r_diag)[kind - 1], z)

    def gather_forward(mat):
        gather_copy(mat, 0).wait_recv()
        for kind in (1, 2, 3):
            gather_copy(mat, kind).start()

    def own_shard(mat):
        if mat == 0:
            return pltpu.make_async_copy(fc1.at[:, lanes(c * part, part)], w1.at[:, pl.ds(0, part)], lsem.at[0])
        return pltpu.make_async_copy(fc2.at[ds(c * part, part), :], w2.at[pl.ds(0, part), :], lsem.at[1])

    load_qkv = pltpu.make_async_copy(wqkv_hbm, wqkv, lsem.at[2])
    load_out = pltpu.make_async_copy(wout_hbm, wout, lsem.at[3])
    load_x = pltpu.make_async_copy(x_hbm, x_ref, lsem.at[4])
    load_small = [
        pltpu.make_async_copy(src, dst, small_sem.at[k])
        for k, (src, dst) in enumerate(((rank_hbm, rank_ref), (kept_hbm, kept_ref), (g1_hbm, g1_ref), (rw_hbm, rw_ref), (g2_hbm, g2_ref)))
    ]
    load_c = pltpu.make_async_copy(c_hbm, c_ref, lsem.at[5])

    def token_copy(i, hop):
        start = (0, 0, 2 * t_own)[hop] + i * tall
        src, dst = tok.at[ds(start, tall), :], tok.at[ds((1, 2, 3)[hop] * t_own + i * tall, tall), :]
        row, column = (r, z_pair) if hop == 1 else (r_sib, z)
        return remote(src, dst, hsend.at[i, hop], hrecv.at[i, hop], row, column)

    def cot_copy(hop):
        src, dst = cot.at[ds((0, 0, 2)[hop] * t_own, t_own), :], cot.at[ds((1, 2, 3)[hop] * t_own, t_own), :]
        row, column = (r, z_pair) if hop == 1 else (r_sib, z)
        return remote(src, dst, csend.at[hop], crecv.at[hop], row, column)

    gh2_to_sib = remote(gh2_part.at[ds(0, t_own), :], gh2_sib, esend.at[0], erecv.at[0], r_sib, z)
    out_to_sib = remote(out_part.at[ds(0, t_own), :], out_sib, esend.at[1], erecv.at[1], r_sib, z)
    out_over = remote(out_part.at[ds(2 * t_own, t_own), :], out_near, esend.at[2], erecv.at[2], r_sib, z)
    out_far_copy = remote(out_part.at[ds(t_own, t_own), :], out_far, esend.at[3], erecv.at[3], r, z_pair)

    def gh2_over(i):
        src = gh2_part.at[ds(2 * t_own + i * tall, tall), :]
        return remote(src, gh2_near.at[ds(i * tall, tall), :], esend.at[4 + i], erecv.at[4 + i], r_sib, z)

    def gh2_far_copy(i):
        src = gh2_part.at[ds(t_own + i * tall, tall), :]
        return remote(src, gh2_far.at[ds(i * tall, tall), :], esend.at[6 + i], erecv.at[6 + i], r, z_pair)

    fc_whole, fc_half, fc_quarter, fc_done, fc_far = (g1w, g2w), (r1a, r1b), (r2a, r2b), (fz1, fz2), (rz1, rz2)
    fc_rows = ((width // 2, width // 4), (part // 2, part // 4))

    def fc_ways(k, m):
        shard = lax.div(z, 2) if k == 0 else 1 - lax.div(z, 2)
        turn = lax.rem(shard + m, 2)
        return r_x + (r_y - r_x) * turn, r_y + (r_x - r_y) * turn, x + (y - x) * turn, y + (x - y) * turn

    def fc_first(k, m):
        n1, _, a1, _ = fc_ways(k, m)
        rows, _ = fc_rows[m]
        src = fc_whole[m].at[k, ds((1 - a1) * rows, rows), :]
        return remote(src, fc_half[m].at[k], s1s.at[k, m], s1r.at[k, m], n1, z)

    def fc_second(k, m):
        _, n2, a1, a2 = fc_ways(k, m)
        rows, less = fc_rows[m]
        src = fc_whole[m].at[k, ds(a1 * rows + (1 - a2) * less, less), :]
        return remote(src, fc_quarter[m].at[k], s2s.at[k, m], s2r.at[k, m], n2, z)

    fc_third = [remote(fc_done[m].at[1], fc_far[m], s3s.at[m], s3r.at[m], r, z_far) for m in range(2)]

    def fc_spread(level, m):
        n1, n2, a1, a2 = fc_ways(0, m)
        rows, less = fc_rows[m]
        place = ds(a1 * rows + a2 * less, less) if level == 0 else ds(a1 * rows, rows)
        held = fc_whole[m].at[0, place, :]
        return remote(held, held, fs.at[level, m], fr.at[level, m], n2 if level == 0 else n1, z)

    fc_share = (
        remote(g1w.at[0], g1w.at[1], ssib.at[0], rsib.at[0], r_sib, z),
        remote(g2w.at[0], g2w.at[1], ssib.at[1], rsib.at[1], r_sib, z),
    )

    def fc_fold_second(k, m):
        fc_first(k, m).wait_recv()
        _, _, a1, a2 = fc_ways(k, m)
        rows, less = fc_rows[m]
        place, whole = ds(a1 * rows + (1 - a2) * less, less), fc_whole[m]
        whole[k, place, :] = whole[k, place, :] + fc_half[m][k, ds((1 - a2) * less, less), :]
        fc_second(k, m).start()

    def fc_fold_third(k):
        for m in range(2):
            fc_second(k, m).wait_recv()
            _, _, a1, a2 = fc_ways(k, m)
            rows, less = fc_rows[m]
            total = fc_whole[m][k, ds(a1 * rows + a2 * less, less), :].astype(F32)
            total = total + fc_half[m][k, ds(a2 * less, less), :].astype(F32) + fc_quarter[m][k].astype(F32)
            fc_done[m][k] = total.astype(BF)
        if k == 1:
            for copy in fc_third:
                copy.start()
        for m in range(2):
            fc_first(k, m).wait_send()
            fc_second(k, m).wait_send()
        if k == 1:
            release(free.at[0], r_sib)
        else:
            release(free.at[1], r_x)
            release(free.at[1], r_y)

    def fc_finish():
        for copy in fc_third:
            copy.wait_recv()
        pl.semaphore_wait(free.at[1], 2)
        for m in range(2):
            _, _, a1, a2 = fc_ways(0, m)
            rows, less = fc_rows[m]
            fc_whole[m][0, ds(a1 * rows + a2 * less, less), :] = fc_done[m][0] + fc_far[m][...]
            fc_spread(0, m).start()

    def fc_widen():
        for m in range(2):
            fc_spread(0, m).wait_recv()
        for m in range(2):
            fc_spread(1, m).start()

    def fc_to_sibling():
        for m in range(2):
            fc_spread(1, m).wait_recv()
        pl.semaphore_wait(free.at[0], 1)
        for copy in fc_share:
            copy.start()

    sizes = tuple(width >> level for level in range(1, 5))

    def hops(j):
        ways = {"x": (r_x, z, x), "y": (r_y, z, y), "z": (r, z_pair, lax.rem(z, 2))}
        return [(r_sib, z, c)] + [ways[axis] for axis in PATHS[j]]

    def base(path, level):
        start = 0
        for (_, _, bit), size in zip(path[:level], sizes):
            start = start + bit * size
        return start

    def core_copy(j):
        src = gw.at[j, ds((1 - c) * half, half), :]
        return remote(src, parts[0].at[j], qs.at[j, 0], qr.at[j, 0], r_sib, z)

    def chunk_copy(j, step):
        path = hops(j)
        if step == 0:
            return core_copy(j)
        if step < 4:
            row, column, bit = path[step]
            start = base(path, step) + (1 - bit) * sizes[step]
            return remote(gw.at[j, ds(start, sizes[step]), :], parts[step].at[j], qs.at[j, step], qr.at[j, step], row, column)
        if step == 4:
            own = gw.at[j, ds(base(path, 4), sizes[3]), :]
            return remote(own, far.at[j], qs.at[j, 4], qr.at[j, 4], r, z_far)
        level = 8 - step
        row, column, _ = path[level]
        held = gw.at[j, ds(base(path, level + 1), sizes[level]), :]
        return remote(held, held, qs.at[j, step], qr.at[j, step], row, column)

    def chunk_step(j, step):
        path = hops(j)
        chunk_copy(j, step - 1).wait()
        if step <= 4:
            row, column, _ = path[step - 1]
            pl.semaphore_signal(
                chunk_free.at[j, step - 1], inc=1, device_id={"rows": row, "mlp": column}, device_id_type=MESH
            )
            start = base(path, min(step, 4))
            if step < 4:
                start = base(path, step) + (1 - path[step][2]) * sizes[step]
            size = sizes[min(step, 3)]
            total = gw[j, ds(start, size), :].astype(F32)
            for level in range(step):
                total = total + parts[level][j, ds(start - base(path, level + 1), size), :].astype(F32)
            gw[j, ds(start, size), :] = total.astype(BF)
        if step == 5:
            own = ds(base(path, 4), sizes[3])
            gw[j, own, :] = gw[j, own, :] + far[j]
        if 5 <= step <= 8:
            pl.semaphore_wait(chunk_free.at[j, 8 - step], 1)
        if step <= 8:
            chunk_copy(j, step).start()

    def small_copy(level):
        row = (r_sib, r_x, r_y)[level]
        return remote(sma.at[level], smr.at[level], sms.at[level], smrs.at[level], row, z)

    def small_z(step):
        src, dst = smz.at[2 * step], smz.at[2 * step + 1]
        return remote(src, dst, smzs.at[step], smzr.at[step], r, (z_pair, z_far)[step])

    barrier = pltpu.get_barrier_semaphore()
    partners = ((r_sib, z), (r_x, z), (r_y, z), (r_diag, z), (r, z_pair), (r, z_far))
    for row, column in partners:
        pl.semaphore_signal(barrier, inc=1, device_id={"rows": row, "mlp": column}, device_id_type=MESH)
    load_c.start()
    load_x.start()
    for copy in load_small:
        copy.start()
    load_qkv.start()
    load_out.start()
    own_shard(0).start()
    own_shard(1).start()
    pl.semaphore_wait(barrier, len(partners))
    gather_copy(0, 0).start()
    gather_copy(1, 0).start()
    load_c.wait()
    for i in range(images):
        work[...] = jnp.zeros_like(work)
        work[0:patches, :] = c_ref[:, i, :]
        cot[i * tall : (i + 1) * tall, :] = work[...]
    cot_copy(0).start()
    cot_copy(1).start()
    load_x.wait()
    for copy in load_small:
        copy.wait()
    for i in range(images):
        forward_rows(i, x_ref, rank_ref, kept_ref, g1_ref, rw_ref, xp, keep, gate, h1, work)

    load_qkv.wait()

    @pl.loop(0, 3 * width // 256)
    def _(j):
        forward_qkv(j, h1, wqkv, qkv)

    @pl.loop(0, HEADS // 2)
    def _(p):
        for i in range(images):
            attend(p, i, width, tall, qkv, keep, probs, context, contextt)

        @pl.when(p == 2)
        def _():
            gather_forward(0)

        @pl.when(p == 4)
        def _():
            gather_forward(1)

    load_out.wait()

    @pl.loop(0, images)
    def _(i):
        forward_out(i, tall, context, wout, xp, keep, gate, g2_ref, attended, middle, tok)
        token_copy(i, 0).start()
        token_copy(i, 1).start()

    own_shard(0).wait()
    own_shard(1).wait()

    def at(block, number, do):
        @pl.when(block == number)
        def _():
            do()

    def before_sibling():
        for i in range(images):
            token_copy(i, 0).wait_recv()
        cot_copy(0).wait_recv()

    h1t[...] = h1[...].T

    @pl.loop(0, 2 * images)
    def _(block):
        at(block, images, before_sibling)
        rows = ds(block * tall, tall)
        hid[rows, 0:part], gpre[rows, 0:part] = mlp_rows(tok[rows, :], cot[rows, :], w1[:, 0:part], w2[0:part, :])

    cot_copy(1).wait_recv()
    cot_copy(2).start()
    for mat in range(2):
        for kind in (1, 2, 3):
            gather_copy(mat, kind).wait_recv()
    for ref in (dg1, dg2, drw):
        ref[...] = jnp.zeros_like(ref)

    def before_near():
        cot_copy(2).wait_recv()
        gh2_to_sib.start()
        out_to_sib.start()

    def forward_token(i):
        token_copy(i, 1).wait_recv()
        token_copy(i, 2).start()

    def send_far(i):
        gh2_over(i).wait_recv()
        rows = ds(t_own + i * tall, tall)
        gh2_part[rows, :] = gh2_part[rows, :] + gh2_near[ds(i * tall, tall), :]
        gh2_far_copy(i).start()

    def before_last():
        send_far(0)
        token_copy(1, 2).wait_recv()

    @pl.loop(0, 8)
    def _(block):
        at(block, 3, lambda: forward_token(0))
        at(block, 4, before_near)
        at(block, 5, lambda: token_copy(0, 2).wait_recv())
        at(block, 6, lambda: forward_token(1))
        at(block, 7, before_last)
        inner = lax.rem(block, 5)
        swap = lax.div(block, 5) * (1 - 2 * inner + 3 * lax.div(inner * (inner - 1), 2))
        spot = block + swap
        rows = ds(spot * tall, tall)

        @pl.when(block < 2 * images)
        def _():
            hid[rows, part:], gpre[rows, part:] = mlp_rows(tok[rows, :], cot[rows, :], w1[:, part:], w2[part:, :])

        @pl.when(block >= 2 * images)
        def _():
            hid[rows, :], gpre[rows, :] = mlp_rows(tok[rows, :], cot[rows, :], w1[...], w2[...])

        share_out = dot_nn(hid[rows, :], w2[...])
        share_gh2 = dot_nt(gpre[rows, :], w1[...])

        @pl.when(block < images)
        def _():
            out[rows, :] = share_out
            gh2[rows, :] = share_gh2

        @pl.when(block >= images)
        def _():
            there = ds(lax.max(spot - images, 0) * tall, tall)
            out_part[there, :] = share_out.astype(BF)
            gh2_part[there, :] = share_gh2.astype(BF)

        at(block, 5, lambda: gh2_over(0).start())
        at(block, 7, lambda: gh2_over(1).start())

    out_over.start()
    turned[...] = tok[...].T
    for m in range(3):
        rows = slice(m * width // 3, (m + 1) * width // 3)
        total = dot_nn(turned[rows, :], gpre[...]).astype(BF)
        g1w[0, rows, :] = total[:, 0:part]
        g1w[1, rows, :] = total[:, part:]
    for k in range(2):
        fc_first(k, 0).start()
    send_far(1)
    turned[...] = hid[...].T
    for m in range(2):
        g2w[m] = dot_nn(turned[m * part : (m + 1) * part, :], cot[...]).astype(BF)
    for k in range(2):
        fc_first(k, 1).start()

    def back_image(i):
        if i == 0:
            gh2_to_sib.wait_recv()
            for n in range(images):
                token_copy(n, 0).wait_send()
                token_copy(n, 1).wait_send()
        gh2_far_copy(i).wait_recv()
        rows = pl.ds(i * tall, tall)
        gh2[rows, :] += gh2_sib[rows, :].astype(F32) + gh2_far[rows, :].astype(F32)
        back_rows(i, tall, cot, gh2, middle, keep, gate, attended, g2_ref, gh2, tok, glogit, dg2)
        context[rows, :] = dot_nt(tok[rows, :], wout[...]).astype(BF)

    def fill(j, total):
        gw[j] = total.astype(BF)
        core_copy(j).start()

    def grad_out_half(n):
        total = 0.0
        for i in range(images):
            total = total + dot_nn(contextt[i], tok[i * tall : (i + 1) * tall, n * half : (n + 1) * half])
        fill(n, total)

    def pair_chunk(p):
        fill(p + 2, dot_nn(h1t[...], pair_columns(qkv, p, width)))

    def finish(i):
        rows = pl.ds(i * tall, tall)
        dy = dot_nt(qkv[rows, :], wqkv[...])
        back_input(i, tall, dy, glogit, rw_ref, xp, h1, g1_ref, gh2, x_ref, dg1, drw)
        if i == images - 1:
            sma[0] = jnp.concatenate([dg1[...], drw[...], dg2[...], jnp.zeros((5, width), F32)], 0)
            small_copy(0).start()

    def small_step(step):
        if step < 3:
            small_copy(step - 1).wait()
            sma[step] = sma[step - 1] + smr[step - 1]
            small_copy(step).start()
        elif step == 3:
            small_copy(2).wait()
            smz[0] = sma[2] + smr[2]
            small_z(0).start()
        else:
            small_z(step - 4).wait()
            if step == 4:
                smz[2] = smz[0] + smz[1]
                small_z(1).start()
            else:
                small_out[...] = smz[2] + smz[3]

    def out_send():
        out_over.wait_recv()
        rows = pl.ds(t_own, t_own)
        out_part[rows, :] = out_part[rows, :] + out_near[...]
        out_far_copy.start()

    def out_finish(i):
        if i == 0:
            out_to_sib.wait_recv()
            out_far_copy.wait_recv()
        rows = pl.ds(i * tall, tall)
        total = middle[rows, :] + out[rows, :] + out_sib[rows, :].astype(F32) + out_far[rows, :].astype(F32)
        c_ref[:, i, :] = total.astype(BF)[0:patches, :]

    def fc_share_end():
        for copy in fc_share:
            copy.wait()

    single = {"fc": fc_finish, "fd": fc_widen, "fe": fc_to_sibling, "ff": fc_share_end, "osend": out_send}
    numbered = (("finish", finish), ("back", back_image), ("out", grad_out_half),
                ("fb", fc_fold_third), ("g", small_step), ("o", out_finish))

    def perform(names):
        for name in names:
            if name in single:
                single[name]()
            elif name[:2] == "fa":
                fc_fold_second(int(name[2]), int(name[3]))
            elif name[0] == "c":
                chunk_step(int(name[1]), int(name[3]))
            else:
                do = next(f for head, f in numbered if name[:-1] == head)
                do(int(name[-1]))

    first, start, stop = ORDER.index("pairs0"), ORDER.index("pairs1"), ORDER.index("last2")
    perform(ORDER[:first])

    @pl.loop(0, HEADS // 4)
    def _(n):
        for p in (2 * n, 2 * n + 1):
            attend_back(p, 0, width, tall, qkv, probs, context)

    perform(ORDER[first + 1 : start])
    marks = [ORDER.index(name) for k in range(3) for name in ("pairs%d" % (k + 1), "last%d" % k)]

    @pl.loop(0, HEADS // 4)
    def _(n):
        for p in (2 * n, 2 * n + 1):
            attend_back(p, 1, width, tall, qkv, probs, context)
        pair_chunk(2 * n)
        for k in range(3):
            at(n, k, lambda k=k: perform(ORDER[marks[2 * k] + 1 : marks[2 * k + 1]]))
        pair_chunk(2 * n + 1)
        for k in range(2):
            at(n, k, lambda k=k: perform(ORDER[marks[2 * k + 1] + 1 : marks[2 * k + 2]]))

    perform(ORDER[stop + 1 :])
    for level in range(2):
        for m in range(2):
            fc_spread(level, m).wait_send()
    for copy in fc_third:
        copy.wait_send()
    for mat in range(2):
        for kind in range(4):
            gather_copy(mat, kind).wait_send()
    for i in range(images):
        token_copy(i, 2).wait_send()
        gh2_over(i).wait_send()
        gh2_far_copy(i).wait_send()
    for hop in range(3):
        cot_copy(hop).wait_send()
    for copy in (gh2_to_sib, out_to_sib, out_over, out_far_copy):
        copy.wait_send()


VMEM = pl.BlockSpec(memory_space=pltpu.VMEM)
ANY = pl.BlockSpec(memory_space=pl.ANY)


def widen_kernel(
    block, gx, gw, gf1, gf2, small, block_out, gx_out, gq_out, go_out, f1_out, f2_out, g1_out, rw_out, g2_out,
    gq_wide, go_wide, f1_wide, f2_wide, store_sem, pass_sem,
):
    _, width, part = gf1.shape
    step = width // WIDEN
    c = lax.rem(lax.axis_index("rows"), 2)
    passed = [pltpu.make_async_copy(src, dst, pass_sem.at[k]) for k, (src, dst) in enumerate(((block, block_out), (gx, gx_out)))]

    def rows_of(i):
        return pl.ds(pl.multiple_of(i * step, 16), step)

    def stores(i):
        rows = rows_of(i)
        pairs = ((gq_wide, gq_out), (go_wide, go_out), (f1_wide, f1_out), (f2_wide, f2_out))
        return [
            pltpu.make_async_copy(src.at[rows, :], dst.at[rows, :], store_sem.at[i, k]) for k, (src, dst) in enumerate(pairs)
        ]

    for copy in passed:
        copy.start()
    g1_out[...], rw_out[...], g2_out[...] = small[0], small[1], small[2]

    @pl.loop(0, WIDEN)
    def _(i):
        rows = rows_of(i)
        for p in range(CHUNKS - 2):
            for b in range(3):
                start = b * width + p * 128
                gq_wide[rows, start : start + 128] = gw[2 + p, rows, b * 128 : (b + 1) * 128].astype(F32)
        for h in range(2):
            go_wide[rows, h * part : (h + 1) * part] = gw[h, rows, :].astype(F32)
        for k in range(2):
            core = c + k - 2 * c * k
            f1_wide[rows, pl.ds(pl.multiple_of(core * part, 128), part)] = gf1[k, rows, :].astype(F32)
        core = lax.div(i * step, part)
        inner = pl.ds(pl.multiple_of(i * step - core * part, 16), step)
        f2_wide[rows, :] = gf2[core + c - 2 * core * c, inner, :].astype(F32)
        for copy in stores(i):
            copy.start()

    @pl.loop(0, WIDEN)
    def _(i):
        for copy in stores(i):
            copy.wait()

    for copy in passed:
        copy.wait()


def widen(*held):
    width = held[3].shape[1]
    tokens = jax.ShapeDtypeStruct(held[0].shape, BF)
    wide = [(width, 3 * width), (width, width), (width, width), (width, width)]
    return pl.pallas_call(
        widen_kernel,
        out_shape=[tokens, tokens] + [jax.ShapeDtypeStruct(dims, F32) for dims in wide] + [jax.ShapeDtypeStruct((width,), F32)] * 3,
        in_specs=[VMEM] * 6,
        out_specs=[ANY] * 6 + [VMEM] * 3,
        scratch_shapes=[pltpu.VMEM(dims, F32) for dims in wide]
        + [pltpu.SemaphoreType.DMA((WIDEN, 4)), pltpu.SemaphoreType.DMA((2,))],
        compiler_params=pltpu.CompilerParams(vmem_limit_bytes=32 * 1024 * 1024),
        name="widen",
    )(*(pltpu.with_memory_space_constraint(a, pltpu.VMEM) for a in held))


def per_device(others, images, patch_rank, kept_count, ln1_gain, router_weight, w_qkv, w_out, ln2_gain, w_fc1, w_fc2, cotangent):
    count, patches, width = images.shape
    tall = -(-patches // 16) * 16
    t = count * tall
    part = w_fc1.shape[1] // 2
    half, eighth = width // 2, width // 8

    def bf(*dims):
        return pltpu.VMEM(dims, BF)

    def f32(*dims):
        return pltpu.VMEM(dims, F32)

    def sem(*dims):
        return pltpu.SemaphoreType.DMA(dims)

    scratch = [
        pltpu.VMEM(patch_rank.shape, jnp.int32), pltpu.SMEM(kept_count.shape, jnp.int32), f32(width), bf(width), f32(width),
        bf(width, 3 * width), bf(width, width), bf(width, 2 * part), bf(2 * part, width),
        bf(t, width), f32(t, 128), f32(t, 128), f32(t, 128), bf(t, width), bf(width, t), bf(t, 3 * width),
        f32(count, HEADS, tall, tall), bf(count, width, tall), bf(t, width), f32(t, width), f32(t, width),
        bf(4 * t, width), bf(4 * t, width), bf(width, 4 * t), f32(t, width), f32(t, width),
        bf(3 * t, width), bf(3 * t, width), bf(t, width), bf(t, width), bf(t, width), bf(t, width), bf(t, width), bf(t, width),
        bf(4 * t, 2 * part), bf(4 * t, 2 * part), bf(tall, width),
        bf(2, width // 2, part), bf(2, part // 2, width), bf(2, width // 4, part), bf(2, part // 4, width),
        bf(2, width // 4, part), bf(2, part // 4, width), bf(width // 4, part), bf(part // 4, width),
        bf(CHUNKS, half, 384), bf(CHUNKS, 2 * eighth, 384), bf(CHUNKS, eighth, 384),
        bf(CHUNKS, eighth // 2, 384), bf(CHUNKS, eighth // 2, 384),
        f32(1, width), f32(1, width), f32(1, width), f32(3, 8, width), f32(3, 8, width), f32(4, 8, width),
        sem(6), sem(2, 4), sem(2, 4), sem(count, 3), sem(count, 3), sem(3), sem(3), sem(8), sem(8),
        sem(2, 2), sem(2, 2), sem(2, 2), sem(2, 2), sem(2), sem(2),
        sem(2, 2), sem(2, 2), sem(2), sem(2), pltpu.SemaphoreType.REGULAR((2,)), pltpu.SemaphoreType.REGULAR((CHUNKS, 4)),
        sem(CHUNKS, 9), sem(CHUNKS, 9), sem(5),
        sem(3), sem(3), sem(2), sem(2),
    ]

    block, gx, gw, gf1, gf2, small = pl.pallas_call(
        mega_kernel,
        out_shape=[
            bf(patches, count, width), bf(patches, count, width), bf(CHUNKS, width, 384),
            bf(2, width, part), bf(2, part, width), f32(8, width),
        ],
        in_specs=[ANY] * 11,
        out_specs=[VMEM] * 6,
        scratch_shapes=scratch,
        compiler_params=pltpu.CompilerParams(
            collective_id=0, has_side_effects=True, vmem_limit_bytes=int(55.5 * 1024) * 1024
        ),
        name="block",
    )(images.transpose(1, 0, 2), patch_rank, kept_count, ln1_gain, router_weight, w_qkv, w_out, ln2_gain, w_fc1, w_fc2,
      cotangent.transpose(1, 0, 2))
    block, gx, gq, go, f1, f2, g1, rw, g2 = widen(block, gx, gw, gf1, gf2, small)
    if others:
        gq, go, f1, f2, g1, rw, g2 = lax.psum((gq, go, f1, f2, g1, rw, g2), "rows", axis_index_groups=others)
    return block.transpose(1, 0, 2), gx.transpose(1, 0, 2), g1, rw, gq, go, g2, f1, f2


def solution(mesh):
    rows = mesh.shape["rows"]
    others = [[8 * g + i for g in range(rows // 8)] for i in range(8)] if rows > 8 else None
    return jax.shard_map(
        functools.partial(per_device, others),
        mesh=mesh,
        in_specs=(
            P(("rows", "mlp"), None, None), P(("rows", "mlp"), None), P(("rows", "mlp")), P(), P(), P(), P(), P(),
            P(None, "mlp"), P("mlp", None), P(("rows", "mlp"), None, None),
        ),
        out_specs=(
            P(("rows", "mlp"), None, None), P(("rows", "mlp"), None, None), P(), P(), P(), P(), P(),
            P(None, "mlp"), P("mlp", None),
        ),
        check_vma=False,
    )
```

```python
import functools
import jax
import jax.numpy as jnp
from jax import lax
from jax.experimental import pallas as pl
from jax.experimental.pallas import tpu as pltpu
from jax.sharding import PartitionSpec as P

HEADS = 12
EPS = 1e-6
FILL = -1e30
BF = jnp.bfloat16
F32 = jnp.float32


def dot_nn(a, b):
    return lax.dot_general(a, b, (((1,), (0,)), ((), ())), preferred_element_type=F32)


def dot_nt(a, b):
    return lax.dot_general(a, b, (((1,), (1,)), ((), ())), preferred_element_type=F32)


def dot_tn(a, b):
    return lax.dot_general(a, b, (((0,), (0,)), ((), ())), preferred_element_type=F32)


def unit_rows(v):
    center = v - jnp.mean(v, -1, keepdims=True)
    scale = lax.rsqrt(jnp.mean(center * center, -1, keepdims=True) + EPS)
    return center * scale, scale


def norm_pull(dy, gain, unit, scale):
    du = dy * gain
    return scale * (
        du
        - jnp.mean(du, -1, keepdims=True)
        - unit * jnp.mean(du * unit, -1, keepdims=True)
    )


def half_mask(rows, h):
    lane = lax.broadcasted_iota(jnp.int32, (rows, 128), 1)
    return (lane < 64) if h == 0 else (lane >= 64)


def forward_rows(i, x_ref, rank_ref, kept_ref, g1_ref, rw_ref, xp, keep, gate, h1, work):
    patches = x_ref.shape[0]
    tall = xp.shape[0] // x_ref.shape[1]
    rows = pl.ds(pl.multiple_of(i * tall, 16), tall)
    work[...] = jnp.zeros_like(work)
    work[0:patches, :] = x_ref[:, i, :]
    v = work[...]
    xp[rows, :] = v
    kept = (rank_ref[pl.ds(i, 1), :] < kept_ref[i]).astype(F32)
    keep_row = jnp.concatenate([kept, jnp.zeros((1, 256 - patches), F32)], 1)
    keep_col = jnp.broadcast_to(keep_row, (128, 256)).T
    keep[rows, :] = keep_col[0:tall, :]
    unit, _ = unit_rows(v.astype(F32))
    low = (unit * g1_ref[...][None]).astype(BF)
    h1[rows, :] = low
    logit = jnp.sum(low.astype(F32) * rw_ref[...][None].astype(F32), -1, keepdims=True)
    gate[rows, :] = jnp.broadcast_to(jax.nn.sigmoid(logit), (tall, 128))


def forward_qkv(j, h1, wqkv, qkv):
    cols = pl.ds(pl.multiple_of(j * 256, 256), 256)
    qkv[:, cols] = dot_nn(h1[...], wqkv[:, cols]).astype(BF)


def attend(p, i, width, tall, qkv, keep, probs, context, contextt):
    rows = pl.ds(pl.multiple_of(i * tall, 16), tall)
    qc = pl.ds(pl.multiple_of(p * 128, 128), 128)
    kc = pl.ds(pl.multiple_of(width + p * 128, 128), 128)
    vc = pl.ds(pl.multiple_of(2 * width + p * 128, 128), 128)
    q, k, v = qkv[rows, qc], qkv[rows, kc], qkv[rows, vc]
    vt = v.T
    kept = keep[rows, 0:1] > 0.5
    outs = []
    for h in range(2):
        kh = jnp.where(half_mask(tall, h), k, jnp.zeros_like(k))
        s = jnp.where(kept, dot_nt(kh, q) * 0.125, FILL)
        e = jnp.exp(s - jnp.max(s, 0, keepdims=True))
        pr = e * (1.0 / jnp.sum(e, 0, keepdims=True))
        probs[i, p * 2 + h] = pr
        outs.append(dot_nn(vt[h * 64 : h * 64 + 64, :], pr.astype(BF)))
    ct = jnp.concatenate(outs, 0)
    contextt[i, pl.ds(pl.multiple_of(p * 128, 128), 128), :] = ct.astype(BF)
    context[rows, qc] = ct.T.astype(BF)


def forward_out(i, tall, context, wout, xp, keep, gate, g2_ref, attended, middle, h2):
    rows = pl.ds(pl.multiple_of(i * tall, 16), tall)
    att = dot_nn(context[rows, :], wout[...])
    attended[rows, :] = att
    mid = xp[rows, :].astype(F32) + keep[rows, 0:1] * gate[rows, 0:1] * att
    middle[rows, :] = mid
    unit, _ = unit_rows(mid)
    h2[rows, :] = (unit * g2_ref[...][None]).astype(BF)


def gelu_pair(pre):
    cdf = 0.5 * (1.0 + lax.erf(pre * 0.7071067811865476))
    pdf = jnp.exp(pre * pre * -0.5) * 0.3989422804014327
    return pre * cdf, cdf + pre * pdf


def mlp_rows(h, c, w1, w2):
    pre = dot_nn(h, w1)
    hidden, slope = gelu_pair(pre)
    grad = dot_nt(c, w2) * slope
    return hidden.astype(BF), grad.astype(BF)


def back_rows(i, tall, c_ref, gh2, middle, keep, gate, attended, g2_ref, gmid, gatt, glogit, dg2):
    rows = pl.ds(pl.multiple_of(i * tall, 16), tall)
    dy = gh2[rows, :]
    unit, scale = unit_rows(middle[rows, :])
    gm = c_ref[rows, :].astype(F32) + norm_pull(dy, g2_ref[...][None], unit, scale)
    gmid[rows, :] = gm
    dg2[...] += jnp.sum(dy * unit, 0, keepdims=True)
    k, g = keep[rows, 0:1], gate[rows, 0:1]
    kept = gm * k
    gatt[rows, :] = (kept * g).astype(BF)
    gl = jnp.sum(kept * attended[rows, :], -1, keepdims=True) * g * (1.0 - g)
    glogit[rows, :] = jnp.broadcast_to(gl, (tall, 128))


def attend_back(p, i, width, tall, qkv, probs, gctx):
    rows = pl.ds(pl.multiple_of(i * tall, 16), tall)
    qc = pl.ds(pl.multiple_of(p * 128, 128), 128)
    kc = pl.ds(pl.multiple_of(width + p * 128, 128), 128)
    vc = pl.ds(pl.multiple_of(2 * width + p * 128, 128), 128)
    q, k, v = qkv[rows, qc], qkv[rows, kc], qkv[rows, vc]
    gc = gctx[rows, qc]
    kt = k.T
    gv, gk, gq = 0.0, 0.0, []
    for h in range(2):
        mask = half_mask(tall, h)
        zero = jnp.zeros_like(v)
        pr = probs[i, p * 2 + h]
        gp = dot_nt(jnp.where(mask, v, zero), gc)
        gs = (pr * (gp - jnp.sum(pr * gp, 0, keepdims=True))).astype(BF)
        gv = gv + dot_nn(pr.astype(BF), jnp.where(mask, gc, zero))
        gk = gk + dot_nn(gs, jnp.where(mask, q, zero))
        gq.append(dot_nn(kt[h * 64 : h * 64 + 64, :], gs))
    qkv[rows, qc] = (jnp.concatenate(gq, 0).T * 0.125).astype(BF)
    qkv[rows, kc] = (gk * 0.125).astype(BF)
    qkv[rows, vc] = gv.astype(BF)


def pair_columns(wqkv, p, width):
    return jnp.concatenate(
        [wqkv[:, pl.ds(pl.multiple_of(b * width + p * 128, 128), 128)] for b in range(3)], 1
    )


def back_input(i, tall, dy, glogit, rw_ref, xp, h1, g1_ref, gmid, gx_ref, dg1, drw):
    rows = pl.ds(pl.multiple_of(i * tall, 16), tall)
    patches = gx_ref.shape[0]
    gl = glogit[rows, 0:1]
    dy = dy + gl * rw_ref[...][None].astype(F32)
    unit, scale = unit_rows(xp[rows, :].astype(F32))
    dg1[...] += jnp.sum(dy * unit, 0, keepdims=True)
    drw[...] += jnp.sum(h1[rows, :].astype(F32) * gl, 0, keepdims=True)
    out = gmid[rows, :] + norm_pull(dy, g1_ref[...][None], unit, scale)
    gx_ref[:, i, :] = out.astype(BF)[0:patches, :]

MESH = pl.DeviceIdType.MESH
CHUNKS = HEADS // 2 + 2
WIDEN = 8
PATHS = ("zxy", "yzx", "xyz", "yxz", "xyz", "yzx", "xzy", "yxz")
ORDER = (
    "back0", "osend", "pairs0", "back1", "pairs1", "fa11", "fa10", "fa01", "last0", "fa00", "out1", "pairs2", "out0",
    "last1", "c3.1", "fb1", "c2.1", "pairs3", "c1.1", "last2", "c4.1", "finish0", "c5.1", "c0.1", "c2.2", "c3.2",
    "c6.1", "finish1", "c1.2", "fb0", "c4.2", "c3.3", "c5.2", "c7.1", "c0.2", "g1", "c2.3", "c6.2", "c1.3", "fc",
    "c4.3", "c3.4", "c0.3", "o0", "g2", "c2.4", "c7.2", "c6.3", "c5.3", "c1.4", "c4.4", "c3.5", "fd", "c0.4", "c6.4",
    "c7.3", "c2.5", "c1.5", "c5.4", "c4.5", "c3.6", "g3", "c7.4", "c0.5", "o1", "c2.6", "c4.6", "g4", "c6.5", "c5.5",
    "c1.6", "c0.6", "c7.5", "fe", "c3.7", "c2.7", "c5.6", "c6.6", "c1.7", "c0.7", "c7.6", "c4.7", "c5.7", "c3.8",
    "c2.8", "c6.7", "c7.7", "c1.8", "c0.8", "c3.9", "c4.8", "g5", "c5.8", "c1.9", "c6.8", "c7.8", "ff", "c2.9",
    "c6.9", "c5.9", "c4.9", "c0.9", "c7.9",
)


def mega_kernel(
    x_hbm, rank_hbm, kept_hbm, g1_hbm, rw_hbm, wqkv_hbm, wout_hbm, g2_hbm, fc1, fc2, c_hbm,
    c_ref, x_ref, gw, g1w, g2w, small_out,
    rank_ref, kept_ref, g1_ref, rw_ref, g2_ref, wqkv, wout, w1, w2, xp, keep, gate, glogit, h1, h1t, qkv, probs, contextt, context, attended, middle,
    tok, cot, turned, out, gh2, out_part, gh2_part, out_sib, gh2_sib, out_near, gh2_near, out_far, gh2_far, hid, gpre, work,
    r1a, r1b, r2a, r2b, fz1, fz2, rz1, rz2,
    q0, q1, q2, q3, far, dg1, dg2, drw, sma, smr, smz,
    lsem, gsend, grecv, hsend, hrecv, csend, crecv, esend, erecv, s1s, s1r, s2s, s2r, s3s, s3r, fs, fr, ssib, rsib, free, chunk_free,
    qs, qr, small_sem, sms, smrs, smzs, smzr,
):
    patches, images, width = x_ref.shape
    t_own = xp.shape[0]
    tall = t_own // images
    half = width // 2
    part = w1.shape[1] // 2
    parts = (q0, q1, q2, q3)
    quarter = (width // 4, part // 4)
    r = lax.axis_index("rows")
    z = lax.axis_index("mlp")
    c, x, y = lax.rem(r, 2), lax.rem(lax.div(r, 2), 2), lax.rem(lax.div(r, 4), 2)
    r_sib, r_x, r_y = r + 1 - 2 * c, r + 2 - 4 * x, r + 4 - 8 * y
    r_diag = r_x + r_y - r
    z_pair, z_far = z + 1 - 2 * lax.rem(z, 2), z + 2 - 4 * lax.div(z, 2)
    q = 2 * y + x

    def ds(start, size):
        return pl.ds(pl.multiple_of(start, 16), size)

    def lanes(start, size):
        return pl.ds(pl.multiple_of(start, 128), size)

    def remote(src, dst, send, recv, row, column):
        return pltpu.make_async_remote_copy(
            src_ref=src, dst_ref=dst, send_sem=send, recv_sem=recv,
            device_id={"rows": row, "mlp": column}, device_id_type=MESH,
        )

    def release(semaphore, row):
        pl.semaphore_signal(semaphore, inc=1, device_id={"rows": row, "mlp": z}, device_id_type=MESH)

    def gather_copy(mat, kind):
        size = quarter[mat]
        sems = gsend.at[mat, kind], grecv.at[mat, kind]
        if mat == 0:
            place = w1.at[ds(q * size, size), pl.ds(part, part)]
            own = fc1.at[ds(q * size, size), lanes(c * part, part)]
        else:
            place = w2.at[ds(part + q * size, size), :]
            own = fc2.at[ds(c * part + q * size, size), :]
        if kind == 0:
            return remote(own, place, *sems, r, z_far)
        return remote(place, place, *sems, (r_x, r_y, r_diag)[kind - 1], z)

    def gather_forward(mat):
        gather_copy(mat, 0).wait_recv()
        for kind in (1, 2, 3):
            gather_copy(mat, kind).start()

    def own_shard(mat):
        if mat == 0:
            return pltpu.make_async_copy(fc1.at[:, lanes(c * part, part)], w1.at[:, pl.ds(0, part)], lsem.at[0])
        return pltpu.make_async_copy(fc2.at[ds(c * part, part), :], w2.at[pl.ds(0, part), :], lsem.at[1])

    load_qkv = pltpu.make_async_copy(wqkv_hbm, wqkv, lsem.at[2])
    load_out = pltpu.make_async_copy(wout_hbm, wout, lsem.at[3])
    load_x = pltpu.make_async_copy(x_hbm, x_ref, lsem.at[4])
    load_small = [
        pltpu.make_async_copy(src, dst, small_sem.at[k])
        for k, (src, dst) in enumerate(((rank_hbm, rank_ref), (kept_hbm, kept_ref), (g1_hbm, g1_ref), (rw_hbm, rw_ref), (g2_hbm, g2_ref)))
    ]
    load_c = pltpu.make_async_copy(c_hbm, c_ref, lsem.at[5])

    def token_copy(i, hop):
        start = (0, 0, 2 * t_own)[hop] + i * tall
        src, dst = tok.at[ds(start, tall), :], tok.at[ds((1, 2, 3)[hop] * t_own + i * tall, tall), :]
        row, column = (r, z_pair) if hop == 1 else (r_sib, z)
        return remote(src, dst, hsend.at[i, hop], hrecv.at[i, hop], row, column)

    def cot_copy(hop):
        src, dst = cot.at[ds((0, 0, 2)[hop] * t_own, t_own), :], cot.at[ds((1, 2, 3)[hop] * t_own, t_own), :]
        row, column = (r, z_pair) if hop == 1 else (r_sib, z)
        return remote(src, dst, csend.at[hop], crecv.at[hop], row, column)

    gh2_to_sib = remote(gh2_part.at[ds(0, t_own), :], gh2_sib, esend.at[0], erecv.at[0], r_sib, z)
    out_to_sib = remote(out_part.at[ds(0, t_own), :], out_sib, esend.at[1], erecv.at[1], r_sib, z)
    out_over = remote(out_part.at[ds(2 * t_own, t_own), :], out_near, esend.at[2], erecv.at[2], r_sib, z)
    out_far_copy = remote(out_part.at[ds(t_own, t_own), :], out_far, esend.at[3], erecv.at[3], r, z_pair)

    def gh2_over(i):
        src = gh2_part.at[ds(2 * t_own + i * tall, tall), :]
        return remote(src, gh2_near.at[ds(i * tall, tall), :], esend.at[4 + i], erecv.at[4 + i], r_sib, z)

    def gh2_far_copy(i):
        src = gh2_part.at[ds(t_own + i * tall, tall), :]
        return remote(src, gh2_far.at[ds(i * tall, tall), :], esend.at[6 + i], erecv.at[6 + i], r, z_pair)

    fc_whole, fc_half, fc_quarter, fc_done, fc_far = (g1w, g2w), (r1a, r1b), (r2a, r2b), (fz1, fz2), (rz1, rz2)
    fc_rows = ((width // 2, width // 4), (part // 2, part // 4))

    def fc_ways(k, m):
        shard = lax.div(z, 2) if k == 0 else 1 - lax.div(z, 2)
        turn = lax.rem(shard + m, 2)
        return r_x + (r_y - r_x) * turn, r_y + (r_x - r_y) * turn, x + (y - x) * turn, y + (x - y) * turn

    def fc_first(k, m):
        n1, _, a1, _ = fc_ways(k, m)
        rows, _ = fc_rows[m]
        src = fc_whole[m].at[k, ds((1 - a1) * rows, rows), :]
        return remote(src, fc_half[m].at[k], s1s.at[k, m], s1r.at[k, m], n1, z)

    def fc_second(k, m):
        _, n2, a1, a2 = fc_ways(k, m)
        rows, less = fc_rows[m]
        src = fc_whole[m].at[k, ds(a1 * rows + (1 - a2) * less, less), :]
        return remote(src, fc_quarter[m].at[k], s2s.at[k, m], s2r.at[k, m], n2, z)

    fc_third = [remote(fc_done[m].at[1], fc_far[m], s3s.at[m], s3r.at[m], r, z_far) for m in range(2)]

    def fc_spread(level, m):
        n1, n2, a1, a2 = fc_ways(0, m)
        rows, less = fc_rows[m]
        place = ds(a1 * rows + a2 * less, less) if level == 0 else ds(a1 * rows, rows)
        held = fc_whole[m].at[0, place, :]
        return remote(held, held, fs.at[level, m], fr.at[level, m], n2 if level == 0 else n1, z)

    fc_share = (
        remote(g1w.at[0], g1w.at[1], ssib.at[0], rsib.at[0], r_sib, z),
        remote(g2w.at[0], g2w.at[1], ssib.at[1], rsib.at[1], r_sib, z),
    )

    def fc_fold_second(k, m):
        fc_first(k, m).wait_recv()
        _, _, a1, a2 = fc_ways(k, m)
        rows, less = fc_rows[m]
        place, whole = ds(a1 * rows + (1 - a2) * less, less), fc_whole[m]
        whole[k, place, :] = whole[k, place, :] + fc_half[m][k, ds((1 - a2) * less, less), :]
        fc_second(k, m).start()

    def fc_fold_third(k):
        for m in range(2):
            fc_second(k, m).wait_recv()
            _, _, a1, a2 = fc_ways(k, m)
            rows, less = fc_rows[m]
            total = fc_whole[m][k, ds(a1 * rows + a2 * less, less), :].astype(F32)
            total = total + fc_half[m][k, ds(a2 * less, less), :].astype(F32) + fc_quarter[m][k].astype(F32)
            fc_done[m][k] = total.astype(BF)
        if k == 1:
            for copy in fc_third:
                copy.start()
        for m in range(2):
            fc_first(k, m).wait_send()
            fc_second(k, m).wait_send()
        if k == 1:
            release(free.at[0], r_sib)
        else:
            release(free.at[1], r_x)
            release(free.at[1], r_y)

    def fc_finish():
        for copy in fc_third:
            copy.wait_recv()
        pl.semaphore_wait(free.at[1], 2)
        for m in range(2):
            _, _, a1, a2 = fc_ways(0, m)
            rows, less = fc_rows[m]
            fc_whole[m][0, ds(a1 * rows + a2 * less, less), :] = fc_done[m][0] + fc_far[m][...]
            fc_spread(0, m).start()

    def fc_widen():
        for m in range(2):
            fc_spread(0, m).wait_recv()
        for m in range(2):
            fc_spread(1, m).start()

    def fc_to_sibling():
        for m in range(2):
            fc_spread(1, m).wait_recv()
        pl.semaphore_wait(free.at[0], 1)
        for copy in fc_share:
            copy.start()

    sizes = tuple(width >> level for level in range(1, 5))

    def hops(j):
        ways = {"x": (r_x, z, x), "y": (r_y, z, y), "z": (r, z_pair, lax.rem(z, 2))}
        return [(r_sib, z, c)] + [ways[axis] for axis in PATHS[j]]

    def base(path, level):
        start = 0
        for (_, _, bit), size in zip(path[:level], sizes):
            start = start + bit * size
        return start

    def core_copy(j):
        src = gw.at[j, ds((1 - c) * half, half), :]
        return remote(src, parts[0].at[j], qs.at[j, 0], qr.at[j, 0], r_sib, z)

    def chunk_copy(j, step):
        path = hops(j)
        if step == 0:
            return core_copy(j)
        if step < 4:
            row, column, bit = path[step]
            start = base(path, step) + (1 - bit) * sizes[step]
            return remote(gw.at[j, ds(start, sizes[step]), :], parts[step].at[j], qs.at[j, step], qr.at[j, step], row, column)
        if step == 4:
            own = gw.at[j, ds(base(path, 4), sizes[3]), :]
            return remote(own, far.at[j], qs.at[j, 4], qr.at[j, 4], r, z_far)
        level = 8 - step
        row, column, _ = path[level]
        held = gw.at[j, ds(base(path, level + 1), sizes[level]), :]
        return remote(held, held, qs.at[j, step], qr.at[j, step], row, column)

    def chunk_step(j, step):
        path, last = hops(j), chunk_copy(j, step - 1)
        last.wait_recv()
        if step <= 4:
            start = base(path, min(step, 4))
            if step < 4:
                start = base(path, step) + (1 - path[step][2]) * sizes[step]
            size = sizes[min(step, 3)]
            total = gw[j, ds(start, size), :].astype(F32)
            for level in range(step):
                total = total + parts[level][j, ds(start - base(path, level + 1), size), :].astype(F32)
            gw[j, ds(start, size), :] = total.astype(BF)
        if step == 5:
            last.wait_send()
            own = ds(base(path, 4), sizes[3])
            gw[j, own, :] = gw[j, own, :] + far[j]
        if 5 <= step <= 8:
            pl.semaphore_wait(chunk_free.at[j, 8 - step], 1)
        if step <= 8:
            chunk_copy(j, step).start()
        if step != 5:
            last.wait_send()
        if step <= 4:
            row, column, _ = path[step - 1]
            pl.semaphore_signal(
                chunk_free.at[j, step - 1], inc=1, device_id={"rows": row, "mlp": column}, device_id_type=MESH
            )

    def small_copy(level):
        row = (r_sib, r_x, r_y)[level]
        return remote(sma.at[level], smr.at[level], sms.at[level], smrs.at[level], row, z)

    def small_z(step):
        src, dst = smz.at[2 * step], smz.at[2 * step + 1]
        return remote(src, dst, smzs.at[step], smzr.at[step], r, (z_pair, z_far)[step])

    barrier = pltpu.get_barrier_semaphore()
    partners = ((r_sib, z), (r_x, z), (r_y, z), (r_diag, z), (r, z_pair), (r, z_far))
    for row, column in partners:
        pl.semaphore_signal(barrier, inc=1, device_id={"rows": row, "mlp": column}, device_id_type=MESH)
    load_c.start()
    load_x.start()
    for copy in load_small:
        copy.start()
    load_qkv.start()
    load_out.start()
    own_shard(0).start()
    own_shard(1).start()
    pl.semaphore_wait(barrier, len(partners))
    gather_copy(0, 0).start()
    gather_copy(1, 0).start()
    load_c.wait()
    for i in range(images):
        work[...] = jnp.zeros_like(work)
        work[0:patches, :] = c_ref[:, i, :]
        cot[i * tall : (i + 1) * tall, :] = work[...]
    cot_copy(0).start()
    cot_copy(1).start()
    load_x.wait()
    for copy in load_small:
        copy.wait()
    for i in range(images):
        forward_rows(i, x_ref, rank_ref, kept_ref, g1_ref, rw_ref, xp, keep, gate, h1, work)

    load_qkv.wait()

    @pl.loop(0, 3 * width // 256)
    def _(j):
        forward_qkv(j, h1, wqkv, qkv)

    @pl.loop(0, HEADS // 2)
    def _(p):
        for i in range(images):
            attend(p, i, width, tall, qkv, keep, probs, context, contextt)

        @pl.when(p == 2)
        def _():
            gather_forward(0)

        @pl.when(p == 4)
        def _():
            gather_forward(1)

    load_out.wait()

    @pl.loop(0, images)
    def _(i):
        forward_out(i, tall, context, wout, xp, keep, gate, g2_ref, attended, middle, tok)
        token_copy(i, 0).start()
        token_copy(i, 1).start()

    own_shard(0).wait()
    own_shard(1).wait()

    def at(block, number, do):
        @pl.when(block == number)
        def _():
            do()

    def before_sibling():
        for i in range(images):
            token_copy(i, 0).wait_recv()
        cot_copy(0).wait_recv()

    h1t[...] = h1[...].T

    @pl.loop(0, 2 * images)
    def _(block):
        at(block, images, before_sibling)
        rows = ds(block * tall, tall)
        hid[rows, 0:part], gpre[rows, 0:part] = mlp_rows(tok[rows, :], cot[rows, :], w1[:, 0:part], w2[0:part, :])

    cot_copy(1).wait_recv()
    cot_copy(2).start()
    for mat in range(2):
        for kind in (1, 2, 3):
            gather_copy(mat, kind).wait_recv()
    for ref in (dg1, dg2, drw):
        ref[...] = jnp.zeros_like(ref)

    def before_near():
        cot_copy(2).wait_recv()
        gh2_to_sib.start()
        out_to_sib.start()

    def forward_token(i):
        token_copy(i, 1).wait_recv()
        token_copy(i, 2).start()

    def send_far(i):
        gh2_over(i).wait_recv()
        rows = ds(t_own + i * tall, tall)
        gh2_part[rows, :] = gh2_part[rows, :] + gh2_near[ds(i * tall, tall), :]
        gh2_far_copy(i).start()

    def before_last():
        send_far(0)
        token_copy(1, 2).wait_recv()

    @pl.loop(0, 8)
    def _(block):
        at(block, 3, lambda: forward_token(0))
        at(block, 4, before_near)
        at(block, 5, lambda: token_copy(0, 2).wait_recv())
        at(block, 6, lambda: forward_token(1))
        at(block, 7, before_last)
        inner = lax.rem(block, 5)
        swap = lax.div(block, 5) * (1 - 2 * inner + 3 * lax.div(inner * (inner - 1), 2))
        spot = block + swap
        rows = ds(spot * tall, tall)

        @pl.when(block < 2 * images)
        def _():
            hid[rows, part:], gpre[rows, part:] = mlp_rows(tok[rows, :], cot[rows, :], w1[:, part:], w2[part:, :])

        @pl.when(block >= 2 * images)
        def _():
            hid[rows, :], gpre[rows, :] = mlp_rows(tok[rows, :], cot[rows, :], w1[...], w2[...])

        share_out = dot_nn(hid[rows, :], w2[...])
        share_gh2 = dot_nt(gpre[rows, :], w1[...])

        @pl.when(block < images)
        def _():
            out[rows, :] = share_out
            gh2[rows, :] = share_gh2

        @pl.when(block >= images)
        def _():
            there = ds(lax.max(spot - images, 0) * tall, tall)
            out_part[there, :] = share_out.astype(BF)
            gh2_part[there, :] = share_gh2.astype(BF)

        at(block, 5, lambda: gh2_over(0).start())
        at(block, 7, lambda: gh2_over(1).start())

    out_over.start()
    turned[...] = tok[...].T
    for m in range(3):
        rows = slice(m * width // 3, (m + 1) * width // 3)
        total = dot_nn(turned[rows, :], gpre[...]).astype(BF)
        g1w[0, rows, :] = total[:, 0:part]
        g1w[1, rows, :] = total[:, part:]
    for k in range(2):
        fc_first(k, 0).start()
    send_far(1)
    turned[...] = hid[...].T
    for m in range(2):
        g2w[m] = dot_nn(turned[m * part : (m + 1) * part, :], cot[...]).astype(BF)
    for k in range(2):
        fc_first(k, 1).start()

    def back_image(i):
        if i == 0:
            gh2_to_sib.wait_recv()
            for n in range(images):
                token_copy(n, 0).wait_send()
                token_copy(n, 1).wait_send()
        gh2_far_copy(i).wait_recv()
        rows = pl.ds(i * tall, tall)
        gh2[rows, :] += gh2_sib[rows, :].astype(F32) + gh2_far[rows, :].astype(F32)
        back_rows(i, tall, cot, gh2, middle, keep, gate, attended, g2_ref, gh2, tok, glogit, dg2)
        context[rows, :] = dot_nt(tok[rows, :], wout[...]).astype(BF)

    def fill(j, total):
        gw[j] = total.astype(BF)
        core_copy(j).start()

    def grad_out_half(n):
        total = 0.0
        for i in range(images):
            total = total + dot_nn(contextt[i], tok[i * tall : (i + 1) * tall, n * half : (n + 1) * half])
        fill(n, total)

    def pair_chunk(p):
        fill(p + 2, dot_nn(h1t[...], pair_columns(qkv, p, width)))

    def finish(i):
        rows = pl.ds(i * tall, tall)
        dy = dot_nt(qkv[rows, :], wqkv[...])
        back_input(i, tall, dy, glogit, rw_ref, xp, h1, g1_ref, gh2, x_ref, dg1, drw)
        if i == images - 1:
            sma[0] = jnp.concatenate([dg1[...], drw[...], dg2[...], jnp.zeros((5, width), F32)], 0)
            small_copy(0).start()

    def small_step(step):
        if step < 3:
            small_copy(step - 1).wait()
            sma[step] = sma[step - 1] + smr[step - 1]
            small_copy(step).start()
        elif step == 3:
            small_copy(2).wait()
            smz[0] = sma[2] + smr[2]
            small_z(0).start()
        else:
            small_z(step - 4).wait()
            if step == 4:
                smz[2] = smz[0] + smz[1]
                small_z(1).start()
            else:
                small_out[...] = smz[2] + smz[3]

    def out_send():
        out_over.wait_recv()
        rows = pl.ds(t_own, t_own)
        out_part[rows, :] = out_part[rows, :] + out_near[...]
        out_far_copy.start()

    def out_finish(i):
        if i == 0:
            out_to_sib.wait_recv()
            out_far_copy.wait_recv()
        rows = pl.ds(i * tall, tall)
        total = middle[rows, :] + out[rows, :] + out_sib[rows, :].astype(F32) + out_far[rows, :].astype(F32)
        c_ref[:, i, :] = total.astype(BF)[0:patches, :]

    def fc_share_end():
        for copy in fc_share:
            copy.wait()

    single = {"fc": fc_finish, "fd": fc_widen, "fe": fc_to_sibling, "ff": fc_share_end, "osend": out_send}
    numbered = (("finish", finish), ("back", back_image), ("out", grad_out_half),
                ("fb", fc_fold_third), ("g", small_step), ("o", out_finish))

    def perform(names):
        for name in names:
            if name in single:
                single[name]()
            elif name[:2] == "fa":
                fc_fold_second(int(name[2]), int(name[3]))
            elif name[0] == "c":
                chunk_step(int(name[1]), int(name[3]))
            else:
                do = next(f for head, f in numbered if name[:-1] == head)
                do(int(name[-1]))

    first, start, stop = ORDER.index("pairs0"), ORDER.index("pairs1"), ORDER.index("last2")
    perform(ORDER[:first])

    @pl.loop(0, HEADS // 4)
    def _(n):
        for p in (2 * n, 2 * n + 1):
            attend_back(p, 0, width, tall, qkv, probs, context)

    perform(ORDER[first + 1 : start])
    marks = [ORDER.index(name) for k in range(3) for name in ("pairs%d" % (k + 1), "last%d" % k)]

    @pl.loop(0, HEADS // 4)
    def _(n):
        for p in (2 * n, 2 * n + 1):
            attend_back(p, 1, width, tall, qkv, probs, context)
        pair_chunk(2 * n)
        for k in range(3):
            at(n, k, lambda k=k: perform(ORDER[marks[2 * k] + 1 : marks[2 * k + 1]]))
        pair_chunk(2 * n + 1)
        for k in range(2):
            at(n, k, lambda k=k: perform(ORDER[marks[2 * k + 1] + 1 : marks[2 * k + 2]]))

    perform(ORDER[stop + 1 :])
    for level in range(2):
        for m in range(2):
            fc_spread(level, m).wait_send()
    for copy in fc_third:
        copy.wait_send()
    for mat in range(2):
        for kind in range(4):
            gather_copy(mat, kind).wait_send()
    for i in range(images):
        token_copy(i, 2).wait_send()
        gh2_over(i).wait_send()
        gh2_far_copy(i).wait_send()
    for hop in range(3):
        cot_copy(hop).wait_send()
    for copy in (gh2_to_sib, out_to_sib, out_over, out_far_copy):
        copy.wait_send()


VMEM = pl.BlockSpec(memory_space=pltpu.VMEM)
ANY = pl.BlockSpec(memory_space=pl.ANY)


def widen_kernel(
    block, gx, gw, gf1, gf2, small, block_out, gx_out, gq_out, go_out, f1_out, f2_out, g1_out, rw_out, g2_out,
    gq_wide, go_wide, f1_wide, f2_wide, store_sem, pass_sem,
):
    _, width, part = gf1.shape
    step = width // WIDEN
    c = lax.rem(lax.axis_index("rows"), 2)
    passed = [pltpu.make_async_copy(src, dst, pass_sem.at[k]) for k, (src, dst) in enumerate(((block, block_out), (gx, gx_out)))]

    def rows_of(i):
        return pl.ds(pl.multiple_of(i * step, 16), step)

    def stores(i):
        rows = rows_of(i)
        pairs = ((gq_wide, gq_out), (go_wide, go_out), (f1_wide, f1_out), (f2_wide, f2_out))
        return [
            pltpu.make_async_copy(src.at[rows, :], dst.at[rows, :], store_sem.at[i, k]) for k, (src, dst) in enumerate(pairs)
        ]

    for copy in passed:
        copy.start()
    g1_out[...], rw_out[...], g2_out[...] = small[0], small[1], small[2]

    @pl.loop(0, WIDEN)
    def _(i):
        rows = rows_of(i)
        for p in range(CHUNKS - 2):
            for b in range(3):
                start = b * width + p * 128
                gq_wide[rows, start : start + 128] = gw[2 + p, rows, b * 128 : (b + 1) * 128].astype(F32)
        for h in range(2):
            go_wide[rows, h * part : (h + 1) * part] = gw[h, rows, :].astype(F32)
        for k in range(2):
            core = c + k - 2 * c * k
            f1_wide[rows, pl.ds(pl.multiple_of(core * part, 128), part)] = gf1[k, rows, :].astype(F32)
        core = lax.div(i * step, part)
        inner = pl.ds(pl.multiple_of(i * step - core * part, 16), step)
        f2_wide[rows, :] = gf2[core + c - 2 * core * c, inner, :].astype(F32)
        for copy in stores(i):
            copy.start()

    @pl.loop(0, WIDEN)
    def _(i):
        for copy in stores(i):
            copy.wait()

    for copy in passed:
        copy.wait()


def widen(*held):
    width = held[3].shape[1]
    tokens = jax.ShapeDtypeStruct(held[0].shape, BF)
    wide = [(width, 3 * width), (width, width), (width, width), (width, width)]
    return pl.pallas_call(
        widen_kernel,
        out_shape=[tokens, tokens] + [jax.ShapeDtypeStruct(dims, F32) for dims in wide] + [jax.ShapeDtypeStruct((width,), F32)] * 3,
        in_specs=[VMEM] * 6,
        out_specs=[ANY] * 6 + [VMEM] * 3,
        scratch_shapes=[pltpu.VMEM(dims, F32) for dims in wide]
        + [pltpu.SemaphoreType.DMA((WIDEN, 4)), pltpu.SemaphoreType.DMA((2,))],
        compiler_params=pltpu.CompilerParams(vmem_limit_bytes=32 * 1024 * 1024),
        name="widen",
    )(*(pltpu.with_memory_space_constraint(a, pltpu.VMEM) for a in held))


def per_device(others, images, patch_rank, kept_count, ln1_gain, router_weight, w_qkv, w_out, ln2_gain, w_fc1, w_fc2, cotangent):
    count, patches, width = images.shape
    tall = -(-patches // 16) * 16
    t = count * tall
    part = w_fc1.shape[1] // 2
    half, eighth = width // 2, width // 8

    def bf(*dims):
        return pltpu.VMEM(dims, BF)

    def f32(*dims):
        return pltpu.VMEM(dims, F32)

    def sem(*dims):
        return pltpu.SemaphoreType.DMA(dims)

    scratch = [
        pltpu.VMEM(patch_rank.shape, jnp.int32), pltpu.SMEM(kept_count.shape, jnp.int32), f32(width), bf(width), f32(width),
        bf(width, 3 * width), bf(width, width), bf(width, 2 * part), bf(2 * part, width),
        bf(t, width), f32(t, 128), f32(t, 128), f32(t, 128), bf(t, width), bf(width, t), bf(t, 3 * width),
        f32(count, HEADS, tall, tall), bf(count, width, tall), bf(t, width), f32(t, width), f32(t, width),
        bf(4 * t, width), bf(4 * t, width), bf(width, 4 * t), f32(t, width), f32(t, width),
        bf(3 * t, width), bf(3 * t, width), bf(t, width), bf(t, width), bf(t, width), bf(t, width), bf(t, width), bf(t, width),
        bf(4 * t, 2 * part), bf(4 * t, 2 * part), bf(tall, width),
        bf(2, width // 2, part), bf(2, part // 2, width), bf(2, width // 4, part), bf(2, part // 4, width),
        bf(2, width // 4, part), bf(2, part // 4, width), bf(width // 4, part), bf(part // 4, width),
        bf(CHUNKS, half, 384), bf(CHUNKS, 2 * eighth, 384), bf(CHUNKS, eighth, 384),
        bf(CHUNKS, eighth // 2, 384), bf(CHUNKS, eighth // 2, 384),
        f32(1, width), f32(1, width), f32(1, width), f32(3, 8, width), f32(3, 8, width), f32(4, 8, width),
        sem(6), sem(2, 4), sem(2, 4), sem(count, 3), sem(count, 3), sem(3), sem(3), sem(8), sem(8),
        sem(2, 2), sem(2, 2), sem(2, 2), sem(2, 2), sem(2), sem(2),
        sem(2, 2), sem(2, 2), sem(2), sem(2), pltpu.SemaphoreType.REGULAR((2,)), pltpu.SemaphoreType.REGULAR((CHUNKS, 4)),
        sem(CHUNKS, 9), sem(CHUNKS, 9), sem(5),
        sem(3), sem(3), sem(2), sem(2),
    ]

    block, gx, gw, gf1, gf2, small = pl.pallas_call(
        mega_kernel,
        out_shape=[
            bf(patches, count, width), bf(patches, count, width), bf(CHUNKS, width, 384),
            bf(2, width, part), bf(2, part, width), f32(8, width),
        ],
        in_specs=[ANY] * 11,
        out_specs=[VMEM] * 6,
        scratch_shapes=scratch,
        compiler_params=pltpu.CompilerParams(
            collective_id=0, has_side_effects=True, vmem_limit_bytes=int(55.5 * 1024) * 1024
        ),
        name="block",
    )(images.transpose(1, 0, 2), patch_rank, kept_count, ln1_gain, router_weight, w_qkv, w_out, ln2_gain, w_fc1, w_fc2,
      cotangent.transpose(1, 0, 2))
    block, gx, gq, go, f1, f2, g1, rw, g2 = widen(block, gx, gw, gf1, gf2, small)
    if others:
        gq, go, f1, f2, g1, rw, g2 = lax.psum((gq, go, f1, f2, g1, rw, g2), "rows", axis_index_groups=others)
    return block.transpose(1, 0, 2), gx.transpose(1, 0, 2), g1, rw, gq, go, g2, f1, f2


def solution(mesh):
    rows = mesh.shape["rows"]
    others = [[8 * g + i for g in range(rows // 8)] for i in range(8)] if rows > 8 else None
    return jax.shard_map(
        functools.partial(per_device, others),
        mesh=mesh,
        in_specs=(
            P(("rows", "mlp"), None, None), P(("rows", "mlp"), None), P(("rows", "mlp")), P(), P(), P(), P(), P(),
            P(None, "mlp"), P("mlp", None), P(("rows", "mlp"), None, None),
        ),
        out_specs=(
            P(("rows", "mlp"), None, None), P(("rows", "mlp"), None, None), P(), P(), P(), P(), P(),
            P(None, "mlp"), P("mlp", None),
        ),
        check_vma=False,
    )
```

```python
import functools
import jax
import jax.numpy as jnp
from jax import lax
from jax.experimental import pallas as pl
from jax.experimental.pallas import tpu as pltpu
from jax.sharding import PartitionSpec as P

HEADS = 12
EPS = 1e-6
FILL = -1e30
BF = jnp.bfloat16
F32 = jnp.float32


def dot_nn(a, b):
    return lax.dot_general(a, b, (((1,), (0,)), ((), ())), preferred_element_type=F32)


def dot_nt(a, b):
    return lax.dot_general(a, b, (((1,), (1,)), ((), ())), preferred_element_type=F32)


def dot_tn(a, b):
    return lax.dot_general(a, b, (((0,), (0,)), ((), ())), preferred_element_type=F32)


def unit_rows(v):
    center = v - jnp.mean(v, -1, keepdims=True)
    scale = lax.rsqrt(jnp.mean(center * center, -1, keepdims=True) + EPS)
    return center * scale, scale


def norm_pull(dy, gain, unit, scale):
    du = dy * gain
    return scale * (
        du
        - jnp.mean(du, -1, keepdims=True)
        - unit * jnp.mean(du * unit, -1, keepdims=True)
    )


def half_mask(rows, h):
    lane = lax.broadcasted_iota(jnp.int32, (rows, 128), 1)
    return (lane < 64) if h == 0 else (lane >= 64)


def forward_rows(i, x_ref, rank_ref, kept_ref, g1_ref, rw_ref, xp, keep, gate, h1, work):
    patches = x_ref.shape[0]
    tall = xp.shape[0] // x_ref.shape[1]
    rows = pl.ds(pl.multiple_of(i * tall, 16), tall)
    work[...] = jnp.zeros_like(work)
    work[0:patches, :] = x_ref[:, i, :]
    v = work[...]
    xp[rows, :] = v
    kept = (rank_ref[pl.ds(i, 1), :] < kept_ref[i]).astype(F32)
    keep_row = jnp.concatenate([kept, jnp.zeros((1, 256 - patches), F32)], 1)
    keep_col = jnp.broadcast_to(keep_row, (128, 256)).T
    keep[rows, :] = keep_col[0:tall, :]
    unit, _ = unit_rows(v.astype(F32))
    low = (unit * g1_ref[...][None]).astype(BF)
    h1[rows, :] = low
    logit = jnp.sum(low.astype(F32) * rw_ref[...][None].astype(F32), -1, keepdims=True)
    gate[rows, :] = jnp.broadcast_to(jax.nn.sigmoid(logit), (tall, 128))


def forward_qkv(j, h1, wqkv, qkv):
    cols = pl.ds(pl.multiple_of(j * 256, 256), 256)
    qkv[:, cols] = dot_nn(h1[...], wqkv[:, cols]).astype(BF)


def attend(p, i, width, tall, qkv, keep, probs, context, contextt):
    rows = pl.ds(pl.multiple_of(i * tall, 16), tall)
    qc = pl.ds(pl.multiple_of(p * 128, 128), 128)
    kc = pl.ds(pl.multiple_of(width + p * 128, 128), 128)
    vc = pl.ds(pl.multiple_of(2 * width + p * 128, 128), 128)
    q, k, v = qkv[rows, qc], qkv[rows, kc], qkv[rows, vc]
    vt = v.T
    kept = keep[rows, 0:1] > 0.5
    outs = []
    for h in range(2):
        kh = jnp.where(half_mask(tall, h), k, jnp.zeros_like(k))
        s = jnp.where(kept, dot_nt(kh, q) * 0.125, FILL)
        e = jnp.exp(s - jnp.max(s, 0, keepdims=True))
        pr = e * (1.0 / jnp.sum(e, 0, keepdims=True))
        probs[i, p * 2 + h] = pr
        outs.append(dot_nn(vt[h * 64 : h * 64 + 64, :], pr.astype(BF)))
    ct = jnp.concatenate(outs, 0)
    contextt[i, pl.ds(pl.multiple_of(p * 128, 128), 128), :] = ct.astype(BF)
    context[rows, qc] = ct.T.astype(BF)


def forward_out(i, tall, context, wout, xp, keep, gate, g2_ref, attended, middle, h2):
    rows = pl.ds(pl.multiple_of(i * tall, 16), tall)
    att = dot_nn(context[rows, :], wout[...])
    attended[rows, :] = att
    mid = xp[rows, :].astype(F32) + keep[rows, 0:1] * gate[rows, 0:1] * att
    middle[rows, :] = mid
    unit, _ = unit_rows(mid)
    h2[rows, :] = (unit * g2_ref[...][None]).astype(BF)


def gelu_pair(pre):
    cdf = 0.5 * (1.0 + lax.erf(pre * 0.7071067811865476))
    pdf = jnp.exp(pre * pre * -0.5) * 0.3989422804014327
    return pre * cdf, cdf + pre * pdf


def mlp_rows(h, c, w1, w2):
    pre = dot_nn(h, w1)
    hidden, slope = gelu_pair(pre)
    grad = dot_nt(c, w2) * slope
    return hidden.astype(BF), grad.astype(BF)


def back_rows(i, tall, c_ref, gh2, middle, keep, gate, attended, g2_ref, gmid, gatt, glogit, dg2):
    rows = pl.ds(pl.multiple_of(i * tall, 16), tall)
    dy = gh2[rows, :]
    unit, scale = unit_rows(middle[rows, :])
    gm = c_ref[rows, :].astype(F32) + norm_pull(dy, g2_ref[...][None], unit, scale)
    gmid[rows, :] = gm
    dg2[...] += jnp.sum(dy * unit, 0, keepdims=True)
    k, g = keep[rows, 0:1], gate[rows, 0:1]
    kept = gm * k
    gatt[rows, :] = (kept * g).astype(BF)
    gl = jnp.sum(kept * attended[rows, :], -1, keepdims=True) * g * (1.0 - g)
    glogit[rows, :] = jnp.broadcast_to(gl, (tall, 128))


def attend_back(p, i, width, tall, qkv, probs, gctx):
    rows = pl.ds(pl.multiple_of(i * tall, 16), tall)
    qc = pl.ds(pl.multiple_of(p * 128, 128), 128)
    kc = pl.ds(pl.multiple_of(width + p * 128, 128), 128)
    vc = pl.ds(pl.multiple_of(2 * width + p * 128, 128), 128)
    q, k, v = qkv[rows, qc], qkv[rows, kc], qkv[rows, vc]
    gc = gctx[rows, qc]
    kt = k.T
    gv, gk, gq = 0.0, 0.0, []
    for h in range(2):
        mask = half_mask(tall, h)
        zero = jnp.zeros_like(v)
        pr = probs[i, p * 2 + h]
        gp = dot_nt(jnp.where(mask, v, zero), gc)
        gs = (pr * (gp - jnp.sum(pr * gp, 0, keepdims=True))).astype(BF)
        gv = gv + dot_nn(pr.astype(BF), jnp.where(mask, gc, zero))
        gk = gk + dot_nn(gs, jnp.where(mask, q, zero))
        gq.append(dot_nn(kt[h * 64 : h * 64 + 64, :], gs))
    qkv[rows, qc] = (jnp.concatenate(gq, 0).T * 0.125).astype(BF)
    qkv[rows, kc] = (gk * 0.125).astype(BF)
    qkv[rows, vc] = gv.astype(BF)


def pair_columns(wqkv, p, width):
    return jnp.concatenate(
        [wqkv[:, pl.ds(pl.multiple_of(b * width + p * 128, 128), 128)] for b in range(3)], 1
    )


def back_input(i, tall, dy, glogit, rw_ref, xp, h1, g1_ref, gmid, gx_ref, dg1, drw):
    rows = pl.ds(pl.multiple_of(i * tall, 16), tall)
    patches = gx_ref.shape[0]
    gl = glogit[rows, 0:1]
    dy = dy + gl * rw_ref[...][None].astype(F32)
    unit, scale = unit_rows(xp[rows, :].astype(F32))
    dg1[...] += jnp.sum(dy * unit, 0, keepdims=True)
    drw[...] += jnp.sum(h1[rows, :].astype(F32) * gl, 0, keepdims=True)
    out = gmid[rows, :] + norm_pull(dy, g1_ref[...][None], unit, scale)
    gx_ref[:, i, :] = out.astype(BF)[0:patches, :]

MESH = pl.DeviceIdType.MESH
CHUNKS = HEADS // 2 + 2
WIDEN = 8
PATHS = ("zxy", "yzx", "xyz", "yxz", "xyz", "yzx", "xzy", "yxz")
ORDER = (
    "back0", "osend", "pairs0", "back1", "pairs1", "fa11", "fa10", "fa01", "last0", "fa00", "out1", "pairs2", "out0",
    "last1", "c3.1", "fb1", "c2.1", "pairs3", "c1.1", "last2", "c4.1", "finish0", "c5.1", "c0.1", "c2.2", "c3.2",
    "c6.1", "finish1", "c1.2", "fb0", "c4.2", "c3.3", "c5.2", "c7.1", "c0.2", "g1", "c2.3", "c6.2", "c1.3", "fc",
    "c4.3", "c3.4", "c0.3", "o0", "g2", "c2.4", "c7.2", "c6.3", "c5.3", "c1.4", "c4.4", "c3.5", "fd", "c0.4", "c6.4",
    "c7.3", "c2.5", "c1.5", "c5.4", "c4.5", "c3.6", "g3", "c7.4", "c0.5", "o1", "c2.6", "c4.6", "g4", "c6.5", "c5.5",
    "c1.6", "c0.6", "c7.5", "fe", "c3.7", "c2.7", "c5.6", "c6.6", "c1.7", "c0.7", "c7.6", "c4.7", "c5.7", "c3.8",
    "c2.8", "c6.7", "c7.7", "c1.8", "c0.8", "c3.9", "c4.8", "g5", "c5.8", "c1.9", "c6.8", "c7.8", "ff", "c2.9",
    "c6.9", "c5.9", "c4.9", "c0.9", "c7.9",
)


def mega_kernel(
    x_hbm, rank_hbm, kept_hbm, g1_hbm, rw_hbm, wqkv_hbm, wout_hbm, g2_hbm, fc1, fc2, c_hbm,
    c_ref, x_ref, gw, g1w, g2w, small_out,
    rank_ref, kept_ref, g1_ref, rw_ref, g2_ref, wqkv, wout, w1, w2, xp, keep, gate, glogit, h1, h1t, qkv, probs, contextt, context, attended, middle,
    tok, cot, turned, out, gh2, out_part, gh2_part, out_sib, gh2_sib, out_near, gh2_near, out_far, gh2_far, hid, gpre, work,
    r1a, r1b, r2a, r2b, fz1, fz2, rz1, rz2,
    q0, q1, q2, q3, far, dg1, dg2, drw, sma, smr, smz,
    lsem, gsend, grecv, hsend, hrecv, csend, crecv, esend, erecv, s1s, s1r, s2s, s2r, s3s, s3r, fs, fr, ssib, rsib, free, chunk_free,
    qs, qr, small_sem, sms, smrs, smzs, smzr,
):
    patches, images, width = x_ref.shape
    t_own = xp.shape[0]
    tall = t_own // images
    half = width // 2
    part = w1.shape[1] // 2
    parts = (q0, q1, q2, q3)
    quarter = (width // 4, part // 4)
    r = lax.axis_index("rows")
    z = lax.axis_index("mlp")
    c, x, y = lax.rem(r, 2), lax.rem(lax.div(r, 2), 2), lax.rem(lax.div(r, 4), 2)
    r_sib, r_x, r_y = r + 1 - 2 * c, r + 2 - 4 * x, r + 4 - 8 * y
    r_diag = r_x + r_y - r
    z_pair, z_far = z + 1 - 2 * lax.rem(z, 2), z + 2 - 4 * lax.div(z, 2)
    q = 2 * y + x

    def ds(start, size):
        return pl.ds(pl.multiple_of(start, 16), size)

    def lanes(start, size):
        return pl.ds(pl.multiple_of(start, 128), size)

    def remote(src, dst, send, recv, row, column):
        return pltpu.make_async_remote_copy(
            src_ref=src, dst_ref=dst, send_sem=send, recv_sem=recv,
            device_id={"rows": row, "mlp": column}, device_id_type=MESH,
        )

    def release(semaphore, row):
        pl.semaphore_signal(semaphore, inc=1, device_id={"rows": row, "mlp": z}, device_id_type=MESH)

    def gather_copy(mat, kind):
        size = quarter[mat]
        sems = gsend.at[mat, kind], grecv.at[mat, kind]
        if mat == 0:
            place = w1.at[ds(q * size, size), pl.ds(part, part)]
            own = fc1.at[ds(q * size, size), lanes(c * part, part)]
        else:
            place = w2.at[ds(part + q * size, size), :]
            own = fc2.at[ds(c * part + q * size, size), :]
        if kind == 0:
            return remote(own, place, *sems, r, z_far)
        return remote(place, place, *sems, (r_x, r_y, r_diag)[kind - 1], z)

    def gather_forward(mat):
        gather_copy(mat, 0).wait_recv()
        for kind in (1, 2, 3):
            gather_copy(mat, kind).start()

    def own_shard(mat):
        if mat == 0:
            return pltpu.make_async_copy(fc1.at[:, lanes(c * part, part)], w1.at[:, pl.ds(0, part)], lsem.at[0])
        return pltpu.make_async_copy(fc2.at[ds(c * part, part), :], w2.at[pl.ds(0, part), :], lsem.at[1])

    load_qkv = pltpu.make_async_copy(wqkv_hbm, wqkv, lsem.at[2])
    load_out = pltpu.make_async_copy(wout_hbm, wout, lsem.at[3])
    load_x = pltpu.make_async_copy(x_hbm, x_ref, lsem.at[4])
    load_small = [
        pltpu.make_async_copy(src, dst, small_sem.at[k])
        for k, (src, dst) in enumerate(((rank_hbm, rank_ref), (kept_hbm, kept_ref), (g1_hbm, g1_ref), (rw_hbm, rw_ref), (g2_hbm, g2_ref)))
    ]
    load_c = pltpu.make_async_copy(c_hbm, c_ref, lsem.at[5])

    def token_copy(i, hop):
        start = (0, 0, 2 * t_own)[hop] + i * tall
        src, dst = tok.at[ds(start, tall), :], tok.at[ds((1, 2, 3)[hop] * t_own + i * tall, tall), :]
        row, column = (r, z_pair) if hop == 1 else (r_sib, z)
        return remote(src, dst, hsend.at[i, hop], hrecv.at[i, hop], row, column)

    def cot_copy(hop):
        src, dst = cot.at[ds((0, 0, 2)[hop] * t_own, t_own), :], cot.at[ds((1, 2, 3)[hop] * t_own, t_own), :]
        row, column = (r, z_pair) if hop == 1 else (r_sib, z)
        return remote(src, dst, csend.at[hop], crecv.at[hop], row, column)

    gh2_to_sib = remote(gh2_part.at[ds(0, t_own), :], gh2_sib, esend.at[0], erecv.at[0], r_sib, z)
    out_to_sib = remote(out_part.at[ds(0, t_own), :], out_sib, esend.at[1], erecv.at[1], r_sib, z)
    out_over = remote(out_part.at[ds(2 * t_own, t_own), :], out_near, esend.at[2], erecv.at[2], r_sib, z)
    out_far_copy = remote(out_part.at[ds(t_own, t_own), :], out_far, esend.at[3], erecv.at[3], r, z_pair)

    def gh2_over(i):
        src = gh2_part.at[ds(2 * t_own + i * tall, tall), :]
        return remote(src, gh2_near.at[ds(i * tall, tall), :], esend.at[4 + i], erecv.at[4 + i], r_sib, z)

    def gh2_far_copy(i):
        src = gh2_part.at[ds(t_own + i * tall, tall), :]
        return remote(src, gh2_far.at[ds(i * tall, tall), :], esend.at[6 + i], erecv.at[6 + i], r, z_pair)

    fc_whole, fc_half, fc_quarter, fc_done, fc_far = (g1w, g2w), (r1a, r1b), (r2a, r2b), (fz1, fz2), (rz1, rz2)
    fc_rows = ((width // 2, width // 4), (part // 2, part // 4))

    def fc_ways(k, m):
        shard = lax.div(z, 2) if k == 0 else 1 - lax.div(z, 2)
        turn = lax.rem(shard + m, 2)
        return r_x + (r_y - r_x) * turn, r_y + (r_x - r_y) * turn, x + (y - x) * turn, y + (x - y) * turn

    def fc_first(k, m):
        n1, _, a1, _ = fc_ways(k, m)
        rows, _ = fc_rows[m]
        src = fc_whole[m].at[k, ds((1 - a1) * rows, rows), :]
        return remote(src, fc_half[m].at[k], s1s.at[k, m], s1r.at[k, m], n1, z)

    def fc_second(k, m):
        _, n2, a1, a2 = fc_ways(k, m)
        rows, less = fc_rows[m]
        src = fc_whole[m].at[k, ds(a1 * rows + (1 - a2) * less, less), :]
        return remote(src, fc_quarter[m].at[k], s2s.at[k, m], s2r.at[k, m], n2, z)

    fc_third = [remote(fc_done[m].at[1], fc_far[m], s3s.at[m], s3r.at[m], r, z_far) for m in range(2)]

    def fc_spread(level, m):
        n1, n2, a1, a2 = fc_ways(0, m)
        rows, less = fc_rows[m]
        place = ds(a1 * rows + a2 * less, less) if level == 0 else ds(a1 * rows, rows)
        held = fc_whole[m].at[0, place, :]
        return remote(held, held, fs.at[level, m], fr.at[level, m], n2 if level == 0 else n1, z)

    fc_share = (
        remote(g1w.at[0], g1w.at[1], ssib.at[0], rsib.at[0], r_sib, z),
        remote(g2w.at[0], g2w.at[1], ssib.at[1], rsib.at[1], r_sib, z),
    )

    def fc_fold_second(k, m):
        fc_first(k, m).wait_recv()
        _, _, a1, a2 = fc_ways(k, m)
        rows, less = fc_rows[m]
        place, whole = ds(a1 * rows + (1 - a2) * less, less), fc_whole[m]
        whole[k, place, :] = whole[k, place, :] + fc_half[m][k, ds((1 - a2) * less, less), :]
        fc_second(k, m).start()

    def fc_fold_third(k):
        for m in range(2):
            fc_second(k, m).wait_recv()
            _, _, a1, a2 = fc_ways(k, m)
            rows, less = fc_rows[m]
            total = fc_whole[m][k, ds(a1 * rows + a2 * less, less), :].astype(F32)
            total = total + fc_half[m][k, ds(a2 * less, less), :].astype(F32) + fc_quarter[m][k].astype(F32)
            fc_done[m][k] = total.astype(BF)
        if k == 1:
            for copy in fc_third:
                copy.start()
        for m in range(2):
            fc_first(k, m).wait_send()
            fc_second(k, m).wait_send()
        if k == 1:
            release(free.at[0], r_sib)
        else:
            release(free.at[1], r_x)
            release(free.at[1], r_y)

    def fc_finish():
        for copy in fc_third:
            copy.wait_recv()
        pl.semaphore_wait(free.at[1], 2)
        for m in range(2):
            _, _, a1, a2 = fc_ways(0, m)
            rows, less = fc_rows[m]
            fc_whole[m][0, ds(a1 * rows + a2 * less, less), :] = fc_done[m][0] + fc_far[m][...]
            fc_spread(0, m).start()

    def fc_widen():
        for m in range(2):
            fc_spread(0, m).wait_recv()
        for m in range(2):
            fc_spread(1, m).start()

    def fc_to_sibling():
        for m in range(2):
            fc_spread(1, m).wait_recv()
        pl.semaphore_wait(free.at[0], 1)
        for copy in fc_share:
            copy.start()

    sizes = tuple(width >> level for level in range(1, 5))

    def hops(j):
        ways = {"x": (r_x, z, x), "y": (r_y, z, y), "z": (r, z_pair, lax.rem(z, 2))}
        return [(r_sib, z, c)] + [ways[axis] for axis in PATHS[j]]

    def base(path, level):
        start = 0
        for (_, _, bit), size in zip(path[:level], sizes):
            start = start + bit * size
        return start

    def core_copy(j):
        src = gw.at[j, ds((1 - c) * half, half), :]
        return remote(src, parts[0].at[j], qs.at[j, 0], qr.at[j, 0], r_sib, z)

    def chunk_copy(j, step):
        path = hops(j)
        if step == 0:
            return core_copy(j)
        if step < 4:
            row, column, bit = path[step]
            start = base(path, step) + (1 - bit) * sizes[step]
            return remote(gw.at[j, ds(start, sizes[step]), :], parts[step].at[j], qs.at[j, step], qr.at[j, step], row, column)
        if step == 4:
            own = gw.at[j, ds(base(path, 4), sizes[3]), :]
            return remote(own, far.at[j], qs.at[j, 4], qr.at[j, 4], r, z_far)
        level = 8 - step
        row, column, _ = path[level]
        held = gw.at[j, ds(base(path, level + 1), sizes[level]), :]
        return remote(held, held, qs.at[j, step], qr.at[j, step], row, column)

    def chunk_step(j, step):
        path, last = hops(j), chunk_copy(j, step - 1)
        last.wait_recv()
        if step <= 4:
            start = base(path, min(step, 4))
            if step < 4:
                start = base(path, step) + (1 - path[step][2]) * sizes[step]
            size = sizes[min(step, 3)]
            total = gw[j, ds(start, size), :].astype(F32)
            for level in range(step):
                total = total + parts[level][j, ds(start - base(path, level + 1), size), :].astype(F32)
            gw[j, ds(start, size), :] = total.astype(BF)
        if step == 5:
            last.wait_send()
            own = ds(base(path, 4), sizes[3])
            gw[j, own, :] = gw[j, own, :] + far[j]
        if 5 <= step <= 8:
            pl.semaphore_wait(chunk_free.at[j, 8 - step], 1)
        if step <= 8:
            chunk_copy(j, step).start()
        if step != 5:
            last.wait_send()
        if step <= 4:
            row, column, _ = path[step - 1]
            pl.semaphore_signal(
                chunk_free.at[j, step - 1], inc=1, device_id={"rows": row, "mlp": column}, device_id_type=MESH
            )

    def small_copy(level):
        row = (r_sib, r_x, r_y)[level]
        return remote(sma.at[level], smr.at[level], sms.at[level], smrs.at[level], row, z)

    def small_z(step):
        src, dst = smz.at[2 * step], smz.at[2 * step + 1]
        return remote(src, dst, smzs.at[step], smzr.at[step], r, (z_pair, z_far)[step])

    barrier = pltpu.get_barrier_semaphore()
    partners = ((r_sib, z), (r_x, z), (r_y, z), (r_diag, z), (r, z_pair), (r, z_far))
    for row, column in partners:
        pl.semaphore_signal(barrier, inc=1, device_id={"rows": row, "mlp": column}, device_id_type=MESH)
    load_c.start()
    load_x.start()
    for copy in load_small:
        copy.start()
    load_qkv.start()
    load_out.start()
    own_shard(0).start()
    own_shard(1).start()
    pl.semaphore_wait(barrier, len(partners))
    gather_copy(0, 0).start()
    gather_copy(1, 0).start()
    load_c.wait()
    for i in range(images):
        work[...] = jnp.zeros_like(work)
        work[0:patches, :] = c_ref[:, i, :]
        cot[i * tall : (i + 1) * tall, :] = work[...]
    cot_copy(0).start()
    cot_copy(1).start()
    load_x.wait()
    for copy in load_small:
        copy.wait()
    for i in range(images):
        forward_rows(i, x_ref, rank_ref, kept_ref, g1_ref, rw_ref, xp, keep, gate, h1, work)

    load_qkv.wait()

    @pl.loop(0, 3 * width // 256)
    def _(j):
        forward_qkv(j, h1, wqkv, qkv)

    @pl.loop(0, HEADS // 2)
    def _(p):
        for i in range(images):
            attend(p, i, width, tall, qkv, keep, probs, context, contextt)

        @pl.when(p == 0)
        def _():
            gather_forward(0)

        @pl.when(p == 3)
        def _():
            gather_forward(1)

    load_out.wait()

    @pl.loop(0, images)
    def _(i):
        forward_out(i, tall, context, wout, xp, keep, gate, g2_ref, attended, middle, tok)
        token_copy(i, 0).start()
        token_copy(i, 1).start()

    own_shard(0).wait()
    own_shard(1).wait()

    def at(block, number, do):
        @pl.when(block == number)
        def _():
            do()

    def before_sibling():
        for i in range(images):
            token_copy(i, 0).wait_recv()
        cot_copy(0).wait_recv()

    h1t[...] = h1[...].T

    @pl.loop(0, 2 * images)
    def _(block):
        at(block, images, before_sibling)
        rows = ds(block * tall, tall)
        hid[rows, 0:part], gpre[rows, 0:part] = mlp_rows(tok[rows, :], cot[rows, :], w1[:, 0:part], w2[0:part, :])

    cot_copy(1).wait_recv()
    cot_copy(2).start()
    for mat in range(2):
        for kind in (1, 2, 3):
            gather_copy(mat, kind).wait_recv()
    for ref in (dg1, dg2, drw):
        ref[...] = jnp.zeros_like(ref)

    def before_near():
        cot_copy(2).wait_recv()
        gh2_to_sib.start()

    def forward_token(i):
        token_copy(i, 1).wait_recv()
        token_copy(i, 2).start()

    def send_far(i):
        gh2_over(i).wait_recv()
        rows = ds(t_own + i * tall, tall)
        gh2_part[rows, :] = gh2_part[rows, :] + gh2_near[ds(i * tall, tall), :]
        gh2_far_copy(i).start()

    def before_last():
        send_far(0)
        token_copy(1, 2).wait_recv()

    @pl.loop(0, 8)
    def _(block):
        at(block, 3, lambda: forward_token(0))
        at(block, 4, before_near)
        at(block, 5, lambda: token_copy(0, 2).wait_recv())
        at(block, 6, lambda: forward_token(1))
        at(block, 7, before_last)
        inner = lax.rem(block, 5)
        swap = lax.div(block, 5) * (1 - 2 * inner + 3 * lax.div(inner * (inner - 1), 2))
        spot = block + swap
        rows = ds(spot * tall, tall)

        @pl.when(block < 2 * images)
        def _():
            hid[rows, part:], gpre[rows, part:] = mlp_rows(tok[rows, :], cot[rows, :], w1[:, part:], w2[part:, :])

        @pl.when(block >= 2 * images)
        def _():
            hid[rows, :], gpre[rows, :] = mlp_rows(tok[rows, :], cot[rows, :], w1[...], w2[...])

        share_out = dot_nn(hid[rows, :], w2[...])
        share_gh2 = dot_nt(gpre[rows, :], w1[...])

        @pl.when(block < images)
        def _():
            out[rows, :] = share_out
            gh2[rows, :] = share_gh2

        @pl.when(block >= images)
        def _():
            there = ds(lax.max(spot - images, 0) * tall, tall)
            out_part[there, :] = share_out.astype(BF)
            gh2_part[there, :] = share_gh2.astype(BF)

        at(block, 5, lambda: gh2_over(0).start())
        at(block, 7, lambda: gh2_over(1).start())

    out_to_sib.start()
    out_over.start()
    turned[...] = tok[...].T
    for m in range(3):
        rows = slice(m * width // 3, (m + 1) * width // 3)
        total = dot_nn(turned[rows, :], gpre[...]).astype(BF)
        g1w[0, rows, :] = total[:, 0:part]
        g1w[1, rows, :] = total[:, part:]
    for k in range(2):
        fc_first(k, 0).start()
    send_far(1)
    turned[...] = hid[...].T
    for m in range(2):
        g2w[m] = dot_nn(turned[m * part : (m + 1) * part, :], cot[...]).astype(BF)
    for k in range(2):
        fc_first(k, 1).start()

    def back_image(i):
        if i == 0:
            gh2_to_sib.wait_recv()
            for n in range(images):
                token_copy(n, 0).wait_send()
                token_copy(n, 1).wait_send()
        gh2_far_copy(i).wait_recv()
        rows = pl.ds(i * tall, tall)
        gh2[rows, :] += gh2_sib[rows, :].astype(F32) + gh2_far[rows, :].astype(F32)
        back_rows(i, tall, cot, gh2, middle, keep, gate, attended, g2_ref, gh2, tok, glogit, dg2)
        context[rows, :] = dot_nt(tok[rows, :], wout[...]).astype(BF)

    def fill(j, total):
        gw[j] = total.astype(BF)
        core_copy(j).start()

    def grad_out_half(n):
        total = 0.0
        for i in range(images):
            total = total + dot_nn(contextt[i], tok[i * tall : (i + 1) * tall, n * half : (n + 1) * half])
        fill(n, total)

    def pair_chunk(p):
        fill(p + 2, dot_nn(h1t[...], pair_columns(qkv, p, width)))

    def finish(i):
        rows = pl.ds(i * tall, tall)
        dy = dot_nt(qkv[rows, :], wqkv[...])
        back_input(i, tall, dy, glogit, rw_ref, xp, h1, g1_ref, gh2, x_ref, dg1, drw)
        if i == images - 1:
            sma[0] = jnp.concatenate([dg1[...], drw[...], dg2[...], jnp.zeros((5, width), F32)], 0)
            small_copy(0).start()

    def small_step(step):
        if step < 3:
            small_copy(step - 1).wait()
            sma[step] = sma[step - 1] + smr[step - 1]
            small_copy(step).start()
        elif step == 3:
            small_copy(2).wait()
            smz[0] = sma[2] + smr[2]
            small_z(0).start()
        else:
            small_z(step - 4).wait()
            if step == 4:
                smz[2] = smz[0] + smz[1]
                small_z(1).start()
            else:
                small_out[...] = smz[2] + smz[3]

    def out_send():
        out_over.wait_recv()
        rows = pl.ds(t_own, t_own)
        out_part[rows, :] = out_part[rows, :] + out_near[...]
        out_far_copy.start()

    def out_finish(i):
        if i == 0:
            out_to_sib.wait_recv()
            out_far_copy.wait_recv()
        rows = pl.ds(i * tall, tall)
        total = middle[rows, :] + out[rows, :] + out_sib[rows, :].astype(F32) + out_far[rows, :].astype(F32)
        c_ref[:, i, :] = total.astype(BF)[0:patches, :]

    def fc_share_end():
        for copy in fc_share:
            copy.wait()

    single = {"fc": fc_finish, "fd": fc_widen, "fe": fc_to_sibling, "ff": fc_share_end, "osend": out_send}
    numbered = (("finish", finish), ("back", back_image), ("out", grad_out_half),
                ("fb", fc_fold_third), ("g", small_step), ("o", out_finish))

    def perform(names):
        for name in names:
            if name in single:
                single[name]()
            elif name[:2] == "fa":
                fc_fold_second(int(name[2]), int(name[3]))
            elif name[0] == "c":
                chunk_step(int(name[1]), int(name[3]))
            else:
                do = next(f for head, f in numbered if name[:-1] == head)
                do(int(name[-1]))

    first, start, stop = ORDER.index("pairs0"), ORDER.index("pairs1"), ORDER.index("last2")
    perform(ORDER[:first])

    @pl.loop(0, HEADS // 4)
    def _(n):
        for p in (2 * n, 2 * n + 1):
            attend_back(p, 0, width, tall, qkv, probs, context)

    perform(ORDER[first + 1 : start])
    marks = [ORDER.index(name) for k in range(3) for name in ("pairs%d" % (k + 1), "last%d" % k)]

    @pl.loop(0, HEADS // 4)
    def _(n):
        for p in (2 * n, 2 * n + 1):
            attend_back(p, 1, width, tall, qkv, probs, context)
        pair_chunk(2 * n)
        for k in range(3):
            at(n, k, lambda k=k: perform(ORDER[marks[2 * k] + 1 : marks[2 * k + 1]]))
        pair_chunk(2 * n + 1)
        for k in range(2):
            at(n, k, lambda k=k: perform(ORDER[marks[2 * k + 1] + 1 : marks[2 * k + 2]]))

    perform(ORDER[stop + 1 :])
    for level in range(2):
        for m in range(2):
            fc_spread(level, m).wait_send()
    for copy in fc_third:
        copy.wait_send()
    for mat in range(2):
        for kind in range(4):
            gather_copy(mat, kind).wait_send()
    for i in range(images):
        token_copy(i, 2).wait_send()
        gh2_over(i).wait_send()
        gh2_far_copy(i).wait_send()
    for hop in range(3):
        cot_copy(hop).wait_send()
    for copy in (gh2_to_sib, out_to_sib, out_over, out_far_copy):
        copy.wait_send()


VMEM = pl.BlockSpec(memory_space=pltpu.VMEM)
ANY = pl.BlockSpec(memory_space=pl.ANY)


def widen_kernel(
    block, gx, gw, gf1, gf2, small, block_out, gx_out, gq_out, go_out, f1_out, f2_out, g1_out, rw_out, g2_out,
    gq_wide, go_wide, f1_wide, f2_wide, store_sem, pass_sem,
):
    _, width, part = gf1.shape
    step = width // WIDEN
    c = lax.rem(lax.axis_index("rows"), 2)
    passed = [pltpu.make_async_copy(src, dst, pass_sem.at[k]) for k, (src, dst) in enumerate(((block, block_out), (gx, gx_out)))]

    def rows_of(i):
        return pl.ds(pl.multiple_of(i * step, 16), step)

    def stores(i):
        rows = rows_of(i)
        pairs = ((gq_wide, gq_out), (go_wide, go_out), (f1_wide, f1_out), (f2_wide, f2_out))
        return [
            pltpu.make_async_copy(src.at[rows, :], dst.at[rows, :], store_sem.at[i, k]) for k, (src, dst) in enumerate(pairs)
        ]

    for copy in passed:
        copy.start()
    g1_out[...], rw_out[...], g2_out[...] = small[0], small[1], small[2]

    @pl.loop(0, WIDEN)
    def _(i):
        rows = rows_of(i)
        for p in range(CHUNKS - 2):
            for b in range(3):
                start = b * width + p * 128
                gq_wide[rows, start : start + 128] = gw[2 + p, rows, b * 128 : (b + 1) * 128].astype(F32)
        for h in range(2):
            go_wide[rows, h * part : (h + 1) * part] = gw[h, rows, :].astype(F32)
        for k in range(2):
            core = c + k - 2 * c * k
            f1_wide[rows, pl.ds(pl.multiple_of(core * part, 128), part)] = gf1[k, rows, :].astype(F32)
        core = lax.div(i * step, part)
        inner = pl.ds(pl.multiple_of(i * step - core * part, 16), step)
        f2_wide[rows, :] = gf2[core + c - 2 * core * c, inner, :].astype(F32)
        for copy in stores(i):
            copy.start()

    @pl.loop(0, WIDEN)
    def _(i):
        for copy in stores(i):
            copy.wait()

    for copy in passed:
        copy.wait()


def widen(*held):
    width = held[3].shape[1]
    tokens = jax.ShapeDtypeStruct(held[0].shape, BF)
    wide = [(width, 3 * width), (width, width), (width, width), (width, width)]
    return pl.pallas_call(
        widen_kernel,
        out_shape=[tokens, tokens] + [jax.ShapeDtypeStruct(dims, F32) for dims in wide] + [jax.ShapeDtypeStruct((width,), F32)] * 3,
        in_specs=[VMEM] * 6,
        out_specs=[ANY] * 6 + [VMEM] * 3,
        scratch_shapes=[pltpu.VMEM(dims, F32) for dims in wide]
        + [pltpu.SemaphoreType.DMA((WIDEN, 4)), pltpu.SemaphoreType.DMA((2,))],
        compiler_params=pltpu.CompilerParams(vmem_limit_bytes=32 * 1024 * 1024),
        name="widen",
    )(*(pltpu.with_memory_space_constraint(a, pltpu.VMEM) for a in held))


def per_device(others, images, patch_rank, kept_count, ln1_gain, router_weight, w_qkv, w_out, ln2_gain, w_fc1, w_fc2, cotangent):
    count, patches, width = images.shape
    tall = -(-patches // 16) * 16
    t = count * tall
    part = w_fc1.shape[1] // 2
    half, eighth = width // 2, width // 8

    def bf(*dims):
        return pltpu.VMEM(dims, BF)

    def f32(*dims):
        return pltpu.VMEM(dims, F32)

    def sem(*dims):
        return pltpu.SemaphoreType.DMA(dims)

    scratch = [
        pltpu.VMEM(patch_rank.shape, jnp.int32), pltpu.SMEM(kept_count.shape, jnp.int32), f32(width), bf(width), f32(width),
        bf(width, 3 * width), bf(width, width), bf(width, 2 * part), bf(2 * part, width),
        bf(t, width), f32(t, 128), f32(t, 128), f32(t, 128), bf(t, width), bf(width, t), bf(t, 3 * width),
        f32(count, HEADS, tall, tall), bf(count, width, tall), bf(t, width), f32(t, width), f32(t, width),
        bf(4 * t, width), bf(4 * t, width), bf(width, 4 * t), f32(t, width), f32(t, width),
        bf(3 * t, width), bf(3 * t, width), bf(t, width), bf(t, width), bf(t, width), bf(t, width), bf(t, width), bf(t, width),
        bf(4 * t, 2 * part), bf(4 * t, 2 * part), bf(tall, width),
        bf(2, width // 2, part), bf(2, part // 2, width), bf(2, width // 4, part), bf(2, part // 4, width),
        bf(2, width // 4, part), bf(2, part // 4, width), bf(width // 4, part), bf(part // 4, width),
        bf(CHUNKS, half, 384), bf(CHUNKS, 2 * eighth, 384), bf(CHUNKS, eighth, 384),
        bf(CHUNKS, eighth // 2, 384), bf(CHUNKS, eighth // 2, 384),
        f32(1, width), f32(1, width), f32(1, width), f32(3, 8, width), f32(3, 8, width), f32(4, 8, width),
        sem(6), sem(2, 4), sem(2, 4), sem(count, 3), sem(count, 3), sem(3), sem(3), sem(8), sem(8),
        sem(2, 2), sem(2, 2), sem(2, 2), sem(2, 2), sem(2), sem(2),
        sem(2, 2), sem(2, 2), sem(2), sem(2), pltpu.SemaphoreType.REGULAR((2,)), pltpu.SemaphoreType.REGULAR((CHUNKS, 4)),
        sem(CHUNKS, 9), sem(CHUNKS, 9), sem(5),
        sem(3), sem(3), sem(2), sem(2),
    ]

    block, gx, gw, gf1, gf2, small = pl.pallas_call(
        mega_kernel,
        out_shape=[
            bf(patches, count, width), bf(patches, count, width), bf(CHUNKS, width, 384),
            bf(2, width, part), bf(2, part, width), f32(8, width),
        ],
        in_specs=[ANY] * 11,
        out_specs=[VMEM] * 6,
        scratch_shapes=scratch,
        compiler_params=pltpu.CompilerParams(
            collective_id=0, has_side_effects=True, vmem_limit_bytes=int(55.5 * 1024) * 1024
        ),
        name="block",
    )(images.transpose(1, 0, 2), patch_rank, kept_count, ln1_gain, router_weight, w_qkv, w_out, ln2_gain, w_fc1, w_fc2,
      cotangent.transpose(1, 0, 2))
    block, gx, gq, go, f1, f2, g1, rw, g2 = widen(block, gx, gw, gf1, gf2, small)
    if others:
        gq, go, f1, f2, g1, rw, g2 = lax.psum((gq, go, f1, f2, g1, rw, g2), "rows", axis_index_groups=others)
    return block.transpose(1, 0, 2), gx.transpose(1, 0, 2), g1, rw, gq, go, g2, f1, f2


def solution(mesh):
    rows = mesh.shape["rows"]
    others = [[8 * g + i for g in range(rows // 8)] for i in range(8)] if rows > 8 else None
    return jax.shard_map(
        functools.partial(per_device, others),
        mesh=mesh,
        in_specs=(
            P(("rows", "mlp"), None, None), P(("rows", "mlp"), None), P(("rows", "mlp")), P(), P(), P(), P(), P(),
            P(None, "mlp"), P("mlp", None), P(("rows", "mlp"), None, None),
        ),
        out_specs=(
            P(("rows", "mlp"), None, None), P(("rows", "mlp"), None, None), P(), P(), P(), P(), P(),
            P(None, "mlp"), P("mlp", None),
        ),
        check_vma=False,
    )
```

```python
import functools
import jax
import jax.numpy as jnp
from jax import lax
from jax.experimental import pallas as pl
from jax.experimental.pallas import tpu as pltpu
from jax.sharding import PartitionSpec as P

HEADS = 12
EPS = 1e-6
FILL = -1e30
BF = jnp.bfloat16
F32 = jnp.float32


def dot_nn(a, b):
    return lax.dot_general(a, b, (((1,), (0,)), ((), ())), preferred_element_type=F32)


def dot_nt(a, b):
    return lax.dot_general(a, b, (((1,), (1,)), ((), ())), preferred_element_type=F32)


def dot_tn(a, b):
    return lax.dot_general(a, b, (((0,), (0,)), ((), ())), preferred_element_type=F32)


def unit_rows(v):
    center = v - jnp.mean(v, -1, keepdims=True)
    scale = lax.rsqrt(jnp.mean(center * center, -1, keepdims=True) + EPS)
    return center * scale, scale


def norm_pull(dy, gain, unit, scale):
    du = dy * gain
    return scale * (
        du
        - jnp.mean(du, -1, keepdims=True)
        - unit * jnp.mean(du * unit, -1, keepdims=True)
    )


def half_mask(rows, h):
    lane = lax.broadcasted_iota(jnp.int32, (rows, 128), 1)
    return (lane < 64) if h == 0 else (lane >= 64)


def forward_rows(i, x_ref, rank_ref, kept_ref, g1_ref, rw_ref, xp, keep, gate, h1, work):
    patches = x_ref.shape[0]
    tall = xp.shape[0] // x_ref.shape[1]
    rows = pl.ds(pl.multiple_of(i * tall, 16), tall)
    work[...] = jnp.zeros_like(work)
    work[0:patches, :] = x_ref[:, i, :]
    v = work[...]
    xp[rows, :] = v
    kept = (rank_ref[pl.ds(i, 1), :] < kept_ref[i]).astype(F32)
    keep_row = jnp.concatenate([kept, jnp.zeros((1, 256 - patches), F32)], 1)
    keep_col = jnp.broadcast_to(keep_row, (128, 256)).T
    keep[rows, :] = keep_col[0:tall, :]
    unit, _ = unit_rows(v.astype(F32))
    low = (unit * g1_ref[...][None]).astype(BF)
    h1[rows, :] = low
    logit = jnp.sum(low.astype(F32) * rw_ref[...][None].astype(F32), -1, keepdims=True)
    gate[rows, :] = jnp.broadcast_to(jax.nn.sigmoid(logit), (tall, 128))


def forward_qkv(j, h1, wqkv, qkv):
    cols = pl.ds(pl.multiple_of(j * 256, 256), 256)
    qkv[:, cols] = dot_nn(h1[...], wqkv[:, cols]).astype(BF)


def attend(p, i, width, tall, qkv, keep, probs, context, contextt):
    rows = pl.ds(pl.multiple_of(i * tall, 16), tall)
    qc = pl.ds(pl.multiple_of(p * 128, 128), 128)
    kc = pl.ds(pl.multiple_of(width + p * 128, 128), 128)
    vc = pl.ds(pl.multiple_of(2 * width + p * 128, 128), 128)
    q, k, v = qkv[rows, qc], qkv[rows, kc], qkv[rows, vc]
    vt = v.T
    kept = keep[rows, 0:1] > 0.5
    outs = []
    for h in range(2):
        kh = jnp.where(half_mask(tall, h), k, jnp.zeros_like(k))
        s = jnp.where(kept, dot_nt(kh, q) * 0.125, FILL)
        e = jnp.exp(s - jnp.max(s, 0, keepdims=True))
        pr = e * (1.0 / jnp.sum(e, 0, keepdims=True))
        probs[i, p * 2 + h] = pr
        outs.append(dot_nn(vt[h * 64 : h * 64 + 64, :], pr.astype(BF)))
    ct = jnp.concatenate(outs, 0)
    contextt[i, pl.ds(pl.multiple_of(p * 128, 128), 128), :] = ct.astype(BF)
    context[rows, qc] = ct.T.astype(BF)


def forward_out(i, tall, context, wout, xp, keep, gate, g2_ref, attended, middle, h2):
    rows = pl.ds(pl.multiple_of(i * tall, 16), tall)
    att = dot_nn(context[rows, :], wout[...])
    attended[rows, :] = att
    mid = xp[rows, :].astype(F32) + keep[rows, 0:1] * gate[rows, 0:1] * att
    middle[rows, :] = mid
    unit, _ = unit_rows(mid)
    h2[rows, :] = (unit * g2_ref[...][None]).astype(BF)


def gelu_pair(pre):
    cdf = 0.5 * (1.0 + lax.erf(pre * 0.7071067811865476))
    pdf = jnp.exp(pre * pre * -0.5) * 0.3989422804014327
    return pre * cdf, cdf + pre * pdf


def mlp_rows(h, c, w1, w2):
    pre = dot_nn(h, w1)
    hidden, slope = gelu_pair(pre)
    grad = dot_nt(c, w2) * slope
    return hidden.astype(BF), grad.astype(BF)


def back_rows(i, tall, c_ref, gh2, middle, keep, gate, attended, g2_ref, gmid, gatt, glogit, dg2):
    rows = pl.ds(pl.multiple_of(i * tall, 16), tall)
    dy = gh2[rows, :]
    unit, scale = unit_rows(middle[rows, :])
    gm = c_ref[rows, :].astype(F32) + norm_pull(dy, g2_ref[...][None], unit, scale)
    gmid[rows, :] = gm
    dg2[...] += jnp.sum(dy * unit, 0, keepdims=True)
    k, g = keep[rows, 0:1], gate[rows, 0:1]
    kept = gm * k
    gatt[rows, :] = (kept * g).astype(BF)
    gl = jnp.sum(kept * attended[rows, :], -1, keepdims=True) * g * (1.0 - g)
    glogit[rows, :] = jnp.broadcast_to(gl, (tall, 128))


def attend_back(p, i, width, tall, qkv, probs, gctx):
    rows = pl.ds(pl.multiple_of(i * tall, 16), tall)
    qc = pl.ds(pl.multiple_of(p * 128, 128), 128)
    kc = pl.ds(pl.multiple_of(width + p * 128, 128), 128)
    vc = pl.ds(pl.multiple_of(2 * width + p * 128, 128), 128)
    q, k, v = qkv[rows, qc], qkv[rows, kc], qkv[rows, vc]
    gc = gctx[rows, qc]
    kt = k.T
    gv, gk, gq = 0.0, 0.0, []
    for h in range(2):
        mask = half_mask(tall, h)
        zero = jnp.zeros_like(v)
        pr = probs[i, p * 2 + h]
        gp = dot_nt(jnp.where(mask, v, zero), gc)
        gs = (pr * (gp - jnp.sum(pr * gp, 0, keepdims=True))).astype(BF)
        gv = gv + dot_nn(pr.astype(BF), jnp.where(mask, gc, zero))
        gk = gk + dot_nn(gs, jnp.where(mask, q, zero))
        gq.append(dot_nn(kt[h * 64 : h * 64 + 64, :], gs))
    qkv[rows, qc] = (jnp.concatenate(gq, 0).T * 0.125).astype(BF)
    qkv[rows, kc] = (gk * 0.125).astype(BF)
    qkv[rows, vc] = gv.astype(BF)


def pair_columns(wqkv, p, width):
    return jnp.concatenate(
        [wqkv[:, pl.ds(pl.multiple_of(b * width + p * 128, 128), 128)] for b in range(3)], 1
    )


def back_input(i, tall, dy, glogit, rw_ref, xp, h1, g1_ref, gmid, gx_ref, dg1, drw):
    rows = pl.ds(pl.multiple_of(i * tall, 16), tall)
    patches = gx_ref.shape[0]
    gl = glogit[rows, 0:1]
    dy = dy + gl * rw_ref[...][None].astype(F32)
    unit, scale = unit_rows(xp[rows, :].astype(F32))
    dg1[...] += jnp.sum(dy * unit, 0, keepdims=True)
    drw[...] += jnp.sum(h1[rows, :].astype(F32) * gl, 0, keepdims=True)
    out = gmid[rows, :] + norm_pull(dy, g1_ref[...][None], unit, scale)
    gx_ref[:, i, :] = out.astype(BF)[0:patches, :]

MESH = pl.DeviceIdType.MESH
CHUNKS = HEADS // 2 + 2
WIDEN = 16
PATHS = ("zxy", "yzx", "xyz", "yxz", "xyz", "yzx", "xzy", "yxz")
ORDER = (
    "back0", "osend", "pairs0", "back1", "pairs1", "fa11", "fa10", "fa01", "last0", "fa00", "out1", "pairs2", "out0",
    "last1", "c3.1", "fb1", "c2.1", "pairs3", "c1.1", "last2", "c4.1", "finish0", "c5.1", "c0.1", "c2.2", "c3.2",
    "c6.1", "finish1", "c1.2", "fb0", "c4.2", "c3.3", "c5.2", "c7.1", "c0.2", "g1", "c2.3", "c6.2", "c1.3", "fc",
    "c4.3", "c3.4", "c0.3", "o0", "g2", "c2.4", "c7.2", "c6.3", "c5.3", "c1.4", "c4.4", "c3.5", "fd", "c0.4", "c6.4",
    "c7.3", "c2.5", "c1.5", "c5.4", "c4.5", "c3.6", "g3", "c7.4", "c0.5", "o1", "c2.6", "c4.6", "g4", "c6.5", "c5.5",
    "c1.6", "c0.6", "c7.5", "fe", "c3.7", "c2.7", "c5.6", "c6.6", "c1.7", "c0.7", "c7.6", "c4.7", "c5.7", "c3.8",
    "c2.8", "c6.7", "c7.7", "c1.8", "c0.8", "c3.9", "c4.8", "g5", "c5.8", "c1.9", "c6.8", "c7.8", "ff", "c2.9",
    "c6.9", "c5.9", "c4.9", "c0.9", "c7.9",
)


def mega_kernel(
    x_hbm, rank_hbm, kept_hbm, g1_hbm, rw_hbm, wqkv_hbm, wout_hbm, g2_hbm, fc1, fc2, c_hbm,
    c_ref, x_ref, gw, g1w, g2w, small_out,
    rank_ref, kept_ref, g1_ref, rw_ref, g2_ref, wqkv, wout, w1, w2, xp, keep, gate, glogit, h1, h1t, qkv, probs, contextt, context, attended, middle,
    tok, cot, turned, out, gh2, out_part, gh2_part, out_sib, gh2_sib, out_near, gh2_near, out_far, gh2_far, hid, gpre, work,
    r1a, r1b, r2a, r2b, fz1, fz2, rz1, rz2,
    q0, q1, q2, q3, far, dg1, dg2, drw, sma, smr, smz,
    lsem, gsend, grecv, hsend, hrecv, csend, crecv, esend, erecv, s1s, s1r, s2s, s2r, s3s, s3r, fs, fr, ssib, rsib, free, chunk_free,
    qs, qr, small_sem, sms, smrs, smzs, smzr,
):
    patches, images, width = x_ref.shape
    t_own = xp.shape[0]
    tall = t_own // images
    half = width // 2
    part = w1.shape[1] // 2
    parts = (q0, q1, q2, q3)
    quarter = (width // 4, part // 4)
    r = lax.axis_index("rows")
    z = lax.axis_index("mlp")
    c, x, y = lax.rem(r, 2), lax.rem(lax.div(r, 2), 2), lax.rem(lax.div(r, 4), 2)
    r_sib, r_x, r_y = r + 1 - 2 * c, r + 2 - 4 * x, r + 4 - 8 * y
    r_diag = r_x + r_y - r
    z_pair, z_far = z + 1 - 2 * lax.rem(z, 2), z + 2 - 4 * lax.div(z, 2)
    q = 2 * y + x

    def ds(start, size):
        return pl.ds(pl.multiple_of(start, 16), size)

    def lanes(start, size):
        return pl.ds(pl.multiple_of(start, 128), size)

    def remote(src, dst, send, recv, row, column):
        return pltpu.make_async_remote_copy(
            src_ref=src, dst_ref=dst, send_sem=send, recv_sem=recv,
            device_id={"rows": row, "mlp": column}, device_id_type=MESH,
        )

    def release(semaphore, row):
        pl.semaphore_signal(semaphore, inc=1, device_id={"rows": row, "mlp": z}, device_id_type=MESH)

    def gather_copy(mat, kind):
        size = quarter[mat]
        sems = gsend.at[mat, kind], grecv.at[mat, kind]
        if mat == 0:
            place = w1.at[ds(q * size, size), pl.ds(part, part)]
            own = fc1.at[ds(q * size, size), lanes(c * part, part)]
        else:
            place = w2.at[ds(part + q * size, size), :]
            own = fc2.at[ds(c * part + q * size, size), :]
        if kind == 0:
            return remote(own, place, *sems, r, z_far)
        return remote(place, place, *sems, (r_x, r_y, r_diag)[kind - 1], z)

    def gather_forward(mat):
        gather_copy(mat, 0).wait_recv()
        for kind in (1, 2, 3):
            gather_copy(mat, kind).start()

    def own_shard(mat):
        if mat == 0:
            return pltpu.make_async_copy(fc1.at[:, lanes(c * part, part)], w1.at[:, pl.ds(0, part)], lsem.at[0])
        return pltpu.make_async_copy(fc2.at[ds(c * part, part), :], w2.at[pl.ds(0, part), :], lsem.at[1])

    load_qkv = pltpu.make_async_copy(wqkv_hbm, wqkv, lsem.at[2])
    load_out = pltpu.make_async_copy(wout_hbm, wout, lsem.at[3])
    load_x = pltpu.make_async_copy(x_hbm, x_ref, lsem.at[4])
    load_small = [
        pltpu.make_async_copy(src, dst, small_sem.at[k])
        for k, (src, dst) in enumerate(((rank_hbm, rank_ref), (kept_hbm, kept_ref), (g1_hbm, g1_ref), (rw_hbm, rw_ref), (g2_hbm, g2_ref)))
    ]
    load_c = pltpu.make_async_copy(c_hbm, c_ref, lsem.at[5])

    def token_copy(i, hop):
        start = (0, 0, 2 * t_own)[hop] + i * tall
        src, dst = tok.at[ds(start, tall), :], tok.at[ds((1, 2, 3)[hop] * t_own + i * tall, tall), :]
        row, column = (r, z_pair) if hop == 1 else (r_sib, z)
        return remote(src, dst, hsend.at[i, hop], hrecv.at[i, hop], row, column)

    def cot_copy(hop):
        src, dst = cot.at[ds((0, 0, 2)[hop] * t_own, t_own), :], cot.at[ds((1, 2, 3)[hop] * t_own, t_own), :]
        row, column = (r, z_pair) if hop == 1 else (r_sib, z)
        return remote(src, dst, csend.at[hop], crecv.at[hop], row, column)

    gh2_to_sib = remote(gh2_part.at[ds(0, t_own), :], gh2_sib, esend.at[0], erecv.at[0], r_sib, z)
    out_to_sib = remote(out_part.at[ds(0, t_own), :], out_sib, esend.at[1], erecv.at[1], r_sib, z)
    out_over = remote(out_part.at[ds(2 * t_own, t_own), :], out_near, esend.at[2], erecv.at[2], r_sib, z)
    out_far_copy = remote(out_part.at[ds(t_own, t_own), :], out_far, esend.at[3], erecv.at[3], r, z_pair)

    def gh2_over(i):
        src = gh2_part.at[ds(2 * t_own + i * tall, tall), :]
        return remote(src, gh2_near.at[ds(i * tall, tall), :], esend.at[4 + i], erecv.at[4 + i], r_sib, z)

    def gh2_far_copy(i):
        src = gh2_part.at[ds(t_own + i * tall, tall), :]
        return remote(src, gh2_far.at[ds(i * tall, tall), :], esend.at[6 + i], erecv.at[6 + i], r, z_pair)

    fc_whole, fc_half, fc_quarter, fc_done, fc_far = (g1w, g2w), (r1a, r1b), (r2a, r2b), (fz1, fz2), (rz1, rz2)
    fc_rows = ((width // 2, width // 4), (part // 2, part // 4))

    def fc_ways(k, m):
        shard = lax.div(z, 2) if k == 0 else 1 - lax.div(z, 2)
        turn = lax.rem(shard + m, 2)
        return r_x + (r_y - r_x) * turn, r_y + (r_x - r_y) * turn, x + (y - x) * turn, y + (x - y) * turn

    def fc_first(k, m):
        n1, _, a1, _ = fc_ways(k, m)
        rows, _ = fc_rows[m]
        src = fc_whole[m].at[k, ds((1 - a1) * rows, rows), :]
        return remote(src, fc_half[m].at[k], s1s.at[k, m], s1r.at[k, m], n1, z)

    def fc_second(k, m):
        _, n2, a1, a2 = fc_ways(k, m)
        rows, less = fc_rows[m]
        src = fc_whole[m].at[k, ds(a1 * rows + (1 - a2) * less, less), :]
        return remote(src, fc_quarter[m].at[k], s2s.at[k, m], s2r.at[k, m], n2, z)

    fc_third = [remote(fc_done[m].at[1], fc_far[m], s3s.at[m], s3r.at[m], r, z_far) for m in range(2)]

    def fc_spread(level, m):
        n1, n2, a1, a2 = fc_ways(0, m)
        rows, less = fc_rows[m]
        place = ds(a1 * rows + a2 * less, less) if level == 0 else ds(a1 * rows, rows)
        held = fc_whole[m].at[0, place, :]
        return remote(held, held, fs.at[level, m], fr.at[level, m], n2 if level == 0 else n1, z)

    fc_share = (
        remote(g1w.at[0], g1w.at[1], ssib.at[0], rsib.at[0], r_sib, z),
        remote(g2w.at[0], g2w.at[1], ssib.at[1], rsib.at[1], r_sib, z),
    )

    def fc_fold_second(k, m):
        fc_first(k, m).wait_recv()
        _, _, a1, a2 = fc_ways(k, m)
        rows, less = fc_rows[m]
        place, whole = ds(a1 * rows + (1 - a2) * less, less), fc_whole[m]
        whole[k, place, :] = whole[k, place, :] + fc_half[m][k, ds((1 - a2) * less, less), :]
        fc_second(k, m).start()

    def fc_fold_third(k):
        for m in range(2):
            fc_second(k, m).wait_recv()
            _, _, a1, a2 = fc_ways(k, m)
            rows, less = fc_rows[m]
            total = fc_whole[m][k, ds(a1 * rows + a2 * less, less), :].astype(F32)
            total = total + fc_half[m][k, ds(a2 * less, less), :].astype(F32) + fc_quarter[m][k].astype(F32)
            fc_done[m][k] = total.astype(BF)
        if k == 1:
            for copy in fc_third:
                copy.start()
        for m in range(2):
            fc_first(k, m).wait_send()
            fc_second(k, m).wait_send()
        if k == 1:
            release(free.at[0], r_sib)
        else:
            release(free.at[1], r_x)
            release(free.at[1], r_y)

    def fc_finish():
        for copy in fc_third:
            copy.wait_recv()
        pl.semaphore_wait(free.at[1], 2)
        for m in range(2):
            _, _, a1, a2 = fc_ways(0, m)
            rows, less = fc_rows[m]
            fc_whole[m][0, ds(a1 * rows + a2 * less, less), :] = fc_done[m][0] + fc_far[m][...]
            fc_spread(0, m).start()

    def fc_widen():
        for m in range(2):
            fc_spread(0, m).wait_recv()
        for m in range(2):
            fc_spread(1, m).start()

    def fc_to_sibling():
        for m in range(2):
            fc_spread(1, m).wait_recv()
        pl.semaphore_wait(free.at[0], 1)
        for copy in fc_share:
            copy.start()

    sizes = tuple(width >> level for level in range(1, 5))

    def hops(j):
        ways = {"x": (r_x, z, x), "y": (r_y, z, y), "z": (r, z_pair, lax.rem(z, 2))}
        return [(r_sib, z, c)] + [ways[axis] for axis in PATHS[j]]

    def base(path, level):
        start = 0
        for (_, _, bit), size in zip(path[:level], sizes):
            start = start + bit * size
        return start

    def core_copy(j):
        src = gw.at[j, ds((1 - c) * half, half), :]
        return remote(src, parts[0].at[j], qs.at[j, 0], qr.at[j, 0], r_sib, z)

    def chunk_copy(j, step):
        path = hops(j)
        if step == 0:
            return core_copy(j)
        if step < 4:
            row, column, bit = path[step]
            start = base(path, step) + (1 - bit) * sizes[step]
            return remote(gw.at[j, ds(start, sizes[step]), :], parts[step].at[j], qs.at[j, step], qr.at[j, step], row, column)
        if step == 4:
            own = gw.at[j, ds(base(path, 4), sizes[3]), :]
            return remote(own, far.at[j], qs.at[j, 4], qr.at[j, 4], r, z_far)
        level = 8 - step
        row, column, _ = path[level]
        held = gw.at[j, ds(base(path, level + 1), sizes[level]), :]
        return remote(held, held, qs.at[j, step], qr.at[j, step], row, column)

    def chunk_step(j, step):
        path, last = hops(j), chunk_copy(j, step - 1)
        last.wait_recv()
        if step <= 4:
            start = base(path, min(step, 4))
            if step < 4:
                start = base(path, step) + (1 - path[step][2]) * sizes[step]
            size = sizes[min(step, 3)]
            total = gw[j, ds(start, size), :].astype(F32)
            for level in range(step):
                total = total + parts[level][j, ds(start - base(path, level + 1), size), :].astype(F32)
            gw[j, ds(start, size), :] = total.astype(BF)
        if step == 5:
            last.wait_send()
            own = ds(base(path, 4), sizes[3])
            gw[j, own, :] = gw[j, own, :] + far[j]
        if 5 <= step <= 8:
            pl.semaphore_wait(chunk_free.at[j, 8 - step], 1)
        if step <= 8:
            chunk_copy(j, step).start()
        if step != 5:
            last.wait_send()
        if step <= 4:
            row, column, _ = path[step - 1]
            pl.semaphore_signal(
                chunk_free.at[j, step - 1], inc=1, device_id={"rows": row, "mlp": column}, device_id_type=MESH
            )

    def small_copy(level):
        row = (r_sib, r_x, r_y)[level]
        return remote(sma.at[level], smr.at[level], sms.at[level], smrs.at[level], row, z)

    def small_z(step):
        src, dst = smz.at[2 * step], smz.at[2 * step + 1]
        return remote(src, dst, smzs.at[step], smzr.at[step], r, (z_pair, z_far)[step])

    barrier = pltpu.get_barrier_semaphore()
    partners = ((r_sib, z), (r_x, z), (r_y, z), (r_diag, z), (r, z_pair), (r, z_far))
    for row, column in partners:
        pl.semaphore_signal(barrier, inc=1, device_id={"rows": row, "mlp": column}, device_id_type=MESH)
    load_c.start()
    load_x.start()
    for copy in load_small:
        copy.start()
    load_qkv.start()
    load_out.start()
    own_shard(0).start()
    own_shard(1).start()
    pl.semaphore_wait(barrier, len(partners))
    gather_copy(0, 0).start()
    gather_copy(1, 0).start()
    load_c.wait()
    for i in range(images):
        work[...] = jnp.zeros_like(work)
        work[0:patches, :] = c_ref[:, i, :]
        cot[i * tall : (i + 1) * tall, :] = work[...]
    cot_copy(0).start()
    cot_copy(1).start()
    load_x.wait()
    for copy in load_small:
        copy.wait()
    for i in range(images):
        forward_rows(i, x_ref, rank_ref, kept_ref, g1_ref, rw_ref, xp, keep, gate, h1, work)

    load_qkv.wait()

    @pl.loop(0, 3 * width // 256)
    def _(j):
        forward_qkv(j, h1, wqkv, qkv)

    @pl.loop(0, HEADS // 2)
    def _(p):
        for i in range(images):
            attend(p, i, width, tall, qkv, keep, probs, context, contextt)

        @pl.when(p == 2)
        def _():
            gather_forward(0)

        @pl.when(p == 4)
        def _():
            gather_forward(1)

    load_out.wait()

    @pl.loop(0, images)
    def _(i):
        forward_out(i, tall, context, wout, xp, keep, gate, g2_ref, attended, middle, tok)
        token_copy(i, 0).start()
        token_copy(i, 1).start()

    own_shard(0).wait()
    own_shard(1).wait()

    def at(block, number, do):
        @pl.when(block == number)
        def _():
            do()

    def before_sibling():
        for i in range(images):
            token_copy(i, 0).wait_recv()
        cot_copy(0).wait_recv()

    h1t[...] = h1[...].T

    @pl.loop(0, 2 * images)
    def _(block):
        at(block, images, before_sibling)
        rows = ds(block * tall, tall)
        hid[rows, 0:part], gpre[rows, 0:part] = mlp_rows(tok[rows, :], cot[rows, :], w1[:, 0:part], w2[0:part, :])

    cot_copy(1).wait_recv()
    cot_copy(2).start()
    for mat in range(2):
        for kind in (1, 2, 3):
            gather_copy(mat, kind).wait_recv()
    for ref in (dg1, dg2, drw):
        ref[...] = jnp.zeros_like(ref)

    def before_near():
        cot_copy(2).wait_recv()
        gh2_to_sib.start()
        out_to_sib.start()

    def forward_token(i):
        token_copy(i, 1).wait_recv()
        token_copy(i, 2).start()

    def send_far(i):
        gh2_over(i).wait_recv()
        rows = ds(t_own + i * tall, tall)
        gh2_part[rows, :] = gh2_part[rows, :] + gh2_near[ds(i * tall, tall), :]
        gh2_far_copy(i).start()

    def before_last():
        send_far(0)
        token_copy(1, 2).wait_recv()

    @pl.loop(0, 8)
    def _(block):
        at(block, 3, lambda: forward_token(0))
        at(block, 4, before_near)
        at(block, 5, lambda: token_copy(0, 2).wait_recv())
        at(block, 6, lambda: forward_token(1))
        at(block, 7, before_last)
        inner = lax.rem(block, 5)
        swap = lax.div(block, 5) * (1 - 2 * inner + 3 * lax.div(inner * (inner - 1), 2))
        spot = block + swap
        rows = ds(spot * tall, tall)

        @pl.when(block < 2 * images)
        def _():
            hid[rows, part:], gpre[rows, part:] = mlp_rows(tok[rows, :], cot[rows, :], w1[:, part:], w2[part:, :])

        @pl.when(block >= 2 * images)
        def _():
            hid[rows, :], gpre[rows, :] = mlp_rows(tok[rows, :], cot[rows, :], w1[...], w2[...])

        share_out = dot_nn(hid[rows, :], w2[...])
        share_gh2 = dot_nt(gpre[rows, :], w1[...])

        @pl.when(block < images)
        def _():
            out[rows, :] = share_out
            gh2[rows, :] = share_gh2

        @pl.when(block >= images)
        def _():
            there = ds(lax.max(spot - images, 0) * tall, tall)
            out_part[there, :] = share_out.astype(BF)
            gh2_part[there, :] = share_gh2.astype(BF)

        at(block, 5, lambda: gh2_over(0).start())
        at(block, 7, lambda: gh2_over(1).start())

    out_over.start()
    turned[...] = tok[...].T
    for m in range(3):
        rows = slice(m * width // 3, (m + 1) * width // 3)
        total = dot_nn(turned[rows, :], gpre[...]).astype(BF)
        g1w[0, rows, :] = total[:, 0:part]
        g1w[1, rows, :] = total[:, part:]
    for k in range(2):
        fc_first(k, 0).start()
    send_far(1)
    turned[...] = hid[...].T
    for m in range(2):
        g2w[m] = dot_nn(turned[m * part : (m + 1) * part, :], cot[...]).astype(BF)
    for k in range(2):
        fc_first(k, 1).start()

    def back_image(i):
        if i == 0:
            gh2_to_sib.wait_recv()
            for n in range(images):
                token_copy(n, 0).wait_send()
                token_copy(n, 1).wait_send()
        gh2_far_copy(i).wait_recv()
        rows = pl.ds(i * tall, tall)
        gh2[rows, :] += gh2_sib[rows, :].astype(F32) + gh2_far[rows, :].astype(F32)
        back_rows(i, tall, cot, gh2, middle, keep, gate, attended, g2_ref, gh2, tok, glogit, dg2)
        context[rows, :] = dot_nt(tok[rows, :], wout[...]).astype(BF)

    def fill(j, total):
        gw[j] = total.astype(BF)
        core_copy(j).start()

    def grad_out_half(n):
        total = 0.0
        for i in range(images):
            total = total + dot_nn(contextt[i], tok[i * tall : (i + 1) * tall, n * half : (n + 1) * half])
        fill(n, total)

    def pair_chunk(p):
        fill(p + 2, dot_nn(h1t[...], pair_columns(qkv, p, width)))

    def finish(i):
        rows = pl.ds(i * tall, tall)
        dy = dot_nt(qkv[rows, :], wqkv[...])
        back_input(i, tall, dy, glogit, rw_ref, xp, h1, g1_ref, gh2, x_ref, dg1, drw)
        if i == images - 1:
            sma[0] = jnp.concatenate([dg1[...], drw[...], dg2[...], jnp.zeros((5, width), F32)], 0)
            small_copy(0).start()

    def small_step(step):
        if step < 3:
            small_copy(step - 1).wait()
            sma[step] = sma[step - 1] + smr[step - 1]
            small_copy(step).start()
        elif step == 3:
            small_copy(2).wait()
            smz[0] = sma[2] + smr[2]
            small_z(0).start()
        else:
            small_z(step - 4).wait()
            if step == 4:
                smz[2] = smz[0] + smz[1]
                small_z(1).start()
            else:
                small_out[...] = smz[2] + smz[3]

    def out_send():
        out_over.wait_recv()
        rows = pl.ds(t_own, t_own)
        out_part[rows, :] = out_part[rows, :] + out_near[...]
        out_far_copy.start()

    def out_finish(i):
        if i == 0:
            out_to_sib.wait_recv()
            out_far_copy.wait_recv()
        rows = pl.ds(i * tall, tall)
        total = middle[rows, :] + out[rows, :] + out_sib[rows, :].astype(F32) + out_far[rows, :].astype(F32)
        c_ref[:, i, :] = total.astype(BF)[0:patches, :]

    def fc_share_end():
        for copy in fc_share:
            copy.wait()

    single = {"fc": fc_finish, "fd": fc_widen, "fe": fc_to_sibling, "ff": fc_share_end, "osend": out_send}
    numbered = (("finish", finish), ("back", back_image), ("out", grad_out_half),
                ("fb", fc_fold_third), ("g", small_step), ("o", out_finish))

    def perform(names):
        for name in names:
            if name in single:
                single[name]()
            elif name[:2] == "fa":
                fc_fold_second(int(name[2]), int(name[3]))
            elif name[0] == "c":
                chunk_step(int(name[1]), int(name[3]))
            else:
                do = next(f for head, f in numbered if name[:-1] == head)
                do(int(name[-1]))

    first, start, stop = ORDER.index("pairs0"), ORDER.index("pairs1"), ORDER.index("last2")
    perform(ORDER[:first])

    @pl.loop(0, HEADS // 4)
    def _(n):
        for p in (2 * n, 2 * n + 1):
            attend_back(p, 0, width, tall, qkv, probs, context)

    perform(ORDER[first + 1 : start])
    marks = [ORDER.index(name) for k in range(3) for name in ("pairs%d" % (k + 1), "last%d" % k)]

    @pl.loop(0, HEADS // 4)
    def _(n):
        for p in (2 * n, 2 * n + 1):
            attend_back(p, 1, width, tall, qkv, probs, context)
        pair_chunk(2 * n)
        for k in range(3):
            at(n, k, lambda k=k: perform(ORDER[marks[2 * k] + 1 : marks[2 * k + 1]]))
        pair_chunk(2 * n + 1)
        for k in range(2):
            at(n, k, lambda k=k: perform(ORDER[marks[2 * k + 1] + 1 : marks[2 * k + 2]]))

    perform(ORDER[stop + 1 :])
    for level in range(2):
        for m in range(2):
            fc_spread(level, m).wait_send()
    for copy in fc_third:
        copy.wait_send()
    for mat in range(2):
        for kind in range(4):
            gather_copy(mat, kind).wait_send()
    for i in range(images):
        token_copy(i, 2).wait_send()
        gh2_over(i).wait_send()
        gh2_far_copy(i).wait_send()
    for hop in range(3):
        cot_copy(hop).wait_send()
    for copy in (gh2_to_sib, out_to_sib, out_over, out_far_copy):
        copy.wait_send()


VMEM = pl.BlockSpec(memory_space=pltpu.VMEM)
ANY = pl.BlockSpec(memory_space=pl.ANY)


def widen_kernel(
    block, gx, gw, gf1, gf2, small, block_out, gx_out, gq_out, go_out, f1_out, f2_out, g1_out, rw_out, g2_out,
    gq_wide, go_wide, f1_wide, f2_wide, store_sem, pass_sem,
):
    _, width, part = gf1.shape
    step = width // WIDEN
    c = lax.rem(lax.axis_index("rows"), 2)
    passed = [pltpu.make_async_copy(src, dst, pass_sem.at[k]) for k, (src, dst) in enumerate(((block, block_out), (gx, gx_out)))]

    def rows_of(i):
        return pl.ds(pl.multiple_of(i * step, 16), step)

    def stores(i):
        rows = rows_of(i)
        pairs = ((gq_wide, gq_out), (go_wide, go_out), (f1_wide, f1_out), (f2_wide, f2_out))
        return [
            pltpu.make_async_copy(src.at[rows, :], dst.at[rows, :], store_sem.at[i, k]) for k, (src, dst) in enumerate(pairs)
        ]

    for copy in passed:
        copy.start()
    g1_out[...], rw_out[...], g2_out[...] = small[0], small[1], small[2]

    @pl.loop(0, WIDEN)
    def _(i):
        rows = rows_of(i)
        for p in range(CHUNKS - 2):
            for b in range(3):
                start = b * width + p * 128
                gq_wide[rows, start : start + 128] = gw[2 + p, rows, b * 128 : (b + 1) * 128].astype(F32)
        for h in range(2):
            go_wide[rows, h * part : (h + 1) * part] = gw[h, rows, :].astype(F32)
        for k in range(2):
            core = c + k - 2 * c * k
            f1_wide[rows, pl.ds(pl.multiple_of(core * part, 128), part)] = gf1[k, rows, :].astype(F32)
        core = lax.div(i * step, part)
        inner = pl.ds(pl.multiple_of(i * step - core * part, 16), step)
        f2_wide[rows, :] = gf2[core + c - 2 * core * c, inner, :].astype(F32)
        for copy in stores(i):
            copy.start()

    @pl.loop(0, WIDEN)
    def _(i):
        for copy in stores(i):
            copy.wait()

    for copy in passed:
        copy.wait()


def widen(*held):
    width = held[3].shape[1]
    tokens = jax.ShapeDtypeStruct(held[0].shape, BF)
    wide = [(width, 3 * width), (width, width), (width, width), (width, width)]
    return pl.pallas_call(
        widen_kernel,
        out_shape=[tokens, tokens] + [jax.ShapeDtypeStruct(dims, F32) for dims in wide] + [jax.ShapeDtypeStruct((width,), F32)] * 3,
        in_specs=[VMEM] * 6,
        out_specs=[ANY] * 6 + [VMEM] * 3,
        scratch_shapes=[pltpu.VMEM(dims, F32) for dims in wide]
        + [pltpu.SemaphoreType.DMA((WIDEN, 4)), pltpu.SemaphoreType.DMA((2,))],
        compiler_params=pltpu.CompilerParams(vmem_limit_bytes=32 * 1024 * 1024),
        name="widen",
    )(*(pltpu.with_memory_space_constraint(a, pltpu.VMEM) for a in held))


def per_device(others, images, patch_rank, kept_count, ln1_gain, router_weight, w_qkv, w_out, ln2_gain, w_fc1, w_fc2, cotangent):
    count, patches, width = images.shape
    tall = -(-patches // 16) * 16
    t = count * tall
    part = w_fc1.shape[1] // 2
    half, eighth = width // 2, width // 8

    def bf(*dims):
        return pltpu.VMEM(dims, BF)

    def f32(*dims):
        return pltpu.VMEM(dims, F32)

    def sem(*dims):
        return pltpu.SemaphoreType.DMA(dims)

    scratch = [
        pltpu.VMEM(patch_rank.shape, jnp.int32), pltpu.SMEM(kept_count.shape, jnp.int32), f32(width), bf(width), f32(width),
        bf(width, 3 * width), bf(width, width), bf(width, 2 * part), bf(2 * part, width),
        bf(t, width), f32(t, 128), f32(t, 128), f32(t, 128), bf(t, width), bf(width, t), bf(t, 3 * width),
        f32(count, HEADS, tall, tall), bf(count, width, tall), bf(t, width), f32(t, width), f32(t, width),
        bf(4 * t, width), bf(4 * t, width), bf(width, 4 * t), f32(t, width), f32(t, width),
        bf(3 * t, width), bf(3 * t, width), bf(t, width), bf(t, width), bf(t, width), bf(t, width), bf(t, width), bf(t, width),
        bf(4 * t, 2 * part), bf(4 * t, 2 * part), bf(tall, width),
        bf(2, width // 2, part), bf(2, part // 2, width), bf(2, width // 4, part), bf(2, part // 4, width),
        bf(2, width // 4, part), bf(2, part // 4, width), bf(width // 4, part), bf(part // 4, width),
        bf(CHUNKS, half, 384), bf(CHUNKS, 2 * eighth, 384), bf(CHUNKS, eighth, 384),
        bf(CHUNKS, eighth // 2, 384), bf(CHUNKS, eighth // 2, 384),
        f32(1, width), f32(1, width), f32(1, width), f32(3, 8, width), f32(3, 8, width), f32(4, 8, width),
        sem(6), sem(2, 4), sem(2, 4), sem(count, 3), sem(count, 3), sem(3), sem(3), sem(8), sem(8),
        sem(2, 2), sem(2, 2), sem(2, 2), sem(2, 2), sem(2), sem(2),
        sem(2, 2), sem(2, 2), sem(2), sem(2), pltpu.SemaphoreType.REGULAR((2,)), pltpu.SemaphoreType.REGULAR((CHUNKS, 4)),
        sem(CHUNKS, 9), sem(CHUNKS, 9), sem(5),
        sem(3), sem(3), sem(2), sem(2),
    ]

    block, gx, gw, gf1, gf2, small = pl.pallas_call(
        mega_kernel,
        out_shape=[
            bf(patches, count, width), bf(patches, count, width), bf(CHUNKS, width, 384),
            bf(2, width, part), bf(2, part, width), f32(8, width),
        ],
        in_specs=[ANY] * 11,
        out_specs=[VMEM] * 6,
        scratch_shapes=scratch,
        compiler_params=pltpu.CompilerParams(
            collective_id=0, has_side_effects=True, vmem_limit_bytes=int(55.5 * 1024) * 1024
        ),
        name="block",
    )(images.transpose(1, 0, 2), patch_rank, kept_count, ln1_gain, router_weight, w_qkv, w_out, ln2_gain, w_fc1, w_fc2,
      cotangent.transpose(1, 0, 2))
    block, gx, gq, go, f1, f2, g1, rw, g2 = widen(block, gx, gw, gf1, gf2, small)
    if others:
        gq, go, f1, f2, g1, rw, g2 = lax.psum((gq, go, f1, f2, g1, rw, g2), "rows", axis_index_groups=others)
    return block.transpose(1, 0, 2), gx.transpose(1, 0, 2), g1, rw, gq, go, g2, f1, f2


def solution(mesh):
    rows = mesh.shape["rows"]
    others = [[8 * g + i for g in range(rows // 8)] for i in range(8)] if rows > 8 else None
    return jax.shard_map(
        functools.partial(per_device, others),
        mesh=mesh,
        in_specs=(
            P(("rows", "mlp"), None, None), P(("rows", "mlp"), None), P(("rows", "mlp")), P(), P(), P(), P(), P(),
            P(None, "mlp"), P("mlp", None), P(("rows", "mlp"), None, None),
        ),
        out_specs=(
            P(("rows", "mlp"), None, None), P(("rows", "mlp"), None, None), P(), P(), P(), P(), P(),
            P(None, "mlp"), P("mlp", None),
        ),
        check_vma=False,
    )
```
